32 devices in a mesh: section: 4 (over y, x), dp: 2 (over core), tensor: 4 (over z).
Axes of the slice: x: 2, y: 2, z: 4, core: 2. Of those that a mesh axis runs over, the one named last changes fastest.
Arguments:
- queries: bfloat16 [1024, 2048], P(('section', 'dp'), 'tensor'), may hold values from -6 to 6
- images: bfloat16 [2, 800, 8192], P('dp', 'section', 'tensor'), may hold values from -6 to 6
- kv_weight: bfloat16 [2, 8192, 256], P(None, 'tensor', 'dp'), may hold values from -0.0625 to 0.0625
- q_gain: float32 [128], replicated, may hold values from 1 to 10
- k_gain: float32 [128], replicated, may hold values from 0.1 to 1.9
- tile_mask: int32 [1024, 4], P(('section', 'dp')), may hold values 0 or 1
Outputs:
- context: bfloat16 [1024, 2048], P(('section', 'dp'), 'tensor')
The draws below stay inside these ranges and needn't reach their ends.
All inputs are finite; a program needn't handle non-finite values. No bound on the sum of `tile_mask` on one device may be relied on, other than what follows from the above.
Results may differ from the reference program's by a relative error of at most 0.04.
Values may be sent and summed in bfloat16 or wider, within the bound.
No kernel may reach another device: no remote copies, remote signals or barrier semaphores. Data moves between devices by JAX's collectives and lax.ppermute only.
A program may use at most 64 MiB of HBM per device.

```python
import math
import jax
import jax.numpy as jnp
from jax import lax

D = 8192
HD = 128
TILES = 4
TOK_DEV = 128
HQ = 16
KVH = 2
IMG = 800
IMAGES = 2
TOKENS = 1024
N_SECTION = 4
N_DP = 2
N_TENSOR = 4


def draw_q_gain(key, part):
    lower = math.log(1.0)
    upper = math.log(4.0)
    return jnp.exp(jax.random.uniform(key, (HD,), jnp.float32, lower, upper))


def set_ends(drawn, key, smallest, top_value):
    dims = drawn.shape
    index_at = [jax.random.randint(jax.random.fold_in(key, axis), (), 0, dims[axis]) for axis in range(len(dims))]
    drawn = drawn.at[tuple(index_at)].set(smallest)
    longest = dims.index(max(dims))
    index_at[longest] = (index_at[longest] + 1) % dims[longest]
    return drawn.at[tuple(index_at)].set(top_value)


def block_levels(own_key, extent, split, smallest, high):
    level = 1.0
    for position, blocks in split:
        draws = jax.random.uniform(jax.random.fold_in(jax.random.fold_in(own_key, 6), position), (blocks,), jnp.float32, smallest / len(split), high / len(split))
        level = level * jnp.repeat(jnp.exp(draws), extent[position] // blocks).reshape((-1,) + (1,) * (len(extent) - 1 - position))
    return level


def noise(rng, dims, scale, bound, shards=(), held_as=jnp.bfloat16):
    drawn = jax.random.normal(rng, dims, jnp.float32) * scale
    if len(shards) > 0:
        drawn = block_levels(rng, dims, shards, -0.22, 0.18) * drawn
    return jnp.clip(drawn, min=-bound, max=bound).astype(held_as)


def setup_inputs(seed: int = 0) -> dict:
    splits = jax.random.split(jax.random.key(seed), 7)
    queries = noise(splits[0], (TOKENS, HQ * HD), 1.0, 6.0, ((0, 8), (1, 4)))
    images = noise(splits[1], (IMAGES, IMG, D), 1.0, 6.0, ((0, 2), (1, 4), (2, 4)))
    kv_weight = noise(splits[2], (2, D, KVH * HD), D ** -0.5, 0.0625, ((1, 4), (2, 2)))
    q_gain = draw_q_gain(jax.random.fold_in(splits[6], 71), 0)
    k_gain = jnp.clip(1.0 + 0.18 * jax.random.normal(splits[4], (HD,), jnp.float32), 0.1, 1.9)
    tile_mask = set_ends((jax.random.randint(splits[5], (TOKENS, TILES), 0, 4) < 3).astype(jnp.int32), jax.random.fold_in(splits[5], 1), 0, 1)
    return {"queries": queries, "images": images, "kv_weight": kv_weight, "q_gain": q_gain, "k_gain": k_gain, "tile_mask": tile_mask}


EPSILON = 1e-05
MASKED_SCORE = -1e+30

def normalize(values, gain_vec):
    mean_sq = lax.optimization_barrier(jnp.mean(values * values, axis=-1, keepdims=True))
    return values * lax.rsqrt(mean_sq + EPSILON) * gain_vec

def reference(queries, images, kv_weight, q_gain, k_gain, tile_mask):
    kv_width = KVH * HD
    cat_weight = jnp.concatenate([kv_weight[0], kv_weight[1]], axis=1)
    block_len = D // N_TENSOR
    q_all = queries.reshape(N_SECTION, N_DP, TOK_DEV, HQ, HD)
    mask_all = tile_mask.reshape(N_SECTION, N_DP, TOK_DEV, TILES)
    tile_len = IMG // TILES
    key_tile = jnp.arange(IMG, dtype=jnp.int32) // tile_len
    group_size = HQ // KVH
    results = []
    for image_idx in range(N_DP):
        features = images[image_idx]
        summed = jnp.zeros((IMG, 2 * kv_width), jnp.float32)
        for shard_idx in range(N_TENSOR):
            partial_value = jnp.dot(features[:, shard_idx * block_len:(shard_idx + 1) * block_len], cat_weight[shard_idx * block_len:(shard_idx + 1) * block_len], preferred_element_type=jnp.float32)
            summed = summed + lax.optimization_barrier(partial_value.astype(jnp.bfloat16)).astype(jnp.float32)
        key_rows = normalize(summed[:, :kv_width].reshape(IMG, KVH, HD), k_gain).astype(jnp.bfloat16)
        value_rows = summed[:, kv_width:].reshape(IMG, KVH, HD).astype(jnp.bfloat16)
        query_rows = q_all[:, image_idx].reshape(-1, HQ, HD).astype(jnp.float32)
        q_normed = (normalize(query_rows, q_gain) * HD ** (-0.5)).astype(jnp.bfloat16)
        tile_rows = mask_all[:, image_idx].reshape(-1, TILES)
        visible = jnp.take(tile_rows, key_tile, axis=1) > 0
        has_any = lax.optimization_barrier(jnp.sum(tile_rows, axis=1)) > 0

        def one_head(head_idx):
            q_head = lax.dynamic_index_in_dim(q_normed, head_idx, 1, keepdims=False)
            kv_idx = head_idx // group_size
            key_head = lax.dynamic_index_in_dim(key_rows, kv_idx, 1, keepdims=False)
            value_head = lax.dynamic_index_in_dim(value_rows, kv_idx, 1, keepdims=False)
            scores = jnp.dot(q_head, key_head.T, preferred_element_type=jnp.float32)
            row_top = lax.optimization_barrier(jnp.max(jnp.where(visible, scores, MASKED_SCORE), axis=1, keepdims=True))
            probabilities = jnp.where(visible, jnp.exp(scores - row_top), 0.0)
            row_total = lax.optimization_barrier(jnp.sum(probabilities, axis=1))
            mixture = jnp.dot(probabilities.astype(jnp.bfloat16), value_head, preferred_element_type=jnp.float32)
            divided = mixture / jnp.where(has_any, row_total, 1.0)[:, None]
            return jnp.where(has_any[:, None], divided, 0.0).astype(jnp.bfloat16)
        heads_out = lax.map(one_head, jnp.arange(HQ, dtype=jnp.int32))
        results.append(jnp.transpose(heads_out, (1, 0, 2)).reshape(N_SECTION, TOK_DEV, HQ * HD))
    return jnp.stack(results, axis=1).reshape(TOKENS, HQ * HD)
```

```python
import functools

import jax
import jax.numpy as jnp
from jax import lax
from jax.experimental import pallas as pl
from jax.experimental.pallas import tpu as pltpu
from jax.sharding import PartitionSpec as P

EPSILON = 1e-05
MASKED_SCORE = -1e30
TOP_FLOOR = -1e29
VMEM = pl.BlockSpec(memory_space=pltpu.VMEM)


def normalize(values, gain_vec):
    mean_sq = jnp.mean(values * values, axis=-1, keepdims=True)
    return values * lax.rsqrt(mean_sq + EPSILON) * gain_vec


def project(x, w):
    width = w.shape[2]
    both = jnp.dot(
        x, jnp.concatenate([w[0], w[1]], axis=1), preferred_element_type=jnp.float32
    ).astype(jnp.bfloat16)
    return both[:, :width], both[:, width:]


def own_kernel(head_dim, x_ref, w_ref, q_ref, q_gain_ref, mask_ref, own_ref, qt_ref, bias_ref):
    keys, values = project(x_ref[0], w_ref[...])
    for head in range(keys.shape[1] // head_dim):
        cols = slice(head * head_dim, (head + 1) * head_dim)
        own_ref[2 * head] = keys[:, cols]
        own_ref[2 * head + 1] = values[:, cols]
    tokens = q_ref.shape[0]
    bias = jnp.where(mask_ref[...] > 0, 0.0, MASKED_SCORE).astype(jnp.float32).T
    for head in range(q_ref.shape[1] // head_dim):
        rows = q_ref[:, head * head_dim : (head + 1) * head_dim].astype(jnp.float32)
        normed = normalize(rows, q_gain_ref[...]) * head_dim ** (-0.5)
        qt_ref[:, head * tokens : (head + 1) * tokens] = normed.T.astype(jnp.bfloat16)
        bias_ref[:, head * tokens : (head + 1) * tokens] = bias


def other_kernel(head_dim, n_dp, x_ref, own_ref, *refs):
    w_refs = refs[: n_dp - 1]
    out_refs = refs[n_dp - 1 : -1]
    held = refs[-1]
    d = lax.axis_index("dp")
    t = lax.axis_index("tensor")
    pieces = own_ref.shape[0]
    for i in range(pieces):
        held[d * pieces + i] = own_ref[i]
    x = x_ref[0]
    for k in range(1, n_dp):
        keys, values = project(x, w_refs[k - 1][...])
        base = (d ^ k) * pieces
        for head in range(pieces // 2):
            cols = slice(head * head_dim, (head + 1) * head_dim)
            held[base + 2 * head] = keys[:, cols]
            held[base + 2 * head + 1] = values[:, cols]
    for k, out in enumerate(out_refs):
        out[...] = held[t ^ k]


def sum_kernel(k_gain_ref, *refs):
    out = refs[-1]
    total = refs[0][...].astype(jnp.float32)
    for ref in refs[1:-1]:
        total = total + ref[...].astype(jnp.float32)
    is_key = lax.axis_index("tensor") % 2 == 0
    out[...] = jnp.where(is_key, normalize(total, k_gain_ref[...]), total).astype(jnp.bfloat16)


def attend_kernel(n_section, tile_len, qt_ref, bias_ref, *refs):
    out = refs[-1]
    same = refs[:n_section]
    pair = refs[n_section:-1]
    s = lax.axis_index("section")
    is_key = lax.axis_index("tensor") % 2 == 0
    rows, head_dim = same[0].shape
    qt = qt_ref[...]
    scores, biases, tops = [], [], []
    for k in range(n_section):
        keys = jnp.where(is_key, same[k][...], pair[k][...])
        part = jnp.dot(keys, qt, preferred_element_type=jnp.float32)
        bias = bias_ref[pl.ds(((s ^ k) * rows) // tile_len, 1), :]
        scores.append(part)
        biases.append(bias)
        tops.append(jnp.max(part, axis=0, keepdims=True) + bias)
    top = functools.reduce(jnp.maximum, tops)
    top = jnp.maximum(top, TOP_FLOOR)
    row_sum = jnp.zeros_like(top)
    mixed = jnp.zeros((head_dim, qt.shape[1]), jnp.float32)
    for k in range(n_section):
        weights = jnp.exp(scores[k] + (biases[k] - top))
        row_sum = row_sum + jnp.sum(weights, axis=0, keepdims=True)
        values = jnp.where(is_key, pair[k][...], same[k][...])
        mixed = mixed + lax.dot_general(
            values,
            weights.astype(jnp.bfloat16),
            (((0,), (0,)), ((), ())),
            preferred_element_type=jnp.float32,
        )
    has_any = jnp.max(bias_ref[...], axis=0, keepdims=True) > -1.0
    context = jnp.where(has_any, mixed / jnp.where(has_any, row_sum, 1.0), 0.0)
    tokens = out.shape[0]
    for head in range(out.shape[1] // head_dim):
        out[:, head * head_dim : (head + 1) * head_dim] = context[
            :, head * tokens : (head + 1) * tokens
        ].T.astype(jnp.bfloat16)


def on_device(queries, images, kv_weight, q_gain, k_gain, tile_mask):
    n_section = lax.axis_size("section")
    n_dp = lax.axis_size("dp")
    n_tensor = lax.axis_size("tensor")
    head_dim = q_gain.shape[0]
    tokens, q_width = queries.shape
    rows = images.shape[1]
    tiles = tile_mask.shape[1]
    own_heads = kv_weight.shape[2] // head_dim
    tile_len = rows * n_section // tiles
    assert own_heads * n_dp * 2 == n_tensor and tile_len % rows == 0
    pairs = tokens * (q_width // head_dim)
    piece = jax.ShapeDtypeStruct((rows, head_dim), jnp.bfloat16)
    params = pltpu.CompilerParams(vmem_limit_bytes=48 * 1024 * 1024)

    def swap(value, axis, k, size):
        return lax.ppermute(value, axis, [(i, i ^ k) for i in range(size)])

    others = [swap(kv_weight, "dp", k, n_dp) for k in range(1, n_dp)]
    own, qt, bias = pl.pallas_call(
        functools.partial(own_kernel, head_dim),
        out_shape=[
            jax.ShapeDtypeStruct((2 * own_heads, rows, head_dim), jnp.bfloat16),
            jax.ShapeDtypeStruct((head_dim, pairs), jnp.bfloat16),
            jax.ShapeDtypeStruct((tiles, pairs), jnp.float32),
        ],
        in_specs=[VMEM] * 5,
        out_specs=[VMEM] * 3,
        compiler_params=params,
        cost_estimate=pl.CostEstimate(
            flops=2 * rows * images.shape[2] * 2 * kv_weight.shape[2],
            bytes_accessed=4 * 1024 * 1024,
            transcendentals=0,
        ),
        name="own_head",
    )(images, kv_weight, queries, q_gain.reshape(1, -1), tile_mask)
    parts = pl.pallas_call(
        functools.partial(other_kernel, head_dim, n_dp),
        out_shape=[piece] * n_tensor,
        in_specs=[VMEM] * (n_dp + 1),
        out_specs=[VMEM] * n_tensor,
        scratch_shapes=[pltpu.VMEM((n_tensor, rows, head_dim), jnp.bfloat16)],
        compiler_params=params,
        name="other_heads",
    )(images, own, *others)
    arrived = [parts[0]] + [swap(parts[k], "tensor", k, n_tensor) for k in range(1, n_tensor)]
    summed = pl.pallas_call(
        sum_kernel,
        out_shape=piece,
        in_specs=[VMEM] * (n_tensor + 1),
        out_specs=VMEM,
        compiler_params=params,
        name="sum_norm",
    )(k_gain.reshape(1, -1), *arrived)
    axes = ("section", "tensor")
    gathered = []
    for kt in range(2):
        for ks in range(n_section):
            if kt == 0 and ks == 0:
                gathered.append(summed)
                continue
            hops = [
                (a * n_tensor + b, (a ^ ks) * n_tensor + (b ^ kt))
                for a in range(n_section)
                for b in range(n_tensor)
            ]
            gathered.append(lax.ppermute(summed, axes, hops))
    return pl.pallas_call(
        functools.partial(attend_kernel, n_section, tile_len),
        out_shape=jax.ShapeDtypeStruct((tokens, q_width), jnp.bfloat16),
        in_specs=[VMEM] * (2 * n_section + 2),
        out_specs=VMEM,
        compiler_params=params,
        name="attend",
    )(qt, bias, *gathered)


def solution(mesh):
    in_specs = (
        P(("section", "dp"), "tensor"),
        P("dp", "section", "tensor"),
        P(None, "tensor", "dp"),
        P(),
        P(),
        P(("section", "dp"), None),
    )
    out_specs = P(("section", "dp"), "tensor")
    return jax.shard_map(
        on_device, mesh=mesh, in_specs=in_specs, out_specs=out_specs, check_vma=False
    )
```

```python
import functools

import jax
import jax.numpy as jnp
from jax import lax
from jax.experimental import pallas as pl
from jax.experimental.pallas import tpu as pltpu
from jax.sharding import PartitionSpec as P

EPSILON = 1e-05
MASKED_SCORE = -1e30
TOP_FLOOR = -1e29
VMEM = pl.BlockSpec(memory_space=pltpu.VMEM)
HBM = pl.BlockSpec(memory_space=pltpu.HBM)
F32 = jnp.float32
MIB = 1024 * 1024
LIMIT = 24 * MIB
BF16 = jnp.bfloat16


def shape_of(dims, dtype=BF16):
    return jax.ShapeDtypeStruct(dims, dtype)


def call(
    kernel, outs, n_in, name, flops=0, size=0, exps=0, in_specs=None, scratch=()
):
    many = isinstance(outs, list)
    return pl.pallas_call(
        kernel,
        out_shape=outs,
        in_specs=in_specs or [VMEM] * n_in,
        out_specs=[VMEM] * len(outs) if many else VMEM,
        scratch_shapes=scratch,
        compiler_params=pltpu.CompilerParams(vmem_limit_bytes=LIMIT),
        cost_estimate=pl.CostEstimate(flops=flops, bytes_accessed=size, transcendentals=exps),
        name=name,
    )


def normalize(values, gain_vec):
    mean_sq = jnp.mean(values * values, axis=-1, keepdims=True)
    return values * lax.rsqrt(mean_sq + EPSILON) * gain_vec


def project(x, w):
    return jnp.dot(
        x, jnp.concatenate([w[0], w[1]], axis=1), preferred_element_type=F32
    ).astype(BF16)


def store_heads(ref, base, both, head_dim):
    width = both.shape[1] // 2
    for head in range(width // head_dim):
        lo = head * head_dim
        ref[base + head, 0] = both[:, lo : lo + head_dim]
        ref[base + head, 1] = both[:, width + lo : width + lo + head_dim]


def own_kernel(
    head_dim, x_hbm, w_hbm, q_hbm, q_gain_hbm, k_gain_hbm, mask_hbm,
    own_ref, x_ref, k_gain_ref, qt_ref, bias_ref,
    w_ref, q_ref, q_gain_ref, mask_ref, sems,
):
    moves = [
        (q_hbm, q_ref),
        (q_gain_hbm, q_gain_ref),
        (mask_hbm, mask_ref),
        (k_gain_hbm, k_gain_ref),
        (x_hbm, x_ref),
        (w_hbm, w_ref),
    ]
    copies = [pltpu.make_async_copy(a, b, sems.at[i]) for i, (a, b) in enumerate(moves)]
    for copy in copies:
        copy.start()
    for copy in copies[:4]:
        copy.wait()
    tokens = q_ref.shape[0]
    bias = jnp.where(mask_ref[...] > 0, 0.0, MASKED_SCORE).astype(F32)
    for head in range(q_ref.shape[1] // head_dim):
        rows = q_ref[:, head * head_dim : (head + 1) * head_dim].astype(F32)
        normed = normalize(rows, q_gain_ref[...]) * head_dim ** (-0.5)
        qt_ref[:, head * tokens : (head + 1) * tokens] = normed.T.astype(BF16)
        bias_ref[:, head * tokens : (head + 1) * tokens] = bias
    for copy in copies[4:]:
        copy.wait()
    store_heads(own_ref, 0, project(x_ref[0], w_ref[...]), head_dim)


def split_half(held, send_ref, keep_ref, partner_heads, own_heads):
    for i in range(send_ref.shape[0]):
        send_ref[i] = held[partner_heads + i]
        keep_ref[i] = held[own_heads + i]


def other_kernel(head_dim, n_dp, n_tensor, x_ref, own_ref, *refs):
    w_refs = refs[: n_dp - 1]
    send_ref, keep_ref, held = refs[n_dp - 1 :]
    d = lax.axis_index("dp")
    t = lax.axis_index("tensor")
    own_heads = own_ref.shape[0]
    held[pl.ds(d * own_heads, own_heads)] = own_ref[...]
    for k in range(1, n_dp):
        store_heads(held, (d ^ k) * own_heads, project(x_ref[0], w_refs[k - 1][...]), head_dim)
    half = send_ref.shape[0]
    upper = t // (n_tensor // 2)
    split_half(held, send_ref, keep_ref, (1 - upper) * half, upper * half)


def add_kernel(bit, keep_ref, arrived_ref, send_ref, next_ref, held):
    held[...] = (keep_ref[...].astype(F32) + arrived_ref[...].astype(F32)).astype(BF16)
    half = send_ref.shape[0]
    upper = (lax.axis_index("tensor") // bit) % 2
    split_half(held, send_ref, next_ref, (1 - upper) * half, upper * half)


def add_last_kernel(keep_ref, arrived_ref, out_ref):
    out_ref[...] = (keep_ref[...].astype(F32) + arrived_ref[...].astype(F32)).astype(BF16)


def norm_kernel(k_gain_ref, keep_ref, arrived_ref, kv_ref):
    total = keep_ref[0].astype(F32) + arrived_ref[0].astype(F32)
    kv_ref[0] = normalize(total[0], k_gain_ref[...]).astype(BF16)
    kv_ref[1] = total[1].astype(BF16)


def attend_kernel(steps, tile_len, first, last, head_dim, qt_ref, bias_ref, *refs):
    parts, refs = refs[: len(steps)], refs[len(steps) :]
    if not first:
        top_in, sum_in, mixed_in = refs[:3]
        refs = refs[3:]
    s = lax.axis_index("section")
    rows = parts[0].shape[1]
    qt = qt_ref[...]
    scores, biases = [], []
    top = TOP_FLOOR if first else top_in[...]
    for k, part in zip(steps, parts):
        score = jnp.dot(part[0], qt, preferred_element_type=F32)
        bias = bias_ref[pl.ds(((s ^ k) * rows) // tile_len, 1), :]
        scores.append(score)
        biases.append(bias)
        top = jnp.maximum(top, jnp.max(score, axis=0, keepdims=True) + bias)
    row_sum, mixed = 0.0, 0.0
    if not first:
        scale = jnp.exp(top_in[...] - top)
        row_sum = sum_in[...] * scale
        mixed = mixed_in[...] * scale
    for part, score, bias in zip(parts, scores, biases):
        weights = jnp.exp(score + (bias - top))
        row_sum = row_sum + jnp.sum(weights, axis=0, keepdims=True)
        mixed = mixed + lax.dot_general(
            part[1], weights.astype(BF16), (((0,), (0,)), ((), ())), preferred_element_type=F32
        )
    if not last:
        top_out, sum_out, mixed_out = refs
        top_out[...] = top
        sum_out[...] = row_sum
        mixed_out[...] = mixed
        return
    (out,) = refs
    has_any = jnp.max(bias_ref[...], axis=0, keepdims=True) > -1.0
    context = jnp.where(has_any, mixed / jnp.where(has_any, row_sum, 1.0), 0.0)
    tokens = out.shape[0]
    for head in range(out.shape[1] // head_dim):
        out[:, head * head_dim : (head + 1) * head_dim] = context[
            :, head * tokens : (head + 1) * tokens
        ].T.astype(BF16)


def on_device(queries, images, kv_weight, q_gain, k_gain, tile_mask):
    n_section = lax.axis_size("section")
    n_dp = lax.axis_size("dp")
    n_tensor = lax.axis_size("tensor")
    head_dim = q_gain.shape[0]
    tokens, q_width = queries.shape
    rows, features = images.shape[1:]
    tiles = tile_mask.shape[1]
    own_heads = kv_weight.shape[2] // head_dim
    heads = own_heads * n_dp
    tile_len = rows * n_section // tiles
    assert heads * 2 == n_tensor and tile_len % rows == 0
    pairs = tokens * (q_width // head_dim)
    work = 4 * rows * features * kv_weight.shape[2]

    def swap(value, axis, k):
        return lax.ppermute(value, axis, [(i, i ^ k) for i in range(lax.axis_size(axis))])

    others = [swap(kv_weight, "dp", k) for k in range(1, n_dp)]
    own, x, gain, qt, bias = call(
        functools.partial(own_kernel, head_dim),
        [
            shape_of((own_heads, 2, rows, head_dim)),
            shape_of(images.shape),
            shape_of((1, head_dim), F32),
            shape_of((head_dim, pairs)),
            shape_of((tiles, pairs), F32),
        ],
        6,
        "own_head",
        flops=work,
        size=2 * (images.size + kv_weight.size),
        in_specs=[HBM] * 6,
        scratch=[
            pltpu.VMEM(kv_weight.shape, BF16),
            pltpu.VMEM(queries.shape, BF16),
            pltpu.VMEM((1, head_dim), F32),
            pltpu.VMEM((tiles, tokens), jnp.int32),
            pltpu.SemaphoreType.DMA((6,)),
        ],
    )(
        *[
            pltpu.with_memory_space_constraint(value, pltpu.HBM)
            for value in (
                images, kv_weight, queries, q_gain.reshape(1, -1), k_gain.reshape(1, -1), tile_mask.T,
            )
        ]
    )
    half = shape_of((heads // 2, 2, rows, head_dim))
    send, keep = call(
        functools.partial(other_kernel, head_dim, n_dp, n_tensor),
        [half, half],
        n_dp + 1,
        "other_heads",
        flops=work * (n_dp - 1),
        scratch=[pltpu.VMEM((heads, 2, rows, head_dim), BF16)],
    )(x, own, *others)
    bit = n_tensor // 2
    while bit > 1:
        arrived = swap(send, "tensor", bit)
        bit //= 2
        now = keep.shape
        if bit > 1:
            half = shape_of((now[0] // 2, *now[1:]))
            send, keep = call(
                functools.partial(add_kernel, bit),
                [half, half],
                2,
                "add_part",
                scratch=[pltpu.VMEM(now, BF16)],
            )(keep, arrived)
        else:
            send = keep = call(add_last_kernel, shape_of(now), 2, "add_pair")(keep, arrived)
    arrived = swap(send, "tensor", 1)
    kv = call(norm_kernel, shape_of((2, rows, head_dim)), 3, "sum_norm")(gain, keep, arrived)

    gathered = [kv] + [swap(kv, "section", k) for k in range(1, n_section)]
    state = []
    for steps in ([0], list(range(1, n_section - 1)), [n_section - 1]):
        first, last = steps[0] == 0, steps[-1] == n_section - 1
        outs = (
            shape_of((tokens, q_width))
            if last
            else [shape_of((1, pairs), F32), shape_of((1, pairs), F32), shape_of((head_dim, pairs), F32)]
        )
        state = call(
            functools.partial(attend_kernel, steps, tile_len, first, last, head_dim),
            outs,
            2 + len(steps) + len(state),
            "attend",
            flops=4 * pairs * rows * head_dim * len(steps),
            exps=pairs * rows * len(steps),
        )(qt, bias, *[gathered[k] for k in steps], *state)
    return state


def solution(mesh):
    in_specs = (
        P(("section", "dp"), "tensor"),
        P("dp", "section", "tensor"),
        P(None, "tensor", "dp"),
        P(),
        P(),
        P(("section", "dp"), None),
    )
    out_specs = P(("section", "dp"), "tensor")
    return jax.shard_map(
        on_device, mesh=mesh, in_specs=in_specs, out_specs=out_specs, check_vma=False
    )
```

```python
import functools

import jax
import jax.numpy as jnp
from jax import lax
from jax.experimental import pallas as pl
from jax.experimental.pallas import tpu as pltpu
from jax.sharding import PartitionSpec as P

EPSILON = 1e-05
MASKED_SCORE = -1e30
TOP_FLOOR = -1e29
VMEM = pl.BlockSpec(memory_space=pltpu.VMEM)
HBM = pl.BlockSpec(memory_space=pltpu.HBM)
F32 = jnp.float32
BF16 = jnp.bfloat16
LIMIT = 24 * 1024 * 1024
CHUNKS = 4


def shape_of(dims, dtype=BF16):
    return jax.ShapeDtypeStruct(dims, dtype)


def call(kernel, outs, name, in_specs, flops=0, size=0, exps=0, scratch=()):
    many = isinstance(outs, list)
    return pl.pallas_call(
        kernel,
        out_shape=outs,
        in_specs=in_specs,
        out_specs=[VMEM] * len(outs) if many else VMEM,
        scratch_shapes=scratch,
        compiler_params=pltpu.CompilerParams(vmem_limit_bytes=LIMIT),
        cost_estimate=pl.CostEstimate(flops=flops, bytes_accessed=size, transcendentals=exps),
        name=name,
    )


def in_hbm(*values):
    return [pltpu.with_memory_space_constraint(value, pltpu.HBM) for value in values]


def normalize(values, gain_vec):
    mean_sq = jnp.mean(values * values, axis=-1, keepdims=True)
    return values * lax.rsqrt(mean_sq + EPSILON) * gain_vec


def part_pair(both, send_ref, keep_ref):
    width = both.shape[1] // 2
    both = both.astype(BF16)
    even = lax.axis_index("tensor") % 2 == 0
    for head in range(send_ref.shape[0]):
        lo = head * send_ref.shape[2]
        keys = both[:, lo : lo + send_ref.shape[2]]
        values = both[:, width + lo : width + lo + send_ref.shape[2]]
        send_ref[head] = jnp.where(even, values, keys)
        keep_ref[head] = jnp.where(even, keys, values)


def own_kernel(x_hbm, w_hbm, send_ref, keep_ref, x_ref, w_ref, sems):
    step = x_ref.shape[1] // CHUNKS
    copies = []
    for i in range(CHUNKS):
        cols = pl.ds(i * step, step)
        copies.append(
            (
                pltpu.make_async_copy(w_hbm.at[:, cols], w_ref.at[:, cols], sems.at[0, i]),
                pltpu.make_async_copy(x_hbm.at[0, :, cols], x_ref.at[:, cols], sems.at[1, i]),
            )
        )
        for copy in copies[-1]:
            copy.start()
    both = None
    for i in range(CHUNKS):
        for copy in copies[i]:
            copy.wait()
        cols = slice(i * step, (i + 1) * step)
        part = jnp.dot(
            x_ref[:, cols],
            jnp.concatenate([w_ref[0, cols], w_ref[1, cols]], axis=1),
            preferred_element_type=F32,
        )
        both = part if both is None else both + part
    part_pair(both, send_ref, keep_ref)


def other_kernel(x_ref, w_ref, send_ref, keep_ref):
    both = jnp.dot(
        x_ref[...],
        jnp.concatenate([w_ref[0], w_ref[1]], axis=1),
        preferred_element_type=F32,
    )
    part_pair(both, send_ref, keep_ref)


def query_kernel(
    q_hbm, q_gain_hbm, k_gain_hbm, mask_hbm, qt_ref, bias_ref, k_gain_ref,
    q_ref, q_gain_ref, mask_ref, sems,
):
    moves = [
        (q_hbm, q_ref),
        (q_gain_hbm, q_gain_ref),
        (mask_hbm, mask_ref),
        (k_gain_hbm, k_gain_ref),
    ]
    copies = [pltpu.make_async_copy(a, b, sems.at[i]) for i, (a, b) in enumerate(moves)]
    for copy in copies:
        copy.start()
    for copy in copies:
        copy.wait()
    tokens = q_ref.shape[0]
    head_dim = q_gain_ref.shape[1]
    bias = jnp.where(mask_ref[...] > 0, 0.0, MASKED_SCORE).astype(F32)
    for head in range(q_ref.shape[1] // head_dim):
        rows = q_ref[:, head * head_dim : (head + 1) * head_dim].astype(F32)
        normed = normalize(rows, q_gain_ref[...]) * head_dim ** (-0.5)
        qt_ref[:, head * tokens : (head + 1) * tokens] = normed.T.astype(BF16)
        bias_ref[:, head * tokens : (head + 1) * tokens] = bias


def pair_kernel(k, keep_ref, arrived_ref, mine_ref, *send_refs):
    heads = keep_ref.shape[0]
    pair = lax.axis_index("tensor") // 2
    group = lax.axis_index("dp") ^ k
    own = pair % heads
    total = keep_ref[own].astype(F32) + arrived_ref[own].astype(F32)
    mine_ref[...] = jnp.where(pair // heads == group, total, 0.0)
    for j, ref in enumerate(send_refs, 1):
        head = (pair ^ j) % heads
        ref[...] = (keep_ref[head].astype(F32) + arrived_ref[head].astype(F32)).astype(BF16)


def norm_kernel(k_gain_ref, *refs):
    out = refs[-1]
    total = refs[0][...].astype(F32)
    for ref in refs[1:-1]:
        total = total + ref[...].astype(F32)
    even = lax.axis_index("tensor") % 2 == 0
    out[...] = jnp.where(even, normalize(total, k_gain_ref[...]), total).astype(BF16)


def attend_kernel(step, tile_len, first, last, qt_ref, bias_ref, same_ref, pair_ref, *refs):
    rows, head_dim = same_ref.shape
    even = lax.axis_index("tensor") % 2 == 0
    keys = jnp.where(even, same_ref[...], pair_ref[...])
    values = jnp.where(even, pair_ref[...], same_ref[...])
    section = lax.axis_index("section") ^ step
    bias = bias_ref[pl.ds((section * rows) // tile_len, 1), :]
    score = jnp.dot(keys, qt_ref[...], preferred_element_type=F32)
    top = jnp.maximum(jnp.max(score, axis=0, keepdims=True) + bias, TOP_FLOOR)
    if not first:
        top_in, sum_in, mixed_in = refs[:3]
        refs = refs[3:]
        top = jnp.maximum(top, top_in[...])
    weights = jnp.exp(score + (bias - top))
    row_sum = jnp.sum(weights, axis=0, keepdims=True)
    mixed = lax.dot_general(
        values, weights.astype(BF16), (((0,), (0,)), ((), ())), preferred_element_type=F32
    )
    if not first:
        scale = jnp.exp(top_in[...] - top)
        row_sum = row_sum + sum_in[...] * scale
        mixed = mixed + mixed_in[...] * scale
    if not last:
        top_out, sum_out, mixed_out = refs
        top_out[...] = top
        sum_out[...] = row_sum
        mixed_out[...] = mixed
        return
    (out,) = refs
    has_any = jnp.max(bias_ref[...], axis=0, keepdims=True) > -1.0
    context = jnp.where(has_any, mixed / jnp.where(has_any, row_sum, 1.0), 0.0)
    tokens = out.shape[0]
    for head in range(out.shape[1] // head_dim):
        out[:, head * head_dim : (head + 1) * head_dim] = context[
            :, head * tokens : (head + 1) * tokens
        ].T.astype(BF16)


def on_device(queries, images, kv_weight, q_gain, k_gain, tile_mask):
    n_section = lax.axis_size("section")
    n_dp = lax.axis_size("dp")
    n_tensor = lax.axis_size("tensor")
    head_dim = q_gain.shape[0]
    tokens, q_width = queries.shape
    rows, features = images.shape[1:]
    tiles = tile_mask.shape[1]
    own_heads = kv_weight.shape[2] // head_dim
    n_pair = n_tensor // 2
    tile_len = rows * n_section // tiles
    assert own_heads * n_dp == n_pair and tile_len % rows == 0
    pairs = tokens * (q_width // head_dim)
    work = 4 * rows * features * kv_weight.shape[2]

    def swap(value, axis, k):
        return lax.ppermute(value, axis, [(i, i ^ k) for i in range(lax.axis_size(axis))])

    others = [swap(kv_weight, "dp", k) for k in range(1, n_dp)]
    halves = [shape_of((own_heads, rows, head_dim))] * 2
    send, keep, x = call(
        own_kernel,
        [*halves, shape_of((rows, features))],
        "own_head",
        [HBM] * 2,
        flops=work,
        size=2 * (images.size + kv_weight.size),
        scratch=[pltpu.VMEM(kv_weight.shape, BF16), pltpu.SemaphoreType.DMA((2, CHUNKS))],
    )(*in_hbm(images, kv_weight))
    qt, bias, gain = call(
        query_kernel,
        [
            shape_of((head_dim, pairs)),
            shape_of((tiles, pairs), F32),
            shape_of((1, head_dim), F32),
        ],
        "queries",
        [HBM] * 4,
        size=2 * queries.size,
        scratch=[
            pltpu.VMEM(queries.shape, BF16),
            pltpu.VMEM((1, head_dim), F32),
            pltpu.VMEM((tiles, tokens), jnp.int32),
            pltpu.SemaphoreType.DMA((4,)),
        ],
    )(*in_hbm(queries, q_gain.reshape(1, -1), k_gain.reshape(1, -1), tile_mask.T))

    kept, arrived = [], []
    for k in range(n_dp):
        if k > 0:
            send, keep = call(
                other_kernel, halves, "other_head", [VMEM] * 2, flops=work
            )(x, others[k - 1])
        outs = [shape_of((rows, head_dim), F32)] + [shape_of((rows, head_dim))] * (n_pair - 1)
        mine, *sends = call(functools.partial(pair_kernel, k), outs, "pair_sum", [VMEM] * 2)(
            keep, swap(send, "tensor", 1)
        )
        kept.append(mine)
        for j, value in enumerate(sends, 1):
            hops = [
                (d * n_tensor + t, d * n_tensor + (t ^ (2 * j)))
                for d in range(n_dp)
                for t in range(n_tensor)
                if ((t // 2) ^ j) // own_heads == d ^ k
            ]
            arrived.append(lax.ppermute(value, ("dp", "tensor"), hops))
    mine = call(
        norm_kernel,
        shape_of((rows, head_dim)),
        "sum_norm",
        [VMEM] * (1 + len(kept) + len(arrived)),
    )(gain, *kept, *arrived)

    same, pair = [mine], [swap(mine, "tensor", 1)]
    for step in range(1, n_section):
        high = 1 << (step.bit_length() - 1)
        same.append(swap(same[step ^ high], "section", high))
    for step in range(1, n_section):
        pair.append(swap(pair[0], "section", 1) if step == 1 else swap(same[step], "tensor", 1))
    state = []
    for step in range(n_section):
        last = step == n_section - 1
        outs = (
            shape_of((tokens, q_width))
            if last
            else [
                shape_of((1, pairs), F32),
                shape_of((1, pairs), F32),
                shape_of((head_dim, pairs), F32),
            ]
        )
        state = call(
            functools.partial(attend_kernel, step, tile_len, step == 0, last),
            outs,
            "attend",
            [VMEM] * (4 + len(state)),
            flops=4 * pairs * rows * head_dim,
            exps=pairs * rows,
        )(qt, bias, same[step], pair[step], *state)
    return state


def solution(mesh):
    in_specs = (
        P(("section", "dp"), "tensor"),
        P("dp", "section", "tensor"),
        P(None, "tensor", "dp"),
        P(),
        P(),
        P(("section", "dp"), None),
    )
    out_specs = P(("section", "dp"), "tensor")
    return jax.shard_map(
        on_device, mesh=mesh, in_specs=in_specs, out_specs=out_specs, check_vma=False
    )
```

```python
import functools

import jax
import jax.numpy as jnp
from jax import lax
from jax.experimental import pallas as pl
from jax.experimental.pallas import tpu as pltpu
from jax.sharding import PartitionSpec as P

EPSILON = 1e-05
MASKED_SCORE = -1e30
TOP_FLOOR = -1e29
VMEM = pl.BlockSpec(memory_space=pltpu.VMEM)
HBM = pl.BlockSpec(memory_space=pltpu.HBM)
F32 = jnp.float32
BF16 = jnp.bfloat16
LIMIT = 24 * 1024 * 1024
CHUNKS = 4


def shape_of(dims, dtype=BF16):
    return jax.ShapeDtypeStruct(dims, dtype)


def call(kernel, outs, name, in_specs, flops=0, size=0, exps=0, scratch=()):
    many = isinstance(outs, list)
    return pl.pallas_call(
        kernel,
        out_shape=outs,
        in_specs=in_specs,
        out_specs=[VMEM] * len(outs) if many else VMEM,
        scratch_shapes=scratch,
        compiler_params=pltpu.CompilerParams(vmem_limit_bytes=LIMIT),
        cost_estimate=pl.CostEstimate(flops=flops, bytes_accessed=size, transcendentals=exps),
        name=name,
    )


def in_hbm(*values):
    return [pltpu.with_memory_space_constraint(value, pltpu.HBM) for value in values]


def normalize(values, gain_vec):
    mean_sq = jnp.mean(values * values, axis=-1, keepdims=True)
    return values * lax.rsqrt(mean_sq + EPSILON) * gain_vec


def store_heads(ref, base, both, head_dim):
    width = both.shape[1] // 2
    both = both.astype(BF16)
    for head in range(width // head_dim):
        lo = head * head_dim
        ref[base + 2 * head] = both[:, lo : lo + head_dim]
        ref[base + 2 * head + 1] = both[:, width + lo : width + lo + head_dim]


def own_kernel(x_hbm, w_hbm, own_ref, x_ref, w_ref, sems):
    step = x_ref.shape[1] // CHUNKS
    copies = []
    for i in range(CHUNKS):
        cols = pl.ds(i * step, step)
        copies.append(
            (
                pltpu.make_async_copy(w_hbm.at[:, cols], w_ref.at[:, cols], sems.at[0, i]),
                pltpu.make_async_copy(x_hbm.at[0, :, cols], x_ref.at[:, cols], sems.at[1, i]),
            )
        )
        for copy in copies[-1]:
            copy.start()
    both = None
    for i in range(CHUNKS):
        for copy in copies[i]:
            copy.wait()
        cols = slice(i * step, (i + 1) * step)
        part = jnp.dot(
            x_ref[:, cols],
            jnp.concatenate([w_ref[0, cols], w_ref[1, cols]], axis=1),
            preferred_element_type=F32,
        )
        both = part if both is None else both + part
    store_heads(own_ref, 0, both, own_ref.shape[2])


def other_kernel(x_ref, own_ref, *refs):
    w_refs, parts_ref = refs[:-1], refs[-1]
    pieces = own_ref.shape[0]
    d = lax.axis_index("dp")
    parts_ref[pl.ds(d * pieces, pieces)] = own_ref[...]
    for k, w_ref in enumerate(w_refs, 1):
        both = jnp.dot(
            x_ref[...],
            jnp.concatenate([w_ref[0], w_ref[1]], axis=1),
            preferred_element_type=F32,
        )
        store_heads(parts_ref, (d ^ k) * pieces, both, own_ref.shape[2])


def query_kernel(
    q_hbm, q_gain_hbm, k_gain_hbm, mask_hbm, qt_ref, bias_ref, k_gain_ref,
    q_ref, q_gain_ref, mask_ref, sems,
):
    moves = [
        (q_hbm, q_ref),
        (q_gain_hbm, q_gain_ref),
        (mask_hbm, mask_ref),
        (k_gain_hbm, k_gain_ref),
    ]
    copies = [pltpu.make_async_copy(a, b, sems.at[i]) for i, (a, b) in enumerate(moves)]
    for copy in copies:
        copy.start()
    for copy in copies:
        copy.wait()
    tokens = q_ref.shape[0]
    head_dim = q_gain_ref.shape[1]
    bias = jnp.where(mask_ref[...] > 0, 0.0, MASKED_SCORE).astype(F32)
    for head in range(q_ref.shape[1] // head_dim):
        rows = q_ref[:, head * head_dim : (head + 1) * head_dim].astype(F32)
        normed = normalize(rows, q_gain_ref[...]) * head_dim ** (-0.5)
        qt_ref[:, head * tokens : (head + 1) * tokens] = normed.T.astype(BF16)
        bias_ref[:, head * tokens : (head + 1) * tokens] = bias


def norm_kernel(k_gain_ref, parts_ref, out_ref):
    total = parts_ref[0].astype(F32)
    for i in range(1, parts_ref.shape[0]):
        total = total + parts_ref[i].astype(F32)
    is_key = lax.axis_index("kind") == 0
    total = jnp.where(is_key, normalize(total, k_gain_ref[...]), total).astype(BF16)
    for i in range(out_ref.shape[0]):
        out_ref[i] = total


def attend_kernel(tile_len, qt_ref, bias_ref, kv_ref, out_ref):
    n_section = kv_ref.shape[0] // 2
    rows, head_dim = kv_ref.shape[1:]
    qt = qt_ref[...]
    scores, biases = [], []
    top = TOP_FLOOR
    for section in range(n_section):
        score = jnp.dot(kv_ref[2 * section], qt, preferred_element_type=F32)
        tile = section * rows // tile_len
        bias = bias_ref[tile : tile + 1, :]
        scores.append(score)
        biases.append(bias)
        top = jnp.maximum(top, jnp.max(score, axis=0, keepdims=True) + bias)
    row_sum, mixed = 0.0, 0.0
    for section in range(n_section):
        weights = jnp.exp(scores[section] + (biases[section] - top))
        row_sum = row_sum + jnp.sum(weights, axis=0, keepdims=True)
        mixed = mixed + lax.dot_general(
            kv_ref[2 * section + 1],
            weights.astype(BF16),
            (((0,), (0,)), ((), ())),
            preferred_element_type=F32,
        )
    has_any = jnp.max(bias_ref[...], axis=0, keepdims=True) > -1.0
    context = jnp.where(has_any, mixed / jnp.where(has_any, row_sum, 1.0), 0.0)
    tokens = out_ref.shape[0]
    for head in range(out_ref.shape[1] // head_dim):
        out_ref[:, head * head_dim : (head + 1) * head_dim] = context[
            :, head * tokens : (head + 1) * tokens
        ].T.astype(BF16)


def on_device(queries, images, kv_weight, q_gain, k_gain, tile_mask):
    n_section = lax.axis_size("section")
    n_dp = lax.axis_size("dp")
    n_tensor = lax.axis_size("pair") * lax.axis_size("kind")
    head_dim = q_gain.shape[0]
    tokens, q_width = queries.shape
    rows, features = images.shape[1:]
    tiles = tile_mask.shape[1]
    own_heads = kv_weight.shape[2] // head_dim
    tile_len = rows * n_section // tiles
    assert 2 * own_heads * n_dp == n_tensor and tile_len % rows == 0
    pairs = tokens * (q_width // head_dim)
    work = 4 * rows * features * kv_weight.shape[2]

    n_kind = lax.axis_size("kind")
    pieces = 2 * own_heads

    others = [
        lax.ppermute(kv_weight, "dp", [(i, i ^ k) for i in range(n_dp)]) for k in range(1, n_dp)
    ]
    own, x = call(
        own_kernel,
        [shape_of((pieces, rows, head_dim)), shape_of((rows, features))],
        "own_head",
        [HBM] * 2,
        flops=work,
        size=2 * (images.size + kv_weight.size),
        scratch=[pltpu.VMEM(kv_weight.shape, BF16), pltpu.SemaphoreType.DMA((2, CHUNKS))],
    )(*in_hbm(images, kv_weight))
    qt, bias, gain = call(
        query_kernel,
        [
            shape_of((head_dim, pairs)),
            shape_of((tiles, pairs), F32),
            shape_of((1, head_dim), F32),
        ],
        "queries",
        [HBM] * 4,
        size=2 * queries.size,
        scratch=[
            pltpu.VMEM(queries.shape, BF16),
            pltpu.VMEM((1, head_dim), F32),
            pltpu.VMEM((tiles, tokens), jnp.int32),
            pltpu.SemaphoreType.DMA((4,)),
        ],
    )(*in_hbm(queries, q_gain.reshape(1, -1), k_gain.reshape(1, -1), tile_mask.T))

    parts = call(
        other_kernel,
        shape_of((n_tensor, rows, head_dim)),
        "other_heads",
        [VMEM] * (n_dp + 1),
        flops=work * (n_dp - 1),
    )(x, own, *others)
    parts = lax.all_to_all(parts, ("pair", "kind"), 0, 0, tiled=True)
    copies = call(
        norm_kernel, shape_of((n_section * n_kind, rows, head_dim)), "sum_norm", [VMEM] * 2
    )(gain, parts)
    kv = lax.all_to_all(copies, ("section", "kind"), 0, 0, tiled=True)
    return call(
        functools.partial(attend_kernel, tile_len),
        shape_of((tokens, q_width)),
        "attend",
        [VMEM] * 3,
        flops=4 * pairs * rows * head_dim * n_section,
        exps=pairs * rows * n_section,
    )(qt, bias, kv)


def solution(mesh):
    sizes = mesh.shape
    mesh = jax.sharding.Mesh(
        mesh.devices.reshape(sizes["section"], sizes["dp"], sizes["tensor"] // 2, 2),
        ("section", "dp", "pair", "kind"),
    )
    tensor = ("pair", "kind")
    in_specs = (
        P(("section", "dp"), tensor),
        P("dp", "section", tensor),
        P(None, tensor, "dp"),
        P(),
        P(),
        P(("section", "dp"), None),
    )
    out_specs = P(("section", "dp"), tensor)
    return jax.shard_map(
        on_device, mesh=mesh, in_specs=in_specs, out_specs=out_specs, check_vma=False
    )
```

```python
import functools

import jax
import jax.numpy as jnp
from jax import lax
from jax.experimental import pallas as pl
from jax.experimental.pallas import tpu as pltpu
from jax.sharding import PartitionSpec as P

EPSILON = 1e-05
MASKED_SCORE = -1e30
TOP_FLOOR = -1e29
VMEM = pl.BlockSpec(memory_space=pltpu.VMEM)
HBM = pl.BlockSpec(memory_space=pltpu.HBM)
F32 = jnp.float32
MIB = 1024 * 1024
LIMIT = 24 * MIB
BF16 = jnp.bfloat16


def shape_of(dims, dtype=BF16):
    return jax.ShapeDtypeStruct(dims, dtype)


def call(
    kernel, outs, n_in, name, flops=0, size=0, exps=0, in_specs=None, scratch=(), aliases=None
):
    many = isinstance(outs, list)
    return pl.pallas_call(
        kernel,
        out_shape=outs,
        in_specs=in_specs or [VMEM] * n_in,
        out_specs=[VMEM] * len(outs) if many else VMEM,
        scratch_shapes=scratch,
        input_output_aliases=aliases or {},
        compiler_params=pltpu.CompilerParams(vmem_limit_bytes=LIMIT),
        cost_estimate=pl.CostEstimate(flops=flops, bytes_accessed=size, transcendentals=exps),
        name=name,
    )


def normalize(values, gain_vec):
    mean_sq = jnp.mean(values * values, axis=-1, keepdims=True)
    return values * lax.rsqrt(mean_sq + EPSILON) * gain_vec


def project(x, w):
    return jnp.dot(
        x, jnp.concatenate([w[0], w[1]], axis=1), preferred_element_type=F32
    ).astype(BF16)


def store_heads(ref, base, both, head_dim):
    width = both.shape[1] // 2
    for head in range(width // head_dim):
        lo = head * head_dim
        ref[base + head, 0] = both[:, lo : lo + head_dim]
        ref[base + head, 1] = both[:, width + lo : width + lo + head_dim]


def prepare_queries(hbm, vmem, sems, qt_ref, bias_ref):
    copies = [pltpu.make_async_copy(a, b, sems.at[i]) for i, (a, b) in enumerate(zip(hbm, vmem))]
    for copy in copies:
        copy.start()
    for copy in copies:
        copy.wait()
    q_ref, q_gain_ref, mask_ref = vmem
    tokens = q_ref.shape[0]
    head_dim = q_gain_ref.shape[1]
    bias = jnp.where(mask_ref[...] > 0, 0.0, MASKED_SCORE).astype(F32)
    for head in range(q_ref.shape[1] // head_dim):
        rows = q_ref[:, head * head_dim : (head + 1) * head_dim].astype(F32)
        normed = normalize(rows, q_gain_ref[...]) * head_dim ** (-0.5)
        qt_ref[:, head * tokens : (head + 1) * tokens] = normed.T.astype(BF16)
        bias_ref[:, head * tokens : (head + 1) * tokens] = bias


def own_kernel(
    head_dim, x_hbm, w_hbm, k_gain_hbm, own_ref, x_ref, k_gain_ref, w_ref, sems
):
    moves = [(k_gain_hbm, k_gain_ref), (x_hbm, x_ref), (w_hbm, w_ref)]
    copies = [pltpu.make_async_copy(a, b, sems.at[i]) for i, (a, b) in enumerate(moves)]
    for copy in copies:
        copy.start()
    for copy in copies:
        copy.wait()
    store_heads(own_ref, 0, project(x_ref[0], w_ref[...]), head_dim)


def split_half(held, send_ref, keep_ref, partner_heads, own_heads):
    for i in range(send_ref.shape[0]):
        send_ref[i] = held[partner_heads + i]
        keep_ref[i] = held[own_heads + i]


def other_kernel(head_dim, n_dp, n_tensor, x_ref, own_ref, *refs):
    w_refs, refs = refs[: n_dp - 1], refs[n_dp - 1 :]
    query_hbm, (send_ref, keep_ref, qt_ref, bias_ref) = refs[:3], refs[3:7]
    held, query_vmem, sems = refs[7], refs[8:11], refs[11]
    d = lax.axis_index("dp")
    t = lax.axis_index("tensor")
    own_heads = own_ref.shape[0]
    held[pl.ds(d * own_heads, own_heads)] = own_ref[...]
    for k in range(1, n_dp):
        store_heads(held, (d ^ k) * own_heads, project(x_ref[0], w_refs[k - 1][...]), head_dim)
    half = send_ref.shape[0]
    upper = t // (n_tensor // 2)
    split_half(held, send_ref, keep_ref, (1 - upper) * half, upper * half)

    @pl.when(d % 2 == 0)
    def _():
        prepare_queries(query_hbm, query_vmem, sems, qt_ref, bias_ref)


def late_kernel(*refs):
    query_hbm, (qt_ref, bias_ref) = refs[2:5], refs[5:7]
    query_vmem, sems = refs[7:10], refs[10]

    @pl.when(lax.axis_index("dp") % 2 == 1)
    def _():
        prepare_queries(query_hbm, query_vmem, sems, qt_ref, bias_ref)


def add_kernel(bit, keep_ref, arrived_ref, send_ref, next_ref, held):
    held[...] = (keep_ref[...].astype(F32) + arrived_ref[...].astype(F32)).astype(BF16)
    half = send_ref.shape[0]
    upper = (lax.axis_index("tensor") // bit) % 2
    split_half(held, send_ref, next_ref, (1 - upper) * half, upper * half)


def add_last_kernel(keep_ref, arrived_ref, bias_ref, out_ref):
    out_ref[...] = (keep_ref[...].astype(F32) + arrived_ref[...].astype(F32)).astype(BF16)


def norm_kernel(k_gain_ref, keep_ref, arrived_ref, kv_ref):
    total = keep_ref[0].astype(F32) + arrived_ref[0].astype(F32)
    kv_ref[0] = normalize(total[0], k_gain_ref[...]).astype(BF16)
    kv_ref[1] = total[1].astype(BF16)


def attend_kernel(steps, tile_len, first, last, head_dim, qt_ref, bias_ref, *refs):
    parts, refs = refs[: len(steps)], refs[len(steps) :]
    if not first:
        top_in, sum_in, mixed_in = refs[:3]
        refs = refs[3:]
    s = lax.axis_index("section")
    rows = parts[0].shape[1]
    qt = qt_ref[...]
    scores, biases = [], []
    top = TOP_FLOOR if first else top_in[...]
    for k, part in zip(steps, parts):
        score = jnp.dot(part[0], qt, preferred_element_type=F32)
        bias = bias_ref[pl.ds(((s ^ k) * rows) // tile_len, 1), :]
        scores.append(score)
        biases.append(bias)
        top = jnp.maximum(top, jnp.max(score, axis=0, keepdims=True) + bias)
    row_sum, mixed = 0.0, 0.0
    if not first:
        scale = jnp.exp(top_in[...] - top)
        row_sum = sum_in[...] * scale
        mixed = mixed_in[...] * scale
    for part, score, bias in zip(parts, scores, biases):
        weights = jnp.exp(score + (bias - top))
        row_sum = row_sum + jnp.sum(weights, axis=0, keepdims=True)
        mixed = mixed + lax.dot_general(
            part[1], weights.astype(BF16), (((0,), (0,)), ((), ())), preferred_element_type=F32
        )
    if not last:
        top_out, sum_out, mixed_out = refs
        top_out[...] = top
        sum_out[...] = row_sum
        mixed_out[...] = mixed
        return
    (out,) = refs
    has_any = jnp.max(bias_ref[...], axis=0, keepdims=True) > -1.0
    inverse = jnp.where(has_any, 1.0 / jnp.where(has_any, row_sum, 1.0), 0.0)
    context = (mixed * inverse).astype(BF16)
    tokens = out.shape[0]
    for head in range(out.shape[1] // head_dim):
        out[:, head * head_dim : (head + 1) * head_dim] = context[
            :, head * tokens : (head + 1) * tokens
        ].T


def on_device(queries, images, kv_weight, q_gain, k_gain, tile_mask):
    n_section = lax.axis_size("section")
    n_dp = lax.axis_size("dp")
    n_tensor = lax.axis_size("tensor")
    head_dim = q_gain.shape[0]
    tokens, q_width = queries.shape
    rows, features = images.shape[1:]
    tiles = tile_mask.shape[1]
    own_heads = kv_weight.shape[2] // head_dim
    heads = own_heads * n_dp
    tile_len = rows * n_section // tiles
    assert heads * 2 == n_tensor and tile_len % rows == 0
    pairs = tokens * (q_width // head_dim)
    work = 4 * rows * features * kv_weight.shape[2]

    def swap(value, axis, k):
        return lax.ppermute(value, axis, [(i, i ^ k) for i in range(lax.axis_size(axis))])

    others = [swap(kv_weight, "dp", k) for k in range(1, n_dp)]
    in_hbm = [
        pltpu.with_memory_space_constraint(value, pltpu.HBM)
        for value in (
            images, kv_weight, k_gain.reshape(1, -1), queries, q_gain.reshape(1, -1), tile_mask.T,
        )
    ]
    own, x, gain = call(
        functools.partial(own_kernel, head_dim),
        [
            shape_of((own_heads, 2, rows, head_dim)),
            shape_of(images.shape),
            shape_of((1, head_dim), F32),
        ],
        3,
        "own_head",
        flops=work,
        size=2 * (images.size + kv_weight.size),
        in_specs=[HBM] * 3,
        scratch=[pltpu.VMEM(kv_weight.shape, BF16), pltpu.SemaphoreType.DMA((3,))],
    )(*in_hbm[:3])
    half = shape_of((heads // 2, 2, rows, head_dim))
    prepared = [shape_of((head_dim, pairs)), shape_of((tiles, pairs), F32)]
    query_scratch = [
        pltpu.VMEM(queries.shape, BF16),
        pltpu.VMEM((1, head_dim), F32),
        pltpu.VMEM((tiles, tokens), jnp.int32),
        pltpu.SemaphoreType.DMA((3,)),
    ]
    send, keep, qt, bias = call(
        functools.partial(other_kernel, head_dim, n_dp, n_tensor),
        [half, half, *prepared],
        n_dp + 1,
        "other_heads",
        flops=work * (n_dp - 1),
        in_specs=[VMEM] * (n_dp + 1) + [HBM] * 3,
        scratch=[pltpu.VMEM((heads, 2, rows, head_dim), BF16), *query_scratch],
    )(x, own, *others, *in_hbm[3:])
    qt, bias = call(
        late_kernel,
        prepared,
        5,
        "late_queries",
        in_specs=[VMEM] * 2 + [HBM] * 3,
        scratch=query_scratch,
        aliases={0: 0, 1: 1},
        flops=work,
    )(qt, bias, *in_hbm[3:])
    bit = n_tensor // 2
    while bit > 1:
        arrived = swap(send, "tensor", bit)
        bit //= 2
        now = keep.shape
        if bit > 1:
            half = shape_of((now[0] // 2, *now[1:]))
            send, keep = call(
                functools.partial(add_kernel, bit),
                [half, half],
                2,
                "add_part",
                scratch=[pltpu.VMEM(now, BF16)],
            )(keep, arrived)
        else:
            send = keep = call(add_last_kernel, shape_of(now), 3, "add_pair")(keep, arrived, bias)
    arrived = swap(send, "tensor", 1)
    kv = call(norm_kernel, shape_of((2, rows, head_dim)), 3, "sum_norm")(gain, keep, arrived)

    gathered = [kv] + [swap(kv, "section", k) for k in range(1, n_section)]
    state = []
    for steps in ([0], list(range(1, n_section - 1)), [n_section - 1]):
        first, last = steps[0] == 0, steps[-1] == n_section - 1
        outs = (
            shape_of((tokens, q_width))
            if last
            else [shape_of((1, pairs), F32), shape_of((1, pairs), F32), shape_of((head_dim, pairs), F32)]
        )
        state = call(
            functools.partial(attend_kernel, steps, tile_len, first, last, head_dim),
            outs,
            2 + len(steps) + len(state),
            "attend",
            flops=4 * pairs * rows * head_dim * len(steps),
            exps=pairs * rows * len(steps),
        )(qt, bias, *[gathered[k] for k in steps], *state)
    return state


def solution(mesh):
    in_specs = (
        P(("section", "dp"), "tensor"),
        P("dp", "section", "tensor"),
        P(None, "tensor", "dp"),
        P(),
        P(),
        P(("section", "dp"), None),
    )
    out_specs = P(("section", "dp"), "tensor")
    return jax.shard_map(
        on_device, mesh=mesh, in_specs=in_specs, out_specs=out_specs, check_vma=False
    )
```

```python
import functools

import jax
import jax.numpy as jnp
from jax import lax
from jax.experimental import pallas as pl
from jax.experimental.pallas import tpu as pltpu
from jax.sharding import PartitionSpec as P

EPSILON = 1e-05
MASKED_SCORE = -1e30
TOP_FLOOR = -1e29
VMEM = pl.BlockSpec(memory_space=pltpu.VMEM)
HBM = pl.BlockSpec(memory_space=pltpu.HBM)
F32 = jnp.float32
MIB = 1024 * 1024
LIMIT = 24 * MIB
BF16 = jnp.bfloat16


def shape_of(dims, dtype=BF16):
    return jax.ShapeDtypeStruct(dims, dtype)


def call(
    kernel, outs, n_in, name, flops=0, size=0, exps=0, in_specs=None, scratch=(), aliases=None
):
    many = isinstance(outs, list)
    return pl.pallas_call(
        kernel,
        out_shape=outs,
        in_specs=in_specs or [VMEM] * n_in,
        out_specs=[VMEM] * len(outs) if many else VMEM,
        scratch_shapes=scratch,
        input_output_aliases=aliases or {},
        compiler_params=pltpu.CompilerParams(vmem_limit_bytes=LIMIT),
        cost_estimate=pl.CostEstimate(flops=flops, bytes_accessed=size, transcendentals=exps),
        name=name,
    )


def normalize(values, gain_vec):
    mean_sq = jnp.mean(values * values, axis=-1, keepdims=True)
    return values * lax.rsqrt(mean_sq + EPSILON) * gain_vec


def project(x, w):
    return jnp.dot(
        x, jnp.concatenate([w[0], w[1]], axis=1), preferred_element_type=F32
    ).astype(BF16)


def store_heads(ref, base, both, head_dim):
    width = both.shape[1] // 2
    for head in range(width // head_dim):
        lo = head * head_dim
        ref[base + head, 0] = both[:, lo : lo + head_dim]
        ref[base + head, 1] = both[:, width + lo : width + lo + head_dim]


def prepare_queries(hbm, vmem, sems, qt_ref, bias_ref):
    copies = [pltpu.make_async_copy(a, b, sems.at[i]) for i, (a, b) in enumerate(zip(hbm, vmem))]
    for copy in copies:
        copy.start()
    for copy in copies:
        copy.wait()
    q_ref, q_gain_ref, mask_ref = vmem
    tokens = q_ref.shape[0]
    head_dim = q_gain_ref.shape[1]
    bias = jnp.where(mask_ref[...] > 0, 0.0, MASKED_SCORE).astype(F32)
    for head in range(q_ref.shape[1] // head_dim):
        rows = q_ref[:, head * head_dim : (head + 1) * head_dim].astype(F32)
        normed = normalize(rows, q_gain_ref[...]) * head_dim ** (-0.5)
        qt_ref[:, head * tokens : (head + 1) * tokens] = normed.T.astype(BF16)
        bias_ref[:, head * tokens : (head + 1) * tokens] = bias


def own_kernel(
    head_dim, x_hbm, w_hbm, k_gain_hbm, own_ref, x_ref, k_gain_ref, w_ref, sems
):
    moves = [(k_gain_hbm, k_gain_ref), (x_hbm, x_ref), (w_hbm, w_ref)]
    copies = [pltpu.make_async_copy(a, b, sems.at[i]) for i, (a, b) in enumerate(moves)]
    for copy in copies:
        copy.start()
    for copy in copies:
        copy.wait()
    store_heads(own_ref, 0, project(x_ref[0], w_ref[...]), head_dim)


def split_half(held, send_ref, keep_ref, partner_heads, own_heads):
    for i in range(send_ref.shape[0]):
        send_ref[i] = held[partner_heads + i]
        keep_ref[i] = held[own_heads + i]


def other_kernel(head_dim, n_dp, n_tensor, x_ref, own_ref, *refs):
    w_refs, refs = refs[: n_dp - 1], refs[n_dp - 1 :]
    query_hbm, (send_ref, keep_ref, qt_ref, bias_ref) = refs[:3], refs[3:7]
    held, query_vmem, sems = refs[7], refs[8:11], refs[11]
    d = lax.axis_index("dp")
    t = lax.axis_index("tensor")
    own_heads = own_ref.shape[0]
    held[pl.ds(d * own_heads, own_heads)] = own_ref[...]
    for k in range(1, n_dp):
        store_heads(held, (d ^ k) * own_heads, project(x_ref[0], w_refs[k - 1][...]), head_dim)
    half = send_ref.shape[0]
    upper = t // (n_tensor // 2)
    split_half(held, send_ref, keep_ref, (1 - upper) * half, upper * half)

    @pl.when(d % 2 == 1)
    def _():
        prepare_queries(query_hbm, query_vmem, sems, qt_ref, bias_ref)


def late_kernel(*refs):
    query_hbm, (qt_ref, bias_ref) = refs[2:5], refs[5:7]
    query_vmem, sems = refs[7:10], refs[10]

    @pl.when(lax.axis_index("dp") % 2 == 0)
    def _():
        prepare_queries(query_hbm, query_vmem, sems, qt_ref, bias_ref)


def add_kernel(bit, keep_ref, arrived_ref, send_ref, next_ref, held):
    held[...] = (keep_ref[...].astype(F32) + arrived_ref[...].astype(F32)).astype(BF16)
    half = send_ref.shape[0]
    upper = (lax.axis_index("tensor") // bit) % 2
    split_half(held, send_ref, next_ref, (1 - upper) * half, upper * half)


def add_last_kernel(keep_ref, arrived_ref, bias_ref, out_ref):
    out_ref[...] = (keep_ref[...].astype(F32) + arrived_ref[...].astype(F32)).astype(BF16)


def norm_kernel(k_gain_ref, keep_ref, arrived_ref, kv_ref):
    total = keep_ref[0].astype(F32) + arrived_ref[0].astype(F32)
    kv_ref[0] = normalize(total[0], k_gain_ref[...]).astype(BF16)
    kv_ref[1] = total[1].astype(BF16)


def attend_kernel(steps, tile_len, first, last, head_dim, qt_ref, bias_ref, *refs):
    parts, refs = refs[: len(steps)], refs[len(steps) :]
    if not first:
        top_in, sum_in, mixed_in = refs[:3]
        refs = refs[3:]
    s = lax.axis_index("section")
    rows = parts[0].shape[1]
    qt = qt_ref[...]
    scores, biases = [], []
    top = TOP_FLOOR if first else top_in[...]
    for k, part in zip(steps, parts):
        score = jnp.dot(part[0], qt, preferred_element_type=F32)
        bias = bias_ref[pl.ds(((s ^ k) * rows) // tile_len, 1), :]
        scores.append(score)
        biases.append(bias)
        top = jnp.maximum(top, jnp.max(score, axis=0, keepdims=True) + bias)
    row_sum, mixed = 0.0, 0.0
    if not first:
        scale = jnp.exp(top_in[...] - top)
        row_sum = sum_in[...] * scale
        mixed = mixed_in[...] * scale
    for part, score, bias in zip(parts, scores, biases):
        weights = jnp.exp(score + (bias - top))
        row_sum = row_sum + jnp.sum(weights, axis=0, keepdims=True)
        mixed = mixed + lax.dot_general(
            part[1], weights.astype(BF16), (((0,), (0,)), ((), ())), preferred_element_type=F32
        )
    if not last:
        top_out, sum_out, mixed_out = refs
        top_out[...] = top
        sum_out[...] = row_sum
        mixed_out[...] = mixed
        return
    (out,) = refs
    has_any = jnp.max(bias_ref[...], axis=0, keepdims=True) > -1.0
    inverse = jnp.where(has_any, 1.0 / jnp.where(has_any, row_sum, 1.0), 0.0)
    context = (mixed * inverse).astype(BF16)
    tokens = out.shape[0]
    for head in range(out.shape[1] // head_dim):
        out[:, head * head_dim : (head + 1) * head_dim] = context[
            :, head * tokens : (head + 1) * tokens
        ].T


def on_device(queries, images, kv_weight, q_gain, k_gain, tile_mask):
    n_section = lax.axis_size("section")
    n_dp = lax.axis_size("dp")
    n_tensor = lax.axis_size("tensor")
    head_dim = q_gain.shape[0]
    tokens, q_width = queries.shape
    rows, features = images.shape[1:]
    tiles = tile_mask.shape[1]
    own_heads = kv_weight.shape[2] // head_dim
    heads = own_heads * n_dp
    tile_len = rows * n_section // tiles
    assert heads * 2 == n_tensor and tile_len % rows == 0
    pairs = tokens * (q_width // head_dim)
    work = 4 * rows * features * kv_weight.shape[2]

    def swap(value, axis, k):
        return lax.ppermute(value, axis, [(i, i ^ k) for i in range(lax.axis_size(axis))])

    others = [swap(kv_weight, "dp", k) for k in range(1, n_dp)]
    in_hbm = [
        pltpu.with_memory_space_constraint(value, pltpu.HBM)
        for value in (
            images, kv_weight, k_gain.reshape(1, -1), queries, q_gain.reshape(1, -1), tile_mask.T,
        )
    ]
    own, x, gain = call(
        functools.partial(own_kernel, head_dim),
        [
            shape_of((own_heads, 2, rows, head_dim)),
            shape_of(images.shape),
            shape_of((1, head_dim), F32),
        ],
        3,
        "own_head",
        flops=work,
        size=2 * (images.size + kv_weight.size),
        in_specs=[HBM] * 3,
        scratch=[pltpu.VMEM(kv_weight.shape, BF16), pltpu.SemaphoreType.DMA((3,))],
    )(*in_hbm[:3])
    half = shape_of((heads // 2, 2, rows, head_dim))
    prepared = [shape_of((head_dim, pairs)), shape_of((tiles, pairs), F32)]
    query_scratch = [
        pltpu.VMEM(queries.shape, BF16),
        pltpu.VMEM((1, head_dim), F32),
        pltpu.VMEM((tiles, tokens), jnp.int32),
        pltpu.SemaphoreType.DMA((3,)),
    ]
    send, keep, qt, bias = call(
        functools.partial(other_kernel, head_dim, n_dp, n_tensor),
        [half, half, *prepared],
        n_dp + 1,
        "other_heads",
        flops=work * (n_dp - 1),
        in_specs=[VMEM] * (n_dp + 1) + [HBM] * 3,
        scratch=[pltpu.VMEM((heads, 2, rows, head_dim), BF16), *query_scratch],
    )(x, own, *others, *in_hbm[3:])
    qt, bias = call(
        late_kernel,
        prepared,
        5,
        "late_queries",
        in_specs=[VMEM] * 2 + [HBM] * 3,
        scratch=query_scratch,
        aliases={0: 0, 1: 1},
        flops=work,
    )(qt, bias, *in_hbm[3:])
    bit = n_tensor // 2
    while bit > 1:
        arrived = swap(send, "tensor", bit)
        bit //= 2
        now = keep.shape
        if bit > 1:
            half = shape_of((now[0] // 2, *now[1:]))
            send, keep = call(
                functools.partial(add_kernel, bit),
                [half, half],
                2,
                "add_part",
                scratch=[pltpu.VMEM(now, BF16)],
            )(keep, arrived)
        else:
            send = keep = call(add_last_kernel, shape_of(now), 3, "add_pair")(keep, arrived, bias)
    arrived = swap(send, "tensor", 1)
    kv = call(norm_kernel, shape_of((2, rows, head_dim)), 3, "sum_norm")(gain, keep, arrived)

    gathered = [kv] + [swap(kv, "section", k) for k in range(1, n_section)]
    state = []
    for steps in ([0], list(range(1, n_section - 1)), [n_section - 1]):
        first, last = steps[0] == 0, steps[-1] == n_section - 1
        outs = (
            shape_of((tokens, q_width))
            if last
            else [shape_of((1, pairs), F32), shape_of((1, pairs), F32), shape_of((head_dim, pairs), F32)]
        )
        state = call(
            functools.partial(attend_kernel, steps, tile_len, first, last, head_dim),
            outs,
            2 + len(steps) + len(state),
            "attend",
            flops=4 * pairs * rows * head_dim * len(steps),
            exps=pairs * rows * len(steps),
        )(qt, bias, *[gathered[k] for k in steps], *state)
    return state


def solution(mesh):
    in_specs = (
        P(("section", "dp"), "tensor"),
        P("dp", "section", "tensor"),
        P(None, "tensor", "dp"),
        P(),
        P(),
        P(("section", "dp"), None),
    )
    out_specs = P(("section", "dp"), "tensor")
    return jax.shard_map(
        on_device, mesh=mesh, in_specs=in_specs, out_specs=out_specs, check_vma=False
    )
```

```python
import functools

import jax
import jax.numpy as jnp
from jax import lax
from jax.experimental import pallas as pl
from jax.experimental.pallas import tpu as pltpu
from jax.sharding import PartitionSpec as P

EPSILON = 1e-05
MASKED_SCORE = -1e30
TOP_FLOOR = -1e29
VMEM = pl.BlockSpec(memory_space=pltpu.VMEM)
HBM = pl.BlockSpec(memory_space=pltpu.HBM)
F32 = jnp.float32
MIB = 1024 * 1024
LIMIT = 24 * MIB
BF16 = jnp.bfloat16


def shape_of(dims, dtype=BF16):
    return jax.ShapeDtypeStruct(dims, dtype)


def call(
    kernel, outs, n_in, name, flops=0, size=0, exps=0, in_specs=None, scratch=(), aliases=None
):
    many = isinstance(outs, list)
    return pl.pallas_call(
        kernel,
        out_shape=outs,
        in_specs=in_specs or [VMEM] * n_in,
        out_specs=[VMEM] * len(outs) if many else VMEM,
        scratch_shapes=scratch,
        input_output_aliases=aliases or {},
        compiler_params=pltpu.CompilerParams(vmem_limit_bytes=LIMIT),
        cost_estimate=pl.CostEstimate(flops=flops, bytes_accessed=size, transcendentals=exps),
        name=name,
    )


def normalize(values, gain_vec):
    mean_sq = jnp.mean(values * values, axis=-1, keepdims=True)
    return values * lax.rsqrt(mean_sq + EPSILON) * gain_vec


def project(x, w):
    return jnp.dot(
        x, jnp.concatenate([w[0], w[1]], axis=1), preferred_element_type=F32
    ).astype(BF16)


def store_heads(ref, base, both, head_dim):
    width = both.shape[1] // 2
    for head in range(width // head_dim):
        lo = head * head_dim
        ref[base + head, 0] = both[:, lo : lo + head_dim]
        ref[base + head, 1] = both[:, width + lo : width + lo + head_dim]


def prepare_queries(hbm, vmem, sems, qt_ref, bias_ref):
    copies = [pltpu.make_async_copy(a, b, sems.at[i]) for i, (a, b) in enumerate(zip(hbm, vmem))]
    for copy in copies:
        copy.start()
    for copy in copies:
        copy.wait()
    q_ref, q_gain_ref, mask_ref = vmem
    tokens = q_ref.shape[0]
    head_dim = q_gain_ref.shape[1]
    bias = jnp.where(mask_ref[...] > 0, 0.0, MASKED_SCORE).astype(F32)
    for head in range(q_ref.shape[1] // head_dim):
        rows = q_ref[:, head * head_dim : (head + 1) * head_dim].astype(F32)
        normed = normalize(rows, q_gain_ref[...]) * head_dim ** (-0.5)
        qt_ref[:, head * tokens : (head + 1) * tokens] = normed.T.astype(BF16)
        bias_ref[:, head * tokens : (head + 1) * tokens] = bias


def own_kernel(
    head_dim, x_hbm, w_hbm, k_gain_hbm, own_ref, x_ref, k_gain_ref, w_ref, sems
):
    moves = [(k_gain_hbm, k_gain_ref), (x_hbm, x_ref), (w_hbm, w_ref)]
    copies = [pltpu.make_async_copy(a, b, sems.at[i]) for i, (a, b) in enumerate(moves)]
    for copy in copies:
        copy.start()
    for copy in copies:
        copy.wait()
    store_heads(own_ref, 0, project(x_ref[0], w_ref[...]), head_dim)


def split_half(held, send_ref, keep_ref, partner_heads, own_heads):
    for i in range(send_ref.shape[0]):
        send_ref[i] = held[partner_heads + i]
        keep_ref[i] = held[own_heads + i]


def other_kernel(head_dim, n_dp, n_tensor, x_ref, own_ref, *refs):
    w_refs, refs = refs[: n_dp - 1], refs[n_dp - 1 :]
    query_hbm, (send_ref, keep_ref, qt_ref, bias_ref) = refs[:3], refs[3:7]
    held, query_vmem, sems = refs[7], refs[8:11], refs[11]
    d = lax.axis_index("dp")
    t = lax.axis_index("tensor")
    own_heads = own_ref.shape[0]
    held[pl.ds(d * own_heads, own_heads)] = own_ref[...]
    for k in range(1, n_dp):
        store_heads(held, (d ^ k) * own_heads, project(x_ref[0], w_refs[k - 1][...]), head_dim)
    half = send_ref.shape[0]
    upper = t // (n_tensor // 2)
    split_half(held, send_ref, keep_ref, (1 - upper) * half, upper * half)

    @pl.when(d % 2 == 0)
    def _():
        prepare_queries(query_hbm, query_vmem, sems, qt_ref, bias_ref)


def late_kernel(*refs):
    query_hbm, (qt_ref, bias_ref) = refs[2:5], refs[5:7]
    query_vmem, sems = refs[7:10], refs[10]

    @pl.when(lax.axis_index("dp") % 2 == 1)
    def _():
        prepare_queries(query_hbm, query_vmem, sems, qt_ref, bias_ref)


def add_kernel(bit, keep_ref, arrived_ref, send_ref, next_ref, held):
    held[...] = (keep_ref[...].astype(F32) + arrived_ref[...].astype(F32)).astype(BF16)
    half = send_ref.shape[0]
    upper = (lax.axis_index("tensor") // bit) % 2
    split_half(held, send_ref, next_ref, (1 - upper) * half, upper * half)


def add_last_kernel(keep_ref, arrived_ref, bias_ref, out_ref):
    out_ref[...] = (keep_ref[...].astype(F32) + arrived_ref[...].astype(F32)).astype(BF16)


def finish_rows(k_gain, one, two):
    keys = one[0].astype(F32) + two[0].astype(F32)
    values = one[1].astype(F32) + two[1].astype(F32)
    return normalize(keys, k_gain).astype(BF16), values.astype(BF16)


def norm_kernel(k_gain_ref, keep_ref, arrived_ref, kv_ref):
    kv_ref[0], kv_ref[1] = finish_rows(k_gain_ref[...], keep_ref.at[0], arrived_ref.at[0])


def attend_kernel(near, far, tile_len, first, last, head_dim, k_gain_ref, qt_ref, bias_ref, *refs):
    near_refs, refs = refs[: len(near)], refs[len(near) :]
    far_refs, refs = refs[: 2 * len(far)], refs[2 * len(far) :]
    if not first:
        top_in, sum_in, mixed_in = refs[:3]
        refs = refs[3:]
    s = lax.axis_index("section")
    qt = qt_ref[...]
    parts = [(part[0], part[1]) for part in near_refs]
    for one, two in zip(far_refs[::2], far_refs[1::2]):
        parts.append(finish_rows(k_gain_ref[...], one.at[0], two.at[0]))
    rows = parts[0][0].shape[0]
    scores, biases = [], []
    top = TOP_FLOOR if first else top_in[...]
    for step, (keys, _) in zip((*near, *far), parts):
        score = jnp.dot(keys, qt, preferred_element_type=F32)
        bias = bias_ref[pl.ds(((s ^ step) * rows) // tile_len, 1), :]
        scores.append(score)
        biases.append(bias)
        top = jnp.maximum(top, jnp.max(score, axis=0, keepdims=True) + bias)
    row_sum, mixed = 0.0, 0.0
    if not first:
        scale = jnp.exp(top_in[...] - top)
        row_sum = sum_in[...] * scale
        mixed = mixed_in[...] * scale
    for (_, values), score, bias in zip(parts, scores, biases):
        weights = jnp.exp(score + (bias - top))
        row_sum = row_sum + jnp.sum(weights, axis=0, keepdims=True)
        mixed = mixed + lax.dot_general(
            values, weights.astype(BF16), (((0,), (0,)), ((), ())), preferred_element_type=F32
        )
    if not last:
        top_out, sum_out, mixed_out = refs
        top_out[...] = top
        sum_out[...] = row_sum
        mixed_out[...] = mixed
        return
    (out,) = refs
    has_any = jnp.max(bias_ref[...], axis=0, keepdims=True) > -1.0
    inverse = jnp.where(has_any, 1.0 / jnp.where(has_any, row_sum, 1.0), 0.0)
    context = (mixed * inverse).astype(BF16)
    tokens = out.shape[0]
    for head in range(out.shape[1] // head_dim):
        out[:, head * head_dim : (head + 1) * head_dim] = context[
            :, head * tokens : (head + 1) * tokens
        ].T


def on_device(queries, images, kv_weight, q_gain, k_gain, tile_mask):
    n_section = lax.axis_size("section")
    n_dp = lax.axis_size("dp")
    n_tensor = lax.axis_size("tensor")
    head_dim = q_gain.shape[0]
    tokens, q_width = queries.shape
    rows, features = images.shape[1:]
    tiles = tile_mask.shape[1]
    own_heads = kv_weight.shape[2] // head_dim
    heads = own_heads * n_dp
    tile_len = rows * n_section // tiles
    assert heads * 2 == n_tensor and tile_len % rows == 0 and n_section >= 4
    pairs = tokens * (q_width // head_dim)
    work = 4 * rows * features * kv_weight.shape[2]

    def swap(value, axis, k):
        return lax.ppermute(value, axis, [(i, i ^ k) for i in range(lax.axis_size(axis))])

    others = [swap(kv_weight, "dp", k) for k in range(1, n_dp)]
    in_hbm = [
        pltpu.with_memory_space_constraint(value, pltpu.HBM)
        for value in (
            images, kv_weight, k_gain.reshape(1, -1), queries, q_gain.reshape(1, -1), tile_mask.T,
        )
    ]
    own, x, gain = call(
        functools.partial(own_kernel, head_dim),
        [
            shape_of((own_heads, 2, rows, head_dim)),
            shape_of(images.shape),
            shape_of((1, head_dim), F32),
        ],
        3,
        "own_head",
        flops=work,
        size=2 * (images.size + kv_weight.size),
        in_specs=[HBM] * 3,
        scratch=[pltpu.VMEM(kv_weight.shape, BF16), pltpu.SemaphoreType.DMA((3,))],
    )(*in_hbm[:3])
    half = shape_of((heads // 2, 2, rows, head_dim))
    prepared = [shape_of((head_dim, pairs)), shape_of((tiles, pairs), F32)]
    query_scratch = [
        pltpu.VMEM(queries.shape, BF16),
        pltpu.VMEM((1, head_dim), F32),
        pltpu.VMEM((tiles, tokens), jnp.int32),
        pltpu.SemaphoreType.DMA((3,)),
    ]
    send, keep, qt, bias = call(
        functools.partial(other_kernel, head_dim, n_dp, n_tensor),
        [half, half, *prepared],
        n_dp + 1,
        "other_heads",
        flops=work * (n_dp - 1),
        in_specs=[VMEM] * (n_dp + 1) + [HBM] * 3,
        scratch=[pltpu.VMEM((heads, 2, rows, head_dim), BF16), *query_scratch],
    )(x, own, *others, *in_hbm[3:])
    qt, bias = call(
        late_kernel,
        prepared,
        5,
        "late_queries",
        in_specs=[VMEM] * 2 + [HBM] * 3,
        scratch=query_scratch,
        aliases={0: 0, 1: 1},
        flops=work,
    )(qt, bias, *in_hbm[3:])
    bit = n_tensor // 2
    while bit > 1:
        arrived = swap(send, "tensor", bit)
        bit //= 2
        now = keep.shape
        if bit > 1:
            half = shape_of((now[0] // 2, *now[1:]))
            send, keep = call(
                functools.partial(add_kernel, bit),
                [half, half],
                2,
                "add_part",
                scratch=[pltpu.VMEM(now, BF16)],
            )(keep, arrived)
        else:
            send = keep = call(add_last_kernel, shape_of(now), 3, "add_pair")(keep, arrived, bias)
    far = [step for step in range(1, n_section) if step & (step - 1)]
    near = [step for step in range(1, n_section) if not step & (step - 1)]
    arrived = swap(send, "tensor", 1)
    halves = [swap(send, "section", step) for step in far]
    kv = call(norm_kernel, shape_of((2, rows, head_dim)), 3, "sum_norm")(gain, keep, arrived)
    finished = [swap(kv, "section", step) for step in near]
    both = []
    for value in halves:
        both += [value, swap(value, "tensor", 1)]
    state = []
    for here, there, operands in (
        ([0], [], [kv]),
        (near, [], finished),
        ([], far, both),
    ):
        first, last = here == [0], len(there) > 0
        outs = (
            shape_of((tokens, q_width))
            if last
            else [shape_of((1, pairs), F32), shape_of((1, pairs), F32), shape_of((head_dim, pairs), F32)]
        )
        parts = len(here) + len(there)
        state = call(
            functools.partial(attend_kernel, here, there, tile_len, first, last, head_dim),
            outs,
            3 + len(operands) + len(state),
            "attend",
            flops=4 * pairs * rows * head_dim * parts,
            exps=pairs * rows * parts,
        )(gain, qt, bias, *operands, *state)
    return state


def solution(mesh):
    in_specs = (
        P(("section", "dp"), "tensor"),
        P("dp", "section", "tensor"),
        P(None, "tensor", "dp"),
        P(),
        P(),
        P(("section", "dp"), None),
    )
    out_specs = P(("section", "dp"), "tensor")
    return jax.shard_map(
        on_device, mesh=mesh, in_specs=in_specs, out_specs=out_specs, check_vma=False
    )
```

```python
import functools

import jax
import jax.numpy as jnp
from jax import lax
from jax.experimental import pallas as pl
from jax.experimental.pallas import tpu as pltpu
from jax.sharding import PartitionSpec as P

EPSILON = 1e-05
MASKED_SCORE = -1e30
TOP_FLOOR = -1e29
VMEM = pl.BlockSpec(memory_space=pltpu.VMEM)
HBM = pl.BlockSpec(memory_space=pltpu.HBM)
F32 = jnp.float32
MIB = 1024 * 1024
LIMIT = 24 * MIB
BF16 = jnp.bfloat16


def shape_of(dims, dtype=BF16):
    return jax.ShapeDtypeStruct(dims, dtype)


def call(
    kernel, outs, n_in, name, flops=0, size=0, exps=0, in_specs=None, scratch=()
):
    many = isinstance(outs, list)
    return pl.pallas_call(
        kernel,
        out_shape=outs,
        in_specs=in_specs or [VMEM] * n_in,
        out_specs=[VMEM] * len(outs) if many else VMEM,
        scratch_shapes=scratch,
        compiler_params=pltpu.CompilerParams(vmem_limit_bytes=LIMIT),
        cost_estimate=pl.CostEstimate(flops=flops, bytes_accessed=size, transcendentals=exps),
        name=name,
    )


def normalize(values, gain_vec):
    mean_sq = jnp.mean(values * values, axis=-1, keepdims=True)
    return values * lax.rsqrt(mean_sq + EPSILON) * gain_vec


def project(x, w):
    return jnp.dot(
        x, jnp.concatenate([w[0], w[1]], axis=1), preferred_element_type=F32
    ).astype(BF16)


def store_heads(ref, base, both, head_dim):
    width = both.shape[1] // 2
    for head in range(width // head_dim):
        lo = head * head_dim
        ref[base + head, 0] = both[:, lo : lo + head_dim]
        ref[base + head, 1] = both[:, width + lo : width + lo + head_dim]


def prepare_queries(hbm, vmem, sems, qt_ref, bias_ref):
    copies = [pltpu.make_async_copy(a, b, sems.at[i]) for i, (a, b) in enumerate(zip(hbm, vmem))]
    for copy in copies:
        copy.start()
    for copy in copies:
        copy.wait()
    q_ref, q_gain_ref, mask_ref = vmem
    tokens = q_ref.shape[0]
    head_dim = q_gain_ref.shape[1]
    bias = jnp.where(mask_ref[...] > 0, 0.0, MASKED_SCORE).astype(F32)
    for head in range(q_ref.shape[1] // head_dim):
        rows = q_ref[:, head * head_dim : (head + 1) * head_dim].astype(F32)
        normed = normalize(rows, q_gain_ref[...]) * head_dim ** (-0.5)
        qt_ref[:, head * tokens : (head + 1) * tokens] = normed.T.astype(BF16)
        bias_ref[:, head * tokens : (head + 1) * tokens] = bias


def own_kernel(
    head_dim, x_hbm, w_hbm, k_gain_hbm, own_ref, x_ref, k_gain_ref, w_ref, sems
):
    moves = [(k_gain_hbm, k_gain_ref), (x_hbm, x_ref), (w_hbm, w_ref)]
    copies = [pltpu.make_async_copy(a, b, sems.at[i]) for i, (a, b) in enumerate(moves)]
    for copy in copies:
        copy.start()
    for copy in copies:
        copy.wait()
    store_heads(own_ref, 0, project(x_ref[0], w_ref[...]), head_dim)


def split_half(held, send_ref, keep_ref, partner_heads, own_heads):
    for i in range(send_ref.shape[0]):
        send_ref[i] = held[partner_heads + i]
        keep_ref[i] = held[own_heads + i]


def other_kernel(head_dim, x_ref, w_ref, other_ref):
    store_heads(other_ref, 0, project(x_ref[0], w_ref[...]), head_dim)


def spread_kernel(n_dp, n_tensor, own_ref, *refs):
    others, (send_ref, keep_ref, held) = refs[: n_dp - 1], refs[n_dp - 1 :]
    d = lax.axis_index("dp")
    own_heads = own_ref.shape[0]
    for k, ref in enumerate((own_ref, *others)):
        held[pl.ds((d ^ k) * own_heads, own_heads)] = ref[...]
    half = send_ref.shape[0]
    upper = lax.axis_index("tensor") // (n_tensor // 2)
    split_half(held, send_ref, keep_ref, (1 - upper) * half, upper * half)


def query_kernel(*refs):
    prepare_queries(refs[:3], refs[5:8], refs[8], *refs[3:5])


def pair_kernel(own_ref, other_ref, first_ref, second_ref, bias_ref, out_ref):
    mine = lax.axis_index("tensor") // 2 == lax.axis_index("dp")
    keep = jnp.where(mine, own_ref[...], other_ref[...]).astype(F32)
    arrived = jnp.where(mine, first_ref[...], second_ref[...]).astype(F32)
    out_ref[...] = (keep + arrived).astype(BF16)


def add_kernel(bit, keep_ref, arrived_ref, send_ref, next_ref, held):
    held[...] = (keep_ref[...].astype(F32) + arrived_ref[...].astype(F32)).astype(BF16)
    half = send_ref.shape[0]
    upper = (lax.axis_index("tensor") // bit) % 2
    split_half(held, send_ref, next_ref, (1 - upper) * half, upper * half)


def add_last_kernel(keep_ref, arrived_ref, out_ref):
    out_ref[...] = (keep_ref[...].astype(F32) + arrived_ref[...].astype(F32)).astype(BF16)


def finish_rows(k_gain, one, two):
    keys = one[0].astype(F32) + two[0].astype(F32)
    values = one[1].astype(F32) + two[1].astype(F32)
    return normalize(keys, k_gain).astype(BF16), values.astype(BF16)


def norm_kernel(k_gain_ref, keep_ref, arrived_ref, kv_ref):
    kv_ref[0], kv_ref[1] = finish_rows(k_gain_ref[...], keep_ref.at[0], arrived_ref.at[0])


def attend_kernel(near, far, tile_len, first, last, head_dim, k_gain_ref, qt_ref, bias_ref, *refs):
    near_refs, refs = refs[: len(near)], refs[len(near) :]
    far_refs, refs = refs[: 2 * len(far)], refs[2 * len(far) :]
    if not first:
        top_in, sum_in, mixed_in = refs[:3]
        refs = refs[3:]
    s = lax.axis_index("section")
    qt = qt_ref[...]
    parts = [(part[0], part[1]) for part in near_refs]
    for one, two in zip(far_refs[::2], far_refs[1::2]):
        parts.append(finish_rows(k_gain_ref[...], one.at[0], two.at[0]))
    rows = parts[0][0].shape[0]
    scores, biases = [], []
    top = TOP_FLOOR if first else top_in[...]
    for step, (keys, _) in zip((*near, *far), parts):
        score = jnp.dot(keys, qt, preferred_element_type=F32)
        bias = bias_ref[pl.ds(((s ^ step) * rows) // tile_len, 1), :]
        scores.append(score)
        biases.append(bias)
        top = jnp.maximum(top, jnp.max(score, axis=0, keepdims=True) + bias)
    row_sum, mixed = 0.0, 0.0
    if not first:
        scale = jnp.exp(top_in[...] - top)
        row_sum = sum_in[...] * scale
        mixed = mixed_in[...] * scale
    for (_, values), score, bias in zip(parts, scores, biases):
        weights = jnp.exp(score + (bias - top))
        row_sum = row_sum + jnp.sum(weights, axis=0, keepdims=True)
        mixed = mixed + lax.dot_general(
            values, weights.astype(BF16), (((0,), (0,)), ((), ())), preferred_element_type=F32
        )
    if not last:
        top_out, sum_out, mixed_out = refs
        top_out[...] = top
        sum_out[...] = row_sum
        mixed_out[...] = mixed
        return
    (out,) = refs
    has_any = jnp.max(bias_ref[...], axis=0, keepdims=True) > -1.0
    inverse = jnp.where(has_any, 1.0 / jnp.where(has_any, row_sum, 1.0), 0.0)
    context = (mixed * inverse).astype(BF16)
    tokens = out.shape[0]
    for head in range(out.shape[1] // head_dim):
        out[:, head * head_dim : (head + 1) * head_dim] = context[
            :, head * tokens : (head + 1) * tokens
        ].T


def swap(value, axis, k):
    return lax.ppermute(value, axis, [(i, i ^ k) for i in range(lax.axis_size(axis))])


def sum_two_heads(own, other, bias):
    devices = [(d, t) for d in range(2) for t in range(4)]

    def exchange(value, senders):
        hops = [
            (4 * d + t, 4 * d + (t ^ 2) if (t // 2 == d) == senders else 4 * (1 - d) + t)
            for d, t in devices
        ]
        return lax.ppermute(value, ("dp", "tensor"), hops)

    first = exchange(own, False)
    rest = other(1)
    second = exchange(rest, True)
    return call(pair_kernel, shape_of(own.shape), 5, "pair_sum")(own, rest, first, second, bias)


def sum_many_heads(own, others):
    n_dp, n_tensor = lax.axis_size("dp"), lax.axis_size("tensor")
    heads = own.shape[0] * n_dp
    half = shape_of((heads // 2, *own.shape[1:]))
    send, keep = call(
        functools.partial(spread_kernel, n_dp, n_tensor),
        [half, half],
        n_dp,
        "spread",
        scratch=[pltpu.VMEM((heads, *own.shape[1:]), BF16)],
    )(own, *others)
    bit = n_tensor // 2
    while bit > 1:
        arrived = swap(send, "tensor", bit)
        bit //= 2
        now = keep.shape
        if bit > 1:
            half = shape_of((now[0] // 2, *now[1:]))
            send, keep = call(
                functools.partial(add_kernel, bit),
                [half, half],
                2,
                "add_part",
                scratch=[pltpu.VMEM(now, BF16)],
            )(keep, arrived)
        else:
            send = keep = call(add_last_kernel, shape_of(now), 2, "add_pair")(keep, arrived)
    return send, keep


def on_device(queries, images, kv_weight, q_gain, k_gain, tile_mask):
    n_section = lax.axis_size("section")
    n_dp = lax.axis_size("dp")
    n_tensor = lax.axis_size("tensor")
    head_dim = q_gain.shape[0]
    tokens, q_width = queries.shape
    rows, features = images.shape[1:]
    tiles = tile_mask.shape[1]
    own_heads = kv_weight.shape[2] // head_dim
    heads = own_heads * n_dp
    tile_len = rows * n_section // tiles
    assert heads * 2 == n_tensor and tile_len % rows == 0 and n_section >= 4
    pairs = tokens * (q_width // head_dim)
    work = 4 * rows * features * kv_weight.shape[2]

    others = [swap(kv_weight, "dp", k) for k in range(1, n_dp)]
    in_hbm = [
        pltpu.with_memory_space_constraint(value, pltpu.HBM)
        for value in (
            images, kv_weight, k_gain.reshape(1, -1), queries, q_gain.reshape(1, -1), tile_mask.T,
        )
    ]
    own, x, gain = call(
        functools.partial(own_kernel, head_dim),
        [
            shape_of((own_heads, 2, rows, head_dim)),
            shape_of(images.shape),
            shape_of((1, head_dim), F32),
        ],
        3,
        "own_head",
        flops=work,
        size=2 * (images.size + kv_weight.size),
        in_specs=[HBM] * 3,
        scratch=[pltpu.VMEM(kv_weight.shape, BF16), pltpu.SemaphoreType.DMA((3,))],
    )(*in_hbm[:3])
    qt, bias = call(
        query_kernel,
        [shape_of((head_dim, pairs)), shape_of((tiles, pairs), F32)],
        3,
        "queries",
        in_specs=[HBM] * 3,
        scratch=[
            pltpu.VMEM(queries.shape, BF16),
            pltpu.VMEM((1, head_dim), F32),
            pltpu.VMEM((tiles, tokens), jnp.int32),
            pltpu.SemaphoreType.DMA((3,)),
        ],
    )(*in_hbm[3:])

    def other(k):
        return call(
            functools.partial(other_kernel, head_dim), shape_of(own.shape), 2, "other_heads", flops=work
        )(x, others[k - 1])

    if n_dp == 2 and own_heads == 1:
        send = keep = sum_two_heads(own, other, bias)
    else:
        send, keep = sum_many_heads(own, [other(k) for k in range(1, n_dp)])
    far = [step for step in range(1, n_section) if step & (step - 1)]
    near = [step for step in range(1, n_section) if not step & (step - 1)]
    arrived = swap(send, "tensor", 1)
    halves = [swap(send, "section", step) for step in far]
    kv = call(norm_kernel, shape_of((2, rows, head_dim)), 3, "sum_norm")(gain, keep, arrived)
    finished = [swap(kv, "section", step) for step in near]
    both = []
    for value in halves:
        both += [value, swap(value, "tensor", 1)]
    state = []
    for here, there, operands in (
        ([0], [], [kv]),
        (near, [], finished),
        ([], far, both),
    ):
        first, last = here == [0], len(there) > 0
        outs = (
            shape_of((tokens, q_width))
            if last
            else [shape_of((1, pairs), F32), shape_of((1, pairs), F32), shape_of((head_dim, pairs), F32)]
        )
        parts = len(here) + len(there)
        state = call(
            functools.partial(attend_kernel, here, there, tile_len, first, last, head_dim),
            outs,
            3 + len(operands) + len(state),
            "attend",
            flops=4 * pairs * rows * head_dim * parts,
            exps=pairs * rows * parts,
        )(gain, qt, bias, *operands, *state)
    return state


def solution(mesh):
    in_specs = (
        P(("section", "dp"), "tensor"),
        P("dp", "section", "tensor"),
        P(None, "tensor", "dp"),
        P(),
        P(),
        P(("section", "dp"), None),
    )
    out_specs = P(("section", "dp"), "tensor")
    return jax.shard_map(
        on_device, mesh=mesh, in_specs=in_specs, out_specs=out_specs, check_vma=False
    )
```

```python
import functools

import jax
import jax.numpy as jnp
from jax import lax
from jax.experimental import pallas as pl
from jax.experimental.pallas import tpu as pltpu
from jax.sharding import PartitionSpec as P

EPSILON = 1e-05
MASKED_SCORE = -1e30
TOP_FLOOR = -1e29
VMEM = pl.BlockSpec(memory_space=pltpu.VMEM)
HBM = pl.BlockSpec(memory_space=pltpu.HBM)
F32 = jnp.float32
MIB = 1024 * 1024
LIMIT = 24 * MIB
BF16 = jnp.bfloat16


def shape_of(dims, dtype=BF16):
    return jax.ShapeDtypeStruct(dims, dtype)


def call(
    kernel, outs, n_in, name, flops=0, size=0, exps=0, in_specs=None, scratch=()
):
    many = isinstance(outs, list)
    return pl.pallas_call(
        kernel,
        out_shape=outs,
        in_specs=in_specs or [VMEM] * n_in,
        out_specs=[VMEM] * len(outs) if many else VMEM,
        scratch_shapes=scratch,
        compiler_params=pltpu.CompilerParams(vmem_limit_bytes=LIMIT),
        cost_estimate=pl.CostEstimate(flops=flops, bytes_accessed=size, transcendentals=exps),
        name=name,
    )


def normalize(values, gain_vec):
    mean_sq = jnp.mean(values * values, axis=-1, keepdims=True)
    return values * lax.rsqrt(mean_sq + EPSILON) * gain_vec


def project(x, w):
    return jnp.dot(
        x, jnp.concatenate([w[0], w[1]], axis=1), preferred_element_type=F32
    ).astype(BF16)


def store_heads(ref, base, both, head_dim):
    width = both.shape[1] // 2
    for head in range(width // head_dim):
        lo = head * head_dim
        ref[base + head, 0] = both[:, lo : lo + head_dim]
        ref[base + head, 1] = both[:, width + lo : width + lo + head_dim]


def prepare_queries(hbm, vmem, sems, qt_ref, bias_ref):
    copies = [pltpu.make_async_copy(a, b, sems.at[i]) for i, (a, b) in enumerate(zip(hbm, vmem))]
    for copy in copies:
        copy.start()
    for copy in copies:
        copy.wait()
    q_ref, q_gain_ref, mask_ref = vmem
    tokens = q_ref.shape[0]
    head_dim = q_gain_ref.shape[1]
    bias = jnp.where(mask_ref[...] > 0, 0.0, MASKED_SCORE).astype(F32)
    for head in range(q_ref.shape[1] // head_dim):
        rows = q_ref[:, head * head_dim : (head + 1) * head_dim].astype(F32)
        normed = normalize(rows, q_gain_ref[...]) * head_dim ** (-0.5)
        qt_ref[:, head * tokens : (head + 1) * tokens] = normed.T.astype(BF16)
        bias_ref[:, head * tokens : (head + 1) * tokens] = bias


def own_kernel(
    head_dim, x_hbm, w_hbm, k_gain_hbm, own_ref, x_ref, k_gain_ref, w_ref, sems
):
    moves = [(k_gain_hbm, k_gain_ref), (x_hbm, x_ref), (w_hbm, w_ref)]
    copies = [pltpu.make_async_copy(a, b, sems.at[i]) for i, (a, b) in enumerate(moves)]
    for copy in copies:
        copy.start()
    for copy in copies:
        copy.wait()
    store_heads(own_ref, 0, project(x_ref[0], w_ref[...]), head_dim)


def split_half(held, send_ref, keep_ref, partner_heads, own_heads):
    for i in range(send_ref.shape[0]):
        send_ref[i] = held[partner_heads + i]
        keep_ref[i] = held[own_heads + i]


def other_kernel(head_dim, x_ref, w_ref, other_ref):
    store_heads(other_ref, 0, project(x_ref[0], w_ref[...]), head_dim)


def spread_kernel(n_dp, n_tensor, own_ref, *refs):
    others, (send_ref, keep_ref, held) = refs[: n_dp - 1], refs[n_dp - 1 :]
    d = lax.axis_index("dp")
    own_heads = own_ref.shape[0]
    for k, ref in enumerate((own_ref, *others)):
        held[pl.ds((d ^ k) * own_heads, own_heads)] = ref[...]
    half = send_ref.shape[0]
    upper = lax.axis_index("tensor") // (n_tensor // 2)
    split_half(held, send_ref, keep_ref, (1 - upper) * half, upper * half)


def query_kernel(*refs):
    prepare_queries(refs[:3], refs[5:8], refs[8], *refs[3:5])


def pair_kernel(own_ref, other_ref, first_ref, second_ref, bias_ref, out_ref):
    mine = lax.axis_index("tensor") // 2 == lax.axis_index("dp")
    keep = jnp.where(mine, own_ref[...], other_ref[...]).astype(F32)
    arrived = jnp.where(mine, first_ref[...], second_ref[...]).astype(F32)
    out_ref[...] = (keep + arrived).astype(BF16)


def add_kernel(bit, keep_ref, arrived_ref, send_ref, next_ref, held):
    held[...] = (keep_ref[...].astype(F32) + arrived_ref[...].astype(F32)).astype(BF16)
    half = send_ref.shape[0]
    upper = (lax.axis_index("tensor") // bit) % 2
    split_half(held, send_ref, next_ref, (1 - upper) * half, upper * half)


def add_last_kernel(keep_ref, arrived_ref, out_ref):
    out_ref[...] = (keep_ref[...].astype(F32) + arrived_ref[...].astype(F32)).astype(BF16)


def finish_rows(k_gain, one, two):
    keys = one[0].astype(F32) + two[0].astype(F32)
    values = one[1].astype(F32) + two[1].astype(F32)
    return normalize(keys, k_gain).astype(BF16), values.astype(BF16)


def norm_kernel(k_gain_ref, keep_ref, arrived_ref, kv_ref):
    kv_ref[0], kv_ref[1] = finish_rows(k_gain_ref[...], keep_ref.at[0], arrived_ref.at[0])


def attend_kernel(near, far, tile_len, first, last, head_dim, k_gain_ref, qt_ref, bias_ref, *refs):
    near_refs, refs = refs[: len(near)], refs[len(near) :]
    far_refs, refs = refs[: 2 * len(far)], refs[2 * len(far) :]
    if not first:
        top_in, sum_in, mixed_in = refs[:3]
        refs = refs[3:]
    s = lax.axis_index("section")
    qt = qt_ref[...]
    parts = [(part[0], part[1]) for part in near_refs]
    for one, two in zip(far_refs[::2], far_refs[1::2]):
        parts.append(finish_rows(k_gain_ref[...], one.at[0], two.at[0]))
    rows = parts[0][0].shape[0]
    scores, biases = [], []
    top = TOP_FLOOR if first else top_in[...]
    for step, (keys, _) in zip((*near, *far), parts):
        score = jnp.dot(keys, qt, preferred_element_type=F32)
        bias = bias_ref[pl.ds(((s ^ step) * rows) // tile_len, 1), :]
        scores.append(score)
        biases.append(bias)
        top = jnp.maximum(top, jnp.max(score, axis=0, keepdims=True) + bias)
    row_sum, mixed = 0.0, 0.0
    if not first:
        scale = jnp.exp(top_in[...] - top)
        row_sum = sum_in[...] * scale
        mixed = mixed_in[...] * scale
    for (_, values), score, bias in zip(parts, scores, biases):
        weights = jnp.exp(score + (bias - top))
        row_sum = row_sum + jnp.sum(weights, axis=0, keepdims=True)
        mixed = mixed + lax.dot_general(
            values, weights.astype(BF16), (((0,), (0,)), ((), ())), preferred_element_type=F32
        )
    if not last:
        top_out, sum_out, mixed_out = refs
        top_out[...] = top
        sum_out[...] = row_sum
        mixed_out[...] = mixed
        return
    (out,) = refs
    has_any = jnp.max(bias_ref[...], axis=0, keepdims=True) > -1.0
    inverse = jnp.where(has_any, 1.0 / jnp.where(has_any, row_sum, 1.0), 0.0)
    context = (mixed * inverse).astype(BF16)
    tokens = out.shape[0]
    for head in range(out.shape[1] // head_dim):
        out[:, head * head_dim : (head + 1) * head_dim] = context[
            :, head * tokens : (head + 1) * tokens
        ].T


def swap(value, axis, k):
    return lax.ppermute(value, axis, [(i, i ^ k) for i in range(lax.axis_size(axis))])


def sum_two_heads(own, other, bias):
    devices = [(d, t) for d in range(2) for t in range(4)]

    def exchange(value, senders):
        hops = [
            (4 * d + t, 4 * d + (t ^ 3) if (t // 2 == d) == senders else 4 * (1 - d) + t)
            for d, t in devices
        ]
        return lax.ppermute(value, ("dp", "tensor"), hops)

    first = exchange(own, False)
    rest = other(1)
    second = exchange(rest, True)
    return call(pair_kernel, shape_of(own.shape), 5, "pair_sum")(own, rest, first, second, bias)


def sum_many_heads(own, others):
    n_dp, n_tensor = lax.axis_size("dp"), lax.axis_size("tensor")
    heads = own.shape[0] * n_dp
    half = shape_of((heads // 2, *own.shape[1:]))
    send, keep = call(
        functools.partial(spread_kernel, n_dp, n_tensor),
        [half, half],
        n_dp,
        "spread",
        scratch=[pltpu.VMEM((heads, *own.shape[1:]), BF16)],
    )(own, *others)
    bit = n_tensor // 2
    while bit > 1:
        arrived = swap(send, "tensor", bit)
        bit //= 2
        now = keep.shape
        if bit > 1:
            half = shape_of((now[0] // 2, *now[1:]))
            send, keep = call(
                functools.partial(add_kernel, bit),
                [half, half],
                2,
                "add_part",
                scratch=[pltpu.VMEM(now, BF16)],
            )(keep, arrived)
        else:
            send = keep = call(add_last_kernel, shape_of(now), 2, "add_pair")(keep, arrived)
    return send, keep


def on_device(queries, images, kv_weight, q_gain, k_gain, tile_mask):
    n_section = lax.axis_size("section")
    n_dp = lax.axis_size("dp")
    n_tensor = lax.axis_size("tensor")
    head_dim = q_gain.shape[0]
    tokens, q_width = queries.shape
    rows, features = images.shape[1:]
    tiles = tile_mask.shape[1]
    own_heads = kv_weight.shape[2] // head_dim
    heads = own_heads * n_dp
    tile_len = rows * n_section // tiles
    assert heads * 2 == n_tensor and tile_len % rows == 0 and n_section >= 4
    pairs = tokens * (q_width // head_dim)
    work = 4 * rows * features * kv_weight.shape[2]

    others = [swap(kv_weight, "dp", k) for k in range(1, n_dp)]
    in_hbm = [
        pltpu.with_memory_space_constraint(value, pltpu.HBM)
        for value in (
            images, kv_weight, k_gain.reshape(1, -1), queries, q_gain.reshape(1, -1), tile_mask.T,
        )
    ]
    own, x, gain = call(
        functools.partial(own_kernel, head_dim),
        [
            shape_of((own_heads, 2, rows, head_dim)),
            shape_of(images.shape),
            shape_of((1, head_dim), F32),
        ],
        3,
        "own_head",
        flops=work,
        size=2 * (images.size + kv_weight.size),
        in_specs=[HBM] * 3,
        scratch=[pltpu.VMEM(kv_weight.shape, BF16), pltpu.SemaphoreType.DMA((3,))],
    )(*in_hbm[:3])
    qt, bias = call(
        query_kernel,
        [shape_of((head_dim, pairs)), shape_of((tiles, pairs), F32)],
        3,
        "queries",
        in_specs=[HBM] * 3,
        scratch=[
            pltpu.VMEM(queries.shape, BF16),
            pltpu.VMEM((1, head_dim), F32),
            pltpu.VMEM((tiles, tokens), jnp.int32),
            pltpu.SemaphoreType.DMA((3,)),
        ],
    )(*in_hbm[3:])

    def other(k):
        return call(
            functools.partial(other_kernel, head_dim), shape_of(own.shape), 2, "other_heads", flops=work
        )(x, others[k - 1])

    if n_dp == 2 and own_heads == 1:
        send = keep = sum_two_heads(own, other, bias)
    else:
        send, keep = sum_many_heads(own, [other(k) for k in range(1, n_dp)])
    far = [step for step in range(1, n_section) if step & (step - 1)]
    near = [step for step in range(1, n_section) if not step & (step - 1)]
    arrived = swap(send, "tensor", 1)
    halves = [swap(send, "section", step) for step in far]
    kv = call(norm_kernel, shape_of((2, rows, head_dim)), 3, "sum_norm")(gain, keep, arrived)
    finished = [swap(kv, "section", step) for step in near]
    both = []
    for value in halves:
        both += [value, swap(value, "tensor", 1)]
    state = []
    for here, there, operands in (
        ([0], [], [kv]),
        (near, [], finished),
        ([], far, both),
    ):
        first, last = here == [0], len(there) > 0
        outs = (
            shape_of((tokens, q_width))
            if last
            else [shape_of((1, pairs), F32), shape_of((1, pairs), F32), shape_of((head_dim, pairs), F32)]
        )
        parts = len(here) + len(there)
        state = call(
            functools.partial(attend_kernel, here, there, tile_len, first, last, head_dim),
            outs,
            3 + len(operands) + len(state),
            "attend",
            flops=4 * pairs * rows * head_dim * parts,
            exps=pairs * rows * parts,
        )(gain, qt, bias, *operands, *state)
    return state


def solution(mesh):
    in_specs = (
        P(("section", "dp"), "tensor"),
        P("dp", "section", "tensor"),
        P(None, "tensor", "dp"),
        P(),
        P(),
        P(("section", "dp"), None),
    )
    out_specs = P(("section", "dp"), "tensor")
    return jax.shard_map(
        on_device, mesh=mesh, in_specs=in_specs, out_specs=out_specs, check_vma=False
    )
```

```python
import functools

import jax
import jax.numpy as jnp
from jax import lax
from jax.experimental import pallas as pl
from jax.experimental.pallas import tpu as pltpu
from jax.sharding import PartitionSpec as P

EPSILON = 1e-05
MASKED_SCORE = -1e30
TOP_FLOOR = -1e29
VMEM = pl.BlockSpec(memory_space=pltpu.VMEM)
HBM = pl.BlockSpec(memory_space=pltpu.HBM)
F32 = jnp.float32
MIB = 1024 * 1024
LIMIT = 24 * MIB
BF16 = jnp.bfloat16


def shape_of(dims, dtype=BF16):
    return jax.ShapeDtypeStruct(dims, dtype)


def call(
    kernel, outs, n_in, name, flops=0, size=0, exps=0, in_specs=None, scratch=()
):
    many = isinstance(outs, list)
    return pl.pallas_call(
        kernel,
        out_shape=outs,
        in_specs=in_specs or [VMEM] * n_in,
        out_specs=[VMEM] * len(outs) if many else VMEM,
        scratch_shapes=scratch,
        compiler_params=pltpu.CompilerParams(vmem_limit_bytes=LIMIT),
        cost_estimate=pl.CostEstimate(flops=flops, bytes_accessed=size, transcendentals=exps),
        name=name,
    )


def normalize(values, gain_vec):
    mean_sq = jnp.mean(values * values, axis=-1, keepdims=True)
    return values * lax.rsqrt(mean_sq + EPSILON) * gain_vec


def project(x, w):
    return jnp.dot(
        x, jnp.concatenate([w[0], w[1]], axis=1), preferred_element_type=F32
    ).astype(BF16)


def store_heads(ref, base, both, head_dim):
    width = both.shape[1] // 2
    for head in range(width // head_dim):
        lo = head * head_dim
        ref[base + head, 0] = both[:, lo : lo + head_dim]
        ref[base + head, 1] = both[:, width + lo : width + lo + head_dim]


def prepare_queries(hbm, vmem, sems, qt_ref, bias_ref):
    copies = [pltpu.make_async_copy(a, b, sems.at[i]) for i, (a, b) in enumerate(zip(hbm, vmem))]
    for copy in copies:
        copy.start()
    for copy in copies:
        copy.wait()
    q_ref, q_gain_ref, mask_ref = vmem
    tokens = q_ref.shape[0]
    head_dim = q_gain_ref.shape[1]
    bias = jnp.where(mask_ref[...] > 0, 0.0, MASKED_SCORE).astype(F32)
    for head in range(q_ref.shape[1] // head_dim):
        rows = q_ref[:, head * head_dim : (head + 1) * head_dim].astype(F32)
        normed = normalize(rows, q_gain_ref[...]) * head_dim ** (-0.5)
        qt_ref[:, head * tokens : (head + 1) * tokens] = normed.T.astype(BF16)
        bias_ref[:, head * tokens : (head + 1) * tokens] = bias


def own_kernel(
    head_dim, x_hbm, w_hbm, k_gain_hbm, own_ref, x_ref, k_gain_ref, w_ref, sems
):
    moves = [(k_gain_hbm, k_gain_ref), (x_hbm, x_ref), (w_hbm, w_ref)]
    copies = [pltpu.make_async_copy(a, b, sems.at[i]) for i, (a, b) in enumerate(moves)]
    for copy in copies:
        copy.start()
    for copy in copies:
        copy.wait()
    store_heads(own_ref, 0, project(x_ref[0], w_ref[...]), head_dim)


def split_half(held, send_ref, keep_ref, partner_heads, own_heads):
    for i in range(send_ref.shape[0]):
        send_ref[i] = held[partner_heads + i]
        keep_ref[i] = held[own_heads + i]


def other_kernel(head_dim, x_ref, w_ref, other_ref):
    store_heads(other_ref, 0, project(x_ref[0], w_ref[...]), head_dim)


def spread_kernel(n_dp, n_tensor, own_ref, *refs):
    others, (send_ref, keep_ref, held) = refs[: n_dp - 1], refs[n_dp - 1 :]
    d = lax.axis_index("dp")
    own_heads = own_ref.shape[0]
    for k, ref in enumerate((own_ref, *others)):
        held[pl.ds((d ^ k) * own_heads, own_heads)] = ref[...]
    half = send_ref.shape[0]
    upper = lax.axis_index("tensor") // (n_tensor // 2)
    split_half(held, send_ref, keep_ref, (1 - upper) * half, upper * half)


def query_kernel(*refs):
    prepare_queries(refs[:3], refs[5:8], refs[8], *refs[3:5])


def first_sum_kernel(own_ref, first_ref, bias_ref, out_ref):
    out_ref[...] = (own_ref[...].astype(F32) + first_ref[...].astype(F32)).astype(BF16)


def has_own_head():
    return lax.axis_index("tensor") // 2 == lax.axis_index("dp")


def second_sum_kernel(first_sum_ref, other_ref, second_ref, out_ref):
    total = (other_ref[...].astype(F32) + second_ref[...].astype(F32)).astype(BF16)
    out_ref[...] = jnp.where(has_own_head(), first_sum_ref[...], total)


def add_kernel(bit, keep_ref, arrived_ref, send_ref, next_ref, held):
    held[...] = (keep_ref[...].astype(F32) + arrived_ref[...].astype(F32)).astype(BF16)
    half = send_ref.shape[0]
    upper = (lax.axis_index("tensor") // bit) % 2
    split_half(held, send_ref, next_ref, (1 - upper) * half, upper * half)


def add_last_kernel(keep_ref, arrived_ref, out_ref):
    out_ref[...] = (keep_ref[...].astype(F32) + arrived_ref[...].astype(F32)).astype(BF16)


def finish_rows(k_gain, one, two):
    keys = one[0].astype(F32) + two[0].astype(F32)
    values = one[1].astype(F32) + two[1].astype(F32)
    return normalize(keys, k_gain).astype(BF16), values.astype(BF16)


def norm_kernel(k_gain_ref, keep_ref, *refs):
    arrived = refs[0][0]
    if len(refs) > 2:
        arrived = jnp.where(has_own_head(), arrived, refs[1][0])
    refs[-1][0], refs[-1][1] = finish_rows(k_gain_ref[...], keep_ref[0], arrived)


def attend_kernel(near, far, tile_len, first, last, head_dim, k_gain_ref, qt_ref, bias_ref, *refs):
    near_refs, refs = refs[: len(near)], refs[len(near) :]
    far_refs, refs = refs[: 2 * len(far)], refs[2 * len(far) :]
    if not first:
        top_in, sum_in, mixed_in = refs[:3]
        refs = refs[3:]
    s = lax.axis_index("section")
    qt = qt_ref[...]
    parts = [(part[0], part[1]) for part in near_refs]
    for one, two in zip(far_refs[::2], far_refs[1::2]):
        parts.append(finish_rows(k_gain_ref[...], one.at[0], two.at[0]))
    rows = parts[0][0].shape[0]
    scores, biases = [], []
    top = TOP_FLOOR if first else top_in[...]
    for step, (keys, _) in zip((*near, *far), parts):
        score = jnp.dot(keys, qt, preferred_element_type=F32)
        bias = bias_ref[pl.ds(((s ^ step) * rows) // tile_len, 1), :]
        scores.append(score)
        biases.append(bias)
        top = jnp.maximum(top, jnp.max(score, axis=0, keepdims=True) + bias)
    row_sum, mixed = 0.0, 0.0
    if not first:
        scale = jnp.exp(top_in[...] - top)
        row_sum = sum_in[...] * scale
        mixed = mixed_in[...] * scale
    for (_, values), score, bias in zip(parts, scores, biases):
        weights = jnp.exp(score + (bias - top))
        row_sum = row_sum + jnp.sum(weights, axis=0, keepdims=True)
        mixed = mixed + lax.dot_general(
            values, weights.astype(BF16), (((0,), (0,)), ((), ())), preferred_element_type=F32
        )
    if not last:
        top_out, sum_out, mixed_out = refs
        top_out[...] = top
        sum_out[...] = row_sum
        mixed_out[...] = mixed
        return
    (out,) = refs
    has_any = jnp.max(bias_ref[...], axis=0, keepdims=True) > -1.0
    inverse = jnp.where(has_any, 1.0 / jnp.where(has_any, row_sum, 1.0), 0.0)
    context = (mixed * inverse).astype(BF16)
    tokens = out.shape[0]
    for head in range(out.shape[1] // head_dim):
        out[:, head * head_dim : (head + 1) * head_dim] = context[
            :, head * tokens : (head + 1) * tokens
        ].T


def swap(value, axis, k):
    return lax.ppermute(value, axis, [(i, i ^ k) for i in range(lax.axis_size(axis))])


def sum_two_heads(own, other, bias):
    devices = [(d, t) for d in range(2) for t in range(4)]

    def exchange(value, senders):
        hops = [
            (4 * d + t, 4 * d + (t ^ 2) if (t // 2 == d) == senders else 4 * (1 - d) + t)
            for d, t in devices
        ]
        return lax.ppermute(value, ("dp", "tensor"), hops)

    def pair_swap(value, takers):
        hops = [
            (4 * d + t, 4 * d + (t ^ 1 if (t // 2 == d) == takers else t)) for d, t in devices
        ]
        return lax.ppermute(value, ("dp", "tensor"), hops)

    first = exchange(own, False)
    rest = other(1)
    second = exchange(rest, True)
    first_sum = call(first_sum_kernel, shape_of(own.shape), 3, "first_sum")(own, first, bias)
    early = pair_swap(first_sum, True)
    total = call(second_sum_kernel, shape_of(own.shape), 3, "second_sum")(first_sum, rest, second)
    return total, [early, pair_swap(total, False)]


def sum_many_heads(own, others):
    n_dp, n_tensor = lax.axis_size("dp"), lax.axis_size("tensor")
    heads = own.shape[0] * n_dp
    half = shape_of((heads // 2, *own.shape[1:]))
    send, keep = call(
        functools.partial(spread_kernel, n_dp, n_tensor),
        [half, half],
        n_dp,
        "spread",
        scratch=[pltpu.VMEM((heads, *own.shape[1:]), BF16)],
    )(own, *others)
    bit = n_tensor // 2
    while bit > 1:
        arrived = swap(send, "tensor", bit)
        bit //= 2
        now = keep.shape
        if bit > 1:
            half = shape_of((now[0] // 2, *now[1:]))
            send, keep = call(
                functools.partial(add_kernel, bit),
                [half, half],
                2,
                "add_part",
                scratch=[pltpu.VMEM(now, BF16)],
            )(keep, arrived)
        else:
            keep = call(add_last_kernel, shape_of(now), 2, "add_pair")(keep, arrived)
    return keep


def on_device(queries, images, kv_weight, q_gain, k_gain, tile_mask):
    n_section = lax.axis_size("section")
    n_dp = lax.axis_size("dp")
    n_tensor = lax.axis_size("tensor")
    head_dim = q_gain.shape[0]
    tokens, q_width = queries.shape
    rows, features = images.shape[1:]
    tiles = tile_mask.shape[1]
    own_heads = kv_weight.shape[2] // head_dim
    heads = own_heads * n_dp
    tile_len = rows * n_section // tiles
    assert heads * 2 == n_tensor and tile_len % rows == 0 and n_section >= 4
    pairs = tokens * (q_width // head_dim)
    work = 4 * rows * features * kv_weight.shape[2]

    others = [swap(kv_weight, "dp", k) for k in range(1, n_dp)]
    in_hbm = [
        pltpu.with_memory_space_constraint(value, pltpu.HBM)
        for value in (
            images, kv_weight, k_gain.reshape(1, -1), queries, q_gain.reshape(1, -1), tile_mask.T,
        )
    ]
    own, x, gain = call(
        functools.partial(own_kernel, head_dim),
        [
            shape_of((own_heads, 2, rows, head_dim)),
            shape_of(images.shape),
            shape_of((1, head_dim), F32),
        ],
        3,
        "own_head",
        flops=work,
        size=2 * (images.size + kv_weight.size),
        in_specs=[HBM] * 3,
        scratch=[pltpu.VMEM(kv_weight.shape, BF16), pltpu.SemaphoreType.DMA((3,))],
    )(*in_hbm[:3])
    qt, bias = call(
        query_kernel,
        [shape_of((head_dim, pairs)), shape_of((tiles, pairs), F32)],
        3,
        "queries",
        in_specs=[HBM] * 3,
        scratch=[
            pltpu.VMEM(queries.shape, BF16),
            pltpu.VMEM((1, head_dim), F32),
            pltpu.VMEM((tiles, tokens), jnp.int32),
            pltpu.SemaphoreType.DMA((3,)),
        ],
    )(*in_hbm[3:])

    def other(k):
        return call(
            functools.partial(other_kernel, head_dim), shape_of(own.shape), 2, "other_heads", flops=work
        )(x, others[k - 1])

    if n_dp == 2 and own_heads == 1:
        total, arrived = sum_two_heads(own, other, bias)
    else:
        total = sum_many_heads(own, [other(k) for k in range(1, n_dp)])
        arrived = [swap(total, "tensor", 1)]
    far = [step for step in range(1, n_section) if step & (step - 1)]
    near = [step for step in range(1, n_section) if not step & (step - 1)]
    halves = [swap(total, "section", step) for step in far]
    kv = call(norm_kernel, shape_of((2, rows, head_dim)), 2 + len(arrived), "sum_norm")(
        gain, total, *arrived
    )
    finished = [swap(kv, "section", step) for step in near]
    both = []
    for value in halves:
        both += [value, swap(value, "tensor", 1)]
    state = []
    for here, there, operands in (
        ([0], [], [kv]),
        (near, [], finished),
        ([], far, both),
    ):
        first, last = here == [0], len(there) > 0
        outs = (
            shape_of((tokens, q_width))
            if last
            else [shape_of((1, pairs), F32), shape_of((1, pairs), F32), shape_of((head_dim, pairs), F32)]
        )
        parts = len(here) + len(there)
        state = call(
            functools.partial(attend_kernel, here, there, tile_len, first, last, head_dim),
            outs,
            3 + len(operands) + len(state),
            "attend",
            flops=4 * pairs * rows * head_dim * parts,
            exps=pairs * rows * parts,
        )(gain, qt, bias, *operands, *state)
    return state


def solution(mesh):
    in_specs = (
        P(("section", "dp"), "tensor"),
        P("dp", "section", "tensor"),
        P(None, "tensor", "dp"),
        P(),
        P(),
        P(("section", "dp"), None),
    )
    out_specs = P(("section", "dp"), "tensor")
    return jax.shard_map(
        on_device, mesh=mesh, in_specs=in_specs, out_specs=out_specs, check_vma=False
    )
```

```python
import functools

import jax
import jax.numpy as jnp
from jax import lax
from jax.experimental import pallas as pl
from jax.experimental.pallas import tpu as pltpu
from jax.sharding import PartitionSpec as P

EPSILON = 1e-05
MASKED_SCORE = -1e30
TOP_FLOOR = -1e29
VMEM = pl.BlockSpec(memory_space=pltpu.VMEM)
HBM = pl.BlockSpec(memory_space=pltpu.HBM)
F32 = jnp.float32
MIB = 1024 * 1024
LIMIT = 24 * MIB
BF16 = jnp.bfloat16


def shape_of(dims, dtype=BF16):
    return jax.ShapeDtypeStruct(dims, dtype)


def call(
    kernel, outs, n_in, name, flops=0, size=0, exps=0, in_specs=None, scratch=()
):
    many = isinstance(outs, list)
    return pl.pallas_call(
        kernel,
        out_shape=outs,
        in_specs=in_specs or [VMEM] * n_in,
        out_specs=[VMEM] * len(outs) if many else VMEM,
        scratch_shapes=scratch,
        compiler_params=pltpu.CompilerParams(vmem_limit_bytes=LIMIT),
        cost_estimate=pl.CostEstimate(flops=flops, bytes_accessed=size, transcendentals=exps),
        name=name,
    )


def normalize(values, gain_vec):
    mean_sq = jnp.mean(values * values, axis=-1, keepdims=True)
    return values * lax.rsqrt(mean_sq + EPSILON) * gain_vec


def project(x, w):
    return jnp.dot(
        x, jnp.concatenate([w[0], w[1]], axis=1), preferred_element_type=F32
    ).astype(BF16)


def store_heads(ref, base, both, head_dim):
    width = both.shape[1] // 2
    for head in range(width // head_dim):
        lo = head * head_dim
        ref[base + head, 0] = both[:, lo : lo + head_dim]
        ref[base + head, 1] = both[:, width + lo : width + lo + head_dim]


def prepare_queries(hbm, vmem, sems, qt_ref, bias_ref):
    copies = [pltpu.make_async_copy(a, b, sems.at[i]) for i, (a, b) in enumerate(zip(hbm, vmem))]
    for copy in copies:
        copy.start()
    for copy in copies:
        copy.wait()
    q_ref, q_gain_ref, mask_ref = vmem
    tokens = q_ref.shape[0]
    head_dim = q_gain_ref.shape[1]
    bias = jnp.where(mask_ref[...] > 0, 0.0, MASKED_SCORE).astype(F32)
    for head in range(q_ref.shape[1] // head_dim):
        rows = q_ref[:, head * head_dim : (head + 1) * head_dim].astype(F32)
        normed = normalize(rows, q_gain_ref[...]) * head_dim ** (-0.5)
        qt_ref[:, head * tokens : (head + 1) * tokens] = normed.T.astype(BF16)
        bias_ref[:, head * tokens : (head + 1) * tokens] = bias


def own_kernel(
    head_dim, x_hbm, w_hbm, k_gain_hbm, own_ref, x_ref, k_gain_ref, w_ref, sems
):
    moves = [(k_gain_hbm, k_gain_ref), (x_hbm, x_ref), (w_hbm, w_ref)]
    copies = [pltpu.make_async_copy(a, b, sems.at[i]) for i, (a, b) in enumerate(moves)]
    for copy in copies:
        copy.start()
    for copy in copies:
        copy.wait()
    store_heads(own_ref, 0, project(x_ref[0], w_ref[...]), head_dim)


def split_half(held, send_ref, keep_ref, partner_heads, own_heads):
    for i in range(send_ref.shape[0]):
        send_ref[i] = held[partner_heads + i]
        keep_ref[i] = held[own_heads + i]


def other_kernel(head_dim, x_ref, w_ref, other_ref):
    store_heads(other_ref, 0, project(x_ref[0], w_ref[...]), head_dim)


def spread_kernel(n_dp, n_tensor, own_ref, *refs):
    others, (send_ref, keep_ref, held) = refs[: n_dp - 1], refs[n_dp - 1 :]
    d = lax.axis_index("dp")
    own_heads = own_ref.shape[0]
    for k, ref in enumerate((own_ref, *others)):
        held[pl.ds((d ^ k) * own_heads, own_heads)] = ref[...]
    half = send_ref.shape[0]
    upper = lax.axis_index("tensor") // (n_tensor // 2)
    split_half(held, send_ref, keep_ref, (1 - upper) * half, upper * half)


def query_kernel(*refs):
    prepare_queries(refs[:3], refs[5:8], refs[8], *refs[3:5])


def pair_kernel(own_ref, other_ref, first_ref, second_ref, bias_ref, out_ref):
    mine = lax.axis_index("tensor") // 2 == lax.axis_index("dp")
    keep = jnp.where(mine, own_ref[...], other_ref[...]).astype(F32)
    arrived = jnp.where(mine, first_ref[...], second_ref[...]).astype(F32)
    out_ref[...] = (keep + arrived).astype(BF16)


def add_kernel(bit, keep_ref, arrived_ref, send_ref, next_ref, held):
    held[...] = (keep_ref[...].astype(F32) + arrived_ref[...].astype(F32)).astype(BF16)
    half = send_ref.shape[0]
    upper = (lax.axis_index("tensor") // bit) % 2
    split_half(held, send_ref, next_ref, (1 - upper) * half, upper * half)


def add_last_kernel(keep_ref, arrived_ref, out_ref):
    out_ref[...] = (keep_ref[...].astype(F32) + arrived_ref[...].astype(F32)).astype(BF16)


def finish_rows(k_gain, one, two):
    keys = one[0].astype(F32) + two[0].astype(F32)
    values = one[1].astype(F32) + two[1].astype(F32)
    return normalize(keys, k_gain).astype(BF16), values.astype(BF16)


def norm_kernel(k_gain_ref, keep_ref, arrived_ref, kv_ref):
    kv_ref[0], kv_ref[1] = finish_rows(k_gain_ref[...], keep_ref.at[0], arrived_ref.at[0])


def attend_kernel(near, far, tile_len, first, last, head_dim, k_gain_ref, qt_ref, bias_ref, *refs):
    near_refs, refs = refs[: len(near)], refs[len(near) :]
    far_refs, refs = refs[: 2 * len(far)], refs[2 * len(far) :]
    if not first:
        top_in, sum_in, mixed_in = refs[:3]
        refs = refs[3:]
    s = lax.axis_index("section")
    qt = qt_ref[...]
    parts = [(part[0], part[1]) for part in near_refs]
    for one, two in zip(far_refs[::2], far_refs[1::2]):
        parts.append(finish_rows(k_gain_ref[...], one.at[0], two.at[0]))
    rows = parts[0][0].shape[0]
    scores, biases = [], []
    top = TOP_FLOOR if first else top_in[...]
    for step, (keys, _) in zip((*near, *far), parts):
        score = jnp.dot(keys, qt, preferred_element_type=F32)
        bias = bias_ref[pl.ds(((s ^ step) * rows) // tile_len, 1), :]
        scores.append(score)
        biases.append(bias)
        top = jnp.maximum(top, jnp.max(score, axis=0, keepdims=True) + bias)
    row_sum, mixed = 0.0, 0.0
    if not first:
        scale = jnp.exp(top_in[...] - top)
        row_sum = sum_in[...] * scale
        mixed = mixed_in[...] * scale
    for (_, values), score, bias in zip(parts, scores, biases):
        weights = jnp.exp(score + (bias - top))
        row_sum = row_sum + jnp.sum(weights, axis=0, keepdims=True)
        mixed = mixed + lax.dot_general(
            values, weights.astype(BF16), (((0,), (0,)), ((), ())), preferred_element_type=F32
        )
    if not last:
        top_out, sum_out, mixed_out = refs
        top_out[...] = top
        sum_out[...] = row_sum
        mixed_out[...] = mixed
        return
    (out,) = refs
    has_any = jnp.max(bias_ref[...], axis=0, keepdims=True) > -1.0
    inverse = jnp.where(has_any, 1.0 / jnp.where(has_any, row_sum, 1.0), 0.0)
    context = (mixed * inverse).astype(BF16)
    tokens = out.shape[0]
    for head in range(out.shape[1] // head_dim):
        out[:, head * head_dim : (head + 1) * head_dim] = context[
            :, head * tokens : (head + 1) * tokens
        ].T


def swap(value, axis, k):
    return lax.ppermute(value, axis, [(i, i ^ k) for i in range(lax.axis_size(axis))])


def sum_two_heads(own, other, bias):
    devices = [(d, t) for d in range(2) for t in range(4)]

    def exchange(value, senders, apart):
        hops = [
            (4 * d + t, 4 * d + (t ^ apart) if (t // 2 == d) == senders else 4 * (1 - d) + t)
            for d, t in devices
        ]
        return lax.ppermute(value, ("dp", "tensor"), hops)

    first = exchange(own, False, 2)
    rest = other(1)
    second = exchange(rest, True, 3)
    return call(pair_kernel, shape_of(own.shape), 5, "pair_sum")(own, rest, first, second, bias)


def sum_many_heads(own, others):
    n_dp, n_tensor = lax.axis_size("dp"), lax.axis_size("tensor")
    heads = own.shape[0] * n_dp
    half = shape_of((heads // 2, *own.shape[1:]))
    send, keep = call(
        functools.partial(spread_kernel, n_dp, n_tensor),
        [half, half],
        n_dp,
        "spread",
        scratch=[pltpu.VMEM((heads, *own.shape[1:]), BF16)],
    )(own, *others)
    bit = n_tensor // 2
    while bit > 1:
        arrived = swap(send, "tensor", bit)
        bit //= 2
        now = keep.shape
        if bit > 1:
            half = shape_of((now[0] // 2, *now[1:]))
            send, keep = call(
                functools.partial(add_kernel, bit),
                [half, half],
                2,
                "add_part",
                scratch=[pltpu.VMEM(now, BF16)],
            )(keep, arrived)
        else:
            send = keep = call(add_last_kernel, shape_of(now), 2, "add_pair")(keep, arrived)
    return send, keep


def on_device(queries, images, kv_weight, q_gain, k_gain, tile_mask):
    n_section = lax.axis_size("section")
    n_dp = lax.axis_size("dp")
    n_tensor = lax.axis_size("tensor")
    head_dim = q_gain.shape[0]
    tokens, q_width = queries.shape
    rows, features = images.shape[1:]
    tiles = tile_mask.shape[1]
    own_heads = kv_weight.shape[2] // head_dim
    heads = own_heads * n_dp
    tile_len = rows * n_section // tiles
    assert heads * 2 == n_tensor and tile_len % rows == 0 and n_section >= 4
    pairs = tokens * (q_width // head_dim)
    work = 4 * rows * features * kv_weight.shape[2]

    others = [swap(kv_weight, "dp", k) for k in range(1, n_dp)]
    in_hbm = [
        pltpu.with_memory_space_constraint(value, pltpu.HBM)
        for value in (
            images, kv_weight, k_gain.reshape(1, -1), queries, q_gain.reshape(1, -1), tile_mask.T,
        )
    ]
    own, x, gain = call(
        functools.partial(own_kernel, head_dim),
        [
            shape_of((own_heads, 2, rows, head_dim)),
            shape_of(images.shape),
            shape_of((1, head_dim), F32),
        ],
        3,
        "own_head",
        flops=work,
        size=2 * (images.size + kv_weight.size),
        in_specs=[HBM] * 3,
        scratch=[pltpu.VMEM(kv_weight.shape, BF16), pltpu.SemaphoreType.DMA((3,))],
    )(*in_hbm[:3])
    qt, bias = call(
        query_kernel,
        [shape_of((head_dim, pairs)), shape_of((tiles, pairs), F32)],
        3,
        "queries",
        in_specs=[HBM] * 3,
        scratch=[
            pltpu.VMEM(queries.shape, BF16),
            pltpu.VMEM((1, head_dim), F32),
            pltpu.VMEM((tiles, tokens), jnp.int32),
            pltpu.SemaphoreType.DMA((3,)),
        ],
    )(*in_hbm[3:])

    def other(k):
        return call(
            functools.partial(other_kernel, head_dim), shape_of(own.shape), 2, "other_heads", flops=work
        )(x, others[k - 1])

    if n_dp == 2 and own_heads == 1:
        send = keep = sum_two_heads(own, other, bias)
    else:
        send, keep = sum_many_heads(own, [other(k) for k in range(1, n_dp)])
    far = [step for step in range(1, n_section) if step & (step - 1)]
    near = [step for step in range(1, n_section) if not step & (step - 1)]
    arrived = swap(send, "tensor", 1)
    halves = [swap(send, "section", step) for step in far]
    kv = call(norm_kernel, shape_of((2, rows, head_dim)), 3, "sum_norm")(gain, keep, arrived)
    finished = [swap(kv, "section", step) for step in near]
    both = []
    for value in halves:
        both += [value, swap(value, "tensor", 1)]
    state = []
    for here, there, operands in (
        ([0], [], [kv]),
        (near, [], finished),
        ([], far, both),
    ):
        first, last = here == [0], len(there) > 0
        outs = (
            shape_of((tokens, q_width))
            if last
            else [shape_of((1, pairs), F32), shape_of((1, pairs), F32), shape_of((head_dim, pairs), F32)]
        )
        parts = len(here) + len(there)
        state = call(
            functools.partial(attend_kernel, here, there, tile_len, first, last, head_dim),
            outs,
            3 + len(operands) + len(state),
            "attend",
            flops=4 * pairs * rows * head_dim * parts,
            exps=pairs * rows * parts,
        )(gain, qt, bias, *operands, *state)
    return state


def solution(mesh):
    in_specs = (
        P(("section", "dp"), "tensor"),
        P("dp", "section", "tensor"),
        P(None, "tensor", "dp"),
        P(),
        P(),
        P(("section", "dp"), None),
    )
    out_specs = P(("section", "dp"), "tensor")
    return jax.shard_map(
        on_device, mesh=mesh, in_specs=in_specs, out_specs=out_specs, check_vma=False
    )
```

```python
import functools

import jax
import jax.numpy as jnp
from jax import lax
from jax.experimental import pallas as pl
from jax.experimental.pallas import tpu as pltpu
from jax.sharding import PartitionSpec as P

EPSILON = 1e-05
MASKED_SCORE = -1e30
TOP_FLOOR = -1e29
VMEM = pl.BlockSpec(memory_space=pltpu.VMEM)
HBM = pl.BlockSpec(memory_space=pltpu.HBM)
F32 = jnp.float32
MIB = 1024 * 1024
LIMIT = 24 * MIB
BF16 = jnp.bfloat16


def shape_of(dims, dtype=BF16):
    return jax.ShapeDtypeStruct(dims, dtype)


def call(
    kernel, outs, n_in, name, flops=0, size=0, exps=0, in_specs=None, scratch=()
):
    many = isinstance(outs, list)
    return pl.pallas_call(
        kernel,
        out_shape=outs,
        in_specs=in_specs or [VMEM] * n_in,
        out_specs=[VMEM] * len(outs) if many else VMEM,
        scratch_shapes=scratch,
        compiler_params=pltpu.CompilerParams(vmem_limit_bytes=LIMIT),
        cost_estimate=pl.CostEstimate(flops=flops, bytes_accessed=size, transcendentals=exps),
        name=name,
    )


def normalize(values, gain_vec):
    mean_sq = jnp.mean(values * values, axis=-1, keepdims=True)
    return values * lax.rsqrt(mean_sq + EPSILON) * gain_vec


def project(x, w):
    return jnp.dot(
        x, jnp.concatenate([w[0], w[1]], axis=1), preferred_element_type=F32
    ).astype(BF16)


def store_heads(ref, base, both, head_dim):
    width = both.shape[1] // 2
    for head in range(width // head_dim):
        lo = head * head_dim
        ref[base + head, 0] = both[:, lo : lo + head_dim]
        ref[base + head, 1] = both[:, width + lo : width + lo + head_dim]


def prepare_queries(hbm, vmem, sems, qt_ref, bias_ref):
    copies = [pltpu.make_async_copy(a, b, sems.at[i]) for i, (a, b) in enumerate(zip(hbm, vmem))]
    for copy in copies:
        copy.start()
    for copy in copies:
        copy.wait()
    q_ref, q_gain_ref, mask_ref = vmem
    tokens = q_ref.shape[0]
    head_dim = q_gain_ref.shape[1]
    bias = jnp.where(mask_ref[...] > 0, 0.0, MASKED_SCORE).astype(F32)
    for head in range(q_ref.shape[1] // head_dim):
        rows = q_ref[:, head * head_dim : (head + 1) * head_dim].astype(F32)
        normed = normalize(rows, q_gain_ref[...]) * head_dim ** (-0.5)
        qt_ref[:, head * tokens : (head + 1) * tokens] = normed.T.astype(BF16)
        bias_ref[:, head * tokens : (head + 1) * tokens] = bias


def own_kernel(
    head_dim, x_hbm, w_hbm, k_gain_hbm, own_ref, x_ref, w_ref, k_gain_ref, sems
):
    moves = [(k_gain_hbm, k_gain_ref), (x_hbm, x_ref), (w_hbm, w_ref)]
    copies = [pltpu.make_async_copy(a, b, sems.at[i]) for i, (a, b) in enumerate(moves)]
    for copy in copies:
        copy.start()
    for copy in copies:
        copy.wait()
    store_heads(own_ref, 0, project(x_ref[0], w_ref[...]), head_dim)


def split_half(held, send_ref, keep_ref, partner_heads, own_heads):
    for i in range(send_ref.shape[0]):
        send_ref[i] = held[partner_heads + i]
        keep_ref[i] = held[own_heads + i]


def other_kernel(head_dim, x_ref, w_ref, other_ref):
    store_heads(other_ref, 0, project(x_ref[0], w_ref[...]), head_dim)


def spread_kernel(n_dp, n_tensor, own_ref, *refs):
    others, (send_ref, keep_ref, held) = refs[: n_dp - 1], refs[n_dp - 1 :]
    d = lax.axis_index("dp")
    own_heads = own_ref.shape[0]
    for k, ref in enumerate((own_ref, *others)):
        held[pl.ds((d ^ k) * own_heads, own_heads)] = ref[...]
    half = send_ref.shape[0]
    upper = lax.axis_index("tensor") // (n_tensor // 2)
    split_half(held, send_ref, keep_ref, (1 - upper) * half, upper * half)


def query_kernel(*refs):
    prepare_queries(refs[:3], refs[5:8], refs[8], *refs[3:5])


def pair_kernel(own_ref, first_ref, stayed_ref, crossed_ref, bias_ref, out_ref):
    mine = lax.axis_index("tensor") // 2 == lax.axis_index("dp")
    one = jnp.where(mine, own_ref[...], stayed_ref[...]).astype(F32)
    two = jnp.where(mine, first_ref[...], crossed_ref[...]).astype(F32)
    out_ref[...] = (one + two).astype(BF16)


def add_kernel(bit, keep_ref, arrived_ref, send_ref, next_ref, held):
    held[...] = (keep_ref[...].astype(F32) + arrived_ref[...].astype(F32)).astype(BF16)
    half = send_ref.shape[0]
    upper = (lax.axis_index("tensor") // bit) % 2
    split_half(held, send_ref, next_ref, (1 - upper) * half, upper * half)


def add_last_kernel(keep_ref, arrived_ref, out_ref):
    out_ref[...] = (keep_ref[...].astype(F32) + arrived_ref[...].astype(F32)).astype(BF16)


def finish_rows(k_gain, one, two):
    keys = one[0].astype(F32) + two[0].astype(F32)
    values = one[1].astype(F32) + two[1].astype(F32)
    return normalize(keys, k_gain).astype(BF16), values.astype(BF16)


def norm_kernel(k_gain_ref, keep_ref, arrived_ref, kv_ref):
    kv_ref[0], kv_ref[1] = finish_rows(k_gain_ref[...], keep_ref.at[0], arrived_ref.at[0])


def attend_kernel(near, far, tile_len, first, last, head_dim, k_gain_ref, qt_ref, bias_ref, *refs):
    near_refs, refs = refs[: len(near)], refs[len(near) :]
    far_refs, refs = refs[: 2 * len(far)], refs[2 * len(far) :]
    if not first:
        top_in, sum_in, mixed_in = refs[:3]
        refs = refs[3:]
    s = lax.axis_index("section")
    qt = qt_ref[...]
    parts = [(part[0], part[1]) for part in near_refs]
    for one, two in zip(far_refs[::2], far_refs[1::2]):
        parts.append(finish_rows(k_gain_ref[...], one.at[0], two.at[0]))
    rows = parts[0][0].shape[0]
    scores, biases = [], []
    top = TOP_FLOOR if first else top_in[...]
    for step, (keys, _) in zip((*near, *far), parts):
        score = jnp.dot(keys, qt, preferred_element_type=F32)
        bias = bias_ref[pl.ds(((s ^ step) * rows) // tile_len, 1), :]
        scores.append(score)
        biases.append(bias)
        top = jnp.maximum(top, jnp.max(score, axis=0, keepdims=True) + bias)
    row_sum, mixed = 0.0, 0.0
    if not first:
        scale = jnp.exp(top_in[...] - top)
        row_sum = sum_in[...] * scale
        mixed = mixed_in[...] * scale
    for (_, values), score, bias in zip(parts, scores, biases):
        weights = jnp.exp(score + (bias - top))
        row_sum = row_sum + jnp.sum(weights, axis=0, keepdims=True)
        mixed = mixed + lax.dot_general(
            values, weights.astype(BF16), (((0,), (0,)), ((), ())), preferred_element_type=F32
        )
    if not last:
        top_out, sum_out, mixed_out = refs
        top_out[...] = top
        sum_out[...] = row_sum
        mixed_out[...] = mixed
        return
    (out,) = refs
    has_any = jnp.max(bias_ref[...], axis=0, keepdims=True) > -1.0
    inverse = jnp.where(has_any, 1.0 / jnp.where(has_any, row_sum, 1.0), 0.0)
    context = (mixed * inverse).astype(BF16)
    tokens = out.shape[0]
    for head in range(out.shape[1] // head_dim):
        out[:, head * head_dim : (head + 1) * head_dim] = context[
            :, head * tokens : (head + 1) * tokens
        ].T


def swap(value, axis, k):
    return lax.ppermute(value, axis, [(i, i ^ k) for i in range(lax.axis_size(axis))])


def sum_two_heads(own, images, w, bias, other):
    devices = [(d, t) for d in range(2) for t in range(4)]

    def permute(value, away, home):
        hops = []
        for d, t in devices:
            to_d, to_t = away(d, t) if t // 2 != d else home(d, t)
            hops.append((4 * d + t, 4 * to_d + to_t))
        return lax.ppermute(value, ("dp", "tensor"), hops)

    other_image = swap(images, "dp", 1)
    first = permute(own, lambda d, t: (d, t ^ 2), lambda d, t: (1 - d, t))
    rest = other(other_image, w)
    stayed = permute(rest, lambda d, t: (1 - d, t), lambda d, t: (1 - d, t))
    crossed = permute(rest, lambda d, t: (1 - d, t ^ 2), lambda d, t: (d, t))
    return call(pair_kernel, shape_of(own.shape), 5, "pair_sum")(
        own, first, stayed, crossed, bias
    )


def sum_many_heads(own, others):
    n_dp, n_tensor = lax.axis_size("dp"), lax.axis_size("tensor")
    heads = own.shape[0] * n_dp
    half = shape_of((heads // 2, *own.shape[1:]))
    send, keep = call(
        functools.partial(spread_kernel, n_dp, n_tensor),
        [half, half],
        n_dp,
        "spread",
        scratch=[pltpu.VMEM((heads, *own.shape[1:]), BF16)],
    )(own, *others)
    bit = n_tensor // 2
    while bit > 1:
        arrived = swap(send, "tensor", bit)
        bit //= 2
        now = keep.shape
        if bit > 1:
            half = shape_of((now[0] // 2, *now[1:]))
            send, keep = call(
                functools.partial(add_kernel, bit),
                [half, half],
                2,
                "add_part",
                scratch=[pltpu.VMEM(now, BF16)],
            )(keep, arrived)
        else:
            keep = call(add_last_kernel, shape_of(now), 2, "add_pair")(keep, arrived)
    return keep


def on_device(queries, images, kv_weight, q_gain, k_gain, tile_mask):
    n_section = lax.axis_size("section")
    n_dp = lax.axis_size("dp")
    n_tensor = lax.axis_size("tensor")
    head_dim = q_gain.shape[0]
    tokens, q_width = queries.shape
    rows, features = images.shape[1:]
    tiles = tile_mask.shape[1]
    own_heads = kv_weight.shape[2] // head_dim
    heads = own_heads * n_dp
    tile_len = rows * n_section // tiles
    assert heads * 2 == n_tensor and tile_len % rows == 0 and n_section >= 4
    pairs = tokens * (q_width // head_dim)
    work = 4 * rows * features * kv_weight.shape[2]

    in_hbm = [
        pltpu.with_memory_space_constraint(value, pltpu.HBM)
        for value in (
            images, kv_weight, k_gain.reshape(1, -1), queries, q_gain.reshape(1, -1), tile_mask.T,
        )
    ]
    own, x, w, gain = call(
        functools.partial(own_kernel, head_dim),
        [
            shape_of((own_heads, 2, rows, head_dim)),
            shape_of(images.shape),
            shape_of(kv_weight.shape),
            shape_of((1, head_dim), F32),
        ],
        3,
        "own_head",
        flops=work,
        size=2 * (images.size + kv_weight.size),
        in_specs=[HBM] * 3,
        scratch=[pltpu.SemaphoreType.DMA((3,))],
    )(*in_hbm[:3])
    qt, bias = call(
        query_kernel,
        [shape_of((head_dim, pairs)), shape_of((tiles, pairs), F32)],
        3,
        "queries",
        in_specs=[HBM] * 3,
        scratch=[
            pltpu.VMEM(queries.shape, BF16),
            pltpu.VMEM((1, head_dim), F32),
            pltpu.VMEM((tiles, tokens), jnp.int32),
            pltpu.SemaphoreType.DMA((3,)),
        ],
    )(*in_hbm[3:])

    def other(rows_of, columns):
        return call(
            functools.partial(other_kernel, head_dim), shape_of(own.shape), 2, "other_heads", flops=work
        )(rows_of, columns)

    if n_dp == 2 and own_heads == 1:
        total = sum_two_heads(own, images, w, bias, other)
    else:
        rest = [other(x, swap(kv_weight, "dp", k)) for k in range(1, n_dp)]
        total = sum_many_heads(own, rest)
    far = [step for step in range(1, n_section) if step & (step - 1)]
    near = [step for step in range(1, n_section) if not step & (step - 1)]
    arrived = swap(total, "tensor", 1)
    halves = [swap(total, "section", step) for step in far]
    kv = call(norm_kernel, shape_of((2, rows, head_dim)), 3, "sum_norm")(gain, total, arrived)
    finished = [swap(kv, "section", step) for step in near]
    both = []
    for value in halves:
        both += [value, swap(value, "tensor", 1)]
    state = []
    for here, there, operands in (
        ([0], [], [kv]),
        (near, [], finished),
        ([], far, both),
    ):
        first, last = here == [0], len(there) > 0
        outs = (
            shape_of((tokens, q_width))
            if last
            else [shape_of((1, pairs), F32), shape_of((1, pairs), F32), shape_of((head_dim, pairs), F32)]
        )
        parts = len(here) + len(there)
        state = call(
            functools.partial(attend_kernel, here, there, tile_len, first, last, head_dim),
            outs,
            3 + len(operands) + len(state),
            "attend",
            flops=4 * pairs * rows * head_dim * parts,
            exps=pairs * rows * parts,
        )(gain, qt, bias, *operands, *state)
    return state


def solution(mesh):
    in_specs = (
        P(("section", "dp"), "tensor"),
        P("dp", "section", "tensor"),
        P(None, "tensor", "dp"),
        P(),
        P(),
        P(("section", "dp"), None),
    )
    out_specs = P(("section", "dp"), "tensor")
    return jax.shard_map(
        on_device, mesh=mesh, in_specs=in_specs, out_specs=out_specs, check_vma=False
    )
```

```python
import functools

import jax
import jax.numpy as jnp
from jax import lax
from jax.experimental import pallas as pl
from jax.experimental.pallas import tpu as pltpu
from jax.sharding import PartitionSpec as P

EPSILON = 1e-05
MASKED_SCORE = -1e30
TOP_FLOOR = -1e29
VMEM = pl.BlockSpec(memory_space=pltpu.VMEM)
HBM = pl.BlockSpec(memory_space=pltpu.HBM)
F32 = jnp.float32
MIB = 1024 * 1024
LIMIT = 24 * MIB
BF16 = jnp.bfloat16


def shape_of(dims, dtype=BF16):
    return jax.ShapeDtypeStruct(dims, dtype)


def call(
    kernel, outs, n_in, name, flops=0, size=0, exps=0, in_specs=None, scratch=()
):
    many = isinstance(outs, list)
    return pl.pallas_call(
        kernel,
        out_shape=outs,
        in_specs=in_specs or [VMEM] * n_in,
        out_specs=[VMEM] * len(outs) if many else VMEM,
        scratch_shapes=scratch,
        compiler_params=pltpu.CompilerParams(vmem_limit_bytes=LIMIT),
        cost_estimate=pl.CostEstimate(flops=flops, bytes_accessed=size, transcendentals=exps),
        name=name,
    )


def normalize(values, gain_vec):
    mean_sq = jnp.mean(values * values, axis=-1, keepdims=True)
    return values * lax.rsqrt(mean_sq + EPSILON) * gain_vec


def project(x, w):
    return jnp.dot(
        x, jnp.concatenate([w[0], w[1]], axis=1), preferred_element_type=F32
    ).astype(BF16)


def store_heads(ref, base, both, head_dim):
    width = both.shape[1] // 2
    for head in range(width // head_dim):
        lo = head * head_dim
        ref[base + head, 0] = both[:, lo : lo + head_dim]
        ref[base + head, 1] = both[:, width + lo : width + lo + head_dim]


def prepare_queries(copies, q_ref, q_gain_ref, mask_ref, qt_ref, bias_ref):
    for copy in copies:
        copy.wait()
    tokens = q_ref.shape[0]
    head_dim = q_gain_ref.shape[1]
    bias = jnp.where(mask_ref[...] > 0, 0.0, MASKED_SCORE).astype(F32)
    for head in range(q_ref.shape[1] // head_dim):
        rows = q_ref[:, head * head_dim : (head + 1) * head_dim].astype(F32)
        normed = normalize(rows, q_gain_ref[...]) * head_dim ** (-0.5)
        qt_ref[:, head * tokens : (head + 1) * tokens] = normed.T.astype(BF16)
        bias_ref[:, head * tokens : (head + 1) * tokens] = bias


def start_copies(sources, targets, sems, first=0):
    copies = [
        pltpu.make_async_copy(a, b, sems.at[first + i]) for i, (a, b) in enumerate(zip(sources, targets))
    ]
    for copy in copies:
        copy.start()
    return copies


def own_kernel(head_dim, x_hbm, w_hbm, own_ref, x_ref, w_ref, sems):
    for copy in start_copies((x_hbm, w_hbm), (x_ref, w_ref), sems):
        copy.wait()
    store_heads(own_ref, 0, project(x_ref[0], w_ref[...]), head_dim)


def other_kernel(head_dim, x_ref, w_ref, other_ref):
    store_heads(other_ref, 0, project(x_ref[0], w_ref[...]), head_dim)


def query_kernel(
    q_hbm, q_gain_hbm, mask_hbm, k_gain_hbm, qt_ref, bias_ref, k_gain_ref,
    q_ref, q_gain_ref, mask_ref, sems,
):
    copies = start_copies(
        (q_hbm, q_gain_hbm, mask_hbm, k_gain_hbm), (q_ref, q_gain_ref, mask_ref, k_gain_ref), sems
    )
    prepare_queries(copies, q_ref, q_gain_ref, mask_ref, qt_ref, bias_ref)


def is_home():
    return lax.axis_index("tensor") // 2 == lax.axis_index("dp")


def away_kernel(head_dim, x_hbm, w_hbm, own_ref, x_ref, w_ref, sems):
    @pl.when(is_home())
    def _():
        own_ref[...] = jnp.zeros_like(own_ref)

    @pl.when(jnp.logical_not(is_home()))
    def _():
        own_kernel(head_dim, x_hbm, w_hbm, own_ref, x_ref, w_ref, sems)


def home_kernel(head_dim, x_hbm, w_other_ref, other_ref, x_ref, sems):
    @pl.when(is_home())
    def _():
        for copy in start_copies((x_hbm,), (x_ref,), sems):
            copy.wait()
        store_heads(other_ref, 0, project(x_ref[0], w_other_ref[...]), head_dim)

    @pl.when(jnp.logical_not(is_home()))
    def _():
        other_ref[...] = jnp.zeros_like(other_ref)


def keep_kernel(
    head_dim, after_ref, w_other_ref, x_hbm, w_hbm, q_hbm, q_gain_hbm, mask_hbm, k_gain_hbm,
    keep_ref, qt_ref, bias_ref, k_gain_ref, x_ref, w_ref, q_ref, q_gain_ref, mask_ref, sems,
):
    copies = start_copies(
        (q_hbm, q_gain_hbm, mask_hbm, k_gain_hbm), (q_ref, q_gain_ref, mask_ref, k_gain_ref), sems
    )
    moves = start_copies((x_hbm, w_hbm), (x_ref, w_ref), sems, len(copies))
    prepare_queries(copies, q_ref, q_gain_ref, mask_ref, qt_ref, bias_ref)
    for copy in moves:
        copy.wait()

    @pl.when(is_home())
    def _():
        store_heads(keep_ref, 0, project(x_ref[0], w_ref[...]), head_dim)

    @pl.when(jnp.logical_not(is_home()))
    def _():
        store_heads(keep_ref, 0, project(x_ref[0], w_other_ref[...]), head_dim)


def split_half(held, send_ref, keep_ref, partner_heads, own_heads):
    for i in range(send_ref.shape[0]):
        send_ref[i] = held[partner_heads + i]
        keep_ref[i] = held[own_heads + i]


def spread_kernel(n_dp, n_tensor, own_ref, *refs):
    others, (send_ref, keep_ref, held) = refs[: n_dp - 1], refs[n_dp - 1 :]
    d = lax.axis_index("dp")
    own_heads = own_ref.shape[0]
    for k, ref in enumerate((own_ref, *others)):
        held[pl.ds((d ^ k) * own_heads, own_heads)] = ref[...]
    half = send_ref.shape[0]
    upper = lax.axis_index("tensor") // (n_tensor // 2)
    split_half(held, send_ref, keep_ref, (1 - upper) * half, upper * half)


def pair_kernel(keep_ref, first_ref, second_ref, out_ref):
    arrived = jnp.where(is_home(), first_ref[...], second_ref[...]).astype(F32)
    out_ref[...] = (keep_ref[...].astype(F32) + arrived).astype(BF16)


def add_kernel(bit, keep_ref, arrived_ref, send_ref, next_ref, held):
    held[...] = (keep_ref[...].astype(F32) + arrived_ref[...].astype(F32)).astype(BF16)
    half = send_ref.shape[0]
    upper = (lax.axis_index("tensor") // bit) % 2
    split_half(held, send_ref, next_ref, (1 - upper) * half, upper * half)


def add_last_kernel(keep_ref, arrived_ref, out_ref):
    out_ref[...] = (keep_ref[...].astype(F32) + arrived_ref[...].astype(F32)).astype(BF16)


def finish_rows(k_gain, one, two):
    keys = one[0].astype(F32) + two[0].astype(F32)
    values = one[1].astype(F32) + two[1].astype(F32)
    return normalize(keys, k_gain).astype(BF16), values.astype(BF16)


def norm_kernel(k_gain_ref, keep_ref, arrived_ref, kv_ref):
    kv_ref[0], kv_ref[1] = finish_rows(k_gain_ref[...], keep_ref.at[0], arrived_ref.at[0])


def attend_kernel(near, far, tile_len, first, last, head_dim, k_gain_ref, qt_ref, bias_ref, *refs):
    near_refs, refs = refs[: len(near)], refs[len(near) :]
    far_refs, refs = refs[: 2 * len(far)], refs[2 * len(far) :]
    if not first:
        top_in, sum_in, mixed_in = refs[:3]
        refs = refs[3:]
    s = lax.axis_index("section")
    qt = qt_ref[...]
    parts = [(part[0], part[1]) for part in near_refs]
    for one, two in zip(far_refs[::2], far_refs[1::2]):
        parts.append(finish_rows(k_gain_ref[...], one.at[0], two.at[0]))
    rows = parts[0][0].shape[0]
    scores, biases = [], []
    top = TOP_FLOOR if first else top_in[...]
    for step, (keys, _) in zip((*near, *far), parts):
        score = jnp.dot(keys, qt, preferred_element_type=F32)
        bias = bias_ref[pl.ds(((s ^ step) * rows) // tile_len, 1), :]
        scores.append(score)
        biases.append(bias)
        top = jnp.maximum(top, jnp.max(score, axis=0, keepdims=True) + bias)
    row_sum, mixed = 0.0, 0.0
    if not first:
        scale = jnp.exp(top_in[...] - top)
        row_sum = sum_in[...] * scale
        mixed = mixed_in[...] * scale
    for (_, values), score, bias in zip(parts, scores, biases):
        weights = jnp.exp(score + (bias - top))
        row_sum = row_sum + jnp.sum(weights, axis=0, keepdims=True)
        mixed = mixed + lax.dot_general(
            values, weights.astype(BF16), (((0,), (0,)), ((), ())), preferred_element_type=F32
        )
    if not last:
        top_out, sum_out, mixed_out = refs
        top_out[...] = top
        sum_out[...] = row_sum
        mixed_out[...] = mixed
        return
    (out,) = refs
    has_any = jnp.max(bias_ref[...], axis=0, keepdims=True) > -1.0
    inverse = jnp.where(has_any, 1.0 / jnp.where(has_any, row_sum, 1.0), 0.0)
    context = (mixed * inverse).astype(BF16)
    tokens = out.shape[0]
    for head in range(out.shape[1] // head_dim):
        out[:, head * head_dim : (head + 1) * head_dim] = context[
            :, head * tokens : (head + 1) * tokens
        ].T


def swap(value, axis, k):
    return lax.ppermute(value, axis, [(i, i ^ k) for i in range(lax.axis_size(axis))])


def exchange_two_heads(value, home_sends):
    hops = []
    for d in range(2):
        for t in range(4):
            sends = (t // 2 == d) == home_sends
            hops.append((4 * d + t, 4 * d + (t ^ 2) if sends else 4 * (1 - d) + t))
    return lax.ppermute(value, ("dp", "tensor"), hops)


def sum_many_heads(own, others):
    n_dp, n_tensor = lax.axis_size("dp"), lax.axis_size("tensor")
    heads = own.shape[0] * n_dp
    half = shape_of((heads // 2, *own.shape[1:]))
    send, keep = call(
        functools.partial(spread_kernel, n_dp, n_tensor),
        [half, half],
        n_dp,
        "spread",
        scratch=[pltpu.VMEM((heads, *own.shape[1:]), BF16)],
    )(own, *others)
    bit = n_tensor // 2
    while bit > 1:
        arrived = swap(send, "tensor", bit)
        bit //= 2
        now = keep.shape
        if bit > 1:
            half = shape_of((now[0] // 2, *now[1:]))
            send, keep = call(
                functools.partial(add_kernel, bit),
                [half, half],
                2,
                "add_part",
                scratch=[pltpu.VMEM(now, BF16)],
            )(keep, arrived)
        else:
            keep = call(add_last_kernel, shape_of(now), 2, "add_pair")(keep, arrived)
    return keep


def on_device(queries, images, kv_weight, q_gain, k_gain, tile_mask):
    n_section = lax.axis_size("section")
    n_dp = lax.axis_size("dp")
    n_tensor = lax.axis_size("tensor")
    head_dim = q_gain.shape[0]
    tokens, q_width = queries.shape
    rows, features = images.shape[1:]
    tiles = tile_mask.shape[1]
    own_heads = kv_weight.shape[2] // head_dim
    heads = own_heads * n_dp
    tile_len = rows * n_section // tiles
    assert heads * 2 == n_tensor and tile_len % rows == 0 and n_section >= 4
    pairs = tokens * (q_width // head_dim)
    work = 4 * rows * features * kv_weight.shape[2]

    x, w, *small = [
        pltpu.with_memory_space_constraint(value, pltpu.HBM)
        for value in (
            images, kv_weight, queries, q_gain.reshape(1, -1), tile_mask.T, k_gain.reshape(1, -1),
        )
    ]
    product = shape_of((own_heads, 2, rows, head_dim))
    x_scratch, w_scratch = pltpu.VMEM(images.shape, BF16), pltpu.VMEM(kv_weight.shape, BF16)
    prepared = [
        shape_of((head_dim, pairs)),
        shape_of((tiles, pairs), F32),
        shape_of((1, head_dim), F32),
    ]
    query_scratch = [
        pltpu.VMEM(queries.shape, BF16),
        pltpu.VMEM((1, head_dim), F32),
        pltpu.VMEM((tiles, tokens), jnp.int32),
    ]
    others = [swap(kv_weight, "dp", k) for k in range(1, n_dp)]
    if n_dp == 2 and own_heads == 1:
        away = call(
            functools.partial(away_kernel, head_dim),
            product,
            2,
            "away_own",
            flops=work,
            in_specs=[HBM] * 2,
            scratch=[x_scratch, w_scratch, pltpu.SemaphoreType.DMA((2,))],
        )(x, w)
        first = exchange_two_heads(away, False)
        home = call(
            functools.partial(home_kernel, head_dim),
            product,
            2,
            "home_other",
            flops=work,
            in_specs=[HBM, VMEM],
            scratch=[x_scratch, pltpu.SemaphoreType.DMA((1,))],
        )(x, others[0])
        second = exchange_two_heads(home, True)
        keep, qt, bias, gain = call(
            functools.partial(keep_kernel, head_dim),
            [product, *prepared],
            8,
            "keep_queries",
            flops=work,
            in_specs=[VMEM] * 2 + [HBM] * 6,
            scratch=[x_scratch, w_scratch, *query_scratch, pltpu.SemaphoreType.DMA((6,))],
        )(home, others[0], x, w, *small)
        total = call(pair_kernel, product, 3, "pair_sum")(keep, first, second)
    else:
        own, x_here = call(
            functools.partial(own_kernel, head_dim),
            [product, shape_of(images.shape)],
            2,
            "own_heads",
            flops=work,
            in_specs=[HBM] * 2,
            scratch=[w_scratch, pltpu.SemaphoreType.DMA((2,))],
        )(x, w)
        qt, bias, gain = call(
            query_kernel,
            prepared,
            4,
            "queries",
            in_specs=[HBM] * 4,
            scratch=[*query_scratch, pltpu.SemaphoreType.DMA((4,))],
        )(*small)
        rest = [
            call(functools.partial(other_kernel, head_dim), product, 2, "other_heads", flops=work)(
                x_here, other
            )
            for other in others
        ]
        total = sum_many_heads(own, rest)
    far = [step for step in range(1, n_section) if step & (step - 1)]
    near = [step for step in range(1, n_section) if not step & (step - 1)]
    arrived = swap(total, "tensor", 1)
    halves = [swap(total, "section", step) for step in far]
    kv = call(norm_kernel, shape_of((2, rows, head_dim)), 3, "sum_norm")(gain, total, arrived)
    finished = [swap(kv, "section", step) for step in near]
    both = []
    for value in halves:
        both += [value, swap(value, "tensor", 1)]
    state = []
    for here, there, operands in (
        ([0], [], [kv]),
        (near, [], finished),
        ([], far, both),
    ):
        first, last = here == [0], len(there) > 0
        outs = (
            shape_of((tokens, q_width))
            if last
            else [shape_of((1, pairs), F32), shape_of((1, pairs), F32), shape_of((head_dim, pairs), F32)]
        )
        parts = len(here) + len(there)
        state = call(
            functools.partial(attend_kernel, here, there, tile_len, first, last, head_dim),
            outs,
            3 + len(operands) + len(state),
            "attend",
            flops=4 * pairs * rows * head_dim * parts,
            exps=pairs * rows * parts,
        )(gain, qt, bias, *operands, *state)
    return state


def solution(mesh):
    in_specs = (
        P(("section", "dp"), "tensor"),
        P("dp", "section", "tensor"),
        P(None, "tensor", "dp"),
        P(),
        P(),
        P(("section", "dp"), None),
    )
    out_specs = P(("section", "dp"), "tensor")
    return jax.shard_map(
        on_device, mesh=mesh, in_specs=in_specs, out_specs=out_specs, check_vma=False
    )
```

```python
import functools

import jax
import jax.numpy as jnp
from jax import lax
from jax.experimental import pallas as pl
from jax.experimental.pallas import tpu as pltpu
from jax.sharding import PartitionSpec as P

EPSILON = 1e-05
MASKED_SCORE = -1e30
TOP_FLOOR = -1e29
VMEM = pl.BlockSpec(memory_space=pltpu.VMEM)
HBM = pl.BlockSpec(memory_space=pltpu.HBM)
F32 = jnp.float32
MIB = 1024 * 1024
LIMIT = 24 * MIB
BF16 = jnp.bfloat16


def shape_of(dims, dtype=BF16):
    return jax.ShapeDtypeStruct(dims, dtype)


def call(
    kernel, outs, n_in, name, flops=0, size=0, exps=0, in_specs=None, scratch=()
):
    many = isinstance(outs, list)
    return pl.pallas_call(
        kernel,
        out_shape=outs,
        in_specs=in_specs or [VMEM] * n_in,
        out_specs=[VMEM] * len(outs) if many else VMEM,
        scratch_shapes=scratch,
        compiler_params=pltpu.CompilerParams(vmem_limit_bytes=LIMIT),
        cost_estimate=pl.CostEstimate(flops=flops, bytes_accessed=size, transcendentals=exps),
        name=name,
    )


def normalize(values, gain_vec):
    mean_sq = jnp.mean(values * values, axis=-1, keepdims=True)
    return values * lax.rsqrt(mean_sq + EPSILON) * gain_vec


def project(x, w):
    return jnp.dot(
        x, jnp.concatenate([w[0], w[1]], axis=1), preferred_element_type=F32
    ).astype(BF16)


def store_heads(ref, base, both, head_dim):
    width = both.shape[1] // 2
    for head in range(width // head_dim):
        lo = head * head_dim
        ref[base + head, 0] = both[:, lo : lo + head_dim]
        ref[base + head, 1] = both[:, width + lo : width + lo + head_dim]


def prepare_queries(copies, q_ref, q_gain_ref, mask_ref, qt_ref, bias_ref):
    for copy in copies:
        copy.wait()
    tokens = q_ref.shape[0]
    head_dim = q_gain_ref.shape[1]
    bias = jnp.where(mask_ref[...] > 0, 0.0, MASKED_SCORE).astype(F32)
    for head in range(q_ref.shape[1] // head_dim):
        rows = q_ref[:, head * head_dim : (head + 1) * head_dim].astype(F32)
        normed = normalize(rows, q_gain_ref[...]) * head_dim ** (-0.5)
        qt_ref[:, head * tokens : (head + 1) * tokens] = normed.T.astype(BF16)
        bias_ref[:, head * tokens : (head + 1) * tokens] = bias


def start_copies(sources, targets, sems, first=0):
    copies = [
        pltpu.make_async_copy(a, b, sems.at[first + i]) for i, (a, b) in enumerate(zip(sources, targets))
    ]
    for copy in copies:
        copy.start()
    return copies


def own_kernel(head_dim, x_hbm, w_hbm, own_ref, x_ref, w_ref, sems):
    for copy in start_copies((x_hbm, w_hbm), (x_ref, w_ref), sems):
        copy.wait()
    store_heads(own_ref, 0, project(x_ref[0], w_ref[...]), head_dim)


def other_kernel(head_dim, x_ref, w_ref, other_ref):
    store_heads(other_ref, 0, project(x_ref[0], w_ref[...]), head_dim)


def query_kernel(
    after_ref, q_hbm, q_gain_hbm, mask_hbm, k_gain_hbm, qt_ref, bias_ref, k_gain_ref,
    q_ref, q_gain_ref, mask_ref, sems,
):
    copies = start_copies(
        (q_hbm, q_gain_hbm, mask_hbm, k_gain_hbm), (q_ref, q_gain_ref, mask_ref, k_gain_ref), sems
    )
    prepare_queries(copies, q_ref, q_gain_ref, mask_ref, qt_ref, bias_ref)


def is_home():
    return lax.axis_index("tensor") // 2 == lax.axis_index("dp")


def away_kernel(head_dim, x_hbm, w_hbm, own_ref, w_ref, x_ref, sems):
    @pl.when(is_home())
    def _():
        own_ref[...] = jnp.zeros_like(own_ref)

    @pl.when(jnp.logical_not(is_home()))
    def _():
        own_kernel(head_dim, x_hbm, w_hbm, own_ref, x_ref, w_ref, sems)


def crossing_kernel(head_dim, x_other_ref, w_ref, other_ref):
    @pl.when(is_home())
    def _():
        other_ref[...] = jnp.zeros_like(other_ref)

    @pl.when(jnp.logical_not(is_home()))
    def _():
        store_heads(other_ref, 0, project(x_other_ref[0], w_ref[...]), head_dim)


def home_kernel(head_dim, after_ref, x_other_ref, x_hbm, w_hbm, keep_ref, pass_ref, x_ref, w_ref, sems):
    @pl.when(is_home())
    def _():
        own_kernel(head_dim, x_hbm, w_hbm, keep_ref, x_ref, w_ref, sems)
        store_heads(pass_ref, 0, project(x_other_ref[0], w_ref[...]), head_dim)

    @pl.when(jnp.logical_not(is_home()))
    def _():
        keep_ref[...] = jnp.zeros_like(keep_ref)
        pass_ref[...] = jnp.zeros_like(pass_ref)


def split_half(held, send_ref, keep_ref, partner_heads, own_heads):
    for i in range(send_ref.shape[0]):
        send_ref[i] = held[partner_heads + i]
        keep_ref[i] = held[own_heads + i]


def spread_kernel(n_dp, n_tensor, own_ref, *refs):
    others, (send_ref, keep_ref, held) = refs[: n_dp - 1], refs[n_dp - 1 :]
    d = lax.axis_index("dp")
    own_heads = own_ref.shape[0]
    for k, ref in enumerate((own_ref, *others)):
        held[pl.ds((d ^ k) * own_heads, own_heads)] = ref[...]
    half = send_ref.shape[0]
    upper = lax.axis_index("tensor") // (n_tensor // 2)
    split_half(held, send_ref, keep_ref, (1 - upper) * half, upper * half)


def arrival_kernel(keep_ref, first_ref, crossed_ref, out_ref):
    complete = keep_ref[...].astype(F32) + first_ref[...].astype(F32)
    out_ref[...] = jnp.where(is_home(), complete, crossed_ref[...].astype(F32))


def pair_kernel(arrival_ref, passed_ref, bias_ref, out_ref):
    passed = jnp.where(is_home(), 0.0, passed_ref[...].astype(F32))
    out_ref[...] = (arrival_ref[...] + passed).astype(BF16)


def add_kernel(bit, keep_ref, arrived_ref, send_ref, next_ref, held):
    held[...] = (keep_ref[...].astype(F32) + arrived_ref[...].astype(F32)).astype(BF16)
    half = send_ref.shape[0]
    upper = (lax.axis_index("tensor") // bit) % 2
    split_half(held, send_ref, next_ref, (1 - upper) * half, upper * half)


def add_last_kernel(keep_ref, arrived_ref, out_ref):
    out_ref[...] = (keep_ref[...].astype(F32) + arrived_ref[...].astype(F32)).astype(BF16)


def finish_rows(k_gain, one, two):
    keys = one[0].astype(F32) + two[0].astype(F32)
    values = one[1].astype(F32) + two[1].astype(F32)
    return normalize(keys, k_gain).astype(BF16), values.astype(BF16)


def norm_kernel(k_gain_ref, keep_ref, arrived_ref, kv_ref):
    kv_ref[0], kv_ref[1] = finish_rows(k_gain_ref[...], keep_ref.at[0], arrived_ref.at[0])


def attend_kernel(near, far, tile_len, first, last, head_dim, k_gain_ref, qt_ref, bias_ref, *refs):
    near_refs, refs = refs[: len(near)], refs[len(near) :]
    far_refs, refs = refs[: 2 * len(far)], refs[2 * len(far) :]
    if not first:
        top_in, sum_in, mixed_in = refs[:3]
        refs = refs[3:]
    s = lax.axis_index("section")
    qt = qt_ref[...]
    parts = [(part[0], part[1]) for part in near_refs]
    for one, two in zip(far_refs[::2], far_refs[1::2]):
        parts.append(finish_rows(k_gain_ref[...], one.at[0], two.at[0]))
    rows = parts[0][0].shape[0]
    scores, biases = [], []
    top = TOP_FLOOR if first else top_in[...]
    for step, (keys, _) in zip((*near, *far), parts):
        score = jnp.dot(keys, qt, preferred_element_type=F32)
        bias = bias_ref[pl.ds(((s ^ step) * rows) // tile_len, 1), :]
        scores.append(score)
        biases.append(bias)
        top = jnp.maximum(top, jnp.max(score, axis=0, keepdims=True) + bias)
    row_sum, mixed = 0.0, 0.0
    if not first:
        scale = jnp.exp(top_in[...] - top)
        row_sum = sum_in[...] * scale
        mixed = mixed_in[...] * scale
    for (_, values), score, bias in zip(parts, scores, biases):
        weights = jnp.exp(score + (bias - top))
        row_sum = row_sum + jnp.sum(weights, axis=0, keepdims=True)
        mixed = mixed + lax.dot_general(
            values, weights.astype(BF16), (((0,), (0,)), ((), ())), preferred_element_type=F32
        )
    if not last:
        top_out, sum_out, mixed_out = refs
        top_out[...] = top
        sum_out[...] = row_sum
        mixed_out[...] = mixed
        return
    (out,) = refs
    has_any = jnp.max(bias_ref[...], axis=0, keepdims=True) > -1.0
    inverse = jnp.where(has_any, 1.0 / jnp.where(has_any, row_sum, 1.0), 0.0)
    context = (mixed * inverse).astype(BF16)
    tokens = out.shape[0]
    for head in range(out.shape[1] // head_dim):
        out[:, head * head_dim : (head + 1) * head_dim] = context[
            :, head * tokens : (head + 1) * tokens
        ].T


def swap(value, axis, k):
    return lax.ppermute(value, axis, [(i, i ^ k) for i in range(lax.axis_size(axis))])


def permute_two_heads(value, away, home):
    hops = []
    for d in range(2):
        for t in range(4):
            to_d, to_t = home(d, t) if t // 2 == d else away(d, t)
            hops.append((4 * d + t, 4 * to_d + to_t))
    return lax.ppermute(value, ("dp", "tensor"), hops)


def sum_many_heads(own, others):
    n_dp, n_tensor = lax.axis_size("dp"), lax.axis_size("tensor")
    heads = own.shape[0] * n_dp
    half = shape_of((heads // 2, *own.shape[1:]))
    send, keep = call(
        functools.partial(spread_kernel, n_dp, n_tensor),
        [half, half],
        n_dp,
        "spread",
        scratch=[pltpu.VMEM((heads, *own.shape[1:]), BF16)],
    )(own, *others)
    bit = n_tensor // 2
    while bit > 1:
        arrived = swap(send, "tensor", bit)
        bit //= 2
        now = keep.shape
        if bit > 1:
            half = shape_of((now[0] // 2, *now[1:]))
            send, keep = call(
                functools.partial(add_kernel, bit),
                [half, half],
                2,
                "add_part",
                scratch=[pltpu.VMEM(now, BF16)],
            )(keep, arrived)
        else:
            keep = call(add_last_kernel, shape_of(now), 2, "add_pair")(keep, arrived)
    return keep


def on_device(queries, images, kv_weight, q_gain, k_gain, tile_mask):
    n_section = lax.axis_size("section")
    n_dp = lax.axis_size("dp")
    n_tensor = lax.axis_size("tensor")
    head_dim = q_gain.shape[0]
    tokens, q_width = queries.shape
    rows, features = images.shape[1:]
    tiles = tile_mask.shape[1]
    own_heads = kv_weight.shape[2] // head_dim
    heads = own_heads * n_dp
    tile_len = rows * n_section // tiles
    assert heads * 2 == n_tensor and tile_len % rows == 0 and n_section >= 4
    pairs = tokens * (q_width // head_dim)
    work = 4 * rows * features * kv_weight.shape[2]

    x, w, *small = [
        pltpu.with_memory_space_constraint(value, pltpu.HBM)
        for value in (
            images, kv_weight, queries, q_gain.reshape(1, -1), tile_mask.T, k_gain.reshape(1, -1),
        )
    ]
    product = shape_of((own_heads, 2, rows, head_dim))
    x_scratch, w_scratch = pltpu.VMEM(images.shape, BF16), pltpu.VMEM(kv_weight.shape, BF16)
    prepared = [
        shape_of((head_dim, pairs)),
        shape_of((tiles, pairs), F32),
        shape_of((1, head_dim), F32),
    ]
    query_scratch = [
        pltpu.VMEM(queries.shape, BF16),
        pltpu.VMEM((1, head_dim), F32),
        pltpu.VMEM((tiles, tokens), jnp.int32),
    ]
    query_call = call(
        query_kernel,
        prepared,
        5,
        "queries",
        in_specs=[VMEM] + [HBM] * 4,
        scratch=[*query_scratch, pltpu.SemaphoreType.DMA((4,))],
    )
    if n_dp == 2 and own_heads == 1:
        x_other = swap(images, "dp", 1)
        own, w_here = call(
            functools.partial(away_kernel, head_dim),
            [product, shape_of(kv_weight.shape)],
            2,
            "away_own",
            flops=work,
            in_specs=[HBM] * 2,
            scratch=[x_scratch, pltpu.SemaphoreType.DMA((2,))],
        )(x, w)
        first = permute_two_heads(own, lambda d, t: (d, t ^ 2), lambda d, t: (1 - d, t))
        crossing = call(
            functools.partial(crossing_kernel, head_dim), product, 2, "away_other", flops=work
        )(x_other, w_here)
        crossed = permute_two_heads(crossing, lambda d, t: (1 - d, t ^ 2), lambda d, t: (d, t))
        keep, passing = call(
            functools.partial(home_kernel, head_dim),
            [product, product],
            4,
            "home_both",
            flops=2 * work,
            in_specs=[VMEM] * 2 + [HBM] * 2,
            scratch=[x_scratch, w_scratch, pltpu.SemaphoreType.DMA((2,))],
        )(crossing, x_other, x, w)
        passed = swap(passing, "dp", 1)
        qt, bias, gain = query_call(keep, *small)
        arrival = call(arrival_kernel, shape_of(product.shape, F32), 3, "arrival")(
            keep, first, crossed
        )
        total = call(pair_kernel, product, 3, "pair_sum")(arrival, passed, bias)
    else:
        own, x_here = call(
            functools.partial(own_kernel, head_dim),
            [product, shape_of(images.shape)],
            2,
            "own_heads",
            flops=work,
            in_specs=[HBM] * 2,
            scratch=[w_scratch, pltpu.SemaphoreType.DMA((2,))],
        )(x, w)
        qt, bias, gain = query_call(own, *small)
        others = [swap(kv_weight, "dp", k) for k in range(1, n_dp)]
        rest = [
            call(functools.partial(other_kernel, head_dim), product, 2, "other_heads", flops=work)(
                x_here, other
            )
            for other in others
        ]
        total = sum_many_heads(own, rest)
    far = [step for step in range(1, n_section) if step & (step - 1)]
    near = [step for step in range(1, n_section) if not step & (step - 1)]
    arrived = swap(total, "tensor", 1)
    halves = [swap(total, "section", step) for step in far]
    kv = call(norm_kernel, shape_of((2, rows, head_dim)), 3, "sum_norm")(gain, total, arrived)
    finished = [swap(kv, "section", step) for step in near]
    both = []
    for value in halves:
        both += [value, swap(value, "tensor", 1)]
    state = []
    for here, there, operands in (
        ([0], [], [kv]),
        (near, [], finished),
        ([], far, both),
    ):
        first, last = here == [0], len(there) > 0
        outs = (
            shape_of((tokens, q_width))
            if last
            else [shape_of((1, pairs), F32), shape_of((1, pairs), F32), shape_of((head_dim, pairs), F32)]
        )
        parts = len(here) + len(there)
        state = call(
            functools.partial(attend_kernel, here, there, tile_len, first, last, head_dim),
            outs,
            3 + len(operands) + len(state),
            "attend",
            flops=4 * pairs * rows * head_dim * parts,
            exps=pairs * rows * parts,
        )(gain, qt, bias, *operands, *state)
    return state


def solution(mesh):
    in_specs = (
        P(("section", "dp"), "tensor"),
        P("dp", "section", "tensor"),
        P(None, "tensor", "dp"),
        P(),
        P(),
        P(("section", "dp"), None),
    )
    out_specs = P(("section", "dp"), "tensor")
    return jax.shard_map(
        on_device, mesh=mesh, in_specs=in_specs, out_specs=out_specs, check_vma=False
    )
```

```python
import functools

import jax
import jax.numpy as jnp
from jax import lax
from jax.experimental import pallas as pl
from jax.experimental.pallas import tpu as pltpu
from jax.sharding import PartitionSpec as P

EPSILON = 1e-05
MASKED_SCORE = -1e30
TOP_FLOOR = -1e29
VMEM = pl.BlockSpec(memory_space=pltpu.VMEM)
HBM = pl.BlockSpec(memory_space=pltpu.HBM)
F32 = jnp.float32
MIB = 1024 * 1024
LIMIT = 24 * MIB
PARTS = 4
BF16 = jnp.bfloat16


def shape_of(dims, dtype=BF16):
    return jax.ShapeDtypeStruct(dims, dtype)


def call(
    kernel, outs, n_in, name, flops=0, size=0, exps=0, in_specs=None, out_specs=None, scratch=()
):
    many = isinstance(outs, list)
    return pl.pallas_call(
        kernel,
        out_shape=outs,
        in_specs=in_specs or [VMEM] * n_in,
        out_specs=out_specs or ([VMEM] * len(outs) if many else VMEM),
        scratch_shapes=scratch,
        compiler_params=pltpu.CompilerParams(vmem_limit_bytes=LIMIT),
        cost_estimate=pl.CostEstimate(flops=flops, bytes_accessed=size, transcendentals=exps),
        name=name,
    )


def normalize(values, gain_vec):
    mean_sq = jnp.mean(values * values, axis=-1, keepdims=True)
    return values * lax.rsqrt(mean_sq + EPSILON) * gain_vec


def project(x, w):
    return jnp.dot(
        x, jnp.concatenate([w[0], w[1]], axis=1), preferred_element_type=F32
    ).astype(BF16)


def store_heads(ref, base, both, head_dim):
    width = both.shape[1] // 2
    for head in range(width // head_dim):
        lo = head * head_dim
        ref[base + head, 0] = both[:, lo : lo + head_dim]
        ref[base + head, 1] = both[:, width + lo : width + lo + head_dim]


def prepare_queries(copies, q_ref, q_gain_ref, mask_ref, qt_ref, bias_ref):
    for copy in copies:
        copy.wait()
    tokens = q_ref.shape[0]
    head_dim = q_gain_ref.shape[1]
    bias = jnp.where(mask_ref[...] > 0, 0.0, MASKED_SCORE).astype(F32)
    for head in range(q_ref.shape[1] // head_dim):
        rows = q_ref[:, head * head_dim : (head + 1) * head_dim].astype(F32)
        normed = normalize(rows, q_gain_ref[...]) * head_dim ** (-0.5)
        qt_ref[:, head * tokens : (head + 1) * tokens] = normed.T.astype(BF16)
        bias_ref[:, head * tokens : (head + 1) * tokens] = bias


def start_copies(sources, targets, sems, first=0):
    copies = [
        pltpu.make_async_copy(a, b, sems.at[first + i]) for i, (a, b) in enumerate(zip(sources, targets))
    ]
    for copy in copies:
        copy.start()
    return copies


def own_kernel(head_dim, x_hbm, w_hbm, own_ref, x_ref, w_ref, sems):
    step = w_ref.shape[1] // PARTS
    spans = [pl.ds(i * step, step) for i in range(PARTS)]
    sources, targets = [x_hbm], [x_ref]
    for span in spans:
        sources += [w_hbm.at[0, span], w_hbm.at[1, span]]
        targets += [w_ref.at[0, span], w_ref.at[1, span]]
    copies = start_copies(sources, targets, sems)
    copies[0].wait()
    total = None
    for i, span in enumerate(spans):
        copies[2 * i + 1].wait()
        copies[2 * i + 2].wait()
        part = jnp.dot(
            x_ref[0, :, span],
            jnp.concatenate([w_ref[0, span], w_ref[1, span]], axis=1),
            preferred_element_type=F32,
        )
        total = part if total is None else total + part
    store_heads(own_ref, 0, total.astype(BF16), head_dim)


def other_kernel(head_dim, x_ref, w_ref, other_ref):
    store_heads(other_ref, 0, project(x_ref[0], w_ref[...]), head_dim)


def query_kernel(
    q_hbm, q_gain_hbm, mask_hbm, k_gain_hbm, qt_ref, bias_ref, k_gain_ref,
    q_ref, q_gain_ref, mask_ref, sems,
):
    copies = start_copies(
        (q_hbm, q_gain_hbm, mask_hbm, k_gain_hbm), (q_ref, q_gain_ref, mask_ref, k_gain_ref), sems
    )
    prepare_queries(copies, q_ref, q_gain_ref, mask_ref, qt_ref, bias_ref)


def is_home():
    return lax.axis_index("tensor") // 2 == lax.axis_index("dp")


def away_kernel(head_dim, x_hbm, w_hbm, own_ref, x_ref, w_ref, sems):
    @pl.when(is_home())
    def _():
        own_ref[...] = jnp.zeros_like(own_ref)

    @pl.when(jnp.logical_not(is_home()))
    def _():
        own_kernel(head_dim, x_hbm, w_hbm, own_ref, x_ref, w_ref, sems)


def home_kernel(head_dim, x_hbm, w_other_ref, other_ref, x_ref, sems):
    @pl.when(is_home())
    def _():
        for copy in start_copies((x_hbm,), (x_ref,), sems):
            copy.wait()
        store_heads(other_ref, 0, project(x_ref[0], w_other_ref[...]), head_dim)

    @pl.when(jnp.logical_not(is_home()))
    def _():
        other_ref[...] = jnp.zeros_like(other_ref)


def keep_kernel(
    head_dim, after_ref, w_other_ref, x_hbm, w_hbm, q_hbm, q_gain_hbm, mask_hbm, k_gain_hbm,
    keep_ref, qt_ref, bias_ref, k_gain_ref, x_ref, w_ref, q_ref, q_gain_ref, mask_ref, sems,
):
    copies = start_copies(
        (q_hbm, q_gain_hbm, mask_hbm, k_gain_hbm), (q_ref, q_gain_ref, mask_ref, k_gain_ref), sems
    )
    moves = start_copies((x_hbm, w_hbm), (x_ref, w_ref), sems, len(copies))
    prepare_queries(copies, q_ref, q_gain_ref, mask_ref, qt_ref, bias_ref)
    for copy in moves:
        copy.wait()

    @pl.when(is_home())
    def _():
        store_heads(keep_ref, 0, project(x_ref[0], w_ref[...]), head_dim)

    @pl.when(jnp.logical_not(is_home()))
    def _():
        store_heads(keep_ref, 0, project(x_ref[0], w_other_ref[...]), head_dim)


def split_half(held, send_ref, keep_ref, partner_heads, own_heads):
    for i in range(send_ref.shape[0]):
        send_ref[i] = held[partner_heads + i]
        keep_ref[i] = held[own_heads + i]


def spread_kernel(n_dp, n_tensor, own_ref, *refs):
    others, (send_ref, keep_ref, held) = refs[: n_dp - 1], refs[n_dp - 1 :]
    d = lax.axis_index("dp")
    own_heads = own_ref.shape[0]
    for k, ref in enumerate((own_ref, *others)):
        held[pl.ds((d ^ k) * own_heads, own_heads)] = ref[...]
    half = send_ref.shape[0]
    upper = lax.axis_index("tensor") // (n_tensor // 2)
    split_half(held, send_ref, keep_ref, (1 - upper) * half, upper * half)


def pair_kernel(keep_ref, first_ref, second_ref, out_ref):
    arrived = jnp.where(is_home(), first_ref[...], second_ref[...]).astype(F32)
    out_ref[...] = (keep_ref[...].astype(F32) + arrived).astype(BF16)


def add_kernel(bit, keep_ref, arrived_ref, send_ref, next_ref, held):
    held[...] = (keep_ref[...].astype(F32) + arrived_ref[...].astype(F32)).astype(BF16)
    half = send_ref.shape[0]
    upper = (lax.axis_index("tensor") // bit) % 2
    split_half(held, send_ref, next_ref, (1 - upper) * half, upper * half)


def add_last_kernel(keep_ref, arrived_ref, out_ref):
    out_ref[...] = (keep_ref[...].astype(F32) + arrived_ref[...].astype(F32)).astype(BF16)


def finish_rows(k_gain, one, two):
    keys = one[0].astype(F32) + two[0].astype(F32)
    values = one[1].astype(F32) + two[1].astype(F32)
    return normalize(keys, k_gain).astype(BF16), values.astype(BF16)


def norm_kernel(k_gain_ref, keep_ref, arrived_ref, kv_ref):
    kv_ref[0], kv_ref[1] = finish_rows(k_gain_ref[...], keep_ref.at[0], arrived_ref.at[0])


def attend_kernel(near, far, tile_len, first, last, head_dim, k_gain_ref, qt_ref, bias_ref, *refs):
    near_refs, refs = refs[: len(near)], refs[len(near) :]
    far_refs, refs = refs[: 2 * len(far)], refs[2 * len(far) :]
    if not first:
        top_in, sum_in, mixed_in = refs[:3]
        refs = refs[3:]
    s = lax.axis_index("section")
    qt = qt_ref[...]
    parts = [(part[0], part[1]) for part in near_refs]
    for one, two in zip(far_refs[::2], far_refs[1::2]):
        parts.append(finish_rows(k_gain_ref[...], one.at[0], two.at[0]))
    rows = parts[0][0].shape[0]
    scores, biases = [], []
    top = TOP_FLOOR if first else top_in[...]
    for step, (keys, _) in zip((*near, *far), parts):
        score = jnp.dot(keys, qt, preferred_element_type=F32)
        bias = bias_ref[pl.ds(((s ^ step) * rows) // tile_len, 1), :]
        scores.append(score)
        biases.append(bias)
        top = jnp.maximum(top, jnp.max(score, axis=0, keepdims=True) + bias)
    all_weights = []
    row_sum, scale = 0.0, None
    if not first:
        scale = jnp.exp(top_in[...] - top)
        row_sum = sum_in[...] * scale
    for score, bias in zip(scores, biases):
        weights = jnp.exp(score + (bias - top))
        row_sum = row_sum + jnp.sum(weights, axis=0, keepdims=True)
        all_weights.append(weights.astype(BF16))

    def mix(columns):
        mixed = 0.0 if first else mixed_in[:, columns] * scale[:, columns]
        for (_, values), weights in zip(parts, all_weights):
            mixed = mixed + lax.dot_general(
                values, weights[:, columns], (((0,), (0,)), ((), ())), preferred_element_type=F32
            )
        return mixed

    if not last:
        top_out, sum_out, mixed_out = refs
        top_out[...] = top
        sum_out[...] = row_sum
        mixed_out[...] = mix(slice(None))
        return
    out_hbm, held, sems = refs
    has_any = jnp.max(bias_ref[...], axis=0, keepdims=True) > -1.0
    inverse = jnp.where(has_any, 1.0 / jnp.where(has_any, row_sum, 1.0), 0.0)
    tokens = held.shape[1]
    copies = []
    for head in range(held.shape[0]):
        columns = slice(head * tokens, (head + 1) * tokens)
        held[head] = (mix(columns) * inverse[:, columns]).astype(BF16).T
        copies.append(
            pltpu.make_async_copy(
                held.at[head], out_hbm.at[:, pl.ds(head * head_dim, head_dim)], sems.at[head]
            )
        )
        copies[-1].start()
    for copy in copies:
        copy.wait()


def swap(value, axis, k):
    return lax.ppermute(value, axis, [(i, i ^ k) for i in range(lax.axis_size(axis))])


def exchange_two_heads(value, home_sends):
    hops = []
    for d in range(2):
        for t in range(4):
            sends = (t // 2 == d) == home_sends
            hops.append((4 * d + t, 4 * d + (t ^ 2) if sends else 4 * (1 - d) + t))
    return lax.ppermute(value, ("dp", "tensor"), hops)


def sum_many_heads(own, others):
    n_dp, n_tensor = lax.axis_size("dp"), lax.axis_size("tensor")
    heads = own.shape[0] * n_dp
    half = shape_of((heads // 2, *own.shape[1:]))
    send, keep = call(
        functools.partial(spread_kernel, n_dp, n_tensor),
        [half, half],
        n_dp,
        "spread",
        scratch=[pltpu.VMEM((heads, *own.shape[1:]), BF16)],
    )(own, *others)
    bit = n_tensor // 2
    while bit > 1:
        arrived = swap(send, "tensor", bit)
        bit //= 2
        now = keep.shape
        if bit > 1:
            half = shape_of((now[0] // 2, *now[1:]))
            send, keep = call(
                functools.partial(add_kernel, bit),
                [half, half],
                2,
                "add_part",
                scratch=[pltpu.VMEM(now, BF16)],
            )(keep, arrived)
        else:
            keep = call(add_last_kernel, shape_of(now), 2, "add_pair")(keep, arrived)
    return keep


def on_device(queries, images, kv_weight, q_gain, k_gain, tile_mask):
    n_section = lax.axis_size("section")
    n_dp = lax.axis_size("dp")
    n_tensor = lax.axis_size("tensor")
    head_dim = q_gain.shape[0]
    tokens, q_width = queries.shape
    rows, features = images.shape[1:]
    tiles = tile_mask.shape[1]
    own_heads = kv_weight.shape[2] // head_dim
    heads = own_heads * n_dp
    tile_len = rows * n_section // tiles
    assert heads * 2 == n_tensor and tile_len % rows == 0 and n_section >= 4
    pairs = tokens * (q_width // head_dim)
    work = 4 * rows * features * kv_weight.shape[2]

    x, w, *small = [
        pltpu.with_memory_space_constraint(value, pltpu.HBM)
        for value in (
            images, kv_weight, queries, q_gain.reshape(1, -1), tile_mask.T, k_gain.reshape(1, -1),
        )
    ]
    product = shape_of((own_heads, 2, rows, head_dim))
    x_scratch, w_scratch = pltpu.VMEM(images.shape, BF16), pltpu.VMEM(kv_weight.shape, BF16)
    prepared = [
        shape_of((head_dim, pairs)),
        shape_of((tiles, pairs), F32),
        shape_of((1, head_dim), F32),
    ]
    query_scratch = [
        pltpu.VMEM(queries.shape, BF16),
        pltpu.VMEM((1, head_dim), F32),
        pltpu.VMEM((tiles, tokens), jnp.int32),
    ]
    others = [swap(kv_weight, "dp", k) for k in range(1, n_dp)]
    if n_dp == 2 and own_heads == 1:
        away = call(
            functools.partial(away_kernel, head_dim),
            product,
            2,
            "away_own",
            flops=work,
            in_specs=[HBM] * 2,
            scratch=[x_scratch, w_scratch, pltpu.SemaphoreType.DMA((1 + 2 * PARTS,))],
        )(x, w)
        first = exchange_two_heads(away, False)
        home = call(
            functools.partial(home_kernel, head_dim),
            product,
            2,
            "home_other",
            flops=work,
            in_specs=[HBM, VMEM],
            scratch=[x_scratch, pltpu.SemaphoreType.DMA((1,))],
        )(x, others[0])
        second = exchange_two_heads(home, True)
        keep, qt, bias, gain = call(
            functools.partial(keep_kernel, head_dim),
            [product, *prepared],
            8,
            "keep_queries",
            flops=work,
            in_specs=[VMEM] * 2 + [HBM] * 6,
            scratch=[x_scratch, w_scratch, *query_scratch, pltpu.SemaphoreType.DMA((6,))],
        )(home, others[0], x, w, *small)
        total = call(pair_kernel, product, 3, "pair_sum")(keep, first, second)
    else:
        own, x_here = call(
            functools.partial(own_kernel, head_dim),
            [product, shape_of(images.shape)],
            2,
            "own_heads",
            flops=work,
            in_specs=[HBM] * 2,
            scratch=[w_scratch, pltpu.SemaphoreType.DMA((1 + 2 * PARTS,))],
        )(x, w)
        qt, bias, gain = call(
            query_kernel,
            prepared,
            4,
            "queries",
            in_specs=[HBM] * 4,
            scratch=[*query_scratch, pltpu.SemaphoreType.DMA((4,))],
        )(*small)
        rest = [
            call(functools.partial(other_kernel, head_dim), product, 2, "other_heads", flops=work)(
                x_here, other
            )
            for other in others
        ]
        total = sum_many_heads(own, rest)
    far = [step for step in range(1, n_section) if step & (step - 1)]
    near = [step for step in range(1, n_section) if not step & (step - 1)]
    arrived = swap(total, "tensor", 1)
    halves = [swap(total, "section", step) for step in far]
    kv = call(norm_kernel, shape_of((2, rows, head_dim)), 3, "sum_norm")(gain, total, arrived)
    finished = [swap(kv, "section", step) for step in near]
    both = []
    for value in halves:
        both += [value, swap(value, "tensor", 1)]
    state = []
    for here, there, operands in (
        ([0], [], [kv]),
        (near, [], finished),
        ([], far, both),
    ):
        first, last = here == [0], len(there) > 0
        outs = (
            shape_of((tokens, q_width))
            if last
            else [shape_of((1, pairs), F32), shape_of((1, pairs), F32), shape_of((head_dim, pairs), F32)]
        )
        parts = len(here) + len(there)
        state = call(
            functools.partial(attend_kernel, here, there, tile_len, first, last, head_dim),
            outs,
            3 + len(operands) + len(state),
            "attend",
            flops=4 * pairs * rows * head_dim * parts,
            exps=pairs * rows * parts,
            out_specs=HBM if last else None,
            scratch=[
                pltpu.VMEM((q_width // head_dim, tokens, head_dim), BF16),
                pltpu.SemaphoreType.DMA((q_width // head_dim,)),
            ]
            if last
            else (),
        )(gain, qt, bias, *operands, *state)
    return state


def solution(mesh):
    in_specs = (
        P(("section", "dp"), "tensor"),
        P("dp", "section", "tensor"),
        P(None, "tensor", "dp"),
        P(),
        P(),
        P(("section", "dp"), None),
    )
    out_specs = P(("section", "dp"), "tensor")
    return jax.shard_map(
        on_device, mesh=mesh, in_specs=in_specs, out_specs=out_specs, check_vma=False
    )
```

```python
import functools

import jax
import jax.numpy as jnp
from jax import lax
from jax.experimental import pallas as pl
from jax.experimental.pallas import tpu as pltpu
from jax.sharding import PartitionSpec as P

EPSILON = 1e-05
MASKED_SCORE = -1e30
TOP_FLOOR = -1e29
VMEM = pl.BlockSpec(memory_space=pltpu.VMEM)
HBM = pl.BlockSpec(memory_space=pltpu.HBM)
F32 = jnp.float32
MIB = 1024 * 1024
LIMIT = 24 * MIB
BF16 = jnp.bfloat16


def shape_of(dims, dtype=BF16):
    return jax.ShapeDtypeStruct(dims, dtype)


def call(
    kernel, outs, n_in, name, flops=0, size=0, exps=0, in_specs=None, scratch=(), aliases=None
):
    many = isinstance(outs, list)
    return pl.pallas_call(
        kernel,
        out_shape=outs,
        in_specs=in_specs or [VMEM] * n_in,
        out_specs=[VMEM] * len(outs) if many else VMEM,
        scratch_shapes=scratch,
        input_output_aliases=aliases or {},
        compiler_params=pltpu.CompilerParams(vmem_limit_bytes=LIMIT),
        cost_estimate=pl.CostEstimate(flops=flops, bytes_accessed=size, transcendentals=exps),
        name=name,
    )


def normalize(values, gain_vec):
    mean_sq = jnp.mean(values * values, axis=-1, keepdims=True)
    return values * lax.rsqrt(mean_sq + EPSILON) * gain_vec


def project(x, w):
    return jnp.dot(
        x, jnp.concatenate([w[0], w[1]], axis=1), preferred_element_type=F32
    ).astype(BF16)


def store_heads(ref, base, both, head_dim):
    width = both.shape[1] // 2
    for head in range(width // head_dim):
        lo = head * head_dim
        ref[base + head, 0] = both[:, lo : lo + head_dim]
        ref[base + head, 1] = both[:, width + lo : width + lo + head_dim]


def prepare_queries(copies, q_ref, q_gain_ref, mask_ref, qt_ref, bias_ref):
    for copy in copies:
        copy.wait()
    tokens = q_ref.shape[0]
    head_dim = q_gain_ref.shape[1]
    bias = jnp.where(mask_ref[...] > 0, 0.0, MASKED_SCORE).astype(F32)
    for head in range(q_ref.shape[1] // head_dim):
        rows = q_ref[:, head * head_dim : (head + 1) * head_dim].astype(F32)
        normed = normalize(rows, q_gain_ref[...]) * head_dim ** (-0.5)
        qt_ref[:, head * tokens : (head + 1) * tokens] = normed.T.astype(BF16)
        bias_ref[:, head * tokens : (head + 1) * tokens] = bias


def start_copies(sources, targets, sems, first=0):
    copies = [
        pltpu.make_async_copy(a, b, sems.at[first + i]) for i, (a, b) in enumerate(zip(sources, targets))
    ]
    for copy in copies:
        copy.start()
    return copies


def own_kernel(head_dim, x_hbm, w_hbm, own_ref, x_ref, w_ref, sems):
    for copy in start_copies((x_hbm, w_hbm), (x_ref, w_ref), sems):
        copy.wait()
    store_heads(own_ref, 0, project(x_ref[0], w_ref[...]), head_dim)


def other_kernel(head_dim, x_ref, w_ref, other_ref):
    store_heads(other_ref, 0, project(x_ref[0], w_ref[...]), head_dim)


def query_kernel(
    q_hbm, q_gain_hbm, mask_hbm, k_gain_hbm, qt_ref, bias_ref, k_gain_ref,
    q_ref, q_gain_ref, mask_ref, sems,
):
    copies = start_copies(
        (q_hbm, q_gain_hbm, mask_hbm, k_gain_hbm), (q_ref, q_gain_ref, mask_ref, k_gain_ref), sems
    )
    prepare_queries(copies, q_ref, q_gain_ref, mask_ref, qt_ref, bias_ref)


def is_home():
    return lax.axis_index("tensor") // 2 == lax.axis_index("dp")


def away_kernel(head_dim, x_hbm, w_hbm, own_ref, x_ref, w_ref, sems):
    @pl.when(is_home())
    def _():
        own_ref[...] = jnp.zeros_like(own_ref)

    @pl.when(jnp.logical_not(is_home()))
    def _():
        own_kernel(head_dim, x_hbm, w_hbm, own_ref, x_ref, w_ref, sems)


def home_kernel(head_dim, x_hbm, w_other_ref, other_ref, x_ref, sems):
    @pl.when(is_home())
    def _():
        for copy in start_copies((x_hbm,), (x_ref,), sems):
            copy.wait()
        store_heads(other_ref, 0, project(x_ref[0], w_other_ref[...]), head_dim)

    @pl.when(jnp.logical_not(is_home()))
    def _():
        other_ref[...] = jnp.zeros_like(other_ref)


def keep_kernel(
    head_dim, after_ref, w_other_ref, x_hbm, w_hbm, q_hbm, q_gain_hbm, mask_hbm, k_gain_hbm,
    keep_ref, qt_ref, bias_ref, k_gain_ref, x_ref, w_ref, q_ref, q_gain_ref, mask_ref, sems,
):
    moves = start_copies((x_hbm, w_hbm), (x_ref, w_ref), sems, 4)

    @pl.when(is_first_core())
    def _():
        query_kernel(
            q_hbm, q_gain_hbm, mask_hbm, k_gain_hbm, qt_ref, bias_ref, k_gain_ref,
            q_ref, q_gain_ref, mask_ref, sems,
        )

    for copy in moves:
        copy.wait()

    @pl.when(is_home())
    def _():
        store_heads(keep_ref, 0, project(x_ref[0], w_ref[...]), head_dim)

    @pl.when(jnp.logical_not(is_home()))
    def _():
        store_heads(keep_ref, 0, project(x_ref[0], w_other_ref[...]), head_dim)


def split_half(held, send_ref, keep_ref, partner_heads, own_heads):
    for i in range(send_ref.shape[0]):
        send_ref[i] = held[partner_heads + i]
        keep_ref[i] = held[own_heads + i]


def spread_kernel(n_dp, n_tensor, own_ref, *refs):
    others, (send_ref, keep_ref, held) = refs[: n_dp - 1], refs[n_dp - 1 :]
    d = lax.axis_index("dp")
    own_heads = own_ref.shape[0]
    for k, ref in enumerate((own_ref, *others)):
        held[pl.ds((d ^ k) * own_heads, own_heads)] = ref[...]
    half = send_ref.shape[0]
    upper = lax.axis_index("tensor") // (n_tensor // 2)
    split_half(held, send_ref, keep_ref, (1 - upper) * half, upper * half)


def is_first_core():
    return lax.axis_index("dp") == 0


def pair_kernel(
    keep_ref, first_ref, second_ref, qt_in, bias_in, k_gain_in, q_hbm, q_gain_hbm, mask_hbm, k_gain_hbm,
    out_ref, qt_ref, bias_ref, k_gain_ref, q_ref, q_gain_ref, mask_ref, sems,
):
    arrived = jnp.where(is_home(), first_ref[...], second_ref[...]).astype(F32)
    out_ref[...] = (keep_ref[...].astype(F32) + arrived).astype(BF16)

    @pl.when(jnp.logical_not(is_first_core()))
    def _():
        query_kernel(
            q_hbm, q_gain_hbm, mask_hbm, k_gain_hbm, qt_ref, bias_ref, k_gain_ref,
            q_ref, q_gain_ref, mask_ref, sems,
        )


def add_kernel(bit, keep_ref, arrived_ref, send_ref, next_ref, held):
    held[...] = (keep_ref[...].astype(F32) + arrived_ref[...].astype(F32)).astype(BF16)
    half = send_ref.shape[0]
    upper = (lax.axis_index("tensor") // bit) % 2
    split_half(held, send_ref, next_ref, (1 - upper) * half, upper * half)


def add_last_kernel(keep_ref, arrived_ref, out_ref):
    out_ref[...] = (keep_ref[...].astype(F32) + arrived_ref[...].astype(F32)).astype(BF16)


def finish_rows(k_gain, one, two):
    keys = one[0].astype(F32) + two[0].astype(F32)
    values = one[1].astype(F32) + two[1].astype(F32)
    return normalize(keys, k_gain).astype(BF16), values.astype(BF16)


def norm_kernel(k_gain_ref, keep_ref, arrived_ref, kv_ref):
    kv_ref[0], kv_ref[1] = finish_rows(k_gain_ref[...], keep_ref.at[0], arrived_ref.at[0])


def attend_kernel(near, far, tile_len, first, last, head_dim, k_gain_ref, qt_ref, bias_ref, *refs):
    near_refs, refs = refs[: len(near)], refs[len(near) :]
    far_refs, refs = refs[: 2 * len(far)], refs[2 * len(far) :]
    if not first:
        top_in, sum_in, mixed_in = refs[:3]
        refs = refs[3:]
    s = lax.axis_index("section")
    qt = qt_ref[...]
    parts = [(part[0], part[1]) for part in near_refs]
    for one, two in zip(far_refs[::2], far_refs[1::2]):
        parts.append(finish_rows(k_gain_ref[...], one.at[0], two.at[0]))
    rows = parts[0][0].shape[0]
    scores, biases = [], []
    top = TOP_FLOOR if first else top_in[...]
    for step, (keys, _) in zip((*near, *far), parts):
        score = jnp.dot(keys, qt, preferred_element_type=F32)
        bias = bias_ref[pl.ds(((s ^ step) * rows) // tile_len, 1), :]
        scores.append(score)
        biases.append(bias)
        top = jnp.maximum(top, jnp.max(score, axis=0, keepdims=True) + bias)
    row_sum, mixed = 0.0, 0.0
    if not first:
        scale = jnp.exp(top_in[...] - top)
        row_sum = sum_in[...] * scale
        mixed = mixed_in[...] * scale
    for (_, values), score, bias in zip(parts, scores, biases):
        weights = jnp.exp(score + (bias - top))
        row_sum = row_sum + jnp.sum(weights, axis=0, keepdims=True)
        mixed = mixed + lax.dot_general(
            values, weights.astype(BF16), (((0,), (0,)), ((), ())), preferred_element_type=F32
        )
    if not last:
        top_out, sum_out, mixed_out = refs
        top_out[...] = top
        sum_out[...] = row_sum
        mixed_out[...] = mixed
        return
    (out,) = refs
    has_any = jnp.max(bias_ref[...], axis=0, keepdims=True) > -1.0
    inverse = jnp.where(has_any, 1.0 / jnp.where(has_any, row_sum, 1.0), 0.0)
    context = (mixed * inverse).astype(BF16)
    tokens = out.shape[0]
    for head in range(out.shape[1] // head_dim):
        out[:, head * head_dim : (head + 1) * head_dim] = context[
            :, head * tokens : (head + 1) * tokens
        ].T


def swap(value, axis, k):
    return lax.ppermute(value, axis, [(i, i ^ k) for i in range(lax.axis_size(axis))])


def exchange_two_heads(value, home_sends):
    hops = []
    for d in range(2):
        for t in range(4):
            sends = (t // 2 == d) == home_sends
            hops.append((4 * d + t, 4 * d + (t ^ 2) if sends else 4 * (1 - d) + t))
    return lax.ppermute(value, ("dp", "tensor"), hops)


def sum_many_heads(own, others):
    n_dp, n_tensor = lax.axis_size("dp"), lax.axis_size("tensor")
    heads = own.shape[0] * n_dp
    half = shape_of((heads // 2, *own.shape[1:]))
    send, keep = call(
        functools.partial(spread_kernel, n_dp, n_tensor),
        [half, half],
        n_dp,
        "spread",
        scratch=[pltpu.VMEM((heads, *own.shape[1:]), BF16)],
    )(own, *others)
    bit = n_tensor // 2
    while bit > 1:
        arrived = swap(send, "tensor", bit)
        bit //= 2
        now = keep.shape
        if bit > 1:
            half = shape_of((now[0] // 2, *now[1:]))
            send, keep = call(
                functools.partial(add_kernel, bit),
                [half, half],
                2,
                "add_part",
                scratch=[pltpu.VMEM(now, BF16)],
            )(keep, arrived)
        else:
            keep = call(add_last_kernel, shape_of(now), 2, "add_pair")(keep, arrived)
    return keep


def on_device(queries, images, kv_weight, q_gain, k_gain, tile_mask):
    n_section = lax.axis_size("section")
    n_dp = lax.axis_size("dp")
    n_tensor = lax.axis_size("tensor")
    head_dim = q_gain.shape[0]
    tokens, q_width = queries.shape
    rows, features = images.shape[1:]
    tiles = tile_mask.shape[1]
    own_heads = kv_weight.shape[2] // head_dim
    heads = own_heads * n_dp
    tile_len = rows * n_section // tiles
    assert heads * 2 == n_tensor and tile_len % rows == 0 and n_section >= 4
    pairs = tokens * (q_width // head_dim)
    work = 4 * rows * features * kv_weight.shape[2]

    x, w, *small = [
        pltpu.with_memory_space_constraint(value, pltpu.HBM)
        for value in (
            images, kv_weight, queries, q_gain.reshape(1, -1), tile_mask.T, k_gain.reshape(1, -1),
        )
    ]
    product = shape_of((own_heads, 2, rows, head_dim))
    x_scratch, w_scratch = pltpu.VMEM(images.shape, BF16), pltpu.VMEM(kv_weight.shape, BF16)
    prepared = [
        shape_of((head_dim, pairs)),
        shape_of((tiles, pairs), F32),
        shape_of((1, head_dim), F32),
    ]
    query_scratch = [
        pltpu.VMEM(queries.shape, BF16),
        pltpu.VMEM((1, head_dim), F32),
        pltpu.VMEM((tiles, tokens), jnp.int32),
    ]
    others = [swap(kv_weight, "dp", k) for k in range(1, n_dp)]
    if n_dp == 2 and own_heads == 1:
        away = call(
            functools.partial(away_kernel, head_dim),
            product,
            2,
            "away_own",
            flops=work,
            in_specs=[HBM] * 2,
            scratch=[x_scratch, w_scratch, pltpu.SemaphoreType.DMA((2,))],
        )(x, w)
        first = exchange_two_heads(away, False)
        home = call(
            functools.partial(home_kernel, head_dim),
            product,
            2,
            "home_other",
            flops=work,
            in_specs=[HBM, VMEM],
            scratch=[x_scratch, pltpu.SemaphoreType.DMA((1,))],
        )(x, others[0])
        second = exchange_two_heads(home, True)
        keep, qt, bias, gain = call(
            functools.partial(keep_kernel, head_dim),
            [product, *prepared],
            8,
            "keep_queries",
            flops=work,
            in_specs=[VMEM] * 2 + [HBM] * 6,
            scratch=[x_scratch, w_scratch, *query_scratch, pltpu.SemaphoreType.DMA((6,))],
        )(home, others[0], x, w, *small)
        total, qt, bias, gain = call(
            pair_kernel,
            [product, *prepared],
            10,
            "pair_sum",
            in_specs=[VMEM] * 6 + [HBM] * 4,
            scratch=[*query_scratch, pltpu.SemaphoreType.DMA((4,))],
            aliases={3: 1, 4: 2, 5: 3},
        )(keep, first, second, qt, bias, gain, *small)
    else:
        own, x_here = call(
            functools.partial(own_kernel, head_dim),
            [product, shape_of(images.shape)],
            2,
            "own_heads",
            flops=work,
            in_specs=[HBM] * 2,
            scratch=[w_scratch, pltpu.SemaphoreType.DMA((2,))],
        )(x, w)
        qt, bias, gain = call(
            query_kernel,
            prepared,
            4,
            "queries",
            in_specs=[HBM] * 4,
            scratch=[*query_scratch, pltpu.SemaphoreType.DMA((4,))],
        )(*small)
        rest = [
            call(functools.partial(other_kernel, head_dim), product, 2, "other_heads", flops=work)(
                x_here, other
            )
            for other in others
        ]
        total = sum_many_heads(own, rest)
    far = [step for step in range(1, n_section) if step & (step - 1)]
    near = [step for step in range(1, n_section) if not step & (step - 1)]
    arrived = swap(total, "tensor", 1)
    halves = [swap(total, "section", step) for step in far]
    kv = call(norm_kernel, shape_of((2, rows, head_dim)), 3, "sum_norm")(gain, total, arrived)
    finished = [swap(kv, "section", step) for step in near]
    both = []
    for value in halves:
        both += [value, swap(value, "tensor", 1)]
    state = []
    for here, there, operands in (
        ([0], [], [kv]),
        (near, [], finished),
        ([], far, both),
    ):
        first, last = here == [0], len(there) > 0
        outs = (
            shape_of((tokens, q_width))
            if last
            else [shape_of((1, pairs), F32), shape_of((1, pairs), F32), shape_of((head_dim, pairs), F32)]
        )
        parts = len(here) + len(there)
        state = call(
            functools.partial(attend_kernel, here, there, tile_len, first, last, head_dim),
            outs,
            3 + len(operands) + len(state),
            "attend",
            flops=4 * pairs * rows * head_dim * parts,
            exps=pairs * rows * parts,
        )(gain, qt, bias, *operands, *state)
    return state


def solution(mesh):
    in_specs = (
        P(("section", "dp"), "tensor"),
        P("dp", "section", "tensor"),
        P(None, "tensor", "dp"),
        P(),
        P(),
        P(("section", "dp"), None),
    )
    out_specs = P(("section", "dp"), "tensor")
    return jax.shard_map(
        on_device, mesh=mesh, in_specs=in_specs, out_specs=out_specs, check_vma=False
    )
```

```python
import functools

import jax
import jax.numpy as jnp
from jax import lax
from jax.experimental import pallas as pl
from jax.experimental.pallas import tpu as pltpu
from jax.sharding import PartitionSpec as P

EPSILON = 1e-05
MASKED_SCORE = -1e30
TOP_FLOOR = -1e29
VMEM = pl.BlockSpec(memory_space=pltpu.VMEM)
HBM = pl.BlockSpec(memory_space=pltpu.HBM)
F32 = jnp.float32
MIB = 1024 * 1024
LIMIT = 24 * MIB
BF16 = jnp.bfloat16


def shape_of(dims, dtype=BF16):
    return jax.ShapeDtypeStruct(dims, dtype)


def call(
    kernel, outs, n_in, name, flops=0, size=0, exps=0, in_specs=None, scratch=()
):
    many = isinstance(outs, list)
    return pl.pallas_call(
        kernel,
        out_shape=outs,
        in_specs=in_specs or [VMEM] * n_in,
        out_specs=[VMEM] * len(outs) if many else VMEM,
        scratch_shapes=scratch,
        compiler_params=pltpu.CompilerParams(vmem_limit_bytes=LIMIT),
        cost_estimate=pl.CostEstimate(flops=flops, bytes_accessed=size, transcendentals=exps),
        name=name,
    )


def normalize(values, gain_vec):
    mean_sq = jnp.mean(values * values, axis=-1, keepdims=True)
    return values * lax.rsqrt(mean_sq + EPSILON) * gain_vec


def project(x, w):
    return jnp.dot(
        x, jnp.concatenate([w[0], w[1]], axis=1), preferred_element_type=F32
    ).astype(BF16)


def store_heads(ref, base, both, head_dim):
    width = both.shape[1] // 2
    for head in range(width // head_dim):
        lo = head * head_dim
        ref[base + head, 0] = both[:, lo : lo + head_dim]
        ref[base + head, 1] = both[:, width + lo : width + lo + head_dim]


def prepare_queries(copies, q_ref, q_gain_ref, mask_ref, qt_ref, bias_ref):
    for copy in copies:
        copy.wait()
    tokens = q_ref.shape[0]
    head_dim = q_gain_ref.shape[1]
    bias = jnp.where(mask_ref[...] > 0, 0.0, MASKED_SCORE).astype(F32)
    for head in range(q_ref.shape[1] // head_dim):
        rows = q_ref[:, head * head_dim : (head + 1) * head_dim].astype(F32)
        normed = normalize(rows, q_gain_ref[...]) * head_dim ** (-0.5)
        qt_ref[:, head * tokens : (head + 1) * tokens] = normed.T.astype(BF16)
        bias_ref[:, head * tokens : (head + 1) * tokens] = bias


def start_copies(sources, targets, sems, first=0):
    copies = [
        pltpu.make_async_copy(a, b, sems.at[first + i]) for i, (a, b) in enumerate(zip(sources, targets))
    ]
    for copy in copies:
        copy.start()
    return copies


def own_kernel(head_dim, x_hbm, w_hbm, own_ref, x_ref, w_ref, sems):
    for copy in start_copies((x_hbm, w_hbm), (x_ref, w_ref), sems):
        copy.wait()
    store_heads(own_ref, 0, project(x_ref[0], w_ref[...]), head_dim)


def other_kernel(head_dim, x_ref, w_ref, other_ref):
    store_heads(other_ref, 0, project(x_ref[0], w_ref[...]), head_dim)


def query_kernel(
    q_hbm, q_gain_hbm, mask_hbm, k_gain_hbm, qt_ref, bias_ref, k_gain_ref,
    q_ref, q_gain_ref, mask_ref, sems,
):
    copies = start_copies(
        (q_hbm, q_gain_hbm, mask_hbm, k_gain_hbm), (q_ref, q_gain_ref, mask_ref, k_gain_ref), sems
    )
    prepare_queries(copies, q_ref, q_gain_ref, mask_ref, qt_ref, bias_ref)


def is_home():
    return lax.axis_index("tensor") // 2 == lax.axis_index("dp")


def away_kernel(head_dim, x_hbm, w_hbm, own_ref, x_ref, w_ref, sems):
    @pl.when(is_home())
    def _():
        own_ref[...] = jnp.zeros_like(own_ref)

    @pl.when(jnp.logical_not(is_home()))
    def _():
        own_kernel(head_dim, x_hbm, w_hbm, own_ref, x_ref, w_ref, sems)


def load_kernel(after_ref, x_hbm, x_ref, sems):
    @pl.when(is_home())
    def _():
        for copy in start_copies((x_hbm,), (x_ref,), sems):
            copy.wait()


def home_kernel(head_dim, x_ref, w_other_ref, other_ref):
    @pl.when(is_home())
    def _():
        store_heads(other_ref, 0, project(x_ref[0], w_other_ref[...]), head_dim)

    @pl.when(jnp.logical_not(is_home()))
    def _():
        other_ref[...] = jnp.zeros_like(other_ref)


def keep_kernel(
    head_dim, after_ref, w_other_ref, x_hbm, w_hbm, q_hbm, q_gain_hbm, mask_hbm, k_gain_hbm,
    keep_ref, qt_ref, bias_ref, k_gain_ref, x_ref, w_ref, q_ref, q_gain_ref, mask_ref, sems,
):
    copies = start_copies(
        (q_hbm, q_gain_hbm, mask_hbm, k_gain_hbm), (q_ref, q_gain_ref, mask_ref, k_gain_ref), sems
    )
    moves = start_copies((x_hbm, w_hbm), (x_ref, w_ref), sems, len(copies))
    prepare_queries(copies, q_ref, q_gain_ref, mask_ref, qt_ref, bias_ref)
    for copy in moves:
        copy.wait()

    @pl.when(is_home())
    def _():
        store_heads(keep_ref, 0, project(x_ref[0], w_ref[...]), head_dim)

    @pl.when(jnp.logical_not(is_home()))
    def _():
        store_heads(keep_ref, 0, project(x_ref[0], w_other_ref[...]), head_dim)


def split_half(held, send_ref, keep_ref, partner_heads, own_heads):
    for i in range(send_ref.shape[0]):
        send_ref[i] = held[partner_heads + i]
        keep_ref[i] = held[own_heads + i]


def spread_kernel(n_dp, n_tensor, own_ref, *refs):
    others, (send_ref, keep_ref, held) = refs[: n_dp - 1], refs[n_dp - 1 :]
    d = lax.axis_index("dp")
    own_heads = own_ref.shape[0]
    for k, ref in enumerate((own_ref, *others)):
        held[pl.ds((d ^ k) * own_heads, own_heads)] = ref[...]
    half = send_ref.shape[0]
    upper = lax.axis_index("tensor") // (n_tensor // 2)
    split_half(held, send_ref, keep_ref, (1 - upper) * half, upper * half)


def pair_kernel(keep_ref, first_ref, second_ref, out_ref):
    arrived = jnp.where(is_home(), first_ref[...], second_ref[...]).astype(F32)
    out_ref[...] = (keep_ref[...].astype(F32) + arrived).astype(BF16)


def add_kernel(bit, keep_ref, arrived_ref, send_ref, next_ref, held):
    held[...] = (keep_ref[...].astype(F32) + arrived_ref[...].astype(F32)).astype(BF16)
    half = send_ref.shape[0]
    upper = (lax.axis_index("tensor") // bit) % 2
    split_half(held, send_ref, next_ref, (1 - upper) * half, upper * half)


def add_last_kernel(keep_ref, arrived_ref, out_ref):
    out_ref[...] = (keep_ref[...].astype(F32) + arrived_ref[...].astype(F32)).astype(BF16)


def finish_rows(k_gain, one, two):
    keys = one[0].astype(F32) + two[0].astype(F32)
    values = one[1].astype(F32) + two[1].astype(F32)
    return normalize(keys, k_gain).astype(BF16), values.astype(BF16)


def norm_kernel(k_gain_ref, keep_ref, arrived_ref, kv_ref):
    kv_ref[0], kv_ref[1] = finish_rows(k_gain_ref[...], keep_ref.at[0], arrived_ref.at[0])


def attend_kernel(near, far, tile_len, first, last, head_dim, k_gain_ref, qt_ref, bias_ref, *refs):
    near_refs, refs = refs[: len(near)], refs[len(near) :]
    far_refs, refs = refs[: 2 * len(far)], refs[2 * len(far) :]
    if not first:
        top_in, sum_in, mixed_in = refs[:3]
        refs = refs[3:]
    s = lax.axis_index("section")
    qt = qt_ref[...]
    parts = [(part[0], part[1]) for part in near_refs]
    for one, two in zip(far_refs[::2], far_refs[1::2]):
        parts.append(finish_rows(k_gain_ref[...], one.at[0], two.at[0]))
    rows = parts[0][0].shape[0]
    scores, biases = [], []
    top = TOP_FLOOR if first else top_in[...]
    for step, (keys, _) in zip((*near, *far), parts):
        score = jnp.dot(keys, qt, preferred_element_type=F32)
        bias = bias_ref[pl.ds(((s ^ step) * rows) // tile_len, 1), :]
        scores.append(score)
        biases.append(bias)
        top = jnp.maximum(top, jnp.max(score, axis=0, keepdims=True) + bias)
    row_sum, mixed = 0.0, 0.0
    if not first:
        scale = jnp.exp(top_in[...] - top)
        row_sum = sum_in[...] * scale
        mixed = mixed_in[...] * scale
    for (_, values), score, bias in zip(parts, scores, biases):
        weights = jnp.exp(score + (bias - top))
        row_sum = row_sum + jnp.sum(weights, axis=0, keepdims=True)
        mixed = mixed + lax.dot_general(
            values, weights.astype(BF16), (((0,), (0,)), ((), ())), preferred_element_type=F32
        )
    if not last:
        top_out, sum_out, mixed_out = refs
        top_out[...] = top
        sum_out[...] = row_sum
        mixed_out[...] = mixed
        return
    (out,) = refs
    has_any = jnp.max(bias_ref[...], axis=0, keepdims=True) > -1.0
    inverse = jnp.where(has_any, 1.0 / jnp.where(has_any, row_sum, 1.0), 0.0)
    context = (mixed * inverse).astype(BF16)
    tokens = out.shape[0]
    for head in range(out.shape[1] // head_dim):
        out[:, head * head_dim : (head + 1) * head_dim] = context[
            :, head * tokens : (head + 1) * tokens
        ].T


def swap(value, axis, k):
    return lax.ppermute(value, axis, [(i, i ^ k) for i in range(lax.axis_size(axis))])


def exchange_two_heads(value, home_sends):
    hops = []
    for d in range(2):
        for t in range(4):
            sends = (t // 2 == d) == home_sends
            hops.append((4 * d + t, 4 * d + (t ^ 2) if sends else 4 * (1 - d) + t))
    return lax.ppermute(value, ("dp", "tensor"), hops)


def sum_many_heads(own, others):
    n_dp, n_tensor = lax.axis_size("dp"), lax.axis_size("tensor")
    heads = own.shape[0] * n_dp
    half = shape_of((heads // 2, *own.shape[1:]))
    send, keep = call(
        functools.partial(spread_kernel, n_dp, n_tensor),
        [half, half],
        n_dp,
        "spread",
        scratch=[pltpu.VMEM((heads, *own.shape[1:]), BF16)],
    )(own, *others)
    bit = n_tensor // 2
    while bit > 1:
        arrived = swap(send, "tensor", bit)
        bit //= 2
        now = keep.shape
        if bit > 1:
            half = shape_of((now[0] // 2, *now[1:]))
            send, keep = call(
                functools.partial(add_kernel, bit),
                [half, half],
                2,
                "add_part",
                scratch=[pltpu.VMEM(now, BF16)],
            )(keep, arrived)
        else:
            keep = call(add_last_kernel, shape_of(now), 2, "add_pair")(keep, arrived)
    return keep


def on_device(queries, images, kv_weight, q_gain, k_gain, tile_mask):
    n_section = lax.axis_size("section")
    n_dp = lax.axis_size("dp")
    n_tensor = lax.axis_size("tensor")
    head_dim = q_gain.shape[0]
    tokens, q_width = queries.shape
    rows, features = images.shape[1:]
    tiles = tile_mask.shape[1]
    own_heads = kv_weight.shape[2] // head_dim
    heads = own_heads * n_dp
    tile_len = rows * n_section // tiles
    assert heads * 2 == n_tensor and tile_len % rows == 0 and n_section >= 4
    pairs = tokens * (q_width // head_dim)
    work = 4 * rows * features * kv_weight.shape[2]

    x, w, *small = [
        pltpu.with_memory_space_constraint(value, pltpu.HBM)
        for value in (
            images, kv_weight, queries, q_gain.reshape(1, -1), tile_mask.T, k_gain.reshape(1, -1),
        )
    ]
    product = shape_of((own_heads, 2, rows, head_dim))
    x_scratch, w_scratch = pltpu.VMEM(images.shape, BF16), pltpu.VMEM(kv_weight.shape, BF16)
    prepared = [
        shape_of((head_dim, pairs)),
        shape_of((tiles, pairs), F32),
        shape_of((1, head_dim), F32),
    ]
    query_scratch = [
        pltpu.VMEM(queries.shape, BF16),
        pltpu.VMEM((1, head_dim), F32),
        pltpu.VMEM((tiles, tokens), jnp.int32),
    ]
    others = [swap(kv_weight, "dp", k) for k in range(1, n_dp)]
    if n_dp == 2 and own_heads == 1:
        away = call(
            functools.partial(away_kernel, head_dim),
            product,
            2,
            "away_own",
            flops=work,
            in_specs=[HBM] * 2,
            scratch=[x_scratch, w_scratch, pltpu.SemaphoreType.DMA((2,))],
        )(x, w)
        first = exchange_two_heads(away, False)
        x_home = call(
            load_kernel,
            shape_of(images.shape),
            2,
            "home_rows",
            in_specs=[VMEM, HBM],
            scratch=[pltpu.SemaphoreType.DMA((1,))],
        )(away, x)
        home = call(
            functools.partial(home_kernel, head_dim), product, 2, "home_other", flops=work
        )(x_home, others[0])
        second = exchange_two_heads(home, True)
        keep, qt, bias, gain = call(
            functools.partial(keep_kernel, head_dim),
            [product, *prepared],
            8,
            "keep_queries",
            flops=work,
            in_specs=[VMEM] * 2 + [HBM] * 6,
            scratch=[x_scratch, w_scratch, *query_scratch, pltpu.SemaphoreType.DMA((6,))],
        )(home, others[0], x, w, *small)
        total = call(pair_kernel, product, 3, "pair_sum")(keep, first, second)
    else:
        own, x_here = call(
            functools.partial(own_kernel, head_dim),
            [product, shape_of(images.shape)],
            2,
            "own_heads",
            flops=work,
            in_specs=[HBM] * 2,
            scratch=[w_scratch, pltpu.SemaphoreType.DMA((2,))],
        )(x, w)
        qt, bias, gain = call(
            query_kernel,
            prepared,
            4,
            "queries",
            in_specs=[HBM] * 4,
            scratch=[*query_scratch, pltpu.SemaphoreType.DMA((4,))],
        )(*small)
        rest = [
            call(functools.partial(other_kernel, head_dim), product, 2, "other_heads", flops=work)(
                x_here, other
            )
            for other in others
        ]
        total = sum_many_heads(own, rest)
    far = [step for step in range(1, n_section) if step & (step - 1)]
    near = [step for step in range(1, n_section) if not step & (step - 1)]
    arrived = swap(total, "tensor", 1)
    halves = [swap(total, "section", step) for step in far]
    kv = call(norm_kernel, shape_of((2, rows, head_dim)), 3, "sum_norm")(gain, total, arrived)
    finished = [swap(kv, "section", step) for step in near]
    both = []
    for value in halves:
        both += [value, swap(value, "tensor", 1)]
    state = []
    for here, there, operands in (
        ([0], [], [kv]),
        (near, [], finished),
        ([], far, both),
    ):
        first, last = here == [0], len(there) > 0
        outs = (
            shape_of((tokens, q_width))
            if last
            else [shape_of((1, pairs), F32), shape_of((1, pairs), F32), shape_of((head_dim, pairs), F32)]
        )
        parts = len(here) + len(there)
        state = call(
            functools.partial(attend_kernel, here, there, tile_len, first, last, head_dim),
            outs,
            3 + len(operands) + len(state),
            "attend",
            flops=4 * pairs * rows * head_dim * parts,
            exps=pairs * rows * parts,
        )(gain, qt, bias, *operands, *state)
    return state


def solution(mesh):
    in_specs = (
        P(("section", "dp"), "tensor"),
        P("dp", "section", "tensor"),
        P(None, "tensor", "dp"),
        P(),
        P(),
        P(("section", "dp"), None),
    )
    out_specs = P(("section", "dp"), "tensor")
    return jax.shard_map(
        on_device, mesh=mesh, in_specs=in_specs, out_specs=out_specs, check_vma=False
    )
```

```python
import functools

import jax
import jax.numpy as jnp
from jax import lax
from jax.experimental import pallas as pl
from jax.experimental.pallas import tpu as pltpu
from jax.sharding import PartitionSpec as P

EPSILON = 1e-05
MASKED_SCORE = -1e30
TOP_FLOOR = -1e29
VMEM = pl.BlockSpec(memory_space=pltpu.VMEM)
HBM = pl.BlockSpec(memory_space=pltpu.HBM)
F32 = jnp.float32
MIB = 1024 * 1024
LIMIT = 24 * MIB
BF16 = jnp.bfloat16


def shape_of(dims, dtype=BF16):
    return jax.ShapeDtypeStruct(dims, dtype)


def call(
    kernel, outs, n_in, name, flops=0, size=0, exps=0, in_specs=None, scratch=()
):
    many = isinstance(outs, list)
    return pl.pallas_call(
        kernel,
        out_shape=outs,
        in_specs=in_specs or [VMEM] * n_in,
        out_specs=[VMEM] * len(outs) if many else VMEM,
        scratch_shapes=scratch,
        compiler_params=pltpu.CompilerParams(vmem_limit_bytes=LIMIT),
        cost_estimate=pl.CostEstimate(flops=flops, bytes_accessed=size, transcendentals=exps),
        name=name,
    )


def normalize(values, gain_vec):
    mean_sq = jnp.mean(values * values, axis=-1, keepdims=True)
    return values * lax.rsqrt(mean_sq + EPSILON) * gain_vec


def project(x, w):
    return jnp.dot(
        x, jnp.concatenate([w[0], w[1]], axis=1), preferred_element_type=F32
    ).astype(BF16)


def store_heads(ref, base, both, head_dim):
    width = both.shape[1] // 2
    for head in range(width // head_dim):
        lo = head * head_dim
        ref[base + head, 0] = both[:, lo : lo + head_dim]
        ref[base + head, 1] = both[:, width + lo : width + lo + head_dim]


def prepare_queries(copies, q_ref, q_gain_ref, mask_ref, qt_ref, bias_ref):
    for copy in copies:
        copy.wait()
    tokens = q_ref.shape[0]
    head_dim = q_gain_ref.shape[1]
    bias = jnp.where(mask_ref[...] > 0, 0.0, MASKED_SCORE).astype(F32)
    for head in range(q_ref.shape[1] // head_dim):
        rows = q_ref[:, head * head_dim : (head + 1) * head_dim].astype(F32)
        normed = normalize(rows, q_gain_ref[...]) * head_dim ** (-0.5)
        qt_ref[:, head * tokens : (head + 1) * tokens] = normed.T.astype(BF16)
        bias_ref[:, head * tokens : (head + 1) * tokens] = bias


def start_copies(sources, targets, sems, first=0):
    copies = [
        pltpu.make_async_copy(a, b, sems.at[first + i]) for i, (a, b) in enumerate(zip(sources, targets))
    ]
    for copy in copies:
        copy.start()
    return copies


def own_kernel(head_dim, x_hbm, w_hbm, own_ref, x_ref, w_ref, sems):
    for copy in start_copies((x_hbm, w_hbm), (x_ref, w_ref), sems):
        copy.wait()
    store_heads(own_ref, 0, project(x_ref[0], w_ref[...]), head_dim)


def other_kernel(head_dim, x_ref, w_ref, other_ref):
    store_heads(other_ref, 0, project(x_ref[0], w_ref[...]), head_dim)


def query_kernel(
    q_hbm, q_gain_hbm, mask_hbm, k_gain_hbm, qt_ref, bias_ref, k_gain_ref,
    q_ref, q_gain_ref, mask_ref, sems,
):
    copies = start_copies(
        (q_hbm, q_gain_hbm, mask_hbm, k_gain_hbm), (q_ref, q_gain_ref, mask_ref, k_gain_ref), sems
    )
    prepare_queries(copies, q_ref, q_gain_ref, mask_ref, qt_ref, bias_ref)


def is_home():
    return lax.axis_index("tensor") // 2 == lax.axis_index("dp")


def away_kernel(head_dim, x_hbm, w_hbm, own_ref, x_ref, w_ref, sems):
    @pl.when(is_home())
    def _():
        own_ref[...] = jnp.zeros_like(own_ref)

    @pl.when(jnp.logical_not(is_home()))
    def _():
        own_kernel(head_dim, x_hbm, w_hbm, own_ref, x_ref, w_ref, sems)


def load_kernel(after_ref, x_hbm, x_ref, sems):
    @pl.when(is_home())
    def _():
        for copy in start_copies((x_hbm,), (x_ref,), sems):
            copy.wait()


def home_kernel(head_dim, x_ref, w_other_ref, other_ref):
    @pl.when(is_home())
    def _():
        store_heads(other_ref, 0, project(x_ref[0], w_other_ref[...]), head_dim)

    @pl.when(jnp.logical_not(is_home()))
    def _():
        other_ref[...] = jnp.zeros_like(other_ref)


def keep_kernel(
    head_dim, after_ref, w_other_ref, x_hbm, w_hbm, q_hbm, q_gain_hbm, mask_hbm, k_gain_hbm,
    keep_ref, qt_ref, bias_ref, k_gain_ref, x_ref, w_ref, q_ref, q_gain_ref, mask_ref, sems,
):
    copies = start_copies(
        (q_hbm, q_gain_hbm, mask_hbm, k_gain_hbm), (q_ref, q_gain_ref, mask_ref, k_gain_ref), sems
    )
    moves = start_copies((x_hbm, w_hbm), (x_ref, w_ref), sems, len(copies))
    prepare_queries(copies, q_ref, q_gain_ref, mask_ref, qt_ref, bias_ref)
    for copy in moves:
        copy.wait()

    @pl.when(is_home())
    def _():
        store_heads(keep_ref, 0, project(x_ref[0], w_ref[...]), head_dim)

    @pl.when(jnp.logical_not(is_home()))
    def _():
        store_heads(keep_ref, 0, project(x_ref[0], w_other_ref[...]), head_dim)


def split_half(held, send_ref, keep_ref, partner_heads, own_heads):
    for i in range(send_ref.shape[0]):
        send_ref[i] = held[partner_heads + i]
        keep_ref[i] = held[own_heads + i]


def spread_kernel(n_dp, n_tensor, own_ref, *refs):
    others, (send_ref, keep_ref, held) = refs[: n_dp - 1], refs[n_dp - 1 :]
    d = lax.axis_index("dp")
    own_heads = own_ref.shape[0]
    for k, ref in enumerate((own_ref, *others)):
        held[pl.ds((d ^ k) * own_heads, own_heads)] = ref[...]
    half = send_ref.shape[0]
    upper = lax.axis_index("tensor") // (n_tensor // 2)
    split_half(held, send_ref, keep_ref, (1 - upper) * half, upper * half)


def pair_kernel(keep_ref, first_ref, second_ref, out_ref):
    arrived = jnp.where(is_home(), first_ref[...], second_ref[...]).astype(F32)
    out_ref[...] = (keep_ref[...].astype(F32) + arrived).astype(BF16)


def add_kernel(bit, keep_ref, arrived_ref, send_ref, next_ref, held):
    held[...] = (keep_ref[...].astype(F32) + arrived_ref[...].astype(F32)).astype(BF16)
    half = send_ref.shape[0]
    upper = (lax.axis_index("tensor") // bit) % 2
    split_half(held, send_ref, next_ref, (1 - upper) * half, upper * half)


def add_last_kernel(keep_ref, arrived_ref, out_ref):
    out_ref[...] = (keep_ref[...].astype(F32) + arrived_ref[...].astype(F32)).astype(BF16)


def finish_rows(k_gain, one, two):
    keys = one[0].astype(F32) + two[0].astype(F32)
    values = one[1].astype(F32) + two[1].astype(F32)
    return normalize(keys, k_gain).astype(BF16), values.astype(BF16)


def norm_kernel(k_gain_ref, keep_ref, arrived_ref, kv_ref):
    kv_ref[0], kv_ref[1] = finish_rows(k_gain_ref[...], keep_ref.at[0], arrived_ref.at[0])


def attend_kernel(near, far, tile_len, first, last, head_dim, k_gain_ref, qt_ref, bias_ref, *refs):
    near_refs, refs = refs[: len(near)], refs[len(near) :]
    far_refs, refs = refs[: 2 * len(far)], refs[2 * len(far) :]
    if not first:
        top_in, sum_in, mixed_in = refs[:3]
        refs = refs[3:]
    s = lax.axis_index("section")
    qt = qt_ref[...]
    parts = [(part[0], part[1]) for part in near_refs]
    for one, two in zip(far_refs[::2], far_refs[1::2]):
        parts.append(finish_rows(k_gain_ref[...], one.at[0], two.at[0]))
    rows = parts[0][0].shape[0]
    scores, biases = [], []
    top = TOP_FLOOR if first else top_in[...]
    for step, (keys, _) in zip((*near, *far), parts):
        score = jnp.dot(keys, qt, preferred_element_type=F32)
        bias = bias_ref[pl.ds(((s ^ step) * rows) // tile_len, 1), :]
        scores.append(score)
        biases.append(bias)
        top = jnp.maximum(top, jnp.max(score, axis=0, keepdims=True) + bias)
    row_sum, mixed = 0.0, 0.0
    if not first:
        scale = jnp.exp(top_in[...] - top)
        row_sum = sum_in[...] * scale
        mixed = mixed_in[...] * scale
    for (_, values), score, bias in zip(parts, scores, biases):
        weights = jnp.exp(score + (bias - top))
        row_sum = row_sum + jnp.sum(weights, axis=0, keepdims=True)
        mixed = mixed + lax.dot_general(
            values, weights.astype(BF16), (((0,), (0,)), ((), ())), preferred_element_type=F32
        )
    if not last:
        top_out, sum_out, mixed_out = refs
        top_out[...] = top
        sum_out[...] = row_sum
        mixed_out[...] = mixed
        return
    (out,) = refs
    has_any = jnp.max(bias_ref[...], axis=0, keepdims=True) > -1.0
    inverse = jnp.where(has_any, 1.0 / jnp.where(has_any, row_sum, 1.0), 0.0)
    context = (mixed * inverse).astype(BF16)
    tokens = out.shape[0]
    for head in range(out.shape[1] // head_dim):
        out[:, head * head_dim : (head + 1) * head_dim] = context[
            :, head * tokens : (head + 1) * tokens
        ].T


def swap(value, axis, k):
    return lax.ppermute(value, axis, [(i, i ^ k) for i in range(lax.axis_size(axis))])


def exchange_two_heads(value, home_sends, apart):
    hops = []
    for d in range(2):
        for t in range(4):
            sends = (t // 2 == d) == home_sends
            hops.append((4 * d + t, 4 * d + (t ^ apart) if sends else 4 * (1 - d) + t))
    return lax.ppermute(value, ("dp", "tensor"), hops)


def sum_many_heads(own, others):
    n_dp, n_tensor = lax.axis_size("dp"), lax.axis_size("tensor")
    heads = own.shape[0] * n_dp
    half = shape_of((heads // 2, *own.shape[1:]))
    send, keep = call(
        functools.partial(spread_kernel, n_dp, n_tensor),
        [half, half],
        n_dp,
        "spread",
        scratch=[pltpu.VMEM((heads, *own.shape[1:]), BF16)],
    )(own, *others)
    bit = n_tensor // 2
    while bit > 1:
        arrived = swap(send, "tensor", bit)
        bit //= 2
        now = keep.shape
        if bit > 1:
            half = shape_of((now[0] // 2, *now[1:]))
            send, keep = call(
                functools.partial(add_kernel, bit),
                [half, half],
                2,
                "add_part",
                scratch=[pltpu.VMEM(now, BF16)],
            )(keep, arrived)
        else:
            keep = call(add_last_kernel, shape_of(now), 2, "add_pair")(keep, arrived)
    return keep


def on_device(queries, images, kv_weight, q_gain, k_gain, tile_mask):
    n_section = lax.axis_size("section")
    n_dp = lax.axis_size("dp")
    n_tensor = lax.axis_size("tensor")
    head_dim = q_gain.shape[0]
    tokens, q_width = queries.shape
    rows, features = images.shape[1:]
    tiles = tile_mask.shape[1]
    own_heads = kv_weight.shape[2] // head_dim
    heads = own_heads * n_dp
    tile_len = rows * n_section // tiles
    assert heads * 2 == n_tensor and tile_len % rows == 0 and n_section >= 4
    pairs = tokens * (q_width // head_dim)
    work = 4 * rows * features * kv_weight.shape[2]

    x, w, *small = [
        pltpu.with_memory_space_constraint(value, pltpu.HBM)
        for value in (
            images, kv_weight, queries, q_gain.reshape(1, -1), tile_mask.T, k_gain.reshape(1, -1),
        )
    ]
    product = shape_of((own_heads, 2, rows, head_dim))
    x_scratch, w_scratch = pltpu.VMEM(images.shape, BF16), pltpu.VMEM(kv_weight.shape, BF16)
    prepared = [
        shape_of((head_dim, pairs)),
        shape_of((tiles, pairs), F32),
        shape_of((1, head_dim), F32),
    ]
    query_scratch = [
        pltpu.VMEM(queries.shape, BF16),
        pltpu.VMEM((1, head_dim), F32),
        pltpu.VMEM((tiles, tokens), jnp.int32),
    ]
    others = [swap(kv_weight, "dp", k) for k in range(1, n_dp)]
    if n_dp == 2 and own_heads == 1:
        away = call(
            functools.partial(away_kernel, head_dim),
            product,
            2,
            "away_own",
            flops=work,
            in_specs=[HBM] * 2,
            scratch=[x_scratch, w_scratch, pltpu.SemaphoreType.DMA((2,))],
        )(x, w)
        first = exchange_two_heads(away, False, 2)
        x_home = call(
            load_kernel,
            shape_of(images.shape),
            2,
            "home_rows",
            in_specs=[VMEM, HBM],
            scratch=[pltpu.SemaphoreType.DMA((1,))],
        )(away, x)
        home = call(
            functools.partial(home_kernel, head_dim), product, 2, "home_other", flops=work
        )(x_home, others[0])
        second = exchange_two_heads(home, True, 3)
        keep, qt, bias, gain = call(
            functools.partial(keep_kernel, head_dim),
            [product, *prepared],
            8,
            "keep_queries",
            flops=work,
            in_specs=[VMEM] * 2 + [HBM] * 6,
            scratch=[x_scratch, w_scratch, *query_scratch, pltpu.SemaphoreType.DMA((6,))],
        )(home, others[0], x, w, *small)
        total = call(pair_kernel, product, 3, "pair_sum")(keep, first, second)
    else:
        own, x_here = call(
            functools.partial(own_kernel, head_dim),
            [product, shape_of(images.shape)],
            2,
            "own_heads",
            flops=work,
            in_specs=[HBM] * 2,
            scratch=[w_scratch, pltpu.SemaphoreType.DMA((2,))],
        )(x, w)
        qt, bias, gain = call(
            query_kernel,
            prepared,
            4,
            "queries",
            in_specs=[HBM] * 4,
            scratch=[*query_scratch, pltpu.SemaphoreType.DMA((4,))],
        )(*small)
        rest = [
            call(functools.partial(other_kernel, head_dim), product, 2, "other_heads", flops=work)(
                x_here, other
            )
            for other in others
        ]
        total = sum_many_heads(own, rest)
    far = [step for step in range(1, n_section) if step & (step - 1)]
    near = [step for step in range(1, n_section) if not step & (step - 1)]
    arrived = swap(total, "tensor", 1)
    halves = [swap(total, "section", step) for step in far]
    kv = call(norm_kernel, shape_of((2, rows, head_dim)), 3, "sum_norm")(gain, total, arrived)
    finished = [swap(kv, "section", step) for step in near]
    both = []
    for value in halves:
        both += [value, swap(value, "tensor", 1)]
    state = []
    for here, there, operands in (
        ([0], [], [kv]),
        (near, [], finished),
        ([], far, both),
    ):
        first, last = here == [0], len(there) > 0
        outs = (
            shape_of((tokens, q_width))
            if last
            else [shape_of((1, pairs), F32), shape_of((1, pairs), F32), shape_of((head_dim, pairs), F32)]
        )
        parts = len(here) + len(there)
        state = call(
            functools.partial(attend_kernel, here, there, tile_len, first, last, head_dim),
            outs,
            3 + len(operands) + len(state),
            "attend",
            flops=4 * pairs * rows * head_dim * parts,
            exps=pairs * rows * parts,
        )(gain, qt, bias, *operands, *state)
    return state


def solution(mesh):
    in_specs = (
        P(("section", "dp"), "tensor"),
        P("dp", "section", "tensor"),
        P(None, "tensor", "dp"),
        P(),
        P(),
        P(("section", "dp"), None),
    )
    out_specs = P(("section", "dp"), "tensor")
    return jax.shard_map(
        on_device, mesh=mesh, in_specs=in_specs, out_specs=out_specs, check_vma=False
    )
```

```python
import functools

import jax
import jax.numpy as jnp
from jax import lax
from jax.experimental import pallas as pl
from jax.experimental.pallas import tpu as pltpu
from jax.sharding import PartitionSpec as P

EPSILON = 1e-05
MASKED_SCORE = -1e30
TOP_FLOOR = -1e29
VMEM = pl.BlockSpec(memory_space=pltpu.VMEM)
HBM = pl.BlockSpec(memory_space=pltpu.HBM)
F32 = jnp.float32
MIB = 1024 * 1024
LIMIT = 24 * MIB
BF16 = jnp.bfloat16


def shape_of(dims, dtype=BF16):
    return jax.ShapeDtypeStruct(dims, dtype)


def call(
    kernel, outs, n_in, name, flops=0, size=0, exps=0, in_specs=None, scratch=()
):
    many = isinstance(outs, list)
    return pl.pallas_call(
        kernel,
        out_shape=outs,
        in_specs=in_specs or [VMEM] * n_in,
        out_specs=[VMEM] * len(outs) if many else VMEM,
        scratch_shapes=scratch,
        compiler_params=pltpu.CompilerParams(vmem_limit_bytes=LIMIT),
        cost_estimate=pl.CostEstimate(flops=flops, bytes_accessed=size, transcendentals=exps),
        name=name,
    )


def normalize(values, gain_vec):
    mean_sq = jnp.mean(values * values, axis=-1, keepdims=True)
    return values * lax.rsqrt(mean_sq + EPSILON) * gain_vec


def project(x, w):
    return jnp.dot(
        x, jnp.concatenate([w[0], w[1]], axis=1), preferred_element_type=F32
    ).astype(BF16)


def store_heads(ref, base, both, head_dim):
    width = both.shape[1] // 2
    for head in range(width // head_dim):
        lo = head * head_dim
        ref[base + head, 0] = both[:, lo : lo + head_dim]
        ref[base + head, 1] = both[:, width + lo : width + lo + head_dim]


def prepare_queries(copies, q_ref, q_gain_ref, mask_ref, qt_ref, bias_ref):
    for copy in copies:
        copy.wait()
    tokens = q_ref.shape[0]
    head_dim = q_gain_ref.shape[1]
    bias = jnp.where(mask_ref[...] > 0, 0.0, MASKED_SCORE).astype(F32)
    for head in range(q_ref.shape[1] // head_dim):
        rows = q_ref[:, head * head_dim : (head + 1) * head_dim].astype(F32)
        normed = normalize(rows, q_gain_ref[...]) * head_dim ** (-0.5)
        qt_ref[:, head * tokens : (head + 1) * tokens] = normed.T.astype(BF16)
        bias_ref[:, head * tokens : (head + 1) * tokens] = bias


def start_copies(sources, targets, sems, first=0):
    copies = [
        pltpu.make_async_copy(a, b, sems.at[first + i]) for i, (a, b) in enumerate(zip(sources, targets))
    ]
    for copy in copies:
        copy.start()
    return copies


def own_kernel(head_dim, x_hbm, w_hbm, own_ref, x_ref, w_ref, sems):
    for copy in start_copies((x_hbm, w_hbm), (x_ref, w_ref), sems):
        copy.wait()
    store_heads(own_ref, 0, project(x_ref[0], w_ref[...]), head_dim)


def other_kernel(head_dim, x_ref, w_ref, other_ref):
    store_heads(other_ref, 0, project(x_ref[0], w_ref[...]), head_dim)


def query_kernel(
    q_hbm, q_gain_hbm, mask_hbm, k_gain_hbm, qt_ref, bias_ref, k_gain_ref,
    q_ref, q_gain_ref, mask_ref, sems,
):
    copies = start_copies(
        (q_hbm, q_gain_hbm, mask_hbm, k_gain_hbm), (q_ref, q_gain_ref, mask_ref, k_gain_ref), sems
    )
    prepare_queries(copies, q_ref, q_gain_ref, mask_ref, qt_ref, bias_ref)


def is_home():
    return lax.axis_index("tensor") // 2 == lax.axis_index("dp")


def away_kernel(head_dim, x_hbm, w_hbm, own_ref, x_ref, w_ref, sems):
    @pl.when(is_home())
    def _():
        own_ref[...] = jnp.zeros_like(own_ref)

    @pl.when(jnp.logical_not(is_home()))
    def _():
        own_kernel(head_dim, x_hbm, w_hbm, own_ref, x_ref, w_ref, sems)


def load_kernel(after_ref, x_hbm, x_ref, sems):
    @pl.when(is_home())
    def _():
        for copy in start_copies((x_hbm,), (x_ref,), sems):
            copy.wait()


def home_kernel(head_dim, x_ref, w_other_ref, other_ref):
    @pl.when(is_home())
    def _():
        store_heads(other_ref, 0, project(x_ref[0], w_other_ref[...]), head_dim)

    @pl.when(jnp.logical_not(is_home()))
    def _():
        other_ref[...] = jnp.zeros_like(other_ref)


def keep_kernel(
    head_dim, after_ref, w_other_ref, x_hbm, w_hbm, q_hbm, q_gain_hbm, mask_hbm, k_gain_hbm,
    keep_ref, qt_ref, bias_ref, k_gain_ref, x_ref, w_ref, q_ref, q_gain_ref, mask_ref, sems,
):
    copies = start_copies(
        (q_hbm, q_gain_hbm, mask_hbm, k_gain_hbm), (q_ref, q_gain_ref, mask_ref, k_gain_ref), sems
    )
    moves = start_copies((x_hbm, w_hbm), (x_ref, w_ref), sems, len(copies))
    prepare_queries(copies, q_ref, q_gain_ref, mask_ref, qt_ref, bias_ref)
    for copy in moves:
        copy.wait()

    @pl.when(is_home())
    def _():
        store_heads(keep_ref, 0, project(x_ref[0], w_ref[...]), head_dim)

    @pl.when(jnp.logical_not(is_home()))
    def _():
        store_heads(keep_ref, 0, project(x_ref[0], w_other_ref[...]), head_dim)


def split_half(held, send_ref, keep_ref, partner_heads, own_heads):
    for i in range(send_ref.shape[0]):
        send_ref[i] = held[partner_heads + i]
        keep_ref[i] = held[own_heads + i]


def spread_kernel(n_dp, n_tensor, own_ref, *refs):
    others, (send_ref, keep_ref, held) = refs[: n_dp - 1], refs[n_dp - 1 :]
    d = lax.axis_index("dp")
    own_heads = own_ref.shape[0]
    for k, ref in enumerate((own_ref, *others)):
        held[pl.ds((d ^ k) * own_heads, own_heads)] = ref[...]
    half = send_ref.shape[0]
    upper = lax.axis_index("tensor") // (n_tensor // 2)
    split_half(held, send_ref, keep_ref, (1 - upper) * half, upper * half)


def first_sum_kernel(keep_ref, first_ref, out_ref):
    out_ref[...] = (keep_ref[...].astype(F32) + first_ref[...].astype(F32)).astype(BF16)


def second_sum_kernel(first_sum_ref, keep_ref, second_ref, out_ref):
    total = (keep_ref[...].astype(F32) + second_ref[...].astype(F32)).astype(BF16)
    out_ref[...] = jnp.where(is_home(), first_sum_ref[...], total)


def add_kernel(bit, keep_ref, arrived_ref, send_ref, next_ref, held):
    held[...] = (keep_ref[...].astype(F32) + arrived_ref[...].astype(F32)).astype(BF16)
    half = send_ref.shape[0]
    upper = (lax.axis_index("tensor") // bit) % 2
    split_half(held, send_ref, next_ref, (1 - upper) * half, upper * half)


def add_last_kernel(keep_ref, arrived_ref, out_ref):
    out_ref[...] = (keep_ref[...].astype(F32) + arrived_ref[...].astype(F32)).astype(BF16)


def finish_rows(k_gain, one, two):
    keys = one[0].astype(F32) + two[0].astype(F32)
    values = one[1].astype(F32) + two[1].astype(F32)
    return normalize(keys, k_gain).astype(BF16), values.astype(BF16)


def norm_kernel(k_gain_ref, keep_ref, *refs):
    arrived_refs, kv_ref = refs[:-1], refs[-1]
    arrived = arrived_refs[0][0]
    if len(arrived_refs) > 1:
        arrived = jnp.where(is_home(), arrived, arrived_refs[1][0])
    kv_ref[0], kv_ref[1] = finish_rows(k_gain_ref[...], keep_ref[0], arrived)


def attend_kernel(near, far, tile_len, first, last, head_dim, k_gain_ref, qt_ref, bias_ref, *refs):
    near_refs, refs = refs[: len(near)], refs[len(near) :]
    far_refs, refs = refs[: 2 * len(far)], refs[2 * len(far) :]
    if not first:
        top_in, sum_in, mixed_in = refs[:3]
        refs = refs[3:]
    s = lax.axis_index("section")
    qt = qt_ref[...]
    parts = [(part[0], part[1]) for part in near_refs]
    for one, two in zip(far_refs[::2], far_refs[1::2]):
        parts.append(finish_rows(k_gain_ref[...], one.at[0], two.at[0]))
    rows = parts[0][0].shape[0]
    scores, biases = [], []
    top = TOP_FLOOR if first else top_in[...]
    for step, (keys, _) in zip((*near, *far), parts):
        score = jnp.dot(keys, qt, preferred_element_type=F32)
        bias = bias_ref[pl.ds(((s ^ step) * rows) // tile_len, 1), :]
        scores.append(score)
        biases.append(bias)
        top = jnp.maximum(top, jnp.max(score, axis=0, keepdims=True) + bias)
    row_sum, mixed = 0.0, 0.0
    if not first:
        scale = jnp.exp(top_in[...] - top)
        row_sum = sum_in[...] * scale
        mixed = mixed_in[...] * scale
    for (_, values), score, bias in zip(parts, scores, biases):
        weights = jnp.exp(score + (bias - top))
        row_sum = row_sum + jnp.sum(weights, axis=0, keepdims=True)
        mixed = mixed + lax.dot_general(
            values, weights.astype(BF16), (((0,), (0,)), ((), ())), preferred_element_type=F32
        )
    if not last:
        top_out, sum_out, mixed_out = refs
        top_out[...] = top
        sum_out[...] = row_sum
        mixed_out[...] = mixed
        return
    (out,) = refs
    has_any = jnp.max(bias_ref[...], axis=0, keepdims=True) > -1.0
    inverse = jnp.where(has_any, 1.0 / jnp.where(has_any, row_sum, 1.0), 0.0)
    context = (mixed * inverse).astype(BF16)
    tokens = out.shape[0]
    for head in range(out.shape[1] // head_dim):
        out[:, head * head_dim : (head + 1) * head_dim] = context[
            :, head * tokens : (head + 1) * tokens
        ].T


def swap(value, axis, k):
    return lax.ppermute(value, axis, [(i, i ^ k) for i in range(lax.axis_size(axis))])


def permute_two_heads(value, away, home):
    hops = []
    for d in range(2):
        for t in range(4):
            to_d, to_t = home(d, t) if t // 2 == d else away(d, t)
            hops.append((4 * d + t, 4 * to_d + to_t))
    return lax.ppermute(value, ("dp", "tensor"), hops)


def across(d, t):
    return d, t ^ 2


def next_core(d, t):
    return 1 - d, t


def next_tensor(d, t):
    return d, t ^ 1


def itself(d, t):
    return d, t


def sum_many_heads(own, others):
    n_dp, n_tensor = lax.axis_size("dp"), lax.axis_size("tensor")
    heads = own.shape[0] * n_dp
    half = shape_of((heads // 2, *own.shape[1:]))
    send, keep = call(
        functools.partial(spread_kernel, n_dp, n_tensor),
        [half, half],
        n_dp,
        "spread",
        scratch=[pltpu.VMEM((heads, *own.shape[1:]), BF16)],
    )(own, *others)
    bit = n_tensor // 2
    while bit > 1:
        arrived = swap(send, "tensor", bit)
        bit //= 2
        now = keep.shape
        if bit > 1:
            half = shape_of((now[0] // 2, *now[1:]))
            send, keep = call(
                functools.partial(add_kernel, bit),
                [half, half],
                2,
                "add_part",
                scratch=[pltpu.VMEM(now, BF16)],
            )(keep, arrived)
        else:
            keep = call(add_last_kernel, shape_of(now), 2, "add_pair")(keep, arrived)
    return keep


def on_device(queries, images, kv_weight, q_gain, k_gain, tile_mask):
    n_section = lax.axis_size("section")
    n_dp = lax.axis_size("dp")
    n_tensor = lax.axis_size("tensor")
    head_dim = q_gain.shape[0]
    tokens, q_width = queries.shape
    rows, features = images.shape[1:]
    tiles = tile_mask.shape[1]
    own_heads = kv_weight.shape[2] // head_dim
    heads = own_heads * n_dp
    tile_len = rows * n_section // tiles
    assert heads * 2 == n_tensor and tile_len % rows == 0 and n_section >= 4
    pairs = tokens * (q_width // head_dim)
    work = 4 * rows * features * kv_weight.shape[2]

    x, w, *small = [
        pltpu.with_memory_space_constraint(value, pltpu.HBM)
        for value in (
            images, kv_weight, queries, q_gain.reshape(1, -1), tile_mask.T, k_gain.reshape(1, -1),
        )
    ]
    product = shape_of((own_heads, 2, rows, head_dim))
    x_scratch, w_scratch = pltpu.VMEM(images.shape, BF16), pltpu.VMEM(kv_weight.shape, BF16)
    prepared = [
        shape_of((head_dim, pairs)),
        shape_of((tiles, pairs), F32),
        shape_of((1, head_dim), F32),
    ]
    query_scratch = [
        pltpu.VMEM(queries.shape, BF16),
        pltpu.VMEM((1, head_dim), F32),
        pltpu.VMEM((tiles, tokens), jnp.int32),
    ]
    others = [swap(kv_weight, "dp", k) for k in range(1, n_dp)]
    if n_dp == 2 and own_heads == 1:
        away = call(
            functools.partial(away_kernel, head_dim),
            product,
            2,
            "away_own",
            flops=work,
            in_specs=[HBM] * 2,
            scratch=[x_scratch, w_scratch, pltpu.SemaphoreType.DMA((2,))],
        )(x, w)
        first = permute_two_heads(away, across, next_core)
        x_home = call(
            load_kernel,
            shape_of(images.shape),
            2,
            "home_rows",
            in_specs=[VMEM, HBM],
            scratch=[pltpu.SemaphoreType.DMA((1,))],
        )(away, x)
        home = call(
            functools.partial(home_kernel, head_dim), product, 2, "home_other", flops=work
        )(x_home, others[0])
        second = permute_two_heads(home, next_core, across)
        keep, qt, bias, gain = call(
            functools.partial(keep_kernel, head_dim),
            [product, *prepared],
            8,
            "keep_queries",
            flops=work,
            in_specs=[VMEM] * 2 + [HBM] * 6,
            scratch=[x_scratch, w_scratch, *query_scratch, pltpu.SemaphoreType.DMA((6,))],
        )(home, others[0], x, w, *small)
        first_sum = call(first_sum_kernel, product, 2, "first_sum")(keep, first)
        arrived = [permute_two_heads(first_sum, itself, next_tensor)]
        total = call(second_sum_kernel, product, 3, "second_sum")(first_sum, keep, second)
        arrived.append(permute_two_heads(total, next_tensor, itself))
    else:
        own, x_here = call(
            functools.partial(own_kernel, head_dim),
            [product, shape_of(images.shape)],
            2,
            "own_heads",
            flops=work,
            in_specs=[HBM] * 2,
            scratch=[w_scratch, pltpu.SemaphoreType.DMA((2,))],
        )(x, w)
        qt, bias, gain = call(
            query_kernel,
            prepared,
            4,
            "queries",
            in_specs=[HBM] * 4,
            scratch=[*query_scratch, pltpu.SemaphoreType.DMA((4,))],
        )(*small)
        rest = [
            call(functools.partial(other_kernel, head_dim), product, 2, "other_heads", flops=work)(
                x_here, other
            )
            for other in others
        ]
        total = sum_many_heads(own, rest)
        arrived = [swap(total, "tensor", 1)]
    far = [step for step in range(1, n_section) if step & (step - 1)]
    near = [step for step in range(1, n_section) if not step & (step - 1)]
    halves = [swap(total, "section", step) for step in far]
    kv = call(norm_kernel, shape_of((2, rows, head_dim)), 2 + len(arrived), "sum_norm")(
        gain, total, *arrived
    )
    finished = [swap(kv, "section", step) for step in near]
    both = []
    for value in halves:
        both += [value, swap(value, "tensor", 1)]
    state = []
    for here, there, operands in (
        ([0], [], [kv]),
        (near, [], finished),
        ([], far, both),
    ):
        first, last = here == [0], len(there) > 0
        outs = (
            shape_of((tokens, q_width))
            if last
            else [shape_of((1, pairs), F32), shape_of((1, pairs), F32), shape_of((head_dim, pairs), F32)]
        )
        parts = len(here) + len(there)
        state = call(
            functools.partial(attend_kernel, here, there, tile_len, first, last, head_dim),
            outs,
            3 + len(operands) + len(state),
            "attend",
            flops=4 * pairs * rows * head_dim * parts,
            exps=pairs * rows * parts,
        )(gain, qt, bias, *operands, *state)
    return state


def solution(mesh):
    in_specs = (
        P(("section", "dp"), "tensor"),
        P("dp", "section", "tensor"),
        P(None, "tensor", "dp"),
        P(),
        P(),
        P(("section", "dp"), None),
    )
    out_specs = P(("section", "dp"), "tensor")
    return jax.shard_map(
        on_device, mesh=mesh, in_specs=in_specs, out_specs=out_specs, check_vma=False
    )
```

```python
import functools

import jax
import jax.numpy as jnp
from jax import lax
from jax.experimental import pallas as pl
from jax.experimental.pallas import tpu as pltpu
from jax.sharding import PartitionSpec as P

EPSILON = 1e-05
MASKED_SCORE = -1e30
TOP_FLOOR = -1e29
VMEM = pl.BlockSpec(memory_space=pltpu.VMEM)
HBM = pl.BlockSpec(memory_space=pltpu.HBM)
F32 = jnp.float32
MIB = 1024 * 1024
LIMIT = 24 * MIB
BF16 = jnp.bfloat16


def shape_of(dims, dtype=BF16):
    return jax.ShapeDtypeStruct(dims, dtype)


def call(
    kernel, outs, n_in, name, flops=0, size=0, exps=0, in_specs=None, scratch=(), aliases=None
):
    many = isinstance(outs, list)
    return pl.pallas_call(
        kernel,
        out_shape=outs,
        in_specs=in_specs or [VMEM] * n_in,
        out_specs=[VMEM] * len(outs) if many else VMEM,
        scratch_shapes=scratch,
        input_output_aliases=aliases or {},
        compiler_params=pltpu.CompilerParams(vmem_limit_bytes=LIMIT),
        cost_estimate=pl.CostEstimate(flops=flops, bytes_accessed=size, transcendentals=exps),
        name=name,
    )


def normalize(values, gain_vec):
    mean_sq = jnp.mean(values * values, axis=-1, keepdims=True)
    return values * lax.rsqrt(mean_sq + EPSILON) * gain_vec


def project(x, w):
    return jnp.dot(
        x, jnp.concatenate([w[0], w[1]], axis=1), preferred_element_type=F32
    ).astype(BF16)


def store_heads(ref, base, both, head_dim):
    width = both.shape[1] // 2
    for head in range(width // head_dim):
        lo = head * head_dim
        ref[base + head, 0] = both[:, lo : lo + head_dim]
        ref[base + head, 1] = both[:, width + lo : width + lo + head_dim]


def prepare_queries(copies, q_ref, q_gain_ref, mask_ref, qt_ref, bias_ref):
    for copy in copies:
        copy.wait()
    tokens = q_ref.shape[0]
    head_dim = q_gain_ref.shape[1]
    bias = jnp.where(mask_ref[...] > 0, 0.0, MASKED_SCORE).astype(F32)
    for head in range(q_ref.shape[1] // head_dim):
        rows = q_ref[:, head * head_dim : (head + 1) * head_dim].astype(F32)
        normed = normalize(rows, q_gain_ref[...]) * head_dim ** (-0.5)
        qt_ref[:, head * tokens : (head + 1) * tokens] = normed.T.astype(BF16)
        bias_ref[:, head * tokens : (head + 1) * tokens] = bias


def start_copies(sources, targets, sems):
    copies = [
        pltpu.make_async_copy(a, b, sems.at[i]) for i, (a, b) in enumerate(zip(sources, targets))
    ]
    for copy in copies:
        copy.start()
    return copies


def own_kernel(head_dim, x_hbm, w_hbm, own_ref, x_ref, w_ref, sems):
    for copy in start_copies((x_hbm, w_hbm), (x_ref, w_ref), sems):
        copy.wait()
    store_heads(own_ref, 0, project(x_ref[0], w_ref[...]), head_dim)


def other_kernel(head_dim, x_ref, w_ref, other_ref):
    store_heads(other_ref, 0, project(x_ref[0], w_ref[...]), head_dim)


def query_kernel(
    q_hbm, q_gain_hbm, mask_hbm, k_gain_hbm, qt_ref, bias_ref, k_gain_ref,
    q_ref, q_gain_ref, mask_ref, sems,
):
    copies = start_copies(
        (q_hbm, q_gain_hbm, mask_hbm, k_gain_hbm), (q_ref, q_gain_ref, mask_ref, k_gain_ref), sems
    )
    prepare_queries(copies, q_ref, q_gain_ref, mask_ref, qt_ref, bias_ref)


def is_home():
    return lax.axis_index("tensor") // 2 == lax.axis_index("dp")


def away_kernel(head_dim, x_hbm, w_hbm, own_ref, x_ref, w_ref, sems):
    @pl.when(is_home())
    def _():
        own_ref[...] = jnp.zeros_like(own_ref)

    @pl.when(jnp.logical_not(is_home()))
    def _():
        own_kernel(head_dim, x_hbm, w_hbm, own_ref, x_ref, w_ref, sems)


def load_kernel(x_in, x_hbm, w_hbm, x_ref, w_ref, sems):
    @pl.when(is_home())
    def _():
        for copy in start_copies((x_hbm, w_hbm), (x_ref, w_ref), sems):
            copy.wait()


def home_kernel(head_dim, x_ref, w_other_ref, other_ref):
    @pl.when(is_home())
    def _():
        store_heads(other_ref, 0, project(x_ref[0], w_other_ref[...]), head_dim)

    @pl.when(jnp.logical_not(is_home()))
    def _():
        other_ref[...] = jnp.zeros_like(other_ref)


def keep_kernel(
    head_dim, after_ref, w_other_ref, x_ref, w_ref, q_hbm, q_gain_hbm, mask_hbm, k_gain_hbm,
    keep_ref, qt_ref, bias_ref, k_gain_ref, q_ref, q_gain_ref, mask_ref, sems,
):
    copies = start_copies(
        (q_hbm, q_gain_hbm, mask_hbm, k_gain_hbm), (q_ref, q_gain_ref, mask_ref, k_gain_ref), sems
    )

    @pl.when(is_home())
    def _():
        store_heads(keep_ref, 0, project(x_ref[0], w_ref[...]), head_dim)

    @pl.when(jnp.logical_not(is_home()))
    def _():
        store_heads(keep_ref, 0, project(x_ref[0], w_other_ref[...]), head_dim)

    prepare_queries(copies, q_ref, q_gain_ref, mask_ref, qt_ref, bias_ref)


def split_half(held, send_ref, keep_ref, partner_heads, own_heads):
    for i in range(send_ref.shape[0]):
        send_ref[i] = held[partner_heads + i]
        keep_ref[i] = held[own_heads + i]


def spread_kernel(n_dp, n_tensor, own_ref, *refs):
    others, (send_ref, keep_ref, held) = refs[: n_dp - 1], refs[n_dp - 1 :]
    d = lax.axis_index("dp")
    own_heads = own_ref.shape[0]
    for k, ref in enumerate((own_ref, *others)):
        held[pl.ds((d ^ k) * own_heads, own_heads)] = ref[...]
    half = send_ref.shape[0]
    upper = lax.axis_index("tensor") // (n_tensor // 2)
    split_half(held, send_ref, keep_ref, (1 - upper) * half, upper * half)


def pair_kernel(keep_ref, first_ref, second_ref, out_ref):
    arrived = jnp.where(is_home(), first_ref[...], second_ref[...]).astype(F32)
    out_ref[...] = (keep_ref[...].astype(F32) + arrived).astype(BF16)


def add_kernel(bit, keep_ref, arrived_ref, send_ref, next_ref, held):
    held[...] = (keep_ref[...].astype(F32) + arrived_ref[...].astype(F32)).astype(BF16)
    half = send_ref.shape[0]
    upper = (lax.axis_index("tensor") // bit) % 2
    split_half(held, send_ref, next_ref, (1 - upper) * half, upper * half)


def add_last_kernel(keep_ref, arrived_ref, out_ref):
    out_ref[...] = (keep_ref[...].astype(F32) + arrived_ref[...].astype(F32)).astype(BF16)


def finish_rows(k_gain, one, two):
    keys = one[0].astype(F32) + two[0].astype(F32)
    values = one[1].astype(F32) + two[1].astype(F32)
    return normalize(keys, k_gain).astype(BF16), values.astype(BF16)


def norm_kernel(k_gain_ref, keep_ref, arrived_ref, kv_ref):
    kv_ref[0], kv_ref[1] = finish_rows(k_gain_ref[...], keep_ref.at[0], arrived_ref.at[0])


def attend_kernel(near, far, tile_len, first, last, head_dim, k_gain_ref, qt_ref, bias_ref, *refs):
    near_refs, refs = refs[: len(near)], refs[len(near) :]
    far_refs, refs = refs[: 2 * len(far)], refs[2 * len(far) :]
    if not first:
        top_in, sum_in, mixed_in = refs[:3]
        refs = refs[3:]
    s = lax.axis_index("section")
    qt = qt_ref[...]
    parts = [(part[0], part[1]) for part in near_refs]
    for one, two in zip(far_refs[::2], far_refs[1::2]):
        parts.append(finish_rows(k_gain_ref[...], one.at[0], two.at[0]))
    rows = parts[0][0].shape[0]
    scores, biases = [], []
    top = TOP_FLOOR if first else top_in[...]
    for step, (keys, _) in zip((*near, *far), parts):
        score = jnp.dot(keys, qt, preferred_element_type=F32)
        bias = bias_ref[pl.ds(((s ^ step) * rows) // tile_len, 1), :]
        scores.append(score)
        biases.append(bias)
        top = jnp.maximum(top, jnp.max(score, axis=0, keepdims=True) + bias)
    row_sum, mixed = 0.0, 0.0
    if not first:
        scale = jnp.exp(top_in[...] - top)
        row_sum = sum_in[...] * scale
        mixed = mixed_in[...] * scale
    for (_, values), score, bias in zip(parts, scores, biases):
        weights = jnp.exp(score + (bias - top))
        row_sum = row_sum + jnp.sum(weights, axis=0, keepdims=True)
        mixed = mixed + lax.dot_general(
            values, weights.astype(BF16), (((0,), (0,)), ((), ())), preferred_element_type=F32
        )
    if not last:
        top_out, sum_out, mixed_out = refs
        top_out[...] = top
        sum_out[...] = row_sum
        mixed_out[...] = mixed
        return
    (out,) = refs
    has_any = jnp.max(bias_ref[...], axis=0, keepdims=True) > -1.0
    inverse = jnp.where(has_any, 1.0 / jnp.where(has_any, row_sum, 1.0), 0.0)
    context = (mixed * inverse).astype(BF16)
    tokens = out.shape[0]
    for head in range(out.shape[1] // head_dim):
        out[:, head * head_dim : (head + 1) * head_dim] = context[
            :, head * tokens : (head + 1) * tokens
        ].T


def swap(value, axis, k):
    return lax.ppermute(value, axis, [(i, i ^ k) for i in range(lax.axis_size(axis))])


def exchange_two_heads(value, home_sends):
    hops = []
    for d in range(2):
        for t in range(4):
            sends = (t // 2 == d) == home_sends
            hops.append((4 * d + t, 4 * d + (t ^ 2) if sends else 4 * (1 - d) + t))
    return lax.ppermute(value, ("dp", "tensor"), hops)


def sum_many_heads(own, others):
    n_dp, n_tensor = lax.axis_size("dp"), lax.axis_size("tensor")
    heads = own.shape[0] * n_dp
    half = shape_of((heads // 2, *own.shape[1:]))
    send, keep = call(
        functools.partial(spread_kernel, n_dp, n_tensor),
        [half, half],
        n_dp,
        "spread",
        scratch=[pltpu.VMEM((heads, *own.shape[1:]), BF16)],
    )(own, *others)
    bit = n_tensor // 2
    while bit > 1:
        arrived = swap(send, "tensor", bit)
        bit //= 2
        now = keep.shape
        if bit > 1:
            half = shape_of((now[0] // 2, *now[1:]))
            send, keep = call(
                functools.partial(add_kernel, bit),
                [half, half],
                2,
                "add_part",
                scratch=[pltpu.VMEM(now, BF16)],
            )(keep, arrived)
        else:
            keep = call(add_last_kernel, shape_of(now), 2, "add_pair")(keep, arrived)
    return keep


def on_device(queries, images, kv_weight, q_gain, k_gain, tile_mask):
    n_section = lax.axis_size("section")
    n_dp = lax.axis_size("dp")
    n_tensor = lax.axis_size("tensor")
    head_dim = q_gain.shape[0]
    tokens, q_width = queries.shape
    rows, features = images.shape[1:]
    tiles = tile_mask.shape[1]
    own_heads = kv_weight.shape[2] // head_dim
    heads = own_heads * n_dp
    tile_len = rows * n_section // tiles
    assert heads * 2 == n_tensor and tile_len % rows == 0 and n_section >= 4
    pairs = tokens * (q_width // head_dim)
    work = 4 * rows * features * kv_weight.shape[2]

    x, w, *small = [
        pltpu.with_memory_space_constraint(value, pltpu.HBM)
        for value in (
            images, kv_weight, queries, q_gain.reshape(1, -1), tile_mask.T, k_gain.reshape(1, -1),
        )
    ]
    product = shape_of((own_heads, 2, rows, head_dim))
    w_scratch = pltpu.VMEM(kv_weight.shape, BF16)
    prepared = [
        shape_of((head_dim, pairs)),
        shape_of((tiles, pairs), F32),
        shape_of((1, head_dim), F32),
    ]
    query_scratch = [
        pltpu.VMEM(queries.shape, BF16),
        pltpu.VMEM((1, head_dim), F32),
        pltpu.VMEM((tiles, tokens), jnp.int32),
    ]
    others = [swap(kv_weight, "dp", k) for k in range(1, n_dp)]
    if n_dp == 2 and own_heads == 1:
        away, x_away = call(
            functools.partial(away_kernel, head_dim),
            [product, shape_of(images.shape)],
            2,
            "away_own",
            flops=work,
            in_specs=[HBM] * 2,
            scratch=[w_scratch, pltpu.SemaphoreType.DMA((2,))],
        )(x, w)
        first = exchange_two_heads(away, False)
        x_here, w_home = call(
            load_kernel,
            [shape_of(images.shape), shape_of(kv_weight.shape)],
            3,
            "home_load",
            in_specs=[VMEM] + [HBM] * 2,
            scratch=[pltpu.SemaphoreType.DMA((2,))],
            aliases={0: 0},
        )(x_away, x, w)
        home = call(
            functools.partial(home_kernel, head_dim), product, 2, "home_other", flops=work
        )(x_here, others[0])
        second = exchange_two_heads(home, True)
        keep, qt, bias, gain = call(
            functools.partial(keep_kernel, head_dim),
            [product, *prepared],
            8,
            "keep_queries",
            flops=work,
            in_specs=[VMEM] * 4 + [HBM] * 4,
            scratch=[*query_scratch, pltpu.SemaphoreType.DMA((4,))],
        )(home, others[0], x_here, w_home, *small)
        total = call(pair_kernel, product, 3, "pair_sum")(keep, first, second)
    else:
        own, x_here = call(
            functools.partial(own_kernel, head_dim),
            [product, shape_of(images.shape)],
            2,
            "own_heads",
            flops=work,
            in_specs=[HBM] * 2,
            scratch=[w_scratch, pltpu.SemaphoreType.DMA((2,))],
        )(x, w)
        qt, bias, gain = call(
            query_kernel,
            prepared,
            4,
            "queries",
            in_specs=[HBM] * 4,
            scratch=[*query_scratch, pltpu.SemaphoreType.DMA((4,))],
        )(*small)
        rest = [
            call(functools.partial(other_kernel, head_dim), product, 2, "other_heads", flops=work)(
                x_here, other
            )
            for other in others
        ]
        total = sum_many_heads(own, rest)
    far = [step for step in range(1, n_section) if step & (step - 1)]
    near = [step for step in range(1, n_section) if not step & (step - 1)]
    arrived = swap(total, "tensor", 1)
    halves = [swap(total, "section", step) for step in far]
    kv = call(norm_kernel, shape_of((2, rows, head_dim)), 3, "sum_norm")(gain, total, arrived)
    finished = [swap(kv, "section", step) for step in near]
    both = []
    for value in halves:
        both += [value, swap(value, "tensor", 1)]
    state = []
    for here, there, operands in (
        ([0], [], [kv]),
        (near, [], finished),
        ([], far, both),
    ):
        first, last = here == [0], len(there) > 0
        outs = (
            shape_of((tokens, q_width))
            if last
            else [shape_of((1, pairs), F32), shape_of((1, pairs), F32), shape_of((head_dim, pairs), F32)]
        )
        parts = len(here) + len(there)
        state = call(
            functools.partial(attend_kernel, here, there, tile_len, first, last, head_dim),
            outs,
            3 + len(operands) + len(state),
            "attend",
            flops=4 * pairs * rows * head_dim * parts,
            exps=pairs * rows * parts,
        )(gain, qt, bias, *operands, *state)
    return state


def solution(mesh):
    in_specs = (
        P(("section", "dp"), "tensor"),
        P("dp", "section", "tensor"),
        P(None, "tensor", "dp"),
        P(),
        P(),
        P(("section", "dp"), None),
    )
    out_specs = P(("section", "dp"), "tensor")
    return jax.shard_map(
        on_device, mesh=mesh, in_specs=in_specs, out_specs=out_specs, check_vma=False
    )
```

```python
import functools

import jax
import jax.numpy as jnp
from jax import lax
from jax.experimental import pallas as pl
from jax.experimental.pallas import tpu as pltpu
from jax.sharding import PartitionSpec as P

EPSILON = 1e-05
MASKED_SCORE = -1e30
TOP_FLOOR = -1e29
VMEM = pl.BlockSpec(memory_space=pltpu.VMEM)
HBM = pl.BlockSpec(memory_space=pltpu.HBM)
F32 = jnp.float32
MIB = 1024 * 1024
LIMIT = 24 * MIB
BF16 = jnp.bfloat16


def shape_of(dims, dtype=BF16):
    return jax.ShapeDtypeStruct(dims, dtype)


def call(
    kernel, outs, n_in, name, flops=0, size=0, exps=0, in_specs=None, scratch=()
):
    many = isinstance(outs, list)
    return pl.pallas_call(
        kernel,
        out_shape=outs,
        in_specs=in_specs or [VMEM] * n_in,
        out_specs=[VMEM] * len(outs) if many else VMEM,
        scratch_shapes=scratch,
        compiler_params=pltpu.CompilerParams(vmem_limit_bytes=LIMIT),
        cost_estimate=pl.CostEstimate(flops=flops, bytes_accessed=size, transcendentals=exps),
        name=name,
    )


def normalize(values, gain_vec):
    mean_sq = jnp.mean(values * values, axis=-1, keepdims=True)
    return values * lax.rsqrt(mean_sq + EPSILON) * gain_vec


def project(x, w):
    return jnp.dot(
        x, jnp.concatenate([w[0], w[1]], axis=1), preferred_element_type=F32
    ).astype(BF16)


def store_heads(ref, base, both, head_dim):
    width = both.shape[1] // 2
    for head in range(width // head_dim):
        lo = head * head_dim
        ref[base + head, 0] = both[:, lo : lo + head_dim]
        ref[base + head, 1] = both[:, width + lo : width + lo + head_dim]


def prepare_queries(copies, q_ref, q_gain_ref, mask_ref, qt_ref, bias_ref):
    for copy in copies:
        copy.wait()
    tokens = q_ref.shape[0]
    head_dim = q_gain_ref.shape[1]
    bias = jnp.where(mask_ref[...] > 0, 0.0, MASKED_SCORE).astype(F32)
    for head in range(q_ref.shape[1] // head_dim):
        rows = q_ref[:, head * head_dim : (head + 1) * head_dim].astype(F32)
        normed = normalize(rows, q_gain_ref[...]) * head_dim ** (-0.5)
        qt_ref[:, head * tokens : (head + 1) * tokens] = normed.T.astype(BF16)
        bias_ref[:, head * tokens : (head + 1) * tokens] = bias


def start_copies(sources, targets, sems, first=0):
    copies = [
        pltpu.make_async_copy(a, b, sems.at[first + i]) for i, (a, b) in enumerate(zip(sources, targets))
    ]
    for copy in copies:
        copy.start()
    return copies


def own_kernel(head_dim, x_hbm, w_hbm, own_ref, x_ref, w_ref, sems):
    for copy in start_copies((x_hbm, w_hbm), (x_ref, w_ref), sems):
        copy.wait()
    store_heads(own_ref, 0, project(x_ref[0], w_ref[...]), head_dim)


def other_kernel(head_dim, x_ref, w_ref, other_ref):
    store_heads(other_ref, 0, project(x_ref[0], w_ref[...]), head_dim)


def query_kernel(
    q_hbm, q_gain_hbm, mask_hbm, k_gain_hbm, qt_ref, bias_ref, k_gain_ref,
    q_ref, q_gain_ref, mask_ref, sems,
):
    copies = start_copies(
        (q_hbm, q_gain_hbm, mask_hbm, k_gain_hbm), (q_ref, q_gain_ref, mask_ref, k_gain_ref), sems
    )
    prepare_queries(copies, q_ref, q_gain_ref, mask_ref, qt_ref, bias_ref)


def is_home():
    return lax.axis_index("tensor") // 2 == lax.axis_index("dp")


def away_kernel(head_dim, x_hbm, w_hbm, own_ref, x_ref, w_ref, sems):
    @pl.when(is_home())
    def _():
        own_ref[...] = jnp.zeros_like(own_ref)

    @pl.when(jnp.logical_not(is_home()))
    def _():
        own_kernel(head_dim, x_hbm, w_hbm, own_ref, x_ref, w_ref, sems)


def load_kernel(after_ref, x_hbm, x_ref, sems):
    @pl.when(is_home())
    def _():
        for copy in start_copies((x_hbm,), (x_ref,), sems):
            copy.wait()


def home_kernel(head_dim, x_ref, w_other_ref, other_ref):
    @pl.when(is_home())
    def _():
        store_heads(other_ref, 0, project(x_ref[0], w_other_ref[...]), head_dim)

    @pl.when(jnp.logical_not(is_home()))
    def _():
        other_ref[...] = jnp.zeros_like(other_ref)


def keep_kernel(
    head_dim, after_ref, w_other_ref, x_hbm, w_hbm, q_hbm, q_gain_hbm, mask_hbm, k_gain_hbm,
    keep_ref, qt_ref, bias_ref, k_gain_ref, x_ref, w_ref, q_ref, q_gain_ref, mask_ref, sems,
):
    copies = start_copies(
        (q_hbm, q_gain_hbm, mask_hbm, k_gain_hbm), (q_ref, q_gain_ref, mask_ref, k_gain_ref), sems
    )
    moves = start_copies((x_hbm, w_hbm), (x_ref, w_ref), sems, len(copies))
    prepare_queries(copies, q_ref, q_gain_ref, mask_ref, qt_ref, bias_ref)
    for copy in moves:
        copy.wait()

    @pl.when(is_home())
    def _():
        store_heads(keep_ref, 0, project(x_ref[0], w_ref[...]), head_dim)

    @pl.when(jnp.logical_not(is_home()))
    def _():
        store_heads(keep_ref, 0, project(x_ref[0], w_other_ref[...]), head_dim)


def split_half(held, send_ref, keep_ref, partner_heads, own_heads):
    for i in range(send_ref.shape[0]):
        send_ref[i] = held[partner_heads + i]
        keep_ref[i] = held[own_heads + i]


def spread_kernel(n_dp, n_tensor, own_ref, *refs):
    others, (send_ref, keep_ref, held) = refs[: n_dp - 1], refs[n_dp - 1 :]
    d = lax.axis_index("dp")
    own_heads = own_ref.shape[0]
    for k, ref in enumerate((own_ref, *others)):
        held[pl.ds((d ^ k) * own_heads, own_heads)] = ref[...]
    half = send_ref.shape[0]
    upper = lax.axis_index("tensor") // (n_tensor // 2)
    split_half(held, send_ref, keep_ref, (1 - upper) * half, upper * half)


def pair_kernel(keep_ref, first_ref, second_ref, out_ref):
    arrived = jnp.where(is_home(), first_ref[...], second_ref[...]).astype(F32)
    out_ref[...] = (keep_ref[...].astype(F32) + arrived).astype(BF16)


def add_kernel(bit, keep_ref, arrived_ref, send_ref, next_ref, held):
    held[...] = (keep_ref[...].astype(F32) + arrived_ref[...].astype(F32)).astype(BF16)
    half = send_ref.shape[0]
    upper = (lax.axis_index("tensor") // bit) % 2
    split_half(held, send_ref, next_ref, (1 - upper) * half, upper * half)


def add_last_kernel(keep_ref, arrived_ref, out_ref):
    out_ref[...] = (keep_ref[...].astype(F32) + arrived_ref[...].astype(F32)).astype(BF16)


def finish_rows(k_gain, one, two):
    keys = one[0].astype(F32) + two[0].astype(F32)
    values = one[1].astype(F32) + two[1].astype(F32)
    return normalize(keys, k_gain).astype(BF16), values.astype(BF16)


def norm_kernel(k_gain_ref, keep_ref, arrived_ref, kv_ref):
    kv_ref[0], kv_ref[1] = finish_rows(k_gain_ref[...], keep_ref.at[0], arrived_ref.at[0])


def part_kernel(half_ref, keys_ref, values_ref):
    keys_ref[...] = half_ref[0, 0]
    values_ref[...] = half_ref[0, 1]


def score_sections(steps, tile_len, keys_of, top, qt_ref, bias_ref):
    s = lax.axis_index("section")
    qt = qt_ref[...]
    scores = []
    for step, keys in zip(steps, keys_of):
        score = jnp.dot(keys, qt, preferred_element_type=F32)
        bias = bias_ref[pl.ds(((s ^ step) * keys.shape[0]) // tile_len, 1), :]
        scores.append((score, bias))
        top = jnp.maximum(top, jnp.max(score, axis=0, keepdims=True) + bias)
    weights = [jnp.exp(score + (bias - top)) for score, bias in scores]
    return top, weights


def mix(values, weights):
    return lax.dot_general(values, weights, (((0,), (0,)), ((), ())), preferred_element_type=F32)


def attend_kernel(steps, tile_len, first, qt_ref, bias_ref, *refs):
    parts, refs = refs[: len(steps)], refs[len(steps) :]
    if not first:
        top_in, sum_in, mixed_in = refs[:3]
        refs = refs[3:]
    top_out, sum_out, mixed_out = refs
    start = TOP_FLOOR if first else top_in[...]
    top, all_weights = score_sections(steps, tile_len, [part[0] for part in parts], start, qt_ref, bias_ref)
    row_sum, mixed = 0.0, 0.0
    if not first:
        scale = jnp.exp(top_in[...] - top)
        row_sum = sum_in[...] * scale
        mixed = mixed_in[...] * scale
    for part, weights in zip(parts, all_weights):
        row_sum = row_sum + jnp.sum(weights, axis=0, keepdims=True)
        mixed = mixed + mix(part[1], weights.astype(BF16))
    top_out[...] = top
    sum_out[...] = row_sum
    mixed_out[...] = mixed


def weigh_kernel(steps, tile_len, k_gain_ref, qt_ref, bias_ref, top_in, sum_in, mixed_in, *refs):
    halves, (weights_out, inverse_out, mixed_out) = refs[:-3], refs[-3:]
    keys_of = [
        normalize(one[...].astype(F32) + two[...].astype(F32), k_gain_ref[...]).astype(BF16)
        for one, two in zip(halves[::2], halves[1::2])
    ]
    top, all_weights = score_sections(steps, tile_len, keys_of, top_in[...], qt_ref, bias_ref)
    scale = jnp.exp(top_in[...] - top)
    row_sum = sum_in[...] * scale
    for i, weights in enumerate(all_weights):
        row_sum = row_sum + jnp.sum(weights, axis=0, keepdims=True)
        weights_out[i] = weights.astype(BF16)
    has_any = jnp.max(bias_ref[...], axis=0, keepdims=True) > -1.0
    inverse_out[...] = jnp.where(has_any, 1.0 / jnp.where(has_any, row_sum, 1.0), 0.0)
    mixed_out[...] = mixed_in[...] * scale


def finish_kernel(weights_ref, inverse_ref, mixed_ref, *refs):
    halves, out = refs[:-1], refs[-1]
    mixed = mixed_ref[...]
    for i, (one, two) in enumerate(zip(halves[::2], halves[1::2])):
        values = (one[...].astype(F32) + two[...].astype(F32)).astype(BF16)
        mixed = mixed + mix(values, weights_ref[i])
    context = (mixed * inverse_ref[...]).astype(BF16)
    tokens, head_dim = out.shape[0], mixed.shape[0]
    for head in range(out.shape[1] // head_dim):
        out[:, head * head_dim : (head + 1) * head_dim] = context[
            :, head * tokens : (head + 1) * tokens
        ].T


def swap(value, axis, k):
    return lax.ppermute(value, axis, [(i, i ^ k) for i in range(lax.axis_size(axis))])


def exchange_two_heads(value, home_sends):
    hops = []
    for d in range(2):
        for t in range(4):
            sends = (t // 2 == d) == home_sends
            hops.append((4 * d + t, 4 * d + (t ^ 2) if sends else 4 * (1 - d) + t))
    return lax.ppermute(value, ("dp", "tensor"), hops)


def sum_many_heads(own, others):
    n_dp, n_tensor = lax.axis_size("dp"), lax.axis_size("tensor")
    heads = own.shape[0] * n_dp
    half = shape_of((heads // 2, *own.shape[1:]))
    send, keep = call(
        functools.partial(spread_kernel, n_dp, n_tensor),
        [half, half],
        n_dp,
        "spread",
        scratch=[pltpu.VMEM((heads, *own.shape[1:]), BF16)],
    )(own, *others)
    bit = n_tensor // 2
    while bit > 1:
        arrived = swap(send, "tensor", bit)
        bit //= 2
        now = keep.shape
        if bit > 1:
            half = shape_of((now[0] // 2, *now[1:]))
            send, keep = call(
                functools.partial(add_kernel, bit),
                [half, half],
                2,
                "add_part",
                scratch=[pltpu.VMEM(now, BF16)],
            )(keep, arrived)
        else:
            keep = call(add_last_kernel, shape_of(now), 2, "add_pair")(keep, arrived)
    return keep


def on_device(queries, images, kv_weight, q_gain, k_gain, tile_mask):
    n_section = lax.axis_size("section")
    n_dp = lax.axis_size("dp")
    n_tensor = lax.axis_size("tensor")
    head_dim = q_gain.shape[0]
    tokens, q_width = queries.shape
    rows, features = images.shape[1:]
    tiles = tile_mask.shape[1]
    own_heads = kv_weight.shape[2] // head_dim
    heads = own_heads * n_dp
    tile_len = rows * n_section // tiles
    assert heads * 2 == n_tensor and tile_len % rows == 0 and n_section >= 4
    pairs = tokens * (q_width // head_dim)
    work = 4 * rows * features * kv_weight.shape[2]

    x, w, *small = [
        pltpu.with_memory_space_constraint(value, pltpu.HBM)
        for value in (
            images, kv_weight, queries, q_gain.reshape(1, -1), tile_mask.T, k_gain.reshape(1, -1),
        )
    ]
    product = shape_of((own_heads, 2, rows, head_dim))
    x_scratch, w_scratch = pltpu.VMEM(images.shape, BF16), pltpu.VMEM(kv_weight.shape, BF16)
    prepared = [
        shape_of((head_dim, pairs)),
        shape_of((tiles, pairs), F32),
        shape_of((1, head_dim), F32),
    ]
    query_scratch = [
        pltpu.VMEM(queries.shape, BF16),
        pltpu.VMEM((1, head_dim), F32),
        pltpu.VMEM((tiles, tokens), jnp.int32),
    ]
    others = [swap(kv_weight, "dp", k) for k in range(1, n_dp)]
    if n_dp == 2 and own_heads == 1:
        away = call(
            functools.partial(away_kernel, head_dim),
            product,
            2,
            "away_own",
            flops=work,
            in_specs=[HBM] * 2,
            scratch=[x_scratch, w_scratch, pltpu.SemaphoreType.DMA((2,))],
        )(x, w)
        first = exchange_two_heads(away, False)
        x_home = call(
            load_kernel,
            shape_of(images.shape),
            2,
            "home_rows",
            in_specs=[VMEM, HBM],
            scratch=[pltpu.SemaphoreType.DMA((1,))],
        )(away, x)
        home = call(
            functools.partial(home_kernel, head_dim), product, 2, "home_other", flops=work
        )(x_home, others[0])
        second = exchange_two_heads(home, True)
        keep, qt, bias, gain = call(
            functools.partial(keep_kernel, head_dim),
            [product, *prepared],
            8,
            "keep_queries",
            flops=work,
            in_specs=[VMEM] * 2 + [HBM] * 6,
            scratch=[x_scratch, w_scratch, *query_scratch, pltpu.SemaphoreType.DMA((6,))],
        )(home, others[0], x, w, *small)
        total = call(pair_kernel, product, 3, "pair_sum")(keep, first, second)
    else:
        own, x_here = call(
            functools.partial(own_kernel, head_dim),
            [product, shape_of(images.shape)],
            2,
            "own_heads",
            flops=work,
            in_specs=[HBM] * 2,
            scratch=[w_scratch, pltpu.SemaphoreType.DMA((2,))],
        )(x, w)
        qt, bias, gain = call(
            query_kernel,
            prepared,
            4,
            "queries",
            in_specs=[HBM] * 4,
            scratch=[*query_scratch, pltpu.SemaphoreType.DMA((4,))],
        )(*small)
        rest = [
            call(functools.partial(other_kernel, head_dim), product, 2, "other_heads", flops=work)(
                x_here, other
            )
            for other in others
        ]
        total = sum_many_heads(own, rest)
    far = [step for step in range(1, n_section) if step & (step - 1)]
    near = [step for step in range(1, n_section) if not step & (step - 1)]
    arrived = swap(total, "tensor", 1)
    halves = [swap(total, "section", step) for step in far]
    kv = call(norm_kernel, shape_of((2, rows, head_dim)), 3, "sum_norm")(gain, total, arrived)
    finished = [swap(kv, "section", step) for step in near]
    row = shape_of((rows, head_dim))
    key_halves, value_halves = [], []
    for value in halves:
        keys, values = call(part_kernel, [row, row], 1, "part")(value)
        key_halves += [keys, swap(keys, "tensor", 1)]
        value_halves += [values, swap(values, "tensor", 1)]
    line, block = shape_of((1, pairs), F32), shape_of((head_dim, pairs), F32)
    state = []
    for steps, operands in (([0], [kv]), (near, finished)):
        state = call(
            functools.partial(attend_kernel, steps, tile_len, steps == [0]),
            [line, line, block],
            2 + len(operands) + len(state),
            "attend",
            flops=4 * pairs * rows * head_dim * len(steps),
            exps=pairs * rows * len(steps),
        )(qt, bias, *operands, *state)
    weighed = call(
        functools.partial(weigh_kernel, far, tile_len),
        [shape_of((len(far), rows, pairs)), line, block],
        6 + len(key_halves),
        "weigh",
        flops=2 * pairs * rows * head_dim * len(far),
        exps=pairs * rows * len(far),
    )(gain, qt, bias, *state, *key_halves)
    return call(
        finish_kernel,
        shape_of((tokens, q_width)),
        3 + len(value_halves),
        "finish",
        flops=2 * pairs * rows * head_dim * len(far),
    )(*weighed, *value_halves)


def solution(mesh):
    in_specs = (
        P(("section", "dp"), "tensor"),
        P("dp", "section", "tensor"),
        P(None, "tensor", "dp"),
        P(),
        P(),
        P(("section", "dp"), None),
    )
    out_specs = P(("section", "dp"), "tensor")
    return jax.shard_map(
        on_device, mesh=mesh, in_specs=in_specs, out_specs=out_specs, check_vma=False
    )
```

```python
import functools

import jax
import jax.numpy as jnp
from jax import lax
from jax.experimental import pallas as pl
from jax.experimental.pallas import tpu as pltpu
from jax.sharding import PartitionSpec as P

EPSILON = 1e-05
MASKED_SCORE = -1e30
TOP_FLOOR = -1e29
VMEM = pl.BlockSpec(memory_space=pltpu.VMEM)
HBM = pl.BlockSpec(memory_space=pltpu.HBM)
F32 = jnp.float32
MIB = 1024 * 1024
LIMIT = 24 * MIB
BF16 = jnp.bfloat16


def shape_of(dims, dtype=BF16):
    return jax.ShapeDtypeStruct(dims, dtype)


def call(
    kernel, outs, n_in, name, flops=0, size=0, exps=0, in_specs=None, scratch=()
):
    many = isinstance(outs, list)
    return pl.pallas_call(
        kernel,
        out_shape=outs,
        in_specs=in_specs or [VMEM] * n_in,
        out_specs=[VMEM] * len(outs) if many else VMEM,
        scratch_shapes=scratch,
        compiler_params=pltpu.CompilerParams(vmem_limit_bytes=LIMIT),
        cost_estimate=pl.CostEstimate(flops=flops, bytes_accessed=size, transcendentals=exps),
        name=name,
    )


def normalize(values, gain_vec):
    mean_sq = jnp.mean(values * values, axis=-1, keepdims=True)
    return values * lax.rsqrt(mean_sq + EPSILON) * gain_vec


def project(x, w):
    return jnp.dot(
        x, jnp.concatenate([w[0], w[1]], axis=1), preferred_element_type=F32
    ).astype(BF16)


def store_heads(ref, base, both, head_dim):
    width = both.shape[1] // 2
    for head in range(width // head_dim):
        lo = head * head_dim
        ref[base + head, :, :head_dim] = both[:, lo : lo + head_dim]
        ref[base + head, :, head_dim:] = both[:, width + lo : width + lo + head_dim]


def prepare_queries(copies, q_ref, q_gain_ref, mask_ref, qt_ref, bias_ref):
    for copy in copies:
        copy.wait()
    tokens = q_ref.shape[0]
    head_dim = q_gain_ref.shape[1]
    bias = jnp.where(mask_ref[...] > 0, 0.0, MASKED_SCORE).astype(F32)
    for head in range(q_ref.shape[1] // head_dim):
        rows = q_ref[:, head * head_dim : (head + 1) * head_dim].astype(F32)
        normed = normalize(rows, q_gain_ref[...]) * head_dim ** (-0.5)
        qt_ref[:, head * tokens : (head + 1) * tokens] = normed.T.astype(BF16)
        bias_ref[:, head * tokens : (head + 1) * tokens] = bias


def start_copies(sources, targets, sems, first=0):
    copies = [
        pltpu.make_async_copy(a, b, sems.at[first + i]) for i, (a, b) in enumerate(zip(sources, targets))
    ]
    for copy in copies:
        copy.start()
    return copies


def own_kernel(head_dim, x_hbm, w_hbm, own_ref, x_ref, w_ref, sems):
    for copy in start_copies((x_hbm, w_hbm), (x_ref, w_ref), sems):
        copy.wait()
    store_heads(own_ref, 0, project(x_ref[0], w_ref[...]), head_dim)


def other_kernel(head_dim, x_ref, w_ref, other_ref):
    store_heads(other_ref, 0, project(x_ref[0], w_ref[...]), head_dim)


def query_kernel(
    q_hbm, q_gain_hbm, mask_hbm, k_gain_hbm, qt_ref, bias_ref, k_gain_ref,
    q_ref, q_gain_ref, mask_ref, sems,
):
    copies = start_copies(
        (q_hbm, q_gain_hbm, mask_hbm, k_gain_hbm), (q_ref, q_gain_ref, mask_ref, k_gain_ref), sems
    )
    prepare_queries(copies, q_ref, q_gain_ref, mask_ref, qt_ref, bias_ref)


def is_home():
    return lax.axis_index("tensor") // 2 == lax.axis_index("dp")


def away_kernel(head_dim, x_hbm, w_hbm, own_ref, x_ref, w_ref, sems):
    @pl.when(is_home())
    def _():
        own_ref[...] = jnp.zeros_like(own_ref)

    @pl.when(jnp.logical_not(is_home()))
    def _():
        own_kernel(head_dim, x_hbm, w_hbm, own_ref, x_ref, w_ref, sems)


def load_kernel(after_ref, x_hbm, x_ref, sems):
    @pl.when(is_home())
    def _():
        for copy in start_copies((x_hbm,), (x_ref,), sems):
            copy.wait()


def home_kernel(head_dim, x_ref, w_other_ref, other_ref):
    @pl.when(is_home())
    def _():
        store_heads(other_ref, 0, project(x_ref[0], w_other_ref[...]), head_dim)

    @pl.when(jnp.logical_not(is_home()))
    def _():
        other_ref[...] = jnp.zeros_like(other_ref)


def keep_kernel(
    head_dim, after_ref, w_other_ref, x_hbm, w_hbm, q_hbm, q_gain_hbm, mask_hbm, k_gain_hbm,
    keep_ref, qt_ref, bias_ref, k_gain_ref, x_ref, w_ref, q_ref, q_gain_ref, mask_ref, sems,
):
    copies = start_copies(
        (q_hbm, q_gain_hbm, mask_hbm, k_gain_hbm), (q_ref, q_gain_ref, mask_ref, k_gain_ref), sems
    )
    moves = start_copies((x_hbm, w_hbm), (x_ref, w_ref), sems, len(copies))
    prepare_queries(copies, q_ref, q_gain_ref, mask_ref, qt_ref, bias_ref)
    for copy in moves:
        copy.wait()

    @pl.when(is_home())
    def _():
        store_heads(keep_ref, 0, project(x_ref[0], w_ref[...]), head_dim)

    @pl.when(jnp.logical_not(is_home()))
    def _():
        store_heads(keep_ref, 0, project(x_ref[0], w_other_ref[...]), head_dim)


def split_half(held, send_ref, keep_ref, partner_heads, own_heads):
    for i in range(send_ref.shape[0]):
        send_ref[i] = held[partner_heads + i]
        keep_ref[i] = held[own_heads + i]


def spread_kernel(n_dp, n_tensor, own_ref, *refs):
    others, (send_ref, keep_ref, held) = refs[: n_dp - 1], refs[n_dp - 1 :]
    d = lax.axis_index("dp")
    own_heads = own_ref.shape[0]
    for k, ref in enumerate((own_ref, *others)):
        held[pl.ds((d ^ k) * own_heads, own_heads)] = ref[...]
    half = send_ref.shape[0]
    upper = lax.axis_index("tensor") // (n_tensor // 2)
    split_half(held, send_ref, keep_ref, (1 - upper) * half, upper * half)


def pair_kernel(keep_ref, first_ref, second_ref, out_ref):
    arrived = jnp.where(is_home(), first_ref[...], second_ref[...]).astype(F32)
    out_ref[...] = (keep_ref[...].astype(F32) + arrived).astype(BF16)


def add_kernel(bit, keep_ref, arrived_ref, send_ref, next_ref, held):
    held[...] = (keep_ref[...].astype(F32) + arrived_ref[...].astype(F32)).astype(BF16)
    half = send_ref.shape[0]
    upper = (lax.axis_index("tensor") // bit) % 2
    split_half(held, send_ref, next_ref, (1 - upper) * half, upper * half)


def add_last_kernel(keep_ref, arrived_ref, out_ref):
    out_ref[...] = (keep_ref[...].astype(F32) + arrived_ref[...].astype(F32)).astype(BF16)


def finish_rows(k_gain, one, two):
    total = one[...].astype(F32) + two[...].astype(F32)
    head_dim = total.shape[1] // 2
    keys = normalize(total[:, :head_dim], k_gain).astype(BF16)
    return keys, total[:, head_dim:].astype(BF16)


def norm_kernel(k_gain_ref, keep_ref, arrived_ref, kv_ref):
    keys, values = finish_rows(k_gain_ref[...], keep_ref.at[0], arrived_ref.at[0])
    kv_ref[:, : keys.shape[1]] = keys
    kv_ref[:, keys.shape[1] :] = values


def attend_kernel(near, far, tile_len, first, last, head_dim, k_gain_ref, qt_ref, bias_ref, *refs):
    near_refs, refs = refs[: len(near)], refs[len(near) :]
    far_refs, refs = refs[: 2 * len(far)], refs[2 * len(far) :]
    if not first:
        top_in, sum_in, mixed_in = refs[:3]
        refs = refs[3:]
    s = lax.axis_index("section")
    qt = qt_ref[...]
    parts = [(part[:, :head_dim], part[:, head_dim:]) for part in near_refs]
    for one, two in zip(far_refs[::2], far_refs[1::2]):
        parts.append(finish_rows(k_gain_ref[...], one.at[0], two.at[0]))
    rows = parts[0][0].shape[0]
    scores, biases = [], []
    top = TOP_FLOOR if first else top_in[...]
    for step, (keys, _) in zip((*near, *far), parts):
        score = jnp.dot(keys, qt, preferred_element_type=F32)
        bias = bias_ref[pl.ds(((s ^ step) * rows) // tile_len, 1), :]
        scores.append(score)
        biases.append(bias)
        top = jnp.maximum(top, jnp.max(score, axis=0, keepdims=True) + bias)
    row_sum, mixed = 0.0, 0.0
    if not first:
        scale = jnp.exp(top_in[...] - top)
        row_sum = sum_in[...] * scale
        mixed = mixed_in[...] * scale
    for (_, values), score, bias in zip(parts, scores, biases):
        weights = jnp.exp(score + (bias - top))
        row_sum = row_sum + jnp.sum(weights, axis=0, keepdims=True)
        mixed = mixed + lax.dot_general(
            values, weights.astype(BF16), (((0,), (0,)), ((), ())), preferred_element_type=F32
        )
    if not last:
        top_out, sum_out, mixed_out = refs
        top_out[...] = top
        sum_out[...] = row_sum
        mixed_out[...] = mixed
        return
    (out,) = refs
    has_any = jnp.max(bias_ref[...], axis=0, keepdims=True) > -1.0
    inverse = jnp.where(has_any, 1.0 / jnp.where(has_any, row_sum, 1.0), 0.0)
    context = (mixed * inverse).astype(BF16)
    tokens = out.shape[0]
    for head in range(out.shape[1] // head_dim):
        out[:, head * head_dim : (head + 1) * head_dim] = context[
            :, head * tokens : (head + 1) * tokens
        ].T


def swap(value, axis, k):
    return lax.ppermute(value, axis, [(i, i ^ k) for i in range(lax.axis_size(axis))])


def exchange_two_heads(value, home_sends):
    hops = []
    for d in range(2):
        for t in range(4):
            sends = (t // 2 == d) == home_sends
            hops.append((4 * d + t, 4 * d + (t ^ 2) if sends else 4 * (1 - d) + t))
    return lax.ppermute(value, ("dp", "tensor"), hops)


def sum_many_heads(own, others):
    n_dp, n_tensor = lax.axis_size("dp"), lax.axis_size("tensor")
    heads = own.shape[0] * n_dp
    half = shape_of((heads // 2, *own.shape[1:]))
    send, keep = call(
        functools.partial(spread_kernel, n_dp, n_tensor),
        [half, half],
        n_dp,
        "spread",
        scratch=[pltpu.VMEM((heads, *own.shape[1:]), BF16)],
    )(own, *others)
    bit = n_tensor // 2
    while bit > 1:
        arrived = swap(send, "tensor", bit)
        bit //= 2
        now = keep.shape
        if bit > 1:
            half = shape_of((now[0] // 2, *now[1:]))
            send, keep = call(
                functools.partial(add_kernel, bit),
                [half, half],
                2,
                "add_part",
                scratch=[pltpu.VMEM(now, BF16)],
            )(keep, arrived)
        else:
            keep = call(add_last_kernel, shape_of(now), 2, "add_pair")(keep, arrived)
    return keep


def on_device(queries, images, kv_weight, q_gain, k_gain, tile_mask):
    n_section = lax.axis_size("section")
    n_dp = lax.axis_size("dp")
    n_tensor = lax.axis_size("tensor")
    head_dim = q_gain.shape[0]
    tokens, q_width = queries.shape
    rows, features = images.shape[1:]
    tiles = tile_mask.shape[1]
    own_heads = kv_weight.shape[2] // head_dim
    heads = own_heads * n_dp
    tile_len = rows * n_section // tiles
    assert heads * 2 == n_tensor and tile_len % rows == 0 and n_section >= 4
    pairs = tokens * (q_width // head_dim)
    work = 4 * rows * features * kv_weight.shape[2]

    x, w, *small = [
        pltpu.with_memory_space_constraint(value, pltpu.HBM)
        for value in (
            images, kv_weight, queries, q_gain.reshape(1, -1), tile_mask.T, k_gain.reshape(1, -1),
        )
    ]
    product = shape_of((own_heads, rows, 2 * head_dim))
    x_scratch, w_scratch = pltpu.VMEM(images.shape, BF16), pltpu.VMEM(kv_weight.shape, BF16)
    prepared = [
        shape_of((head_dim, pairs)),
        shape_of((tiles, pairs), F32),
        shape_of((1, head_dim), F32),
    ]
    query_scratch = [
        pltpu.VMEM(queries.shape, BF16),
        pltpu.VMEM((1, head_dim), F32),
        pltpu.VMEM((tiles, tokens), jnp.int32),
    ]
    others = [swap(kv_weight, "dp", k) for k in range(1, n_dp)]
    if n_dp == 2 and own_heads == 1:
        away = call(
            functools.partial(away_kernel, head_dim),
            product,
            2,
            "away_own",
            flops=work,
            in_specs=[HBM] * 2,
            scratch=[x_scratch, w_scratch, pltpu.SemaphoreType.DMA((2,))],
        )(x, w)
        first = exchange_two_heads(away, False)
        x_home = call(
            load_kernel,
            shape_of(images.shape),
            2,
            "home_rows",
            in_specs=[VMEM, HBM],
            scratch=[pltpu.SemaphoreType.DMA((1,))],
        )(away, x)
        home = call(
            functools.partial(home_kernel, head_dim), product, 2, "home_other", flops=work
        )(x_home, others[0])
        second = exchange_two_heads(home, True)
        keep, qt, bias, gain = call(
            functools.partial(keep_kernel, head_dim),
            [product, *prepared],
            8,
            "keep_queries",
            flops=work,
            in_specs=[VMEM] * 2 + [HBM] * 6,
            scratch=[x_scratch, w_scratch, *query_scratch, pltpu.SemaphoreType.DMA((6,))],
        )(home, others[0], x, w, *small)
        total = call(pair_kernel, product, 3, "pair_sum")(keep, first, second)
    else:
        own, x_here = call(
            functools.partial(own_kernel, head_dim),
            [product, shape_of(images.shape)],
            2,
            "own_heads",
            flops=work,
            in_specs=[HBM] * 2,
            scratch=[w_scratch, pltpu.SemaphoreType.DMA((2,))],
        )(x, w)
        qt, bias, gain = call(
            query_kernel,
            prepared,
            4,
            "queries",
            in_specs=[HBM] * 4,
            scratch=[*query_scratch, pltpu.SemaphoreType.DMA((4,))],
        )(*small)
        rest = [
            call(functools.partial(other_kernel, head_dim), product, 2, "other_heads", flops=work)(
                x_here, other
            )
            for other in others
        ]
        total = sum_many_heads(own, rest)
    far = [step for step in range(1, n_section) if step & (step - 1)]
    near = [step for step in range(1, n_section) if not step & (step - 1)]
    arrived = swap(total, "tensor", 1)
    halves = [swap(total, "section", step) for step in far]
    kv = call(norm_kernel, shape_of((rows, 2 * head_dim)), 3, "sum_norm")(gain, total, arrived)
    finished = [swap(kv, "section", step) for step in near]
    both = []
    for value in halves:
        both += [value, swap(value, "tensor", 1)]
    state = []
    for here, there, operands in (
        ([0], [], [kv]),
        (near, [], finished),
        ([], far, both),
    ):
        first, last = here == [0], len(there) > 0
        outs = (
            shape_of((tokens, q_width))
            if last
            else [shape_of((1, pairs), F32), shape_of((1, pairs), F32), shape_of((head_dim, pairs), F32)]
        )
        parts = len(here) + len(there)
        state = call(
            functools.partial(attend_kernel, here, there, tile_len, first, last, head_dim),
            outs,
            3 + len(operands) + len(state),
            "attend",
            flops=4 * pairs * rows * head_dim * parts,
            exps=pairs * rows * parts,
        )(gain, qt, bias, *operands, *state)
    return state


def solution(mesh):
    in_specs = (
        P(("section", "dp"), "tensor"),
        P("dp", "section", "tensor"),
        P(None, "tensor", "dp"),
        P(),
        P(),
        P(("section", "dp"), None),
    )
    out_specs = P(("section", "dp"), "tensor")
    return jax.shard_map(
        on_device, mesh=mesh, in_specs=in_specs, out_specs=out_specs, check_vma=False
    )
```

```python
import functools

import jax
import jax.numpy as jnp
from jax import lax
from jax.experimental import pallas as pl
from jax.experimental.pallas import tpu as pltpu
from jax.sharding import PartitionSpec as P

EPSILON = 1e-05
MASKED_SCORE = -1e30
TOP_FLOOR = -1e29
VMEM = pl.BlockSpec(memory_space=pltpu.VMEM)
HBM = pl.BlockSpec(memory_space=pltpu.HBM)
F32 = jnp.float32
MIB = 1024 * 1024
LIMIT = 24 * MIB
BF16 = jnp.bfloat16


def shape_of(dims, dtype=BF16):
    return jax.ShapeDtypeStruct(dims, dtype)


def call(
    kernel, outs, n_in, name, flops=0, size=0, exps=0, in_specs=None, scratch=()
):
    many = isinstance(outs, list)
    return pl.pallas_call(
        kernel,
        out_shape=outs,
        in_specs=in_specs or [VMEM] * n_in,
        out_specs=[VMEM] * len(outs) if many else VMEM,
        scratch_shapes=scratch,
        compiler_params=pltpu.CompilerParams(vmem_limit_bytes=LIMIT),
        cost_estimate=pl.CostEstimate(flops=flops, bytes_accessed=size, transcendentals=exps),
        name=name,
    )


def normalize(values, gain_vec):
    mean_sq = jnp.mean(values * values, axis=-1, keepdims=True)
    return values * lax.rsqrt(mean_sq + EPSILON) * gain_vec


def project(x, w):
    return jnp.dot(
        x, jnp.concatenate([w[0], w[1]], axis=1), preferred_element_type=F32
    ).astype(BF16)


def store_heads(ref, base, both, head_dim):
    width = both.shape[1] // 2
    for head in range(width // head_dim):
        lo = head * head_dim
        ref[base + head, :, :head_dim] = both[:, lo : lo + head_dim]
        ref[base + head, :, head_dim:] = both[:, width + lo : width + lo + head_dim]


def prepare_queries(copies, q_ref, q_gain_ref, mask_ref, qt_ref, bias_ref):
    for copy in copies:
        copy.wait()
    tokens = q_ref.shape[0]
    head_dim = q_gain_ref.shape[1]
    bias = jnp.where(mask_ref[...] > 0, 0.0, MASKED_SCORE).astype(F32)
    for head in range(q_ref.shape[1] // head_dim):
        rows = q_ref[:, head * head_dim : (head + 1) * head_dim].astype(F32)
        normed = normalize(rows, q_gain_ref[...]) * head_dim ** (-0.5)
        qt_ref[:, head * tokens : (head + 1) * tokens] = normed.T.astype(BF16)
        bias_ref[:, head * tokens : (head + 1) * tokens] = bias


def start_copies(sources, targets, sems, first=0):
    copies = [
        pltpu.make_async_copy(a, b, sems.at[first + i]) for i, (a, b) in enumerate(zip(sources, targets))
    ]
    for copy in copies:
        copy.start()
    return copies


def own_kernel(head_dim, x_hbm, w_hbm, own_ref, x_ref, w_ref, sems):
    sources = (x_hbm, w_hbm.at[0], w_hbm.at[1])
    rows, keys, values = start_copies(sources, (x_ref, w_ref.at[0], w_ref.at[1]), sems)
    rows.wait()
    for part, copy in enumerate((keys, values)):
        copy.wait()
        product = jnp.dot(x_ref[0], w_ref[part], preferred_element_type=F32).astype(BF16)
        for head in range(own_ref.shape[0]):
            own_ref[head, :, part * head_dim : (part + 1) * head_dim] = product[
                :, head * head_dim : (head + 1) * head_dim
            ]


def other_kernel(head_dim, x_ref, w_ref, other_ref):
    store_heads(other_ref, 0, project(x_ref[0], w_ref[...]), head_dim)


def query_kernel(
    q_hbm, q_gain_hbm, mask_hbm, k_gain_hbm, qt_ref, bias_ref, k_gain_ref,
    q_ref, q_gain_ref, mask_ref, sems,
):
    copies = start_copies(
        (q_hbm, q_gain_hbm, mask_hbm, k_gain_hbm), (q_ref, q_gain_ref, mask_ref, k_gain_ref), sems
    )
    prepare_queries(copies, q_ref, q_gain_ref, mask_ref, qt_ref, bias_ref)


def is_home():
    return lax.axis_index("tensor") // 2 == lax.axis_index("dp")


def away_kernel(head_dim, x_hbm, w_hbm, own_ref, x_ref, w_ref, sems):
    @pl.when(is_home())
    def _():
        own_ref[...] = jnp.zeros_like(own_ref)

    @pl.when(jnp.logical_not(is_home()))
    def _():
        own_kernel(head_dim, x_hbm, w_hbm, own_ref, x_ref, w_ref, sems)


def load_kernel(after_ref, x_hbm, x_ref, sems):
    @pl.when(is_home())
    def _():
        for copy in start_copies((x_hbm,), (x_ref,), sems):
            copy.wait()


def home_kernel(head_dim, x_ref, w_other_ref, other_ref):
    @pl.when(is_home())
    def _():
        store_heads(other_ref, 0, project(x_ref[0], w_other_ref[...]), head_dim)

    @pl.when(jnp.logical_not(is_home()))
    def _():
        other_ref[...] = jnp.zeros_like(other_ref)


def keep_kernel(
    head_dim, after_ref, w_other_ref, x_hbm, w_hbm, q_hbm, q_gain_hbm, mask_hbm, k_gain_hbm,
    keep_ref, qt_ref, bias_ref, k_gain_ref, x_ref, w_ref, q_ref, q_gain_ref, mask_ref, sems,
):
    copies = start_copies(
        (q_hbm, q_gain_hbm, mask_hbm, k_gain_hbm), (q_ref, q_gain_ref, mask_ref, k_gain_ref), sems
    )
    moves = start_copies((x_hbm, w_hbm), (x_ref, w_ref), sems, len(copies))
    prepare_queries(copies, q_ref, q_gain_ref, mask_ref, qt_ref, bias_ref)
    for copy in moves:
        copy.wait()

    @pl.when(is_home())
    def _():
        store_heads(keep_ref, 0, project(x_ref[0], w_ref[...]), head_dim)

    @pl.when(jnp.logical_not(is_home()))
    def _():
        store_heads(keep_ref, 0, project(x_ref[0], w_other_ref[...]), head_dim)


def split_half(held, send_ref, keep_ref, partner_heads, own_heads):
    for i in range(send_ref.shape[0]):
        send_ref[i] = held[partner_heads + i]
        keep_ref[i] = held[own_heads + i]


def spread_kernel(n_dp, n_tensor, own_ref, *refs):
    others, (send_ref, keep_ref, held) = refs[: n_dp - 1], refs[n_dp - 1 :]
    d = lax.axis_index("dp")
    own_heads = own_ref.shape[0]
    for k, ref in enumerate((own_ref, *others)):
        held[pl.ds((d ^ k) * own_heads, own_heads)] = ref[...]
    half = send_ref.shape[0]
    upper = lax.axis_index("tensor") // (n_tensor // 2)
    split_half(held, send_ref, keep_ref, (1 - upper) * half, upper * half)


def pair_kernel(keep_ref, first_ref, second_ref, out_ref):
    arrived = jnp.where(is_home(), first_ref[...], second_ref[...]).astype(F32)
    out_ref[...] = (keep_ref[...].astype(F32) + arrived).astype(BF16)


def add_kernel(bit, keep_ref, arrived_ref, send_ref, next_ref, held):
    held[...] = (keep_ref[...].astype(F32) + arrived_ref[...].astype(F32)).astype(BF16)
    half = send_ref.shape[0]
    upper = (lax.axis_index("tensor") // bit) % 2
    split_half(held, send_ref, next_ref, (1 - upper) * half, upper * half)


def add_last_kernel(keep_ref, arrived_ref, out_ref):
    out_ref[...] = (keep_ref[...].astype(F32) + arrived_ref[...].astype(F32)).astype(BF16)


def finish_rows(k_gain, one, two):
    total = one[...].astype(F32) + two[...].astype(F32)
    head_dim = total.shape[1] // 2
    keys = normalize(total[:, :head_dim], k_gain).astype(BF16)
    return keys, total[:, head_dim:].astype(BF16)


def norm_kernel(k_gain_ref, keep_ref, arrived_ref, kv_ref):
    keys, values = finish_rows(k_gain_ref[...], keep_ref.at[0], arrived_ref.at[0])
    kv_ref[:, : keys.shape[1]] = keys
    kv_ref[:, keys.shape[1] :] = values


def attend_kernel(near, far, tile_len, first, last, head_dim, k_gain_ref, qt_ref, bias_ref, *refs):
    near_refs, refs = refs[: len(near)], refs[len(near) :]
    far_refs, refs = refs[: 2 * len(far)], refs[2 * len(far) :]
    if not first:
        top_in, sum_in, mixed_in = refs[:3]
        refs = refs[3:]
    s = lax.axis_index("section")
    qt = qt_ref[...]
    parts = [(part[:, :head_dim], part[:, head_dim:]) for part in near_refs]
    for one, two in zip(far_refs[::2], far_refs[1::2]):
        parts.append(finish_rows(k_gain_ref[...], one.at[0], two.at[0]))
    rows = parts[0][0].shape[0]
    scores, biases = [], []
    top = TOP_FLOOR if first else top_in[...]
    for step, (keys, _) in zip((*near, *far), parts):
        score = jnp.dot(keys, qt, preferred_element_type=F32)
        bias = bias_ref[pl.ds(((s ^ step) * rows) // tile_len, 1), :]
        scores.append(score)
        biases.append(bias)
        top = jnp.maximum(top, jnp.max(score, axis=0, keepdims=True) + bias)
    row_sum, mixed = 0.0, 0.0
    if not first:
        scale = jnp.exp(top_in[...] - top)
        row_sum = sum_in[...] * scale
        mixed = mixed_in[...] * scale
    for (_, values), score, bias in zip(parts, scores, biases):
        weights = jnp.exp(score + (bias - top))
        row_sum = row_sum + jnp.sum(weights, axis=0, keepdims=True)
        mixed = mixed + lax.dot_general(
            values, weights.astype(BF16), (((0,), (0,)), ((), ())), preferred_element_type=F32
        )
    if not last:
        top_out, sum_out, mixed_out = refs
        top_out[...] = top
        sum_out[...] = row_sum
        mixed_out[...] = mixed
        return
    (out,) = refs
    has_any = jnp.max(bias_ref[...], axis=0, keepdims=True) > -1.0
    inverse = jnp.where(has_any, 1.0 / jnp.where(has_any, row_sum, 1.0), 0.0)
    context = (mixed * inverse).astype(BF16)
    tokens = out.shape[0]
    for head in range(out.shape[1] // head_dim):
        out[:, head * head_dim : (head + 1) * head_dim] = context[
            :, head * tokens : (head + 1) * tokens
        ].T


def swap(value, axis, k):
    return lax.ppermute(value, axis, [(i, i ^ k) for i in range(lax.axis_size(axis))])


def exchange_two_heads(value, home_sends):
    hops = []
    for d in range(2):
        for t in range(4):
            sends = (t // 2 == d) == home_sends
            hops.append((4 * d + t, 4 * d + (t ^ 2) if sends else 4 * (1 - d) + t))
    return lax.ppermute(value, ("dp", "tensor"), hops)


def sum_many_heads(own, others):
    n_dp, n_tensor = lax.axis_size("dp"), lax.axis_size("tensor")
    heads = own.shape[0] * n_dp
    half = shape_of((heads // 2, *own.shape[1:]))
    send, keep = call(
        functools.partial(spread_kernel, n_dp, n_tensor),
        [half, half],
        n_dp,
        "spread",
        scratch=[pltpu.VMEM((heads, *own.shape[1:]), BF16)],
    )(own, *others)
    bit = n_tensor // 2
    while bit > 1:
        arrived = swap(send, "tensor", bit)
        bit //= 2
        now = keep.shape
        if bit > 1:
            half = shape_of((now[0] // 2, *now[1:]))
            send, keep = call(
                functools.partial(add_kernel, bit),
                [half, half],
                2,
                "add_part",
                scratch=[pltpu.VMEM(now, BF16)],
            )(keep, arrived)
        else:
            keep = call(add_last_kernel, shape_of(now), 2, "add_pair")(keep, arrived)
    return keep


def on_device(queries, images, kv_weight, q_gain, k_gain, tile_mask):
    n_section = lax.axis_size("section")
    n_dp = lax.axis_size("dp")
    n_tensor = lax.axis_size("tensor")
    head_dim = q_gain.shape[0]
    tokens, q_width = queries.shape
    rows, features = images.shape[1:]
    tiles = tile_mask.shape[1]
    own_heads = kv_weight.shape[2] // head_dim
    heads = own_heads * n_dp
    tile_len = rows * n_section // tiles
    assert heads * 2 == n_tensor and tile_len % rows == 0 and n_section >= 4
    pairs = tokens * (q_width // head_dim)
    work = 4 * rows * features * kv_weight.shape[2]

    x, w, *small = [
        pltpu.with_memory_space_constraint(value, pltpu.HBM)
        for value in (
            images, kv_weight, queries, q_gain.reshape(1, -1), tile_mask.T, k_gain.reshape(1, -1),
        )
    ]
    product = shape_of((own_heads, rows, 2 * head_dim))
    x_scratch, w_scratch = pltpu.VMEM(images.shape, BF16), pltpu.VMEM(kv_weight.shape, BF16)
    prepared = [
        shape_of((head_dim, pairs)),
        shape_of((tiles, pairs), F32),
        shape_of((1, head_dim), F32),
    ]
    query_scratch = [
        pltpu.VMEM(queries.shape, BF16),
        pltpu.VMEM((1, head_dim), F32),
        pltpu.VMEM((tiles, tokens), jnp.int32),
    ]
    others = [swap(kv_weight, "dp", k) for k in range(1, n_dp)]
    if n_dp == 2 and own_heads == 1:
        away = call(
            functools.partial(away_kernel, head_dim),
            product,
            2,
            "away_own",
            flops=work,
            in_specs=[HBM] * 2,
            scratch=[x_scratch, w_scratch, pltpu.SemaphoreType.DMA((3,))],
        )(x, w)
        first = exchange_two_heads(away, False)
        x_home = call(
            load_kernel,
            shape_of(images.shape),
            2,
            "home_rows",
            in_specs=[VMEM, HBM],
            scratch=[pltpu.SemaphoreType.DMA((1,))],
        )(away, x)
        home = call(
            functools.partial(home_kernel, head_dim), product, 2, "home_other", flops=work
        )(x_home, others[0])
        second = exchange_two_heads(home, True)
        keep, qt, bias, gain = call(
            functools.partial(keep_kernel, head_dim),
            [product, *prepared],
            8,
            "keep_queries",
            flops=work,
            in_specs=[VMEM] * 2 + [HBM] * 6,
            scratch=[x_scratch, w_scratch, *query_scratch, pltpu.SemaphoreType.DMA((6,))],
        )(home, others[0], x, w, *small)
        total = call(pair_kernel, product, 3, "pair_sum")(keep, first, second)
    else:
        own, x_here = call(
            functools.partial(own_kernel, head_dim),
            [product, shape_of(images.shape)],
            2,
            "own_heads",
            flops=work,
            in_specs=[HBM] * 2,
            scratch=[w_scratch, pltpu.SemaphoreType.DMA((3,))],
        )(x, w)
        qt, bias, gain = call(
            query_kernel,
            prepared,
            4,
            "queries",
            in_specs=[HBM] * 4,
            scratch=[*query_scratch, pltpu.SemaphoreType.DMA((4,))],
        )(*small)
        rest = [
            call(functools.partial(other_kernel, head_dim), product, 2, "other_heads", flops=work)(
                x_here, other
            )
            for other in others
        ]
        total = sum_many_heads(own, rest)
    far = [step for step in range(1, n_section) if step & (step - 1)]
    near = [step for step in range(1, n_section) if not step & (step - 1)]
    arrived = swap(total, "tensor", 1)
    halves = [swap(total, "section", step) for step in far]
    kv = call(norm_kernel, shape_of((rows, 2 * head_dim)), 3, "sum_norm")(gain, total, arrived)
    finished = [swap(kv, "section", step) for step in near]
    both = []
    for value in halves:
        both += [value, swap(value, "tensor", 1)]
    state = []
    for here, there, operands in (
        ([0], [], [kv]),
        (near, [], finished),
        ([], far, both),
    ):
        first, last = here == [0], len(there) > 0
        outs = (
            shape_of((tokens, q_width))
            if last
            else [shape_of((1, pairs), F32), shape_of((1, pairs), F32), shape_of((head_dim, pairs), F32)]
        )
        parts = len(here) + len(there)
        state = call(
            functools.partial(attend_kernel, here, there, tile_len, first, last, head_dim),
            outs,
            3 + len(operands) + len(state),
            "attend",
            flops=4 * pairs * rows * head_dim * parts,
            exps=pairs * rows * parts,
        )(gain, qt, bias, *operands, *state)
    return state


def solution(mesh):
    in_specs = (
        P(("section", "dp"), "tensor"),
        P("dp", "section", "tensor"),
        P(None, "tensor", "dp"),
        P(),
        P(),
        P(("section", "dp"), None),
    )
    out_specs = P(("section", "dp"), "tensor")
    return jax.shard_map(
        on_device, mesh=mesh, in_specs=in_specs, out_specs=out_specs, check_vma=False
    )
```

```python
import functools

import jax
import jax.numpy as jnp
from jax import lax
from jax.experimental import pallas as pl
from jax.experimental.pallas import tpu as pltpu
from jax.sharding import PartitionSpec as P

EPSILON = 1e-05
MASKED_SCORE = -1e30
TOP_FLOOR = -1e29
VMEM = pl.BlockSpec(memory_space=pltpu.VMEM)
HBM = pl.BlockSpec(memory_space=pltpu.HBM)
F32 = jnp.float32
MIB = 1024 * 1024
LIMIT = 24 * MIB
BF16 = jnp.bfloat16


def shape_of(dims, dtype=BF16):
    return jax.ShapeDtypeStruct(dims, dtype)


def call(
    kernel, outs, n_in, name, flops=0, size=0, exps=0, in_specs=None, scratch=(), aliases=None
):
    many = isinstance(outs, list)
    return pl.pallas_call(
        kernel,
        out_shape=outs,
        in_specs=in_specs or [VMEM] * n_in,
        out_specs=[VMEM] * len(outs) if many else VMEM,
        scratch_shapes=scratch,
        input_output_aliases=aliases or {},
        compiler_params=pltpu.CompilerParams(vmem_limit_bytes=LIMIT),
        cost_estimate=pl.CostEstimate(flops=flops, bytes_accessed=size, transcendentals=exps),
        name=name,
    )


def normalize(values, gain_vec):
    mean_sq = jnp.mean(values * values, axis=-1, keepdims=True)
    return values * lax.rsqrt(mean_sq + EPSILON) * gain_vec


def project(x, w):
    return jnp.dot(
        x, jnp.concatenate([w[0], w[1]], axis=1), preferred_element_type=F32
    ).astype(BF16)


def store_heads(ref, base, both, head_dim):
    width = both.shape[1] // 2
    for head in range(width // head_dim):
        lo = head * head_dim
        ref[base + head, :, :head_dim] = both[:, lo : lo + head_dim]
        ref[base + head, :, head_dim:] = both[:, width + lo : width + lo + head_dim]


def prepare_queries(copies, q_ref, q_gain_ref, mask_ref, qt_ref, bias_ref):
    for copy in copies:
        copy.wait()
    tokens = q_ref.shape[0]
    head_dim = q_gain_ref.shape[1]
    bias = jnp.where(mask_ref[...] > 0, 0.0, MASKED_SCORE).astype(F32)
    for head in range(q_ref.shape[1] // head_dim):
        rows = q_ref[:, head * head_dim : (head + 1) * head_dim].astype(F32)
        normed = normalize(rows, q_gain_ref[...]) * head_dim ** (-0.5)
        qt_ref[:, head * tokens : (head + 1) * tokens] = normed.T.astype(BF16)
        bias_ref[:, head * tokens : (head + 1) * tokens] = bias


def start_copies(sources, targets, sems):
    copies = [
        pltpu.make_async_copy(a, b, sems.at[i]) for i, (a, b) in enumerate(zip(sources, targets))
    ]
    for copy in copies:
        copy.start()
    return copies


def own_kernel(head_dim, x_hbm, w_hbm, own_ref, x_ref, w_ref, sems):
    for copy in start_copies((x_hbm, w_hbm), (x_ref, w_ref), sems):
        copy.wait()
    store_heads(own_ref, 0, project(x_ref[0], w_ref[...]), head_dim)


def other_kernel(head_dim, x_ref, w_ref, other_ref):
    store_heads(other_ref, 0, project(x_ref[0], w_ref[...]), head_dim)


def query_kernel(
    q_hbm, q_gain_hbm, mask_hbm, k_gain_hbm, qt_ref, bias_ref, k_gain_ref,
    q_ref, q_gain_ref, mask_ref, sems,
):
    copies = start_copies(
        (q_hbm, q_gain_hbm, mask_hbm, k_gain_hbm), (q_ref, q_gain_ref, mask_ref, k_gain_ref), sems
    )
    prepare_queries(copies, q_ref, q_gain_ref, mask_ref, qt_ref, bias_ref)


def is_home():
    return lax.axis_index("tensor") // 2 == lax.axis_index("dp")


def away_kernel(head_dim, x_hbm, w_hbm, own_ref, x_ref, w_ref, sems):
    @pl.when(is_home())
    def _():
        own_ref[...] = jnp.zeros_like(own_ref)

    @pl.when(jnp.logical_not(is_home()))
    def _():
        own_kernel(head_dim, x_hbm, w_hbm, own_ref, x_ref, w_ref, sems)


def load_kernel(x_in, x_hbm, w_hbm, x_ref, w_ref, sems):
    @pl.when(is_home())
    def _():
        for copy in start_copies((x_hbm, w_hbm), (x_ref, w_ref), sems):
            copy.wait()


def home_kernel(head_dim, x_ref, w_other_ref, other_ref):
    @pl.when(is_home())
    def _():
        store_heads(other_ref, 0, project(x_ref[0], w_other_ref[...]), head_dim)

    @pl.when(jnp.logical_not(is_home()))
    def _():
        other_ref[...] = jnp.zeros_like(other_ref)


def keep_kernel(
    head_dim, after_ref, w_other_ref, x_ref, w_ref, q_hbm, q_gain_hbm, mask_hbm, k_gain_hbm,
    keep_ref, qt_ref, bias_ref, k_gain_ref, q_ref, q_gain_ref, mask_ref, sems,
):
    copies = start_copies(
        (q_hbm, q_gain_hbm, mask_hbm, k_gain_hbm), (q_ref, q_gain_ref, mask_ref, k_gain_ref), sems
    )

    @pl.when(is_home())
    def _():
        store_heads(keep_ref, 0, project(x_ref[0], w_ref[...]), head_dim)

    @pl.when(jnp.logical_not(is_home()))
    def _():
        store_heads(keep_ref, 0, project(x_ref[0], w_other_ref[...]), head_dim)

    prepare_queries(copies, q_ref, q_gain_ref, mask_ref, qt_ref, bias_ref)


def split_half(held, send_ref, keep_ref, partner_heads, own_heads):
    for i in range(send_ref.shape[0]):
        send_ref[i] = held[partner_heads + i]
        keep_ref[i] = held[own_heads + i]


def spread_kernel(n_dp, n_tensor, own_ref, *refs):
    others, (send_ref, keep_ref, held) = refs[: n_dp - 1], refs[n_dp - 1 :]
    d = lax.axis_index("dp")
    own_heads = own_ref.shape[0]
    for k, ref in enumerate((own_ref, *others)):
        held[pl.ds((d ^ k) * own_heads, own_heads)] = ref[...]
    half = send_ref.shape[0]
    upper = lax.axis_index("tensor") // (n_tensor // 2)
    split_half(held, send_ref, keep_ref, (1 - upper) * half, upper * half)


def pair_kernel(keep_ref, first_ref, second_ref, out_ref):
    arrived = jnp.where(is_home(), first_ref[...], second_ref[...]).astype(F32)
    out_ref[...] = (keep_ref[...].astype(F32) + arrived).astype(BF16)


def add_kernel(bit, keep_ref, arrived_ref, send_ref, next_ref, held):
    held[...] = (keep_ref[...].astype(F32) + arrived_ref[...].astype(F32)).astype(BF16)
    half = send_ref.shape[0]
    upper = (lax.axis_index("tensor") // bit) % 2
    split_half(held, send_ref, next_ref, (1 - upper) * half, upper * half)


def add_last_kernel(keep_ref, arrived_ref, out_ref):
    out_ref[...] = (keep_ref[...].astype(F32) + arrived_ref[...].astype(F32)).astype(BF16)


def finish_rows(k_gain, one, two):
    total = one[...].astype(F32) + two[...].astype(F32)
    head_dim = total.shape[1] // 2
    keys = normalize(total[:, :head_dim], k_gain).astype(BF16)
    return keys, total[:, head_dim:].astype(BF16)


def norm_kernel(k_gain_ref, keep_ref, arrived_ref, kv_ref):
    keys, values = finish_rows(k_gain_ref[...], keep_ref.at[0], arrived_ref.at[0])
    kv_ref[:, : keys.shape[1]] = keys
    kv_ref[:, keys.shape[1] :] = values


def attend_kernel(near, far, tile_len, first, last, head_dim, k_gain_ref, qt_ref, bias_ref, *refs):
    near_refs, refs = refs[: len(near)], refs[len(near) :]
    far_refs, refs = refs[: 2 * len(far)], refs[2 * len(far) :]
    if not first:
        top_in, sum_in, mixed_in = refs[:3]
        refs = refs[3:]
    s = lax.axis_index("section")
    qt = qt_ref[...]
    parts = [(part[:, :head_dim], part[:, head_dim:]) for part in near_refs]
    for one, two in zip(far_refs[::2], far_refs[1::2]):
        parts.append(finish_rows(k_gain_ref[...], one.at[0], two.at[0]))
    rows = parts[0][0].shape[0]
    scores, biases = [], []
    top = TOP_FLOOR if first else top_in[...]
    for step, (keys, _) in zip((*near, *far), parts):
        score = jnp.dot(keys, qt, preferred_element_type=F32)
        bias = bias_ref[pl.ds(((s ^ step) * rows) // tile_len, 1), :]
        scores.append(score)
        biases.append(bias)
        top = jnp.maximum(top, jnp.max(score, axis=0, keepdims=True) + bias)
    row_sum, mixed = 0.0, 0.0
    if not first:
        scale = jnp.exp(top_in[...] - top)
        row_sum = sum_in[...] * scale
        mixed = mixed_in[...] * scale
    for (_, values), score, bias in zip(parts, scores, biases):
        weights = jnp.exp(score + (bias - top))
        row_sum = row_sum + jnp.sum(weights, axis=0, keepdims=True)
        mixed = mixed + lax.dot_general(
            values, weights.astype(BF16), (((0,), (0,)), ((), ())), preferred_element_type=F32
        )
    if not last:
        top_out, sum_out, mixed_out = refs
        top_out[...] = top
        sum_out[...] = row_sum
        mixed_out[...] = mixed
        return
    (out,) = refs
    has_any = jnp.max(bias_ref[...], axis=0, keepdims=True) > -1.0
    inverse = jnp.where(has_any, 1.0 / jnp.where(has_any, row_sum, 1.0), 0.0)
    context = (mixed * inverse).astype(BF16)
    tokens = out.shape[0]
    for head in range(out.shape[1] // head_dim):
        out[:, head * head_dim : (head + 1) * head_dim] = context[
            :, head * tokens : (head + 1) * tokens
        ].T


def swap(value, axis, k):
    return lax.ppermute(value, axis, [(i, i ^ k) for i in range(lax.axis_size(axis))])


def exchange_two_heads(value, home_sends):
    hops = []
    for d in range(2):
        for t in range(4):
            sends = (t // 2 == d) == home_sends
            hops.append((4 * d + t, 4 * d + (t ^ 2) if sends else 4 * (1 - d) + t))
    return lax.ppermute(value, ("dp", "tensor"), hops)


def sum_many_heads(own, others):
    n_dp, n_tensor = lax.axis_size("dp"), lax.axis_size("tensor")
    heads = own.shape[0] * n_dp
    half = shape_of((heads // 2, *own.shape[1:]))
    send, keep = call(
        functools.partial(spread_kernel, n_dp, n_tensor),
        [half, half],
        n_dp,
        "spread",
        scratch=[pltpu.VMEM((heads, *own.shape[1:]), BF16)],
    )(own, *others)
    bit = n_tensor // 2
    while bit > 1:
        arrived = swap(send, "tensor", bit)
        bit //= 2
        now = keep.shape
        if bit > 1:
            half = shape_of((now[0] // 2, *now[1:]))
            send, keep = call(
                functools.partial(add_kernel, bit),
                [half, half],
                2,
                "add_part",
                scratch=[pltpu.VMEM(now, BF16)],
            )(keep, arrived)
        else:
            keep = call(add_last_kernel, shape_of(now), 2, "add_pair")(keep, arrived)
    return keep


def on_device(queries, images, kv_weight, q_gain, k_gain, tile_mask):
    n_section = lax.axis_size("section")
    n_dp = lax.axis_size("dp")
    n_tensor = lax.axis_size("tensor")
    head_dim = q_gain.shape[0]
    tokens, q_width = queries.shape
    rows, features = images.shape[1:]
    tiles = tile_mask.shape[1]
    own_heads = kv_weight.shape[2] // head_dim
    heads = own_heads * n_dp
    tile_len = rows * n_section // tiles
    assert heads * 2 == n_tensor and tile_len % rows == 0 and n_section >= 4
    pairs = tokens * (q_width // head_dim)
    work = 4 * rows * features * kv_weight.shape[2]

    x, w, *small = [
        pltpu.with_memory_space_constraint(value, pltpu.HBM)
        for value in (
            images, kv_weight, queries, q_gain.reshape(1, -1), tile_mask.T, k_gain.reshape(1, -1),
        )
    ]
    product = shape_of((own_heads, rows, 2 * head_dim))
    w_scratch = pltpu.VMEM(kv_weight.shape, BF16)
    prepared = [
        shape_of((head_dim, pairs)),
        shape_of((tiles, pairs), F32),
        shape_of((1, head_dim), F32),
    ]
    query_scratch = [
        pltpu.VMEM(queries.shape, BF16),
        pltpu.VMEM((1, head_dim), F32),
        pltpu.VMEM((tiles, tokens), jnp.int32),
    ]
    others = [swap(kv_weight, "dp", k) for k in range(1, n_dp)]
    if n_dp == 2 and own_heads == 1:
        away, x_away = call(
            functools.partial(away_kernel, head_dim),
            [product, shape_of(images.shape)],
            2,
            "away_own",
            flops=work,
            in_specs=[HBM] * 2,
            scratch=[w_scratch, pltpu.SemaphoreType.DMA((2,))],
        )(x, w)
        first = exchange_two_heads(away, False)
        x_here, w_home = call(
            load_kernel,
            [shape_of(images.shape), shape_of(kv_weight.shape)],
            3,
            "home_load",
            in_specs=[VMEM] + [HBM] * 2,
            scratch=[pltpu.SemaphoreType.DMA((2,))],
            aliases={0: 0},
        )(x_away, x, w)
        home = call(
            functools.partial(home_kernel, head_dim), product, 2, "home_other", flops=work
        )(x_here, others[0])
        second = exchange_two_heads(home, True)
        keep, qt, bias, gain = call(
            functools.partial(keep_kernel, head_dim),
            [product, *prepared],
            8,
            "keep_queries",
            flops=work,
            in_specs=[VMEM] * 4 + [HBM] * 4,
            scratch=[*query_scratch, pltpu.SemaphoreType.DMA((4,))],
        )(home, others[0], x_here, w_home, *small)
        total = call(pair_kernel, product, 3, "pair_sum")(keep, first, second)
    else:
        own, x_here = call(
            functools.partial(own_kernel, head_dim),
            [product, shape_of(images.shape)],
            2,
            "own_heads",
            flops=work,
            in_specs=[HBM] * 2,
            scratch=[w_scratch, pltpu.SemaphoreType.DMA((2,))],
        )(x, w)
        qt, bias, gain = call(
            query_kernel,
            prepared,
            4,
            "queries",
            in_specs=[HBM] * 4,
            scratch=[*query_scratch, pltpu.SemaphoreType.DMA((4,))],
        )(*small)
        rest = [
            call(functools.partial(other_kernel, head_dim), product, 2, "other_heads", flops=work)(
                x_here, other
            )
            for other in others
        ]
        total = sum_many_heads(own, rest)
    far = [step for step in range(1, n_section) if step & (step - 1)]
    near = [step for step in range(1, n_section) if not step & (step - 1)]
    arrived = swap(total, "tensor", 1)
    halves = [swap(total, "section", step) for step in far]
    kv = call(norm_kernel, shape_of((rows, 2 * head_dim)), 3, "sum_norm")(gain, total, arrived)
    finished = [swap(kv, "section", step) for step in near]
    both = []
    for value in halves:
        both += [value, swap(value, "tensor", 1)]
    state = []
    for here, there, operands in (
        ([0], [], [kv]),
        (near, [], finished),
        ([], far, both),
    ):
        first, last = here == [0], len(there) > 0
        outs = (
            shape_of((tokens, q_width))
            if last
            else [shape_of((1, pairs), F32), shape_of((1, pairs), F32), shape_of((head_dim, pairs), F32)]
        )
        parts = len(here) + len(there)
        state = call(
            functools.partial(attend_kernel, here, there, tile_len, first, last, head_dim),
            outs,
            3 + len(operands) + len(state),
            "attend",
            flops=4 * pairs * rows * head_dim * parts,
            exps=pairs * rows * parts,
        )(gain, qt, bias, *operands, *state)
    return state


def solution(mesh):
    in_specs = (
        P(("section", "dp"), "tensor"),
        P("dp", "section", "tensor"),
        P(None, "tensor", "dp"),
        P(),
        P(),
        P(("section", "dp"), None),
    )
    out_specs = P(("section", "dp"), "tensor")
    return jax.shard_map(
        on_device, mesh=mesh, in_specs=in_specs, out_specs=out_specs, check_vma=False
    )
```

```python
import functools

import jax
import jax.numpy as jnp
from jax import lax
from jax.experimental import pallas as pl
from jax.experimental.pallas import tpu as pltpu
from jax.sharding import PartitionSpec as P

EPSILON = 1e-05
MASKED_SCORE = -1e30
TOP_FLOOR = -1e29
VMEM = pl.BlockSpec(memory_space=pltpu.VMEM)
HBM = pl.BlockSpec(memory_space=pltpu.HBM)
F32 = jnp.float32
MIB = 1024 * 1024
LIMIT = 24 * MIB
BF16 = jnp.bfloat16


def shape_of(dims, dtype=BF16):
    return jax.ShapeDtypeStruct(dims, dtype)


def call(
    kernel, outs, n_in, name, flops=0, size=0, exps=0, in_specs=None, scratch=(), aliases=None
):
    many = isinstance(outs, list)
    return pl.pallas_call(
        kernel,
        out_shape=outs,
        in_specs=in_specs or [VMEM] * n_in,
        out_specs=[VMEM] * len(outs) if many else VMEM,
        scratch_shapes=scratch,
        input_output_aliases=aliases or {},
        compiler_params=pltpu.CompilerParams(vmem_limit_bytes=LIMIT),
        cost_estimate=pl.CostEstimate(flops=flops, bytes_accessed=size, transcendentals=exps),
        name=name,
    )


def normalize(values, gain_vec):
    mean_sq = jnp.mean(values * values, axis=-1, keepdims=True)
    return values * lax.rsqrt(mean_sq + EPSILON) * gain_vec


def project(x, w):
    return jnp.dot(
        x, jnp.concatenate([w[0], w[1]], axis=1), preferred_element_type=F32
    ).astype(BF16)


def store_heads(ref, base, both, head_dim):
    width = both.shape[1] // 2
    for head in range(width // head_dim):
        lo = head * head_dim
        ref[base + head, :, :head_dim] = both[:, lo : lo + head_dim]
        ref[base + head, :, head_dim:] = both[:, width + lo : width + lo + head_dim]


def prepare_queries(copies, q_ref, q_gain_ref, mask_ref, qt_ref, bias_ref):
    for copy in copies:
        copy.wait()
    tokens = q_ref.shape[0]
    head_dim = q_gain_ref.shape[1]
    bias = jnp.where(mask_ref[...] > 0, 0.0, MASKED_SCORE).astype(F32)
    for head in range(q_ref.shape[1] // head_dim):
        rows = q_ref[:, head * head_dim : (head + 1) * head_dim].astype(F32)
        normed = normalize(rows, q_gain_ref[...]) * head_dim ** (-0.5)
        qt_ref[:, head * tokens : (head + 1) * tokens] = normed.T.astype(BF16)
        bias_ref[:, head * tokens : (head + 1) * tokens] = bias


def start_copies(sources, targets, sems):
    copies = [
        pltpu.make_async_copy(a, b, sems.at[i]) for i, (a, b) in enumerate(zip(sources, targets))
    ]
    for copy in copies:
        copy.start()
    return copies


def own_kernel(head_dim, x_hbm, w_hbm, own_ref, x_ref, w_ref, sems):
    for copy in start_copies((x_hbm, w_hbm), (x_ref, w_ref), sems):
        copy.wait()
    store_heads(own_ref, 0, project(x_ref[0], w_ref[...]), head_dim)


def other_kernel(head_dim, x_ref, w_ref, other_ref):
    store_heads(other_ref, 0, project(x_ref[0], w_ref[...]), head_dim)


def query_kernel(
    q_hbm, q_gain_hbm, mask_hbm, k_gain_hbm, qt_ref, bias_ref, k_gain_ref,
    q_ref, q_gain_ref, mask_ref, sems,
):
    copies = start_copies(
        (q_hbm, q_gain_hbm, mask_hbm, k_gain_hbm), (q_ref, q_gain_ref, mask_ref, k_gain_ref), sems
    )
    prepare_queries(copies, q_ref, q_gain_ref, mask_ref, qt_ref, bias_ref)


def is_home():
    return lax.axis_index("tensor") // 2 == lax.axis_index("dp")


def away_kernel(head_dim, x_hbm, w_hbm, own_ref, x_ref, w_ref, sems):
    @pl.when(is_home())
    def _():
        own_ref[...] = jnp.zeros_like(own_ref)

    @pl.when(jnp.logical_not(is_home()))
    def _():
        own_kernel(head_dim, x_hbm, w_hbm, own_ref, x_ref, w_ref, sems)


def load_kernel(x_in, x_hbm, w_hbm, x_ref, w_ref, sems):
    @pl.when(is_home())
    def _():
        for copy in start_copies((x_hbm, w_hbm), (x_ref, w_ref), sems):
            copy.wait()


def home_kernel(head_dim, x_ref, w_other_ref, other_ref):
    @pl.when(is_home())
    def _():
        store_heads(other_ref, 0, project(x_ref[0], w_other_ref[...]), head_dim)

    @pl.when(jnp.logical_not(is_home()))
    def _():
        other_ref[...] = jnp.zeros_like(other_ref)


def keep_kernel(
    head_dim, after_ref, w_other_ref, x_ref, w_ref, q_hbm, q_gain_hbm, mask_hbm, k_gain_hbm,
    keep_ref, qt_ref, bias_ref, k_gain_ref, q_ref, q_gain_ref, mask_ref, sems,
):
    copies = start_copies(
        (q_hbm, q_gain_hbm, mask_hbm, k_gain_hbm), (q_ref, q_gain_ref, mask_ref, k_gain_ref), sems
    )

    @pl.when(is_home())
    def _():
        store_heads(keep_ref, 0, project(x_ref[0], w_ref[...]), head_dim)

    @pl.when(jnp.logical_not(is_home()))
    def _():
        store_heads(keep_ref, 0, project(x_ref[0], w_other_ref[...]), head_dim)

    prepare_queries(copies, q_ref, q_gain_ref, mask_ref, qt_ref, bias_ref)


def split_half(held, send_ref, keep_ref, partner_heads, own_heads):
    for i in range(send_ref.shape[0]):
        send_ref[i] = held[partner_heads + i]
        keep_ref[i] = held[own_heads + i]


def spread_kernel(n_dp, n_tensor, own_ref, *refs):
    others, (send_ref, keep_ref, held) = refs[: n_dp - 1], refs[n_dp - 1 :]
    d = lax.axis_index("dp")
    own_heads = own_ref.shape[0]
    for k, ref in enumerate((own_ref, *others)):
        held[pl.ds((d ^ k) * own_heads, own_heads)] = ref[...]
    half = send_ref.shape[0]
    upper = lax.axis_index("tensor") // (n_tensor // 2)
    split_half(held, send_ref, keep_ref, (1 - upper) * half, upper * half)


def pair_kernel(keep_ref, first_ref, second_ref, out_ref):
    arrived = jnp.where(is_home(), first_ref[...], second_ref[...]).astype(F32)
    out_ref[...] = (keep_ref[...].astype(F32) + arrived).astype(BF16)


def add_kernel(bit, keep_ref, arrived_ref, send_ref, next_ref, held):
    held[...] = (keep_ref[...].astype(F32) + arrived_ref[...].astype(F32)).astype(BF16)
    half = send_ref.shape[0]
    upper = (lax.axis_index("tensor") // bit) % 2
    split_half(held, send_ref, next_ref, (1 - upper) * half, upper * half)


def add_last_kernel(keep_ref, arrived_ref, out_ref):
    out_ref[...] = (keep_ref[...].astype(F32) + arrived_ref[...].astype(F32)).astype(BF16)


def finish_rows(k_gain, one, two):
    total = one[...].astype(F32) + two[...].astype(F32)
    head_dim = total.shape[1] // 2
    keys = normalize(total[:, :head_dim], k_gain).astype(BF16)
    return keys, total[:, head_dim:].astype(BF16)


def norm_kernel(k_gain_ref, keep_ref, arrived_ref, kv_ref):
    keys, values = finish_rows(k_gain_ref[...], keep_ref.at[0], arrived_ref.at[0])
    kv_ref[:, : keys.shape[1]] = keys
    kv_ref[:, keys.shape[1] :] = values


def attend_kernel(near, far, tile_len, first, last, head_dim, k_gain_ref, qt_ref, bias_ref, *refs):
    near_refs, refs = refs[: len(near)], refs[len(near) :]
    far_refs, refs = refs[: 2 * len(far)], refs[2 * len(far) :]
    if not first:
        top_in, sum_in, mixed_in = refs[:3]
        refs = refs[3:]
    s = lax.axis_index("section")
    qt = qt_ref[...]
    parts = [(part[:, :head_dim], part[:, head_dim:]) for part in near_refs]
    for one, two in zip(far_refs[::2], far_refs[1::2]):
        parts.append(finish_rows(k_gain_ref[...], one.at[0], two.at[0]))
    rows = parts[0][0].shape[0]
    scores, biases = [], []
    top = TOP_FLOOR if first else top_in[...]
    for step, (keys, _) in zip((*near, *far), parts):
        score = jnp.dot(keys, qt, preferred_element_type=F32)
        first_step, second_step = step
        step = first_step + lax.axis_index("dp") % 2 * (second_step - first_step)
        bias = bias_ref[pl.ds(((s ^ step) * rows) // tile_len, 1), :]
        scores.append(score)
        biases.append(bias)
        top = jnp.maximum(top, jnp.max(score, axis=0, keepdims=True) + bias)
    row_sum, mixed = 0.0, 0.0
    if not first:
        scale = jnp.exp(top_in[...] - top)
        row_sum = sum_in[...] * scale
        mixed = mixed_in[...] * scale
    for (_, values), score, bias in zip(parts, scores, biases):
        weights = jnp.exp(score + (bias - top))
        row_sum = row_sum + jnp.sum(weights, axis=0, keepdims=True)
        mixed = mixed + lax.dot_general(
            values, weights.astype(BF16), (((0,), (0,)), ((), ())), preferred_element_type=F32
        )
    if not last:
        top_out, sum_out, mixed_out = refs
        top_out[...] = top
        sum_out[...] = row_sum
        mixed_out[...] = mixed
        return
    (out,) = refs
    has_any = jnp.max(bias_ref[...], axis=0, keepdims=True) > -1.0
    inverse = jnp.where(has_any, 1.0 / jnp.where(has_any, row_sum, 1.0), 0.0)
    context = (mixed * inverse).astype(BF16)
    tokens = out.shape[0]
    for head in range(out.shape[1] // head_dim):
        out[:, head * head_dim : (head + 1) * head_dim] = context[
            :, head * tokens : (head + 1) * tokens
        ].T


def swap(value, axis, k):
    return lax.ppermute(value, axis, [(i, i ^ k) for i in range(lax.axis_size(axis))])


def exchange_two_heads(value, home_sends):
    hops = []
    for d in range(2):
        for t in range(4):
            sends = (t // 2 == d) == home_sends
            hops.append((4 * d + t, 4 * d + (t ^ 2) if sends else 4 * (1 - d) + t))
    return lax.ppermute(value, ("dp", "tensor"), hops)


def sum_many_heads(own, others):
    n_dp, n_tensor = lax.axis_size("dp"), lax.axis_size("tensor")
    heads = own.shape[0] * n_dp
    half = shape_of((heads // 2, *own.shape[1:]))
    send, keep = call(
        functools.partial(spread_kernel, n_dp, n_tensor),
        [half, half],
        n_dp,
        "spread",
        scratch=[pltpu.VMEM((heads, *own.shape[1:]), BF16)],
    )(own, *others)
    bit = n_tensor // 2
    while bit > 1:
        arrived = swap(send, "tensor", bit)
        bit //= 2
        now = keep.shape
        if bit > 1:
            half = shape_of((now[0] // 2, *now[1:]))
            send, keep = call(
                functools.partial(add_kernel, bit),
                [half, half],
                2,
                "add_part",
                scratch=[pltpu.VMEM(now, BF16)],
            )(keep, arrived)
        else:
            keep = call(add_last_kernel, shape_of(now), 2, "add_pair")(keep, arrived)
    return keep


def on_device(queries, images, kv_weight, q_gain, k_gain, tile_mask):
    n_section = lax.axis_size("section")
    n_dp = lax.axis_size("dp")
    n_tensor = lax.axis_size("tensor")
    head_dim = q_gain.shape[0]
    tokens, q_width = queries.shape
    rows, features = images.shape[1:]
    tiles = tile_mask.shape[1]
    own_heads = kv_weight.shape[2] // head_dim
    heads = own_heads * n_dp
    tile_len = rows * n_section // tiles
    assert heads * 2 == n_tensor and tile_len % rows == 0 and n_section >= 4
    pairs = tokens * (q_width // head_dim)
    work = 4 * rows * features * kv_weight.shape[2]

    x, w, *small = [
        pltpu.with_memory_space_constraint(value, pltpu.HBM)
        for value in (
            images, kv_weight, queries, q_gain.reshape(1, -1), tile_mask.T, k_gain.reshape(1, -1),
        )
    ]
    product = shape_of((own_heads, rows, 2 * head_dim))
    w_scratch = pltpu.VMEM(kv_weight.shape, BF16)
    prepared = [
        shape_of((head_dim, pairs)),
        shape_of((tiles, pairs), F32),
        shape_of((1, head_dim), F32),
    ]
    query_scratch = [
        pltpu.VMEM(queries.shape, BF16),
        pltpu.VMEM((1, head_dim), F32),
        pltpu.VMEM((tiles, tokens), jnp.int32),
    ]
    others = [swap(kv_weight, "dp", k) for k in range(1, n_dp)]
    if n_dp == 2 and own_heads == 1:
        away, x_away = call(
            functools.partial(away_kernel, head_dim),
            [product, shape_of(images.shape)],
            2,
            "away_own",
            flops=work,
            in_specs=[HBM] * 2,
            scratch=[w_scratch, pltpu.SemaphoreType.DMA((2,))],
        )(x, w)
        first = exchange_two_heads(away, False)
        x_here, w_home = call(
            load_kernel,
            [shape_of(images.shape), shape_of(kv_weight.shape)],
            3,
            "home_load",
            in_specs=[VMEM] + [HBM] * 2,
            scratch=[pltpu.SemaphoreType.DMA((2,))],
            aliases={0: 0},
        )(x_away, x, w)
        home = call(
            functools.partial(home_kernel, head_dim), product, 2, "home_other", flops=work
        )(x_here, others[0])
        second = exchange_two_heads(home, True)
        keep, qt, bias, gain = call(
            functools.partial(keep_kernel, head_dim),
            [product, *prepared],
            8,
            "keep_queries",
            flops=work,
            in_specs=[VMEM] * 4 + [HBM] * 4,
            scratch=[*query_scratch, pltpu.SemaphoreType.DMA((4,))],
        )(home, others[0], x_here, w_home, *small)
        total = call(pair_kernel, product, 3, "pair_sum")(keep, first, second)
    else:
        own, x_here = call(
            functools.partial(own_kernel, head_dim),
            [product, shape_of(images.shape)],
            2,
            "own_heads",
            flops=work,
            in_specs=[HBM] * 2,
            scratch=[w_scratch, pltpu.SemaphoreType.DMA((2,))],
        )(x, w)
        qt, bias, gain = call(
            query_kernel,
            prepared,
            4,
            "queries",
            in_specs=[HBM] * 4,
            scratch=[*query_scratch, pltpu.SemaphoreType.DMA((4,))],
        )(*small)
        rest = [
            call(functools.partial(other_kernel, head_dim), product, 2, "other_heads", flops=work)(
                x_here, other
            )
            for other in others
        ]
        total = sum_many_heads(own, rest)
    far = [step for step in range(1, n_section) if step & (step - 1)]
    near = [step for step in range(1, n_section) if not step & (step - 1)]
    arrived = swap(total, "tensor", 1)
    halves = [swap(total, "section", step) for step in far]
    kv = call(norm_kernel, shape_of((rows, 2 * head_dim)), 3, "sum_norm")(gain, total, arrived)
    near = list(zip(near, reversed(near)))
    far = [(step, step) for step in far]
    finished = []
    for even, odd in near:
        hops = [
            (s * n_dp + d, (s ^ (odd if d % 2 else even)) * n_dp + d)
            for s in range(n_section)
            for d in range(n_dp)
        ]
        finished.append(lax.ppermute(kv, ("section", "dp"), hops))
    both = []
    for value in halves:
        both += [value, swap(value, "tensor", 1)]
    state = []
    for here, there, operands in (
        ([(0, 0)], [], [kv]),
        (near, [], finished),
        ([], far, both),
    ):
        first, last = here == [(0, 0)], len(there) > 0
        outs = (
            shape_of((tokens, q_width))
            if last
            else [shape_of((1, pairs), F32), shape_of((1, pairs), F32), shape_of((head_dim, pairs), F32)]
        )
        parts = len(here) + len(there)
        state = call(
            functools.partial(attend_kernel, here, there, tile_len, first, last, head_dim),
            outs,
            3 + len(operands) + len(state),
            "attend",
            flops=4 * pairs * rows * head_dim * parts,
            exps=pairs * rows * parts,
        )(gain, qt, bias, *operands, *state)
    return state


def solution(mesh):
    in_specs = (
        P(("section", "dp"), "tensor"),
        P("dp", "section", "tensor"),
        P(None, "tensor", "dp"),
        P(),
        P(),
        P(("section", "dp"), None),
    )
    out_specs = P(("section", "dp"), "tensor")
    return jax.shard_map(
        on_device, mesh=mesh, in_specs=in_specs, out_specs=out_specs, check_vma=False
    )
```

```python
import functools

import jax
import jax.numpy as jnp
from jax import lax
from jax.experimental import pallas as pl
from jax.experimental.pallas import tpu as pltpu
from jax.sharding import PartitionSpec as P

EPSILON = 1e-05
MASKED_SCORE = -1e30
TOP_FLOOR = -1e29
VMEM = pl.BlockSpec(memory_space=pltpu.VMEM)
HBM = pl.BlockSpec(memory_space=pltpu.HBM)
F32 = jnp.float32
MIB = 1024 * 1024
LIMIT = 24 * MIB
BF16 = jnp.bfloat16


def shape_of(dims, dtype=BF16):
    return jax.ShapeDtypeStruct(dims, dtype)


def call(
    kernel, outs, n_in, name, flops=0, size=0, exps=0, in_specs=None, scratch=(), aliases=None
):
    many = isinstance(outs, list)
    return pl.pallas_call(
        kernel,
        out_shape=outs,
        in_specs=in_specs or [VMEM] * n_in,
        out_specs=[VMEM] * len(outs) if many else VMEM,
        scratch_shapes=scratch,
        input_output_aliases=aliases or {},
        compiler_params=pltpu.CompilerParams(vmem_limit_bytes=LIMIT),
        cost_estimate=pl.CostEstimate(flops=flops, bytes_accessed=size, transcendentals=exps),
        name=name,
    )


def normalize(values, gain_vec):
    mean_sq = jnp.mean(values * values, axis=-1, keepdims=True)
    return values * lax.rsqrt(mean_sq + EPSILON) * gain_vec


def project(x, w):
    return jnp.dot(
        x, jnp.concatenate([w[0], w[1]], axis=1), preferred_element_type=F32
    ).astype(BF16)


def store_heads(ref, base, both, head_dim):
    width = both.shape[1] // 2
    for head in range(width // head_dim):
        lo = head * head_dim
        ref[base + head, :, :head_dim] = both[:, lo : lo + head_dim]
        ref[base + head, :, head_dim:] = both[:, width + lo : width + lo + head_dim]


def prepare_queries(copies, q_ref, q_gain_ref, mask_ref, qt_ref, bias_ref):
    for copy in copies:
        copy.wait()
    tokens = q_ref.shape[0]
    head_dim = q_gain_ref.shape[1]
    bias = jnp.where(mask_ref[...] > 0, 0.0, MASKED_SCORE).astype(F32)
    for head in range(q_ref.shape[1] // head_dim):
        rows = q_ref[:, head * head_dim : (head + 1) * head_dim].astype(F32)
        normed = normalize(rows, q_gain_ref[...]) * head_dim ** (-0.5)
        qt_ref[:, head * tokens : (head + 1) * tokens] = normed.T.astype(BF16)
        bias_ref[:, head * tokens : (head + 1) * tokens] = bias


def start_copies(sources, targets, sems):
    copies = [
        pltpu.make_async_copy(a, b, sems.at[i]) for i, (a, b) in enumerate(zip(sources, targets))
    ]
    for copy in copies:
        copy.start()
    return copies


def own_kernel(head_dim, x_hbm, w_hbm, own_ref, x_ref, w_ref, sems):
    for copy in start_copies((x_hbm, w_hbm), (x_ref, w_ref), sems):
        copy.wait()
    store_heads(own_ref, 0, project(x_ref[0], w_ref[...]), head_dim)


def other_kernel(head_dim, x_ref, w_ref, other_ref):
    store_heads(other_ref, 0, project(x_ref[0], w_ref[...]), head_dim)


def query_kernel(
    q_hbm, q_gain_hbm, mask_hbm, k_gain_hbm, qt_ref, bias_ref, k_gain_ref,
    q_ref, q_gain_ref, mask_ref, sems,
):
    copies = start_copies(
        (q_hbm, q_gain_hbm, mask_hbm, k_gain_hbm), (q_ref, q_gain_ref, mask_ref, k_gain_ref), sems
    )
    prepare_queries(copies, q_ref, q_gain_ref, mask_ref, qt_ref, bias_ref)


def is_home():
    return lax.axis_index("tensor") // 2 == lax.axis_index("dp")


def away_kernel(head_dim, x_hbm, w_hbm, own_ref, x_ref, w_ref, sems):
    @pl.when(is_home())
    def _():
        own_ref[...] = jnp.zeros_like(own_ref)

    @pl.when(jnp.logical_not(is_home()))
    def _():
        own_kernel(head_dim, x_hbm, w_hbm, own_ref, x_ref, w_ref, sems)


def load_kernel(x_in, x_hbm, w_hbm, x_ref, w_ref, sems):
    @pl.when(is_home())
    def _():
        for copy in start_copies((x_hbm, w_hbm), (x_ref, w_ref), sems):
            copy.wait()


def home_kernel(head_dim, x_ref, w_other_ref, other_ref):
    @pl.when(is_home())
    def _():
        store_heads(other_ref, 0, project(x_ref[0], w_other_ref[...]), head_dim)

    @pl.when(jnp.logical_not(is_home()))
    def _():
        other_ref[...] = jnp.zeros_like(other_ref)


def keep_kernel(
    head_dim, after_ref, w_other_ref, x_ref, w_ref, q_hbm, q_gain_hbm, mask_hbm, k_gain_hbm,
    keep_ref, qt_ref, bias_ref, k_gain_ref, q_ref, q_gain_ref, mask_ref, sems,
):
    copies = start_copies(
        (q_hbm, q_gain_hbm, mask_hbm, k_gain_hbm), (q_ref, q_gain_ref, mask_ref, k_gain_ref), sems
    )

    @pl.when(is_home())
    def _():
        store_heads(keep_ref, 0, project(x_ref[0], w_ref[...]), head_dim)

    @pl.when(jnp.logical_not(is_home()))
    def _():
        store_heads(keep_ref, 0, project(x_ref[0], w_other_ref[...]), head_dim)

    prepare_queries(copies, q_ref, q_gain_ref, mask_ref, qt_ref, bias_ref)


def split_half(held, send_ref, keep_ref, partner_heads, own_heads):
    for i in range(send_ref.shape[0]):
        send_ref[i] = held[partner_heads + i]
        keep_ref[i] = held[own_heads + i]


def spread_kernel(n_dp, n_tensor, own_ref, *refs):
    others, (send_ref, keep_ref, held) = refs[: n_dp - 1], refs[n_dp - 1 :]
    d = lax.axis_index("dp")
    own_heads = own_ref.shape[0]
    for k, ref in enumerate((own_ref, *others)):
        held[pl.ds((d ^ k) * own_heads, own_heads)] = ref[...]
    half = send_ref.shape[0]
    upper = lax.axis_index("tensor") // (n_tensor // 2)
    split_half(held, send_ref, keep_ref, (1 - upper) * half, upper * half)


def pair_kernel(keep_ref, first_ref, second_ref, out_ref):
    arrived = jnp.where(is_home(), first_ref[...], second_ref[...]).astype(F32)
    out_ref[...] = (keep_ref[...].astype(F32) + arrived).astype(BF16)


def add_kernel(bit, keep_ref, arrived_ref, send_ref, next_ref, held):
    held[...] = (keep_ref[...].astype(F32) + arrived_ref[...].astype(F32)).astype(BF16)
    half = send_ref.shape[0]
    upper = (lax.axis_index("tensor") // bit) % 2
    split_half(held, send_ref, next_ref, (1 - upper) * half, upper * half)


def add_last_kernel(keep_ref, arrived_ref, out_ref):
    out_ref[...] = (keep_ref[...].astype(F32) + arrived_ref[...].astype(F32)).astype(BF16)


def finish_rows(k_gain, one, two):
    total = one[...].astype(F32) + two[...].astype(F32)
    head_dim = total.shape[1] // 2
    keys = normalize(total[:, :head_dim], k_gain).astype(BF16)
    return keys, total[:, head_dim:].astype(BF16)


def norm_kernel(k_gain_ref, keep_ref, arrived_ref, kv_ref):
    keys, values = finish_rows(k_gain_ref[...], keep_ref.at[0], arrived_ref.at[0])
    kv_ref[:, : keys.shape[1]] = keys
    kv_ref[:, keys.shape[1] :] = values


def attend_kernel(near, far, tile_len, first, last, head_dim, k_gain_ref, qt_ref, bias_ref, *refs):
    near_refs, refs = refs[: len(near)], refs[len(near) :]
    far_refs, refs = refs[: 2 * len(far)], refs[2 * len(far) :]
    if not first:
        top_in, sum_in, mixed_in = refs[:3]
        refs = refs[3:]
    s = lax.axis_index("section")
    qt = qt_ref[...]
    parts = [(part[:, :head_dim], part[:, head_dim:]) for part in near_refs]
    for one, two in zip(far_refs[::2], far_refs[1::2]):
        parts.append(finish_rows(k_gain_ref[...], one.at[0], two.at[0]))
    rows = parts[0][0].shape[0]
    scores, biases = [], []
    top = TOP_FLOOR if first else top_in[...]
    for step, (keys, _) in zip((*near, *far), parts):
        score = jnp.dot(keys, qt, preferred_element_type=F32)
        bias = bias_ref[pl.ds(((s ^ step) * rows) // tile_len, 1), :]
        scores.append(score)
        biases.append(bias)
        top = jnp.maximum(top, jnp.max(score, axis=0, keepdims=True) + bias)
    row_sum, mixed = 0.0, 0.0
    if not first:
        scale = jnp.exp(top_in[...] - top)
        row_sum = sum_in[...] * scale
        mixed = mixed_in[...] * scale
    for (_, values), score, bias in zip(parts, scores, biases):
        weights = jnp.exp(score + (bias - top))
        row_sum = row_sum + jnp.sum(weights, axis=0, keepdims=True)
        mixed = mixed + lax.dot_general(
            values, weights.astype(BF16), (((0,), (0,)), ((), ())), preferred_element_type=F32
        )
    if not last:
        top_out, sum_out, mixed_out = refs
        top_out[...] = top
        sum_out[...] = row_sum
        mixed_out[...] = mixed
        return
    (out,) = refs
    has_any = jnp.max(bias_ref[...], axis=0, keepdims=True) > -1.0
    inverse = jnp.where(has_any, 1.0 / jnp.where(has_any, row_sum, 1.0), 0.0)
    context = mixed * inverse
    tokens = out.shape[0]
    for head in range(out.shape[1] // head_dim):
        out[:, head * head_dim : (head + 1) * head_dim] = context[
            :, head * tokens : (head + 1) * tokens
        ].T.astype(BF16)


def swap(value, axis, k):
    return lax.ppermute(value, axis, [(i, i ^ k) for i in range(lax.axis_size(axis))])


def exchange_two_heads(value, home_sends):
    hops = []
    for d in range(2):
        for t in range(4):
            sends = (t // 2 == d) == home_sends
            hops.append((4 * d + t, 4 * d + (t ^ 2) if sends else 4 * (1 - d) + t))
    return lax.ppermute(value, ("dp", "tensor"), hops)


def sum_many_heads(own, others):
    n_dp, n_tensor = lax.axis_size("dp"), lax.axis_size("tensor")
    heads = own.shape[0] * n_dp
    half = shape_of((heads // 2, *own.shape[1:]))
    send, keep = call(
        functools.partial(spread_kernel, n_dp, n_tensor),
        [half, half],
        n_dp,
        "spread",
        scratch=[pltpu.VMEM((heads, *own.shape[1:]), BF16)],
    )(own, *others)
    bit = n_tensor // 2
    while bit > 1:
        arrived = swap(send, "tensor", bit)
        bit //= 2
        now = keep.shape
        if bit > 1:
            half = shape_of((now[0] // 2, *now[1:]))
            send, keep = call(
                functools.partial(add_kernel, bit),
                [half, half],
                2,
                "add_part",
                scratch=[pltpu.VMEM(now, BF16)],
            )(keep, arrived)
        else:
            keep = call(add_last_kernel, shape_of(now), 2, "add_pair")(keep, arrived)
    return keep


def on_device(queries, images, kv_weight, q_gain, k_gain, tile_mask):
    n_section = lax.axis_size("section")
    n_dp = lax.axis_size("dp")
    n_tensor = lax.axis_size("tensor")
    head_dim = q_gain.shape[0]
    tokens, q_width = queries.shape
    rows, features = images.shape[1:]
    tiles = tile_mask.shape[1]
    own_heads = kv_weight.shape[2] // head_dim
    heads = own_heads * n_dp
    tile_len = rows * n_section // tiles
    assert heads * 2 == n_tensor and tile_len % rows == 0 and n_section >= 4
    pairs = tokens * (q_width // head_dim)
    work = 4 * rows * features * kv_weight.shape[2]

    x, w, *small = [
        pltpu.with_memory_space_constraint(value, pltpu.HBM)
        for value in (
            images, kv_weight, queries, q_gain.reshape(1, -1), tile_mask.T, k_gain.reshape(1, -1),
        )
    ]
    product = shape_of((own_heads, rows, 2 * head_dim))
    w_scratch = pltpu.VMEM(kv_weight.shape, BF16)
    prepared = [
        shape_of((head_dim, pairs)),
        shape_of((tiles, pairs), F32),
        shape_of((1, head_dim), F32),
    ]
    query_scratch = [
        pltpu.VMEM(queries.shape, BF16),
        pltpu.VMEM((1, head_dim), F32),
        pltpu.VMEM((tiles, tokens), jnp.int32),
    ]
    others = [swap(kv_weight, "dp", k) for k in range(1, n_dp)]
    if n_dp == 2 and own_heads == 1:
        away, x_away = call(
            functools.partial(away_kernel, head_dim),
            [product, shape_of(images.shape)],
            2,
            "away_own",
            flops=work,
            in_specs=[HBM] * 2,
            scratch=[w_scratch, pltpu.SemaphoreType.DMA((2,))],
        )(x, w)
        first = exchange_two_heads(away, False)
        x_here, w_home = call(
            load_kernel,
            [shape_of(images.shape), shape_of(kv_weight.shape)],
            3,
            "home_load",
            in_specs=[VMEM] + [HBM] * 2,
            scratch=[pltpu.SemaphoreType.DMA((2,))],
            aliases={0: 0},
        )(x_away, x, w)
        home = call(
            functools.partial(home_kernel, head_dim), product, 2, "home_other", flops=work
        )(x_here, others[0])
        second = exchange_two_heads(home, True)
        keep, qt, bias, gain = call(
            functools.partial(keep_kernel, head_dim),
            [product, *prepared],
            8,
            "keep_queries",
            flops=work,
            in_specs=[VMEM] * 4 + [HBM] * 4,
            scratch=[*query_scratch, pltpu.SemaphoreType.DMA((4,))],
        )(home, others[0], x_here, w_home, *small)
        total = call(pair_kernel, product, 3, "pair_sum")(keep, first, second)
    else:
        own, x_here = call(
            functools.partial(own_kernel, head_dim),
            [product, shape_of(images.shape)],
            2,
            "own_heads",
            flops=work,
            in_specs=[HBM] * 2,
            scratch=[w_scratch, pltpu.SemaphoreType.DMA((2,))],
        )(x, w)
        qt, bias, gain = call(
            query_kernel,
            prepared,
            4,
            "queries",
            in_specs=[HBM] * 4,
            scratch=[*query_scratch, pltpu.SemaphoreType.DMA((4,))],
        )(*small)
        rest = [
            call(functools.partial(other_kernel, head_dim), product, 2, "other_heads", flops=work)(
                x_here, other
            )
            for other in others
        ]
        total = sum_many_heads(own, rest)
    far = [step for step in range(1, n_section) if step & (step - 1)]
    near = [step for step in range(1, n_section) if not step & (step - 1)]
    arrived = swap(total, "tensor", 1)
    halves = [swap(total, "section", step) for step in far]
    kv = call(norm_kernel, shape_of((rows, 2 * head_dim)), 3, "sum_norm")(gain, total, arrived)
    finished = [swap(kv, "section", step) for step in near]
    both = []
    for value in halves:
        both += [value, swap(value, "tensor", 1)]
    state = []
    for here, there, operands in (
        ([0], [], [kv]),
        (near, [], finished),
        ([], far, both),
    ):
        first, last = here == [0], len(there) > 0
        outs = (
            shape_of((tokens, q_width))
            if last
            else [shape_of((1, pairs), F32), shape_of((1, pairs), F32), shape_of((head_dim, pairs), F32)]
        )
        parts = len(here) + len(there)
        state = call(
            functools.partial(attend_kernel, here, there, tile_len, first, last, head_dim),
            outs,
            3 + len(operands) + len(state),
            "attend",
            flops=4 * pairs * rows * head_dim * parts,
            exps=pairs * rows * parts,
        )(gain, qt, bias, *operands, *state)
    return state


def solution(mesh):
    in_specs = (
        P(("section", "dp"), "tensor"),
        P("dp", "section", "tensor"),
        P(None, "tensor", "dp"),
        P(),
        P(),
        P(("section", "dp"), None),
    )
    out_specs = P(("section", "dp"), "tensor")
    return jax.shard_map(
        on_device, mesh=mesh, in_specs=in_specs, out_specs=out_specs, check_vma=False
    )
```

```python
import functools

import jax
import jax.numpy as jnp
from jax import lax
from jax.experimental import pallas as pl
from jax.experimental.pallas import tpu as pltpu
from jax.sharding import PartitionSpec as P

EPSILON = 1e-05
MASKED_SCORE = -1e30
TOP_FLOOR = -1e29
VMEM = pl.BlockSpec(memory_space=pltpu.VMEM)
HBM = pl.BlockSpec(memory_space=pltpu.HBM)
F32 = jnp.float32
MIB = 1024 * 1024
LIMIT = 24 * MIB
BF16 = jnp.bfloat16


def shape_of(dims, dtype=BF16):
    return jax.ShapeDtypeStruct(dims, dtype)


def call(
    kernel, outs, n_in, name, flops=0, size=0, exps=0, in_specs=None, scratch=(), aliases=None
):
    many = isinstance(outs, list)
    return pl.pallas_call(
        kernel,
        out_shape=outs,
        in_specs=in_specs or [VMEM] * n_in,
        out_specs=[VMEM] * len(outs) if many else VMEM,
        scratch_shapes=scratch,
        input_output_aliases=aliases or {},
        compiler_params=pltpu.CompilerParams(vmem_limit_bytes=LIMIT),
        cost_estimate=pl.CostEstimate(flops=flops, bytes_accessed=size, transcendentals=exps),
        name=name,
    )


def normalize(values, gain_vec):
    mean_sq = jnp.mean(values * values, axis=-1, keepdims=True)
    return values * lax.rsqrt(mean_sq + EPSILON) * gain_vec


def project(x, w):
    return jnp.dot(
        x, jnp.concatenate([w[0], w[1]], axis=1), preferred_element_type=F32
    ).astype(BF16)


def store_heads(ref, base, both, head_dim):
    width = both.shape[1] // 2
    for head in range(width // head_dim):
        lo = head * head_dim
        ref[base + head, :, :head_dim] = both[:, lo : lo + head_dim]
        ref[base + head, :, head_dim:] = both[:, width + lo : width + lo + head_dim]


def prepare_queries(copies, q_ref, q_gain_ref, mask_ref, qt_ref, bias_ref):
    for copy in copies:
        copy.wait()
    tokens = q_ref.shape[0]
    head_dim = q_gain_ref.shape[1]
    bias = jnp.where(mask_ref[...] > 0, 0.0, MASKED_SCORE).astype(F32)
    for head in range(q_ref.shape[1] // head_dim):
        rows = q_ref[:, head * head_dim : (head + 1) * head_dim].astype(F32)
        normed = normalize(rows, q_gain_ref[...]) * head_dim ** (-0.5)
        qt_ref[:, head * tokens : (head + 1) * tokens] = normed.T.astype(BF16)
        bias_ref[:, head * tokens : (head + 1) * tokens] = bias


def start_copies(sources, targets, sems):
    copies = [
        pltpu.make_async_copy(a, b, sems.at[i]) for i, (a, b) in enumerate(zip(sources, targets))
    ]
    for copy in copies:
        copy.start()
    return copies


def own_kernel(head_dim, x_hbm, w_hbm, own_ref, x_ref, w_ref, sems):
    for copy in start_copies((x_hbm, w_hbm), (x_ref, w_ref), sems):
        copy.wait()
    store_heads(own_ref, 0, project(x_ref[0], w_ref[...]), head_dim)


def other_kernel(head_dim, x_ref, w_ref, other_ref):
    store_heads(other_ref, 0, project(x_ref[0], w_ref[...]), head_dim)


def query_kernel(
    q_hbm, q_gain_hbm, mask_hbm, k_gain_hbm, qt_ref, bias_ref, k_gain_ref,
    q_ref, q_gain_ref, mask_ref, sems,
):
    copies = start_copies(
        (q_hbm, q_gain_hbm, mask_hbm, k_gain_hbm), (q_ref, q_gain_ref, mask_ref, k_gain_ref), sems
    )
    prepare_queries(copies, q_ref, q_gain_ref, mask_ref, qt_ref, bias_ref)


def is_home():
    return lax.axis_index("tensor") // 2 == lax.axis_index("dp")


def away_kernel(head_dim, x_hbm, w_hbm, own_ref, x_ref, w_ref, sems):
    @pl.when(is_home())
    def _():
        own_ref[...] = jnp.zeros_like(own_ref)

    @pl.when(jnp.logical_not(is_home()))
    def _():
        own_kernel(head_dim, x_hbm, w_hbm, own_ref, x_ref, w_ref, sems)


def load_kernel(x_in, x_hbm, w_hbm, x_ref, w_ref, sems):
    @pl.when(is_home())
    def _():
        for copy in start_copies((x_hbm, w_hbm), (x_ref, w_ref), sems):
            copy.wait()


def home_kernel(head_dim, x_ref, w_other_ref, other_ref):
    @pl.when(is_home())
    def _():
        store_heads(other_ref, 0, project(x_ref[0], w_other_ref[...]), head_dim)

    @pl.when(jnp.logical_not(is_home()))
    def _():
        other_ref[...] = jnp.zeros_like(other_ref)


def keep_kernel(
    head_dim, after_ref, w_other_ref, x_ref, w_ref, q_hbm, q_gain_hbm, mask_hbm, k_gain_hbm,
    keep_ref, qt_ref, bias_ref, k_gain_ref, q_ref, q_gain_ref, mask_ref, sems,
):
    copies = start_copies(
        (q_hbm, q_gain_hbm, mask_hbm, k_gain_hbm), (q_ref, q_gain_ref, mask_ref, k_gain_ref), sems
    )

    @pl.when(is_home())
    def _():
        store_heads(keep_ref, 0, project(x_ref[0], w_ref[...]), head_dim)

    @pl.when(jnp.logical_not(is_home()))
    def _():
        store_heads(keep_ref, 0, project(x_ref[0], w_other_ref[...]), head_dim)

    prepare_queries(copies, q_ref, q_gain_ref, mask_ref, qt_ref, bias_ref)


def split_half(held, send_ref, keep_ref, partner_heads, own_heads):
    for i in range(send_ref.shape[0]):
        send_ref[i] = held[partner_heads + i]
        keep_ref[i] = held[own_heads + i]


def spread_kernel(n_dp, n_tensor, own_ref, *refs):
    others, (send_ref, keep_ref, held) = refs[: n_dp - 1], refs[n_dp - 1 :]
    d = lax.axis_index("dp")
    own_heads = own_ref.shape[0]
    for k, ref in enumerate((own_ref, *others)):
        held[pl.ds((d ^ k) * own_heads, own_heads)] = ref[...]
    half = send_ref.shape[0]
    upper = lax.axis_index("tensor") // (n_tensor // 2)
    split_half(held, send_ref, keep_ref, (1 - upper) * half, upper * half)


def pair_kernel(keep_ref, first_ref, second_ref, out_ref):
    arrived = jnp.where(is_home(), first_ref[...], second_ref[...]).astype(F32)
    out_ref[...] = (keep_ref[...].astype(F32) + arrived).astype(BF16)


def add_kernel(bit, keep_ref, arrived_ref, send_ref, next_ref, held):
    held[...] = (keep_ref[...].astype(F32) + arrived_ref[...].astype(F32)).astype(BF16)
    half = send_ref.shape[0]
    upper = (lax.axis_index("tensor") // bit) % 2
    split_half(held, send_ref, next_ref, (1 - upper) * half, upper * half)


def add_last_kernel(keep_ref, arrived_ref, out_ref):
    out_ref[...] = (keep_ref[...].astype(F32) + arrived_ref[...].astype(F32)).astype(BF16)


def finish_rows(k_gain, one, two):
    total = one[...].astype(F32) + two[...].astype(F32)
    head_dim = total.shape[1] // 2
    keys = normalize(total[:, :head_dim], k_gain).astype(BF16)
    return keys, total[:, head_dim:].astype(BF16)


def norm_kernel(k_gain_ref, keep_ref, arrived_ref, kv_ref):
    keys, values = finish_rows(k_gain_ref[...], keep_ref.at[0], arrived_ref.at[0])
    kv_ref[:, : keys.shape[1]] = keys
    kv_ref[:, keys.shape[1] :] = values


def attend_kernel(near, far, tile_len, first, last, head_dim, k_gain_ref, qt_ref, bias_ref, *refs):
    near_refs, refs = refs[: len(near)], refs[len(near) :]
    far_refs, refs = refs[: 2 * len(far)], refs[2 * len(far) :]
    if not first:
        top_in, sum_in, mixed_in = refs[:3]
        refs = refs[3:]
    s = lax.axis_index("section")
    qt = qt_ref[...]
    parts = [(part[:, :head_dim], part[:, head_dim:]) for part in near_refs]
    for one, two in zip(far_refs[::2], far_refs[1::2]):
        parts.append(finish_rows(k_gain_ref[...], one.at[0], two.at[0]))
    rows = parts[0][0].shape[0]
    scores, biases = [], []
    top = TOP_FLOOR if first else top_in[...]
    for step, (keys, _) in zip((*near, *far), parts):
        score = jnp.dot(keys, qt, preferred_element_type=F32)
        bias = bias_ref[pl.ds(((s ^ step) * rows) // tile_len, 1), :]
        scores.append(score)
        biases.append(bias)
        top = jnp.maximum(top, jnp.max(score, axis=0, keepdims=True) + bias)
    row_sum, mixed = 0.0, 0.0
    if not first:
        scale = jnp.exp(top_in[...] - top)
        row_sum = sum_in[...] * scale
        mixed = mixed_in[...] * scale
    for (_, values), score, bias in zip(parts, scores, biases):
        weights = jnp.exp(score + (bias - top))
        row_sum = row_sum + jnp.sum(weights, axis=0, keepdims=True)
        mixed = mixed + lax.dot_general(
            values, weights.astype(BF16), (((0,), (0,)), ((), ())), preferred_element_type=F32
        )
    if not last:
        top_out, sum_out, mixed_out = refs
        top_out[...] = top
        sum_out[...] = row_sum
        mixed_out[...] = mixed
        return
    (out,) = refs
    has_any = jnp.max(bias_ref[...], axis=0, keepdims=True) > -1.0
    inverse = jnp.where(has_any, 1.0 / jnp.where(has_any, row_sum, 1.0), 0.0)
    context = (mixed * inverse).astype(BF16)
    tokens = out.shape[0]
    for head in range(out.shape[1] // head_dim):
        out[:, head * head_dim : (head + 1) * head_dim] = context[
            :, head * tokens : (head + 1) * tokens
        ].T


def swap(value, axis, k):
    return lax.ppermute(value, axis, [(i, i ^ k) for i in range(lax.axis_size(axis))])


def exchange_two_heads(value, home_sends):
    hops = []
    for d in range(2):
        for t in range(4):
            sends = (t // 2 == d) == home_sends
            hops.append((4 * d + t, 4 * d + (t ^ 2) if sends else 4 * (1 - d) + t))
    return lax.ppermute(value, ("dp", "tensor"), hops)


def sum_many_heads(own, others):
    n_dp, n_tensor = lax.axis_size("dp"), lax.axis_size("tensor")
    heads = own.shape[0] * n_dp
    half = shape_of((heads // 2, *own.shape[1:]))
    send, keep = call(
        functools.partial(spread_kernel, n_dp, n_tensor),
        [half, half],
        n_dp,
        "spread",
        scratch=[pltpu.VMEM((heads, *own.shape[1:]), BF16)],
    )(own, *others)
    bit = n_tensor // 2
    while bit > 1:
        arrived = swap(send, "tensor", bit)
        bit //= 2
        now = keep.shape
        if bit > 1:
            half = shape_of((now[0] // 2, *now[1:]))
            send, keep = call(
                functools.partial(add_kernel, bit),
                [half, half],
                2,
                "add_part",
                scratch=[pltpu.VMEM(now, BF16)],
            )(keep, arrived)
        else:
            keep = call(add_last_kernel, shape_of(now), 2, "add_pair")(keep, arrived)
    return keep


def on_device(queries, images, kv_weight, q_gain, k_gain, tile_mask):
    n_section = lax.axis_size("section")
    n_dp = lax.axis_size("dp")
    n_tensor = lax.axis_size("tensor")
    head_dim = q_gain.shape[0]
    tokens, q_width = queries.shape
    rows, features = images.shape[1:]
    tiles = tile_mask.shape[1]
    own_heads = kv_weight.shape[2] // head_dim
    heads = own_heads * n_dp
    tile_len = rows * n_section // tiles
    assert heads * 2 == n_tensor and tile_len % rows == 0 and n_section >= 4
    pairs = tokens * (q_width // head_dim)
    work = 4 * rows * features * kv_weight.shape[2]

    x, w, *small = [
        pltpu.with_memory_space_constraint(value, pltpu.HBM)
        for value in (
            images, kv_weight, queries, q_gain.reshape(1, -1), tile_mask.T, k_gain.reshape(1, -1),
        )
    ]
    product = shape_of((own_heads, rows, 2 * head_dim))
    w_scratch = pltpu.VMEM(kv_weight.shape, BF16)
    prepared = [
        shape_of((head_dim, pairs)),
        shape_of((tiles, pairs), F32),
        shape_of((1, head_dim), F32),
    ]
    query_scratch = [
        pltpu.VMEM(queries.shape, BF16),
        pltpu.VMEM((1, head_dim), F32),
        pltpu.VMEM((tiles, tokens), jnp.int32),
    ]
    others = [swap(kv_weight, "dp", k) for k in range(1, n_dp)]
    if n_dp == 2 and own_heads == 1:
        away, x_away = call(
            functools.partial(away_kernel, head_dim),
            [product, shape_of(images.shape)],
            2,
            "away_own",
            flops=work,
            in_specs=[HBM] * 2,
            scratch=[w_scratch, pltpu.SemaphoreType.DMA((2,))],
        )(x, w)
        first = exchange_two_heads(away, False)
        x_here, w_home = call(
            load_kernel,
            [shape_of(images.shape), shape_of(kv_weight.shape)],
            3,
            "home_load",
            in_specs=[VMEM] + [HBM] * 2,
            scratch=[pltpu.SemaphoreType.DMA((2,))],
            aliases={0: 0},
        )(x_away, x, w)
        home = call(
            functools.partial(home_kernel, head_dim), product, 2, "home_other", flops=work
        )(x_here, others[0])
        second = exchange_two_heads(home, True)
        keep, qt, bias, gain = call(
            functools.partial(keep_kernel, head_dim),
            [product, *prepared],
            8,
            "keep_queries",
            flops=work,
            in_specs=[VMEM] * 4 + [HBM] * 4,
            scratch=[*query_scratch, pltpu.SemaphoreType.DMA((4,))],
        )(home, others[0], x_here, w_home, *small)
        total = call(pair_kernel, product, 3, "pair_sum")(keep, first, second)
    else:
        own, x_here = call(
            functools.partial(own_kernel, head_dim),
            [product, shape_of(images.shape)],
            2,
            "own_heads",
            flops=work,
            in_specs=[HBM] * 2,
            scratch=[w_scratch, pltpu.SemaphoreType.DMA((2,))],
        )(x, w)
        qt, bias, gain = call(
            query_kernel,
            prepared,
            4,
            "queries",
            in_specs=[HBM] * 4,
            scratch=[*query_scratch, pltpu.SemaphoreType.DMA((4,))],
        )(*small)
        rest = [
            call(functools.partial(other_kernel, head_dim), product, 2, "other_heads", flops=work)(
                x_here, other
            )
            for other in others
        ]
        total = sum_many_heads(own, rest)
    far = [step for step in range(1, n_section) if step & (step - 1)]
    near = [step for step in range(1, n_section) if not step & (step - 1)]
    arrived = swap(total, "tensor", 1)
    halves = [swap(total, "section", step) for step in far]
    kv = call(norm_kernel, shape_of((rows, 2 * head_dim)), 3, "sum_norm")(gain, total, arrived)
    finished = [swap(kv, "section", step) for step in near]
    both = []
    for value in halves:
        both += [value, swap(value, "tensor", 1)]
    state = []
    for here, there, operands in (
        ([0], [], [kv]),
        *(([step], [], [part]) for step, part in zip(near, finished)),
        ([], far, both),
    ):
        first, last = here == [0], len(there) > 0
        outs = (
            shape_of((tokens, q_width))
            if last
            else [shape_of((1, pairs), F32), shape_of((1, pairs), F32), shape_of((head_dim, pairs), F32)]
        )
        parts = len(here) + len(there)
        state = call(
            functools.partial(attend_kernel, here, there, tile_len, first, last, head_dim),
            outs,
            3 + len(operands) + len(state),
            "attend",
            flops=4 * pairs * rows * head_dim * parts,
            exps=pairs * rows * parts,
        )(gain, qt, bias, *operands, *state)
    return state


def solution(mesh):
    in_specs = (
        P(("section", "dp"), "tensor"),
        P("dp", "section", "tensor"),
        P(None, "tensor", "dp"),
        P(),
        P(),
        P(("section", "dp"), None),
    )
    out_specs = P(("section", "dp"), "tensor")
    return jax.shard_map(
        on_device, mesh=mesh, in_specs=in_specs, out_specs=out_specs, check_vma=False
    )
```
